32 devices in a mesh: dp: 8 (over z, x), expert: 4 (over y, core).
Axes of the slice: x: 2, y: 2, z: 4, core: 2. Of those that a mesh axis runs over, the one named last changes fastest.
Arguments:
- tokens: bfloat16 [16384, 768], P(('dp', 'expert')), may hold values from -6 to 6
- qkv_weight: bfloat16 [3, 768, 768], P(None, 'dp'), may hold values from -0.21875 to 0.21875
- out_weight: bfloat16 [768, 768], P('dp'), may hold values from -1.75 to 1.75
- position_bias_table: float32 [12, 32], replicated, may hold values from -3 to 3
- gain_attn: float32 [768], replicated, may hold values from 0.5 to 1.5
- gain_moe: float32 [768], replicated, may hold values from 0.5 to 1.5
- router: bfloat16 [768, 8], replicated, may hold values from -0.15625 to 0.15625
- w_in: bfloat16 [8, 768, 3072], P('expert'), may hold values from -0.21875 to 0.21875
- w_out: bfloat16 [8, 3072, 768], P('expert'), may hold values from -0.109375 to 0.109375
- routes: int32 [16384, 2], P(('dp', 'expert')), may hold values from 0 to 7, all different within a row; in each aligned block of 512 rows (0 to 511, 512 to 1023, ...) at most 160 rows name the same one
- prefix: int32 [32], P(('dp', 'expert')), may hold values from 51 to 256
- valid_mask: int32 [16384], P(('dp', 'expert')), may hold values from 0 to 1, as said below
- teacher: bfloat16 [16384, 768], P(('dp', 'expert')), may hold values from -6 to 6
- cotangent: bfloat16 [16384, 768], P(('dp', 'expert')), may hold values from -6 to 6
Outputs:
- output: bfloat16 [16384, 768], P(('dp', 'expert'))
- distill_loss: float32 [], replicated
- grad_input: float32 [16384, 768], P(('dp', 'expert'))
- grad_qkv: float32 [3, 768, 768], P(None, 'dp')
- grad_out_weight: float32 [768, 768], P('dp')
- grad_w_in: float32 [8, 768, 3072], P('expert', 'dp')
- grad_w_out: float32 [8, 3072, 768], P('expert', 'dp')
- grad_router: float32 [768, 8], replicated
- grad_table: float32 [12, 32], replicated
- grad_gain_attn: float32 [768], replicated
- grad_gain_moe: float32 [768], replicated
The draws below stay inside these ranges and needn't reach their ends.
Inputs may be any that keep to these rules, and one draw needn't show every extreme that they name: `routes`: each row names 2 different experts. Among the 512 rows of one device no expert is named more than 160 times, a bound that some block reaches. `valid_mask`: the first token of every sequence is valid.
All inputs are finite; a program needn't handle non-finite values.
Results may differ from the reference program's by a relative error of at most 0.015.
Values may be sent and summed in bfloat16 or wider, within the bound.
No kernel may reach another device: no remote copies, remote signals or barrier semaphores. Data moves between devices by JAX's collectives and lax.ppermute only.
A program may use at most 192 MiB of HBM per device.

```python
import math
import jax
import jax.numpy as jnp
import numpy as np
from jax import lax

D = 768
HEADS = 12
HEAD_DIM = 64
FF = 3072
TOP = 2
BUCKETS = 32
TOK_DEV = 512
EXPERTS = 8
SEQS = 32
TOKENS = 16384
CAP = 160


def draw_valid_mask(key, part):
    key = jax.random.fold_in(key, 5)
    draws_int = jax.random.randint(key, (TOKENS,), 0, 1000)
    positions = jnp.arange(TOKENS, dtype=jnp.int32)
    seq_ids = positions // TOK_DEV
    keep_level = 250 + 500 * seq_ids // max(SEQS - 1, 1)
    first_position = positions % TOK_DEV == 0
    return jnp.where(first_position | (draws_int < keep_level), 1, 0).astype(jnp.int32)


def place_ends(entries, rng, low, largest):
    spot = [jax.random.randint(jax.random.fold_in(rng, axis), (), 0, length) for axis, length in enumerate(entries.shape)]
    longest = entries.shape.index(max(entries.shape))
    next_to = spot[:longest] + [(spot[longest] + 1) % entries.shape[longest]] + spot[longest + 1:]
    return entries.at[tuple(spot)].set(low).at[tuple(next_to)].set(largest)


def block_levels(key, shape, cuts, smallest, largest):
    def one(dim, blocks):
        draws = jax.random.uniform(jax.random.fold_in(jax.random.fold_in(key, 6), dim), (blocks,), jnp.float32, smallest / len(cuts), largest / len(cuts))
        return jnp.repeat(jnp.exp(draws), shape[dim] // blocks).reshape((-1,) + (1,) * (len(shape) - dim - 1))

    level = one(*cuts[0])
    for cut in cuts[1:]:
        level = level * one(*cut)
    return level


def deal_out(own_key, own, number, rows, count, top, bound, slope):
    order = jax.random.permutation(own_key, count)
    heavy_load, usual = portions_of(count, rows * top, bound, slope, True), portions_of(count, rows * top, bound, slope, False)
    places = jnp.arange(count)

    def named(tallies, offset_by):
        used = int((tallies > 0).sum())
        fixed = max(1, used // 4)
        passed = fixed + (places - fixed + offset_by * (used - fixed)) % max(1, count - fixed)
        return jnp.zeros((count,), jnp.int32).at[order[jnp.where(places < fixed, places, passed)]].set(jnp.asarray(tallies, jnp.int32))

    tallies = jnp.where(number % 4 == 0, named(heavy_load, number // 4), named(usual, number - number // 4 - 1))
    mixed = jax.random.permutation(jax.random.fold_in(own, 3), count)
    donor, taker = mixed[0:count // 2 * 2:2], mixed[1:count // 2 * 2:2]
    room = jnp.minimum(tallies[donor] - 1, bound - tallies[taker]) // 2
    room = jnp.where((donor == order[0]) | (taker == order[0]) | (tallies[taker] == 0), 0, jnp.maximum(room, 0))
    passed = jax.random.randint(jax.random.fold_in(own, 4), (count // 2,), 0, 1 << 20) % (room + 1)
    tallies = tallies.at[donor].add(-passed).at[taker].add(passed)
    labels = jnp.searchsorted(jnp.cumsum(tallies), jnp.arange(rows * top), side="right").astype(jnp.int32)
    table = labels.reshape(top, rows).T
    table = table[jax.random.permutation(jax.random.fold_in(own, 1), rows)]
    offset_by = jax.random.randint(jax.random.fold_in(own, 2), (rows, 1), 0, top)
    return jnp.take_along_axis(table, (jnp.arange(top)[None, :] + offset_by) % top, axis=1)


def portions_of(amount, total, most, lean, full):
    weights = [(1 << 20) // math.isqrt(standing ** lean) + 1 for standing in range(1, amount + 1)]
    largest = most if full else min(most, max(-(-total // amount), total * weights[0] // sum(weights)))
    least = 1 if total - largest >= amount - 1 else 0
    given, surplus = [largest] + [least] * (amount - 1), total - largest - least * (amount - 1)
    while surplus > 0:
        free = [i for i in range(1, amount) if given[i] < largest] or [i for i in range(1, amount) if given[i] < most]
        pool, remaining = sum([weights[i] for i in free]), surplus
        for i in free:
            extra = min(most - given[i], max(1, remaining * weights[i] // pool), surplus)
            given[i] = given[i] + extra
            surplus = surplus - extra
    return np.array(given)


def bell_draw(stream_key, shape, deviation, most, cuts=(), kind=jnp.bfloat16):
    result = jax.random.normal(stream_key, shape, jnp.float32) * deviation
    if len(cuts) > 0:
        result = block_levels(stream_key, shape, cuts, -0.22, 0.18) * result
    return jnp.clip(result, min=-most, max=most).astype(kind)


def setup_inputs(seed: int = 0) -> dict:
    key_list = jax.random.split(jax.random.key(seed), 15)
    tokens = bell_draw(key_list[0], (TOKENS, D), 1.0, 6.0, ((0, 32),))
    qkv_weight = bell_draw(key_list[1], (3, D, D), D ** -0.5, 0.21875, ((1, 8),))
    out_weight = bell_draw(key_list[2], (D, D), (D // 64) ** -0.5, 1.75, ((0, 8),))
    position_bias_table = bell_draw(key_list[3], (HEADS, BUCKETS), 0.5, 3.0, (), jnp.float32)
    gain_attn = jnp.clip(1.0 + 0.1 * jax.random.normal(key_list[4], (D,), jnp.float32), 0.5, 1.5)
    gain_moe = jnp.clip(1.0 + 0.1 * jax.random.normal(key_list[5], (D,), jnp.float32), 0.5, 1.5)
    router = bell_draw(key_list[6], (D, EXPERTS), (2 * D) ** -0.5, 0.15625)
    w_in = bell_draw(key_list[7], (EXPERTS, D, FF), D ** -0.5, 0.21875, ((0, 4),))
    w_out = bell_draw(key_list[8], (EXPERTS, FF, D), FF ** -0.5, 0.109375, ((0, 4),))
    routes_keys = jax.random.split(jax.random.fold_in(key_list[9], 1), TOKENS // TOK_DEV)
    routes_turns = jax.random.permutation(jax.random.fold_in(key_list[9], 3), TOKENS // TOK_DEV)
    routes = jax.vmap(lambda own, number: deal_out(jax.random.fold_in(key_list[9], 2), own, number, TOK_DEV, EXPERTS, TOP, CAP, 2))(routes_keys, routes_turns).reshape((TOKENS, TOP))
    prefix = place_ends(jax.random.randint(key_list[10], (SEQS,), TOK_DEV // 10, TOK_DEV // 2 + 1), jax.random.fold_in(key_list[10], 1), TOK_DEV // 10, (TOK_DEV // 2 + 1) - 1).astype(jnp.int32)
    valid_mask = draw_valid_mask(jax.random.fold_in(key_list[14], 71), 0)
    teacher = bell_draw(key_list[12], (TOKENS, D), 1.0, 6.0, ((0, 32),))
    cotangent = bell_draw(key_list[13], (TOKENS, D), 1.0, 6.0, ((0, 32),))
    return {"tokens": tokens, "qkv_weight": qkv_weight, "out_weight": out_weight, "position_bias_table": position_bias_table, "gain_attn": gain_attn, "gain_moe": gain_moe, "router": router, "w_in": w_in, "w_out": w_out, "routes": routes, "prefix": prefix, "valid_mask": valid_mask, "teacher": teacher, "cotangent": cotangent}


@jax.custom_vjp
def low(v):
    return lax.optimization_barrier(v.astype(jnp.bfloat16)).astype(jnp.float32)

@jax.custom_vjp
def low_back(v):
    return v

def low_keep(v):
    return (low(v), None)

def low_pass(kept, grad):
    return (grad,)

def back_keep(v):
    return (v, None)

def back_low(kept, grad):
    return (low(grad),)
low.defvjp(low_keep, low_pass)
low_back.defvjp(back_keep, back_low)
EPS = 1e-06
BOUNDS = (12, 16, 23, 32, 46, 64, 91)
TOP_PRECISION = lax.Precision.HIGHEST

def bucket_index(offset):
    distance = jnp.abs(offset)
    far_bucket = 8 + sum([(distance >= cutoff_level).astype(jnp.int32) for cutoff_level in BOUNDS])
    near_bucket = jnp.where(distance < 8, distance, far_bucket)
    return jnp.where(offset > 0, 16, 0) + near_bucket

def norm_apply(inputs, gain_vec):
    return inputs * lax.rsqrt(lax.optimization_barrier(jnp.mean(inputs * inputs, axis=-1, keepdims=True)) + EPS) * gain_vec

def gate_values(logits, routes):
    soft_probs = jax.nn.softmax(logits, axis=-1)
    picked_hot = (routes[:, :, None] == jnp.arange(logits.shape[1], dtype=jnp.int32)[None, None, :]).astype(jnp.float32)
    chosen = lax.optimization_barrier(jnp.sum(soft_probs[:, None, :] * picked_hot, axis=-1))
    return chosen / lax.optimization_barrier(jnp.sum(chosen, axis=1, keepdims=True))

def attend_sequence(queries, key_rows, values, position_bias_table, prefix_len):
    length = queries.shape[0]
    block_rows = min(512, length)
    score_scale = 1.0 / math.sqrt(HEAD_DIM)

    def one_block(row_start):
        q_rows = lax.dynamic_slice_in_dim(queries, row_start, block_rows, 0)
        row_ids = row_start + lax.broadcasted_iota(jnp.int32, (block_rows, length), 0)
        col_ids = lax.broadcasted_iota(jnp.int32, (block_rows, length), 1)
        pos_bias = position_bias_table[:, bucket_index(col_ids - row_ids)]
        raw_scores = low_back(jnp.einsum('qhd,khd->hqk', q_rows, key_rows, precision=TOP_PRECISION) * score_scale + pos_bias)
        visible = ((col_ids <= row_ids) | (col_ids < prefix_len))[None]
        masked = jnp.where(visible, raw_scores, -1e+30)
        row_peak = lax.optimization_barrier(jnp.max(masked, axis=-1, keepdims=True))
        expo_terms = jnp.where(visible, jnp.exp(masked - row_peak), 0.0)
        row_total = lax.optimization_barrier(jnp.sum(expo_terms, axis=-1, keepdims=True))
        weights = low(expo_terms / row_total)
        return jnp.einsum('hqk,khd->qhd', weights, values, precision=TOP_PRECISION)
    starts = jnp.arange(length // block_rows, dtype=jnp.int32) * block_rows
    pieces = lax.map(jax.checkpoint(one_block), starts)
    return pieces.reshape(length, HEADS, HEAD_DIM)

def forward(tokens, qkv_weight, out_weight, position_bias_table, gain_attn, gain_moe, router, w_in, w_out, routes, prefix, valid_mask, teacher):
    normed1 = low(norm_apply(tokens, gain_attn))
    qkv = low_back(low(jnp.einsum('td,cde->cte', normed1, qkv_weight, precision=TOP_PRECISION)))
    shaped = qkv.reshape(3, SEQS, TOK_DEV, HEADS, HEAD_DIM)

    def per_sequence(packed):
        return attend_sequence(packed[0], packed[1], packed[2], position_bias_table, packed[3])
    attended = lax.map(per_sequence, (shaped[0], shaped[1], shaped[2], prefix))
    attended = low_back(low(attended.reshape(TOKENS, D)))
    middle = tokens + low_back(jnp.dot(attended, out_weight, precision=TOP_PRECISION))
    normed2 = low(norm_apply(middle, gain_moe))
    logits = low_back(jnp.dot(normed2, router, precision=TOP_PRECISION))
    gate_vals = gate_values(logits, routes)
    flat_routes = routes.reshape(SEQS, TOK_DEV * TOP)
    route_hits = (flat_routes[:, :, None] == jnp.arange(EXPERTS, dtype=jnp.int32)[None, None, :]).astype(jnp.int32)
    pair_rank = lax.optimization_barrier(jnp.sum((jnp.cumsum(route_hits, axis=1) - 1) * route_hits, axis=-1))
    source_ids = jnp.arange(SEQS, dtype=jnp.int32)[:, None]
    slot_of_pair = ((source_ids * EXPERTS + flat_routes) * CAP + pair_rank).reshape(-1).astype(jnp.int32)
    pair_count = TOKENS * TOP
    slot_pair = jnp.full((SEQS * EXPERTS * CAP,), pair_count, jnp.int32).at[slot_of_pair].set(jnp.arange(pair_count, dtype=jnp.int32))
    slot_token = jnp.where(slot_pair < pair_count, slot_pair // TOP, TOKENS).astype(jnp.int32)
    padded = jnp.concatenate([normed2, jnp.zeros((1, D), jnp.float32)], axis=0)
    expert_rows = low_back(padded[slot_token])
    expert_rows = expert_rows.reshape(SEQS, EXPERTS, CAP, D).transpose(1, 0, 2, 3).reshape(EXPERTS, SEQS * CAP, D)

    def one_expert(packed):
        rows_in, first_w, second_w = packed
        pre_act = low_back(jnp.dot(rows_in, first_w, precision=TOP_PRECISION))
        hidden = low(jax.nn.gelu(pre_act, approximate=True))
        return low_back(low(jnp.dot(hidden, second_w, precision=TOP_PRECISION)))
    produced = lax.map(jax.checkpoint(one_expert), (expert_rows, w_in, w_out))
    produced = produced.reshape(EXPERTS, SEQS, CAP, D).transpose(1, 0, 2, 3).reshape(-1, D)
    picked = produced[slot_of_pair].reshape(TOKENS, TOP, D)
    output = middle + lax.optimization_barrier(jnp.sum(gate_vals[:, :, None] * picked, axis=1))
    misfit = output - teacher
    valid_rows = valid_mask.astype(jnp.float32)[:, None]
    valid_count = jnp.sum(valid_mask.astype(jnp.float32))
    loss_value = jnp.sum(valid_rows * misfit * misfit) / (D * valid_count)
    return (output, loss_value)

def reference(tokens, qkv_weight, out_weight, position_bias_table, gain_attn, gain_moe, router, w_in, w_out, routes, prefix, valid_mask, teacher, cotangent):
    floats = [array.astype(jnp.float32) for array in (tokens, qkv_weight, out_weight, position_bias_table, gain_attn, gain_moe, router, w_in, w_out)]
    teacher_f = teacher.astype(jnp.float32)

    def objective(*params):
        return forward(*params, routes, prefix, valid_mask, teacher_f)
    (output, loss_value), pullback = jax.vjp(objective, *floats)
    weight_loss = jnp.asarray(TOKENS * D / 2, dtype=jnp.float32)
    grads = pullback((cotangent.astype(jnp.float32), weight_loss))
    return (output.astype(jnp.bfloat16), loss_value, grads[0], grads[1], grads[2], grads[7], grads[8], grads[6], grads[3], grads[4], grads[5])
```

```python
import math
import jax
import jax.numpy as jnp
from jax import lax
from jax.experimental import pallas as pl
from jax.experimental.pallas import tpu as pltpu
from jax.sharding import PartitionSpec as P

BLOCK = 128
GELU_A = math.sqrt(2.0 / math.pi)
GELU_B = 0.044715
NT = (((1,), (1,)), ((), ()))
TN = (((0,), (0,)), ((), ()))
VMEM_BYTES = 56 * 1024 * 1024


def dot_f32(left, right, dims=(((1,), (0,)), ((), ()))):
    return lax.dot_general(left, right, dims, preferred_element_type=jnp.float32)


def expert_forward_kernel(pick, rows, w_in, w_out, hidden, slope, produced, total, *, chunk):
    step = pl.program_id(0)

    @pl.when(step == 0)
    def _():
        total[...] = jnp.zeros_like(total)

    for start in range(0, rows.shape[0], chunk):
        part = pl.ds(start, chunk)
        pre = dot_f32(rows[part, :], w_in[0])
        square = pre * pre
        bend = jnp.tanh(pre * (GELU_A + (GELU_A * GELU_B) * square))
        half = 0.5 + 0.5 * bend
        act = (pre * half).astype(jnp.bfloat16)
        lift = pre * (0.5 * GELU_A + (1.5 * GELU_A * GELU_B) * square)
        slope[part, :] = (half + lift * (1.0 - bend * bend)).astype(jnp.bfloat16)
        hidden[part, :] = act
        total[part, :] += dot_f32(act, w_out[0])

    @pl.when(step == pl.num_programs(0) - 1)
    def _():
        produced[...] = total[...].astype(jnp.bfloat16)


def expert_forward(pick, rows, w_in, w_out, tile=512, chunk=256):
    count, width = rows.shape
    inner = w_in.shape[2]
    if count % chunk: chunk = count
    return pl.pallas_call(
        lambda *refs: expert_forward_kernel(*refs, chunk=chunk),
        grid_spec=pltpu.PrefetchScalarGridSpec(
            num_scalar_prefetch=1,
            grid=(inner // tile,),
            in_specs=[
                pl.BlockSpec((count, width), lambda f, pick: (0, 0)),
                pl.BlockSpec((1, width, tile), lambda f, pick: (pick[0], 0, f)),
                pl.BlockSpec((1, tile, width), lambda f, pick: (pick[0], f, 0)),
            ],
            out_specs=[
                pl.BlockSpec((count, tile), lambda f, pick: (0, f)),
                pl.BlockSpec((count, tile), lambda f, pick: (0, f)),
                pl.BlockSpec((count, width), lambda f, pick: (0, 0)),
            ],
            scratch_shapes=[pltpu.VMEM((count, width), jnp.float32)],
        ),
        out_shape=[
            jax.ShapeDtypeStruct((count, inner), jnp.bfloat16),
            jax.ShapeDtypeStruct((count, inner), jnp.bfloat16),
            jax.ShapeDtypeStruct((count, width), jnp.bfloat16),
        ],
        compiler_params=pltpu.CompilerParams(vmem_limit_bytes=VMEM_BYTES),
        cost_estimate=pl.CostEstimate(flops=4 * count * width * inner, bytes_accessed=4 * (width + count) * inner + 4 * count * width, transcendentals=count * inner),
        name="expert_forward",
    )(pick, rows, w_in, w_out)


def expert_backward_kernel(pick, grads, w_in, w_out, slope, grad_pre, grad_rows, total, *, chunk):
    step = pl.program_id(0)

    @pl.when(step == 0)
    def _():
        total[...] = jnp.zeros_like(total)

    for start in range(0, grads.shape[0], chunk):
        part = pl.ds(start, chunk)
        back = dot_f32(grads[part, :], w_out[0], NT) * slope[part, :].astype(jnp.float32)
        back = back.astype(jnp.bfloat16)
        grad_pre[part, :] = back
        total[part, :] += dot_f32(back, w_in[0], NT)

    @pl.when(step == pl.num_programs(0) - 1)
    def _():
        grad_rows[...] = total[...].astype(jnp.bfloat16)


def expert_backward(pick, grads, w_in, w_out, slope, tile=512, chunk=256):
    count, width = grads.shape
    inner = w_in.shape[2]
    if count % chunk: chunk = count
    return pl.pallas_call(
        lambda *refs: expert_backward_kernel(*refs, chunk=chunk),
        grid_spec=pltpu.PrefetchScalarGridSpec(
            num_scalar_prefetch=1,
            grid=(inner // tile,),
            in_specs=[
                pl.BlockSpec((count, width), lambda f, pick: (0, 0)),
                pl.BlockSpec((1, width, tile), lambda f, pick: (pick[0], 0, f)),
                pl.BlockSpec((1, tile, width), lambda f, pick: (pick[0], f, 0)),
                pl.BlockSpec((count, tile), lambda f, pick: (0, f)),
            ],
            out_specs=[
                pl.BlockSpec((count, tile), lambda f, pick: (0, f)),
                pl.BlockSpec((count, width), lambda f, pick: (0, 0)),
            ],
            scratch_shapes=[pltpu.VMEM((count, width), jnp.float32)],
        ),
        out_shape=[
            jax.ShapeDtypeStruct((count, inner), jnp.bfloat16),
            jax.ShapeDtypeStruct((count, width), jnp.bfloat16),
        ],
        compiler_params=pltpu.CompilerParams(vmem_limit_bytes=VMEM_BYTES),
        cost_estimate=pl.CostEstimate(flops=4 * count * width * inner, bytes_accessed=4 * (width + count) * inner + 4 * count * width, transcendentals=0),
        name="expert_backward",
    )(pick, grads, w_in, w_out, slope)


def seen_blocks(row_block, blocks):
    return max(row_block + 1, blocks // 2)


def attention_forward_kernel(far, queries, keys, values, near, attended, probs, *, heads, blocks):
    pair = pl.program_id(0)
    lane = lax.broadcasted_iota(jnp.int32, (BLOCK, 2 * heads), 1)
    for row_block in range(blocks):
        rows = pl.ds(row_block * BLOCK, BLOCK)
        span = seen_blocks(row_block, blocks)
        seen = pl.ds(0, span * BLOCK)
        outs = []
        for head in range(2):
            mine = (lane < heads) if head == 0 else (lane >= heads)
            query = jnp.where(mine, queries[rows, :] * 0.125, 0.0).astype(jnp.bfloat16)
            score = dot_f32(query, keys[seen, :], NT)
            far_bias = far[pair * 2 + head]
            pieces = []
            for key_block in range(span):
                piece = score[:, key_block * BLOCK : (key_block + 1) * BLOCK]
                slot = near_slot(row_block, key_block, blocks)
                pieces.append(piece + (far_bias if slot is None else near[head, slot]))
            peak = pieces[0]
            for piece in pieces[1:]:
                peak = jnp.maximum(peak, piece)
            peak = jnp.max(peak, axis=1, keepdims=True)
            pieces = [jnp.exp(piece - peak) for piece in pieces]
            mass = pieces[0]
            for piece in pieces[1:]:
                mass = mass + piece
            scale = 1.0 / jnp.sum(mass, axis=1, keepdims=True)
            weights = jnp.concatenate([(piece * scale).astype(jnp.bfloat16) for piece in pieces], axis=1)
            probs[head, rows, seen] = weights
            outs.append(dot_f32(weights, values[seen, :]))
        attended[rows, :] = jnp.where(lane < heads, outs[0], outs[1]).astype(jnp.bfloat16)


def near_slot(row_block, key_block, blocks):
    half = blocks // 2
    if key_block < row_block - 1:
        return None
    if key_block == row_block - 1:
        return 0
    if key_block == row_block:
        return 1 + min(row_block, half)
    count = 2 + half
    for row in range(half):
        for key in range(row + 1, half):
            if (row, key) == (row_block, key_block):
                return count
            count += 1
    raise ValueError


def near_pairs(blocks):
    half = blocks // 2
    pairs = [(1, 0)] + [(row, row) for row in range(half + 1)]
    return pairs + [(row, key) for row in range(half) for key in range(row + 1, half)]


def attention_forward(far, qkv_rows, near):
    length, width = qkv_rows.shape[1:]
    pairs = width // 128
    blocks = length // BLOCK
    slots = near.shape[1]
    return pl.pallas_call(
        lambda *refs: attention_forward_kernel(*refs, heads=64, blocks=blocks),
        grid_spec=pltpu.PrefetchScalarGridSpec(
            num_scalar_prefetch=1,
            grid=(pairs,),
            in_specs=[
                pl.BlockSpec((None, length, 128), lambda h, far: (0, 0, h)),
                pl.BlockSpec((None, length, 128), lambda h, far: (1, 0, h)),
                pl.BlockSpec((None, length, 128), lambda h, far: (2, 0, h)),
                pl.BlockSpec((2, slots, BLOCK, BLOCK), lambda h, far: (h, 0, 0, 0)),
            ],
            out_specs=[
                pl.BlockSpec((length, 128), lambda h, far: (0, h)),
                pl.BlockSpec((2, length, length), lambda h, far: (h, 0, 0)),
            ],
        ),
        out_shape=[
            jax.ShapeDtypeStruct((length, width), jnp.bfloat16),
            jax.ShapeDtypeStruct((2 * pairs, length, length), jnp.bfloat16),
        ],
        compiler_params=pltpu.CompilerParams(vmem_limit_bytes=VMEM_BYTES),
        cost_estimate=pl.CostEstimate(flops=8 * pairs * 128 * length * length, bytes_accessed=4 * pairs * length * length, transcendentals=2 * pairs * length * length),
        name="attention_forward",
    )(far, qkv_rows, qkv_rows, qkv_rows, near)


def attention_backward_kernel(queries, keys, values, grads, probs, grad_q, grad_k, grad_v, bands, flow, *, heads, blocks):
    lane = lax.broadcasted_iota(jnp.int32, (BLOCK, 2 * heads), 1)
    query_t = (queries[...] * 0.125).astype(jnp.bfloat16).T
    grad_t = grads[...].T
    half = blocks // 2
    dk, dv = [], []
    dq = [[], []]
    for head in range(2):
        mine = (lane < heads) if head == 0 else (lane >= heads)
        sums = [None] * 4
        for row_block in range(blocks):
            rows = pl.ds(row_block * BLOCK, BLOCK)
            span = seen_blocks(row_block, blocks)
            seen = pl.ds(0, span * BLOCK)
            grad = jnp.where(mine, grads[rows, :], 0.0).astype(jnp.bfloat16)
            soft = probs[head, rows, seen].astype(jnp.float32)
            back = dot_f32(grad, values[seen, :], NT)
            inner = jnp.sum(soft * back, axis=1, keepdims=True)
            score_grad = (soft * (back - inner)).astype(jnp.bfloat16)
            flow[rows, seen] = score_grad
            dq[head].append(dot_f32(score_grad, keys[seen, :]) * 0.125)
            for key_block in range(span):
                band = max(key_block - row_block, -2)
                if band > 1:
                    continue
                tile = score_grad[:, key_block * BLOCK : (key_block + 1) * BLOCK].astype(jnp.float32)
                sums[band + 2] = tile if sums[band + 2] is None else sums[band + 2] + tile
        for band in range(4):
            bands[head, band] = sums[band]
        part = slice(head * heads, (head + 1) * heads)
        key_pieces, value_pieces = [], []
        for key_block in range(blocks):
            first = 0 if key_block < half else key_block
            rows = pl.ds(first * BLOCK, (blocks - first) * BLOCK)
            cols = pl.ds(key_block * BLOCK, BLOCK)
            key_pieces.append(dot_f32(query_t[part, first * BLOCK :], flow[rows, cols]))
            value_pieces.append(dot_f32(grad_t[part, first * BLOCK :], probs[head, rows, cols]))
        dk.append(jnp.concatenate(key_pieces, axis=1))
        dv.append(jnp.concatenate(value_pieces, axis=1))
    for row_block in range(blocks):
        rows = pl.ds(row_block * BLOCK, BLOCK)
        grad_q[rows, :] = jnp.where(lane < heads, dq[0][row_block], dq[1][row_block]).astype(jnp.bfloat16)
    grad_k[...] = jnp.concatenate(dk, axis=0).T.astype(jnp.bfloat16)
    grad_v[...] = jnp.concatenate(dv, axis=0).T.astype(jnp.bfloat16)


def attention_backward(qkv_rows, grads, probs):
    length, width = grads.shape
    pairs = width // 128
    blocks = length // BLOCK
    block = pl.BlockSpec((length, 128), lambda h: (0, h))
    of_three = [pl.BlockSpec((None, length, 128), lambda h, c=c: (c, 0, h)) for c in range(3)]
    return pl.pallas_call(
        lambda *refs: attention_backward_kernel(*refs, heads=64, blocks=blocks),
        grid=(pairs,),
        in_specs=[*of_three, block, pl.BlockSpec((2, length, length), lambda h: (h, 0, 0))],
        out_specs=[block, block, block, pl.BlockSpec((2, 4, BLOCK, BLOCK), lambda h: (h, 0, 0, 0))],
        out_shape=[jax.ShapeDtypeStruct((length, width), jnp.bfloat16)] * 3
        + [jax.ShapeDtypeStruct((2 * pairs, 4, BLOCK, BLOCK), jnp.float32)],
        scratch_shapes=[pltpu.VMEM((length, length), jnp.bfloat16)],
        compiler_params=pltpu.CompilerParams(vmem_limit_bytes=VMEM_BYTES),
        cost_estimate=pl.CostEstimate(flops=20 * pairs * 128 * length * length, bytes_accessed=4 * pairs * length * length, transcendentals=0),
        name="attention_backward",
    )(qkv_rows, qkv_rows, qkv_rows, grads, probs)


EPS = 1e-06
BOUNDS = (12, 16, 23, 32, 46, 64, 91)
TOP_PRECISION = lax.Precision.HIGHEST
AXES = ("dp", "expert")
PAIR = 2


def outer_kernel(picks, left, right, *parts):
    whole = dot_f32(left[...], right[...], TN).astype(jnp.bfloat16)
    rows = whole.shape[0] // len(parts)
    for place, part in enumerate(parts):
        part[0] = whole[place * rows : (place + 1) * rows]


def outer_slices(picks, left, right, rows, pieces):
    depth, width = right.shape
    count = picks.shape[0]
    return pl.pallas_call(
        outer_kernel,
        grid_spec=pltpu.PrefetchScalarGridSpec(
            num_scalar_prefetch=1,
            grid=(count,),
            in_specs=[
                pl.BlockSpec((depth, rows), lambda i, picks: (0, picks[i])),
                pl.BlockSpec((depth, width), lambda i, picks: (0, 0)),
            ],
            out_specs=[pl.BlockSpec((1, rows // pieces, width), lambda i, picks: (i, 0, 0))] * pieces,
        ),
        out_shape=[jax.ShapeDtypeStruct((count, rows // pieces, width), jnp.bfloat16)] * pieces,
        compiler_params=pltpu.CompilerParams(vmem_limit_bytes=VMEM_BYTES),
        cost_estimate=pl.CostEstimate(flops=2 * count * depth * rows * width, bytes_accessed=2 * depth * (count * rows + width) + 2 * count * rows * width, transcendentals=0),
        name="outer_slices",
    )(picks, left, right)


def bucket_index(offset):
    distance = jnp.abs(offset)
    far_bucket = 8 + sum([(distance >= level).astype(jnp.int32) for level in BOUNDS])
    near_bucket = jnp.where(distance < 8, distance, far_bucket)
    return jnp.where(offset > 0, 16, 0) + near_bucket


def norm_apply(inputs, gain_vec):
    return inputs * lax.rsqrt(jnp.mean(inputs * inputs, axis=-1, keepdims=True) + EPS) * gain_vec


def gate_values(logits, routes):
    soft_probs = jax.nn.softmax(logits, axis=-1)
    picked_hot = (
        routes[:, :, None] == jnp.arange(logits.shape[1], dtype=jnp.int32)[None, None, :]
    ).astype(jnp.float32)
    chosen = jnp.sum(soft_probs[:, None, :] * picked_hot, axis=-1)
    return chosen / jnp.sum(chosen, axis=1, keepdims=True)


def tile_offsets(query_block, key_block):
    rows = query_block * BLOCK + lax.broadcasted_iota(jnp.int32, (BLOCK, BLOCK), 0)
    cols = key_block * BLOCK + lax.broadcasted_iota(jnp.int32, (BLOCK, BLOCK), 1)
    return rows, cols


def near_bias(table, prefix_len, blocks):
    buckets = table.shape[1]
    tiles = []
    for query_block, key_block in near_pairs(blocks):
        rows, cols = tile_offsets(query_block, key_block)
        hot = (bucket_index(cols - rows)[None] == jnp.arange(buckets, dtype=jnp.int32)[:, None, None]).astype(jnp.float32)
        tile = jnp.einsum("hb,bxy->hxy", table, hot, precision=TOP_PRECISION)
        if key_block >= query_block:
            tile = jnp.where(((cols <= rows) | (cols < prefix_len))[None], tile, -1e30)
        tiles.append(tile)
    return jnp.stack(tiles, axis=1)


def table_gradient(bands, buckets):
    rows, cols = tile_offsets(0, 0)
    ids = [jnp.full((BLOCK, BLOCK), bucket_far(), jnp.int32)]
    ids += [bucket_index(shift * BLOCK + cols - rows) for shift in (-1, 0, 1)]
    hot = (jnp.stack(ids)[..., None] == jnp.arange(buckets, dtype=jnp.int32)).astype(jnp.float32)
    return jnp.einsum("hdxy,dxyb->hb", bands, hot, precision=TOP_PRECISION)


def bucket_far():
    return 8 + len(BOUNDS)


def on_device(
    tokens,
    qkv_weight,
    out_weight,
    position_bias_table,
    gain_attn,
    gain_moe,
    router,
    w_in,
    w_out,
    routes,
    prefix,
    valid_mask,
    teacher,
    cotangent,
):
    length, width = tokens.shape
    bf16, f32 = jnp.bfloat16, jnp.float32
    expert_count = router.shape[1]
    top_count = routes.shape[1]
    groups = lax.axis_size("expert")
    copies = lax.axis_size("dp")
    inner = w_in.shape[2]
    capacity = 5 * length * top_count // (4 * expert_count)
    total_tokens = length * copies * groups
    sources = 2 * groups
    blocks = length // BLOCK
    here_dp, here_group = lax.axis_index("dp"), lax.axis_index("expert")
    half = (here_dp // PAIR) % 2
    core = here_group % 2
    rest = copies // 4

    def swap(value, dp_mask, group_mask):
        pairs = [
            (i, ((i // groups) ^ dp_mask) * groups + ((i % groups) ^ group_mask))
            for i in range(copies * groups)
        ]
        return lax.ppermute(value, AXES, pairs)

    def bits(count):
        return [1 << place for place in range(count.bit_length() - 1)]

    def all_sum(value):
        for mask in bits(groups):
            value = value + swap(value, 0, mask)
        for mask in bits(copies):
            value = value + swap(value, mask, 0)
        return value

    def exchange(rows):
        parts = rows.reshape(sources, capacity, width)
        got = [parts[0]]
        for away in range(1, sources):
            got.append(swap(parts[away], PAIR * (away // groups), away % groups))
        return jnp.concatenate(got, axis=0)

    def gather_weight(piece, axis):
        columns = piece.shape[-1] // 2
        mine = lax.dynamic_slice_in_dim(piece, core * columns, columns, piece.ndim - 1)
        mine = lax.all_gather(mine, "dp", axis=axis, tiled=True)
        other = swap(mine, 0, 1)
        first, second = jnp.where(core == 0, mine, other), jnp.where(core == 0, other, mine)
        return jnp.concatenate([first, second], axis=-1)

    qkv_full = gather_weight(qkv_weight, 1)
    out_full = gather_weight(out_weight, 0)
    valid_rows = valid_mask.astype(f32)[:, None]
    valid_count = all_sum(jnp.broadcast_to(jnp.sum(valid_rows), (8, 128)))[0, 0]
    prefix_len = prefix[0]
    near = near_bias(position_bias_table, prefix_len, blocks)

    flat_routes = routes.reshape(-1)
    pair_count = length * top_count
    slot_count = sources * capacity
    route_hits = (flat_routes[:, None] == jnp.arange(expert_count, dtype=jnp.int32)[None, :]).astype(bf16)
    lower_ones = (
        lax.broadcasted_iota(jnp.int32, (pair_count, pair_count), 0)
        >= lax.broadcasted_iota(jnp.int32, (pair_count, pair_count), 1)
    ).astype(bf16)
    running = jnp.dot(lower_ones, route_hits, preferred_element_type=f32)
    pair_rank = jnp.sum((running - 1.0) * route_hits.astype(f32), axis=1).astype(jnp.int32)
    away = ((flat_routes % 2) ^ half) * groups + ((flat_routes // 2) ^ here_group)
    slot_of_pair = (away * capacity + pair_rank).reshape(length, top_count)
    slot_hot = (
        slot_of_pair[:, :, None] == lax.broadcasted_iota(jnp.int32, (1, 1, slot_count), 2)
    ).astype(bf16)

    resid = tokens.astype(f32)
    normed1 = norm_apply(resid, gain_attn).astype(bf16)
    qkv_rows = jnp.einsum("td,cde->cte", normed1, qkv_full, preferred_element_type=f32).astype(bf16)
    attended, probs = attention_forward(position_bias_table[:, bucket_far()], qkv_rows, near)
    middle = resid + jnp.dot(attended, out_full, preferred_element_type=f32)
    normed2 = norm_apply(middle, gain_moe).astype(bf16)
    logits = jnp.dot(normed2, router, preferred_element_type=f32)
    gate_vals = gate_values(logits, routes)

    send_rows = jnp.einsum("tks,td->sd", slot_hot, normed2, preferred_element_type=f32).astype(bf16)
    rows_in = exchange(send_rows)
    pick = half.reshape(1).astype(jnp.int32)
    hidden, slope, produced = expert_forward(pick, rows_in, w_in, w_out)
    returned = exchange(produced)
    picked = jnp.einsum("tks,sd->tkd", slot_hot, returned, preferred_element_type=f32)
    output = middle + jnp.sum(gate_vals[:, :, None] * picked, axis=1)
    misfit = output - teacher.astype(f32)
    square_sum = jnp.sum(valid_rows * misfit * misfit)
    grad_y = cotangent.astype(f32) + valid_rows * misfit * (total_tokens / valid_count)
    grad_pairs = (gate_vals[:, :, None] * grad_y[:, None, :]).astype(bf16)
    send_grads = jnp.einsum("tks,tkd->sd", slot_hot, grad_pairs, preferred_element_type=f32).astype(bf16)
    grad_rows = exchange(send_grads)

    out_rows = inner // copies
    in_rows = width // copies
    far_bit = here_dp % 2
    slices = jnp.arange(rest, dtype=jnp.int32) * 4

    def owner_slices(other_half, bit0):
        return (slices + ((half ^ other_half) * 2 + bit0)).astype(jnp.int32)

    def out_units(bit0):
        units = []
        for other_half in (1, 0):
            picks = owner_slices(other_half, bit0)
            if out_rows % 128 == 0:
                units += outer_slices(picks, hidden, grad_rows, out_rows, 2)
            else:
                part = jnp.take(hidden.reshape(-1, copies, out_rows), picks, axis=1)
                part = jnp.einsum("rsf,rd->sfd", part, grad_rows, preferred_element_type=f32).astype(bf16)
                units += [part[:, : out_rows // 2], part[:, out_rows // 2 :]]
        return units

    def in_units(bit0):
        rows_t = rows_in.T.reshape(rest, 2, 2, in_rows, slot_count)
        rows_t = lax.dynamic_index_in_dim(rows_t, bit0, 2, keepdims=False)
        units = []
        for other_half in (1, 0):
            part = lax.dynamic_index_in_dim(rows_t, half ^ other_half, 1, keepdims=False)
            for piece in range(2):
                cols = grad_pre[:, piece * (inner // 2) : (piece + 1) * (inner // 2)]
                units.append(jnp.einsum("sir,rf->sif", part, cols, preferred_element_type=f32).astype(bf16))
        return units

    send_units = out_units(1 - far_bit)
    got_units = [swap(unit, 1, 0) for unit in send_units]
    grad_pre, grad_in_rows = expert_backward(pick, grad_rows, w_in, w_out, slope)
    sent_back = exchange(grad_in_rows)
    send_units = in_units(1 - far_bit)
    got_units += [swap(unit, 1, 0) for unit in send_units]
    keep_units = out_units(far_bit) + in_units(far_bit)

    reduced = []
    token = None
    for got, keep in zip(got_units, keep_units):
        if token is not None:
            got, _ = lax.optimization_barrier((got, token))
        unit = (got.astype(f32) + keep.astype(f32)).astype(bf16)
        for mask in reversed(bits(copies)[2:]):
            bit = (here_dp // mask) % 2
            unit = unit.reshape((2, unit.shape[0] // 2) + unit.shape[1:])
            away_part = lax.dynamic_index_in_dim(unit, 1 - bit, 0, keepdims=False)
            stay_part = lax.dynamic_index_in_dim(unit, bit, 0, keepdims=False)
            token = stay_part
            unit = (swap(away_part, mask, 0).astype(f32) + stay_part.astype(f32)).astype(bf16)
        reduced.append(unit[0])
    final = []
    for first in (0, 4):
        theirs = [swap(unit, PAIR, 0) for unit in reduced[first : first + 2]]
        axis = 0 if first == 0 else 1
        mine = jnp.concatenate(reduced[first + 2 : first + 4], axis=axis).astype(f32)
        theirs = jnp.concatenate(theirs, axis=axis).astype(f32)
        final.append(jnp.stack([jnp.where(half == 0, mine, theirs), jnp.where(half == 0, theirs, mine)]))
    grad_w_out, grad_w_in = final

    grad_gates = jnp.sum(grad_y[:, None, :] * picked, axis=-1)
    grad_normed2 = jnp.einsum("tks,sd->td", slot_hot, sent_back, preferred_element_type=f32)
    gate_out, gate_back = jax.vjp(lambda logit_vals: gate_values(logit_vals, routes), logits)
    grad_logits = gate_back(grad_gates)[0].astype(bf16)
    grad_router = jnp.einsum("td,te->de", normed2, grad_logits, preferred_element_type=f32)
    grad_normed2 = grad_normed2 + jnp.einsum("te,de->td", grad_logits, router, preferred_element_type=f32)
    norm_out, norm_back = jax.vjp(norm_apply, middle, gain_moe)
    grad_mid_norm, grad_gain_moe = norm_back(grad_normed2)
    grad_middle = grad_y + grad_mid_norm
    grad_attn_proj = grad_middle.astype(bf16)
    grad_attended = jnp.einsum("te,de->td", grad_attn_proj, out_full, preferred_element_type=f32).astype(bf16)
    grad_q, grad_k, grad_v, bands = attention_backward(qkv_rows, grad_attended, probs)

    def weight_gradient(left, right):
        return jnp.einsum("td,te->de", left, right, preferred_element_type=f32).astype(bf16)

    mats = [weight_gradient(normed1, part) for part in (grad_q, grad_k, grad_v)]
    mats.append(weight_gradient(attended, grad_attn_proj))
    group_bits = bits(groups)
    share = 4 * in_rows // groups
    if share == in_rows:
        total = jnp.stack([mats[0], mats[2], mats[1], mats[3]]).reshape((2,) * len(group_bits) + (copies, share, width))
    else:
        total = jnp.stack(mats).reshape(4, copies, in_rows, width).transpose(1, 0, 2, 3)
        total = total.reshape((copies,) + (2,) * len(group_bits) + (share, width))
        order = list(range(len(group_bits), 0, -1)) + [0, len(group_bits) + 1, len(group_bits) + 2]
        total = total.transpose(order)
    for mask in group_bits:
        bit = (here_group // mask) % 2
        away_part = lax.dynamic_index_in_dim(total, 1 - bit, 0, keepdims=False)
        stay_part = lax.dynamic_index_in_dim(total, bit, 0, keepdims=False)
        total = (swap(away_part, 0, mask).astype(f32) + stay_part.astype(f32)).astype(bf16)
    for mask in reversed(bits(copies)):
        bit = (here_dp // mask) % 2
        total = total.reshape((2, total.shape[0] // 2) + total.shape[1:])
        away_part = lax.dynamic_index_in_dim(total, 1 - bit, 0, keepdims=False)
        stay_part = lax.dynamic_index_in_dim(total, bit, 0, keepdims=False)
        total = (swap(away_part, mask, 0).astype(f32) + stay_part.astype(f32)).astype(bf16)
    total = total[0]
    for mask in reversed(group_bits):
        bit = (here_group // mask) % 2
        other = swap(total, 0, mask)
        total = jnp.stack([jnp.where(bit == 0, total, other), jnp.where(bit == 0, other, total)])
    order = list(range(len(group_bits) - 1, -1, -1)) + [len(group_bits), len(group_bits) + 1]
    total = total.transpose(order).reshape(4, in_rows, width).astype(f32)
    grad_qkv, grad_out_weight = total[:3], total[3]

    grad_normed1 = sum(
        jnp.einsum("te,de->td", part, qkv_full[c], preferred_element_type=f32)
        for c, part in enumerate((grad_q, grad_k, grad_v))
    )
    first_out, first_back = jax.vjp(norm_apply, resid, gain_attn)
    grad_resid_norm, grad_gain_attn = first_back(grad_normed1)
    grad_input = grad_middle + grad_resid_norm
    grad_table = table_gradient(bands, position_bias_table.shape[1])

    def sum_many(values):
        flat = jnp.concatenate([value.reshape(-1) for value in values])
        size = flat.shape[0]
        flat = jnp.pad(flat, (0, -size % 1024)).reshape(-1, 128)
        flat = all_sum(flat).reshape(-1)
        done, place = [], 0
        for value in values:
            done.append(flat[place : place + value.size].reshape(value.shape))
            place += value.size
        return done

    grad_gain_moe, grad_router, square_total = sum_many((grad_gain_moe, grad_router, square_sum))
    grad_gain_attn, grad_table = sum_many((grad_gain_attn, grad_table))
    distill_loss = square_total / (width * valid_count)
    return (
        output.astype(bf16),
        distill_loss,
        grad_input,
        grad_qkv,
        grad_out_weight,
        grad_w_in,
        grad_w_out,
        grad_router,
        grad_table,
        grad_gain_attn,
        grad_gain_moe,
    )


def solution(mesh):
    rows = P(AXES, None)
    return jax.shard_map(
        on_device,
        mesh=mesh,
        in_specs=(
            rows,
            P(None, "dp", None),
            P("dp", None),
            P(),
            P(),
            P(),
            P(),
            P("expert", None, None),
            P("expert", None, None),
            rows,
            P(AXES),
            P(AXES),
            rows,
            rows,
        ),
        out_specs=(
            rows,
            P(),
            rows,
            P(None, "dp", None),
            P("dp", None),
            P("expert", "dp", None),
            P("expert", "dp", None),
            P(),
            P(),
            P(),
            P(),
        ),
        check_vma=False,
    )
```

```python
import math
import jax
import jax.numpy as jnp
from jax import lax
from jax.experimental import pallas as pl
from jax.experimental.pallas import tpu as pltpu
from jax.sharding import PartitionSpec as P

BLOCK = 128
THIRDS = 3
GELU_A = math.sqrt(2.0 / math.pi)
GELU_B = 0.044715
NT = (((1,), (1,)), ((), ()))
TN = (((0,), (0,)), ((), ()))
VMEM_BYTES = 56 * 1024 * 1024


def cost(micros):
    return pl.CostEstimate(flops=int(micros * 1.1e9), bytes_accessed=0, transcendentals=0)


def dot_f32(left, right, dims=(((1,), (0,)), ((), ()))):
    return lax.dot_general(left, right, dims, preferred_element_type=jnp.float32)


def expert_forward_kernel(pick, rows, w_in, w_out, hidden_t, slope, produced, rows_t, total, *, chunk):
    step = pl.program_id(0)

    @pl.when(step == 0)
    def _():
        total[...] = jnp.zeros_like(total)
        rows_t[...] = rows[...].T

    for start in range(0, rows.shape[0], chunk):
        part = pl.ds(start, chunk)
        pre = dot_f32(rows[part, :], w_in[0])
        square = pre * pre
        bend = jnp.tanh(pre * (GELU_A + (GELU_A * GELU_B) * square))
        half = 0.5 + 0.5 * bend
        act = (pre * half).astype(jnp.bfloat16)
        lift = pre * (0.5 * GELU_A + (1.5 * GELU_A * GELU_B) * square)
        slope[part, :] = (half + lift * (1.0 - bend * bend)).astype(jnp.bfloat16)
        hidden_t[:, part] = act.T
        total[part, :] += dot_f32(act, w_out[0])

    @pl.when(step == pl.num_programs(0) - 1)
    def _():
        produced[...] = total[...].astype(jnp.bfloat16)


def expert_forward(pick, rows, w_in, w_out, tile=512, chunk=256):
    count, width = rows.shape
    inner = w_in.shape[2]
    return pl.pallas_call(
        lambda *refs: expert_forward_kernel(*refs, chunk=chunk),
        grid_spec=pltpu.PrefetchScalarGridSpec(
            num_scalar_prefetch=1,
            grid=(inner // tile,),
            in_specs=[
                pl.BlockSpec((count, width), lambda f, pick: (0, 0)),
                pl.BlockSpec((1, width, tile), lambda f, pick: (pick[0], 0, f)),
                pl.BlockSpec((1, tile, width), lambda f, pick: (pick[0], f, 0)),
            ],
            out_specs=[
                pl.BlockSpec((tile, count), lambda f, pick: (f, 0)),
                pl.BlockSpec((count, tile), lambda f, pick: (0, f)),
                pl.BlockSpec((count, width), lambda f, pick: (0, 0)),
                pl.BlockSpec((width, count), lambda f, pick: (0, 0)),
            ],
            scratch_shapes=[pltpu.VMEM((count, width), jnp.float32)],
        ),
        out_shape=[
            jax.ShapeDtypeStruct((inner, count), jnp.bfloat16),
            jax.ShapeDtypeStruct((count, inner), jnp.bfloat16),
            jax.ShapeDtypeStruct((count, width), jnp.bfloat16),
            jax.ShapeDtypeStruct((width, count), jnp.bfloat16),
        ],
        compiler_params=pltpu.CompilerParams(vmem_limit_bytes=VMEM_BYTES),
        cost_estimate=cost(22),
        name="expert_forward",
    )(pick, rows, w_in, w_out)


def expert_backward_kernel(pick, grads, w_in, w_out, slope, grad_pre, grad_rows, total, *, chunk):
    step = pl.program_id(0)

    @pl.when(step == 0)
    def _():
        total[...] = jnp.zeros_like(total)

    for start in range(0, grads.shape[0], chunk):
        part = pl.ds(start, chunk)
        back = dot_f32(grads[part, :], w_out[0], NT) * slope[part, :].astype(jnp.float32)
        back = back.astype(jnp.bfloat16)
        grad_pre[part, :] = back
        total[part, :] += dot_f32(back, w_in[0], NT)

    @pl.when(step == pl.num_programs(0) - 1)
    def _():
        grad_rows[...] = total[...].astype(jnp.bfloat16)


def expert_backward(pick, grads, w_in, w_out, slope, tile=512, chunk=256):
    count, width = grads.shape
    inner = w_in.shape[2]
    return pl.pallas_call(
        lambda *refs: expert_backward_kernel(*refs, chunk=chunk),
        grid_spec=pltpu.PrefetchScalarGridSpec(
            num_scalar_prefetch=1,
            grid=(inner // tile,),
            in_specs=[
                pl.BlockSpec((count, width), lambda f, pick: (0, 0)),
                pl.BlockSpec((1, width, tile), lambda f, pick: (pick[0], 0, f)),
                pl.BlockSpec((1, tile, width), lambda f, pick: (pick[0], f, 0)),
                pl.BlockSpec((count, tile), lambda f, pick: (0, f)),
            ],
            out_specs=[
                pl.BlockSpec((count, tile), lambda f, pick: (0, f)),
                pl.BlockSpec((count, width), lambda f, pick: (0, 0)),
            ],
            scratch_shapes=[pltpu.VMEM((count, width), jnp.float32)],
        ),
        out_shape=[
            jax.ShapeDtypeStruct((count, inner), jnp.bfloat16),
            jax.ShapeDtypeStruct((count, width), jnp.bfloat16),
        ],
        compiler_params=pltpu.CompilerParams(vmem_limit_bytes=VMEM_BYTES),
        cost_estimate=cost(20),
        name="expert_backward",
    )(pick, grads, w_in, w_out, slope)


def seen_blocks(row_block, blocks):
    return max(row_block + 1, blocks // 2)


def attention_forward_kernel(far, queries, keys, values, near, attended, probs, *, heads, blocks):
    pair = pl.program_id(0)
    lane = lax.broadcasted_iota(jnp.int32, (BLOCK, 2 * heads), 1)
    for row_block in range(blocks):
        rows = pl.ds(row_block * BLOCK, BLOCK)
        span = seen_blocks(row_block, blocks)
        seen = pl.ds(0, span * BLOCK)
        outs = []
        for head in range(2):
            mine = (lane < heads) if head == 0 else (lane >= heads)
            query = jnp.where(mine, queries[rows, :] * 0.125, 0.0).astype(jnp.bfloat16)
            score = dot_f32(query, keys[seen, :], NT)
            far_bias = far[pair * 2 + head]
            pieces = []
            for key_block in range(span):
                piece = score[:, key_block * BLOCK : (key_block + 1) * BLOCK]
                slot = near_slot(row_block, key_block, blocks)
                pieces.append(piece + (far_bias if slot is None else near[head, slot]))
            peak = pieces[0]
            for piece in pieces[1:]:
                peak = jnp.maximum(peak, piece)
            peak = jnp.max(peak, axis=1, keepdims=True)
            pieces = [jnp.exp(piece - peak) for piece in pieces]
            mass = pieces[0]
            for piece in pieces[1:]:
                mass = mass + piece
            scale = 1.0 / jnp.sum(mass, axis=1, keepdims=True)
            weights = jnp.concatenate([(piece * scale).astype(jnp.bfloat16) for piece in pieces], axis=1)
            probs[head, rows, seen] = weights
            outs.append(dot_f32(weights, values[seen, :]))
        attended[rows, :] = jnp.where(lane < heads, outs[0], outs[1]).astype(jnp.bfloat16)


def near_slot(row_block, key_block, blocks):
    half = blocks // 2
    if key_block < row_block - 1:
        return None
    if key_block == row_block - 1:
        return 0
    if key_block == row_block:
        return 1 + min(row_block, half)
    count = 2 + half
    for row in range(half):
        for key in range(row + 1, half):
            if (row, key) == (row_block, key_block):
                return count
            count += 1
    raise ValueError


def near_pairs(blocks):
    half = blocks // 2
    pairs = [(1, 0)] + [(row, row) for row in range(half + 1)]
    return pairs + [(row, key) for row in range(half) for key in range(row + 1, half)]


def attention_forward(far, qkv_rows, near):
    length, width = qkv_rows.shape[1:]
    pairs = width // 128
    blocks = length // BLOCK
    slots = near.shape[1]
    return pl.pallas_call(
        lambda *refs: attention_forward_kernel(*refs, heads=64, blocks=blocks),
        grid_spec=pltpu.PrefetchScalarGridSpec(
            num_scalar_prefetch=1,
            grid=(pairs,),
            in_specs=[
                pl.BlockSpec((None, length, 128), lambda h, far: (0, 0, h)),
                pl.BlockSpec((None, length, 128), lambda h, far: (1, 0, h)),
                pl.BlockSpec((None, length, 128), lambda h, far: (2, 0, h)),
                pl.BlockSpec((2, slots, BLOCK, BLOCK), lambda h, far: (h, 0, 0, 0)),
            ],
            out_specs=[
                pl.BlockSpec((length, 128), lambda h, far: (0, h)),
                pl.BlockSpec((2, length, length), lambda h, far: (h, 0, 0)),
            ],
        ),
        out_shape=[
            jax.ShapeDtypeStruct((length, width), jnp.bfloat16),
            jax.ShapeDtypeStruct((2 * pairs, length, length), jnp.bfloat16),
        ],
        compiler_params=pltpu.CompilerParams(vmem_limit_bytes=VMEM_BYTES),
        cost_estimate=cost(17),
        name="attention_forward",
    )(far, qkv_rows, qkv_rows, qkv_rows, near)


def attention_backward_kernel(queries, keys, values, grads, probs, grad_q, grad_k, grad_v, bands, flow, *, heads, blocks):
    lane = lax.broadcasted_iota(jnp.int32, (BLOCK, 2 * heads), 1)
    query_t = (queries[...] * 0.125).astype(jnp.bfloat16).T
    grad_t = grads[...].T
    half = blocks // 2
    dk, dv = [], []
    dq = [[], []]
    for head in range(2):
        mine = (lane < heads) if head == 0 else (lane >= heads)
        sums = [None] * 4
        for row_block in range(blocks):
            rows = pl.ds(row_block * BLOCK, BLOCK)
            span = seen_blocks(row_block, blocks)
            seen = pl.ds(0, span * BLOCK)
            grad = jnp.where(mine, grads[rows, :], 0.0).astype(jnp.bfloat16)
            soft = probs[head, rows, seen].astype(jnp.float32)
            back = dot_f32(grad, values[seen, :], NT)
            inner = jnp.sum(soft * back, axis=1, keepdims=True)
            score_grad = (soft * (back - inner)).astype(jnp.bfloat16)
            flow[rows, seen] = score_grad
            dq[head].append(dot_f32(score_grad, keys[seen, :]) * 0.125)
            for key_block in range(span):
                band = max(key_block - row_block, -2)
                if band > 1:
                    continue
                tile = score_grad[:, key_block * BLOCK : (key_block + 1) * BLOCK].astype(jnp.float32)
                sums[band + 2] = tile if sums[band + 2] is None else sums[band + 2] + tile
        for band in range(4):
            bands[head, band] = sums[band]
        part = slice(head * heads, (head + 1) * heads)
        key_pieces, value_pieces = [], []
        for key_block in range(blocks):
            first = 0 if key_block < half else key_block
            rows = pl.ds(first * BLOCK, (blocks - first) * BLOCK)
            cols = pl.ds(key_block * BLOCK, BLOCK)
            key_pieces.append(dot_f32(query_t[part, first * BLOCK :], flow[rows, cols]))
            value_pieces.append(dot_f32(grad_t[part, first * BLOCK :], probs[head, rows, cols]))
        dk.append(jnp.concatenate(key_pieces, axis=1))
        dv.append(jnp.concatenate(value_pieces, axis=1))
    for row_block in range(blocks):
        rows = pl.ds(row_block * BLOCK, BLOCK)
        grad_q[rows, :] = jnp.where(lane < heads, dq[0][row_block], dq[1][row_block]).astype(jnp.bfloat16)
    grad_k[...] = jnp.concatenate(dk, axis=0).T.astype(jnp.bfloat16)
    grad_v[...] = jnp.concatenate(dv, axis=0).T.astype(jnp.bfloat16)


def attention_backward(qkv_rows, grads, probs):
    length, width = grads.shape
    pairs = width // 128
    blocks = length // BLOCK
    block = pl.BlockSpec((length, 128), lambda h: (0, h))
    of_three = [pl.BlockSpec((None, length, 128), lambda h, c=c: (c, 0, h)) for c in range(3)]
    return pl.pallas_call(
        lambda *refs: attention_backward_kernel(*refs, heads=64, blocks=blocks),
        grid=(pairs,),
        in_specs=[*of_three, block, pl.BlockSpec((2, length, length), lambda h: (h, 0, 0))],
        out_specs=[block, block, block, pl.BlockSpec((2, 4, BLOCK, BLOCK), lambda h: (h, 0, 0, 0))],
        out_shape=[jax.ShapeDtypeStruct((length, width), jnp.bfloat16)] * 3
        + [jax.ShapeDtypeStruct((2 * pairs, 4, BLOCK, BLOCK), jnp.float32)],
        scratch_shapes=[pltpu.VMEM((length, length), jnp.bfloat16)],
        compiler_params=pltpu.CompilerParams(vmem_limit_bytes=VMEM_BYTES),
        cost_estimate=cost(17),
        name="attention_backward",
    )(qkv_rows, qkv_rows, qkv_rows, grads, probs)


def weight_part_kernel(picks, *refs, count, layout):
    lefts, right, outs = refs[:count], refs[count], refs[count + 1 :]
    left = jnp.concatenate([ref[...] for ref in lefts], axis=0)
    whole = dot_f32(left, right[...]).astype(jnp.bfloat16)
    rows = whole.shape[0] // count
    part, many = rows // THIRDS, count // 2
    place = 0
    for out, pieces in zip(outs, layout):
        for piece in range(pieces):
            half, third = divmod(place, THIRDS)
            for k in range(many):
                start = (half * many + k) * rows + third * part
                out[k, piece] = whole[start : start + part]
            place += 1


def weight_part(picks, left, right, rows, layout, tile):
    depth, width = right.shape
    count = picks.shape[0]
    many, part = count // 2, rows // THIRDS
    if part % 16:
        whole = jnp.take(left.reshape(-1, rows, depth), picks, axis=0)
        whole = jnp.einsum("srd,dw->srw", whole, right, preferred_element_type=jnp.float32).astype(jnp.bfloat16)
        whole = whole.reshape(2, many, THIRDS, part, width).transpose(1, 0, 2, 3, 4).reshape(many, 2 * THIRDS, part, width)
        starts = [sum(layout[:place]) for place in range(len(layout))]
        return [whole[:, start : start + pieces] for start, pieces in zip(starts, layout)]
    return pl.pallas_call(
        lambda *refs: weight_part_kernel(*refs, count=count, layout=layout),
        grid_spec=pltpu.PrefetchScalarGridSpec(
            num_scalar_prefetch=1,
            grid=(width // tile,),
            in_specs=[pl.BlockSpec((rows, depth), lambda i, picks, k=k: (picks[k], 0)) for k in range(count)]
            + [pl.BlockSpec((depth, tile), lambda i, picks: (0, i))],
            out_specs=[pl.BlockSpec((many, pieces, part, tile), lambda i, picks: (0, 0, 0, i)) for pieces in layout],
        ),
        out_shape=[jax.ShapeDtypeStruct((many, pieces, part, width), jnp.bfloat16) for pieces in layout],
        compiler_params=pltpu.CompilerParams(vmem_limit_bytes=VMEM_BYTES),
        cost_estimate=cost(5),
        name="weight_part",
    )(picks, *([left] * count), right)


EPS = 1e-06
BOUNDS = (12, 16, 23, 32, 46, 64, 91)
TOP_PRECISION = lax.Precision.HIGHEST
AXES = ("dp", "expert")
PAIR = 2


def after(value, *others):
    return lax.optimization_barrier((value, *others))[0]


def bucket_index(offset):
    distance = jnp.abs(offset)
    far_bucket = 8 + sum([(distance >= level).astype(jnp.int32) for level in BOUNDS])
    near_bucket = jnp.where(distance < 8, distance, far_bucket)
    return jnp.where(offset > 0, 16, 0) + near_bucket


def norm_apply(inputs, gain_vec):
    return inputs * lax.rsqrt(jnp.mean(inputs * inputs, axis=-1, keepdims=True) + EPS) * gain_vec


def gate_values(logits, routes):
    soft_probs = jax.nn.softmax(logits, axis=-1)
    picked_hot = (
        routes[:, :, None] == jnp.arange(logits.shape[1], dtype=jnp.int32)[None, None, :]
    ).astype(jnp.float32)
    chosen = jnp.sum(soft_probs[:, None, :] * picked_hot, axis=-1)
    return chosen / jnp.sum(chosen, axis=1, keepdims=True)


def tile_offsets(query_block, key_block):
    rows = query_block * BLOCK + lax.broadcasted_iota(jnp.int32, (BLOCK, BLOCK), 0)
    cols = key_block * BLOCK + lax.broadcasted_iota(jnp.int32, (BLOCK, BLOCK), 1)
    return rows, cols


def near_bias(table, prefix_len, blocks):
    buckets = table.shape[1]
    tiles = []
    for query_block, key_block in near_pairs(blocks):
        rows, cols = tile_offsets(query_block, key_block)
        hot = (bucket_index(cols - rows)[None] == jnp.arange(buckets, dtype=jnp.int32)[:, None, None]).astype(jnp.float32)
        tile = jnp.einsum("hb,bxy->hxy", table, hot, precision=TOP_PRECISION)
        if key_block >= query_block:
            tile = jnp.where(((cols <= rows) | (cols < prefix_len))[None], tile, -1e30)
        tiles.append(tile)
    return jnp.stack(tiles, axis=1)


def table_gradient(bands, buckets):
    rows, cols = tile_offsets(0, 0)
    ids = [jnp.full((BLOCK, BLOCK), bucket_far(), jnp.int32)]
    ids += [bucket_index(shift * BLOCK + cols - rows) for shift in (-1, 0, 1)]
    hot = (jnp.stack(ids)[..., None] == jnp.arange(buckets, dtype=jnp.int32)).astype(jnp.float32)
    return jnp.einsum("hdxy,dxyb->hb", bands, hot, precision=TOP_PRECISION)


def bucket_far():
    return 8 + len(BOUNDS)


def on_device(
    tokens,
    qkv_weight,
    out_weight,
    position_bias_table,
    gain_attn,
    gain_moe,
    router,
    w_in,
    w_out,
    routes,
    prefix,
    valid_mask,
    teacher,
    cotangent,
):
    length, width = tokens.shape
    bf16, f32 = jnp.bfloat16, jnp.float32
    expert_count = router.shape[1]
    top_count = routes.shape[1]
    groups = lax.axis_size("expert")
    copies = lax.axis_size("dp")
    inner = w_in.shape[2]
    capacity = 5 * length * top_count // (4 * expert_count)
    total_tokens = length * copies * groups
    sources = 2 * groups
    blocks = length // BLOCK
    here_dp, here_group = lax.axis_index("dp"), lax.axis_index("expert")
    half = (here_dp // PAIR) % 2
    core = here_group % 2
    rest = copies // 4

    def swap(value, dp_mask, group_mask):
        pairs = [
            (i, ((i // groups) ^ dp_mask) * groups + ((i % groups) ^ group_mask))
            for i in range(copies * groups)
        ]
        return lax.ppermute(value, AXES, pairs)

    def bits(count):
        return [1 << place for place in range(count.bit_length() - 1)]

    def all_sum(value):
        for mask in bits(groups):
            value = value + swap(value, 0, mask)
        for mask in bits(copies):
            value = value + swap(value, mask, 0)
        return value

    near_count = groups

    def across(value, place):
        return swap(value, PAIR * (place // (groups // 2)), 2 * (place % (groups // 2)))

    def send_out(rows):
        parts = rows.reshape(2, near_count, capacity, width)
        got = [across(parts[:, place], place) for place in range(1, near_count)]
        relay = jnp.stack([parts[1, 0]] + [pair[1] for pair in got])
        relay = swap(relay, 0, 1)
        direct = jnp.stack([parts[0, 0]] + [pair[0] for pair in got])
        return jnp.concatenate([direct, relay]).reshape(slot_count, width)

    def send_back(rows):
        parts = rows.reshape(2, near_count, capacity, width)
        relay = swap(parts[1], 0, 1)
        got = [across(jnp.stack([parts[0, place], relay[place]]), place) for place in range(1, near_count)]
        return parts[0, 0], relay, got

    def collect(own, relay, got):
        direct = jnp.stack([own] + [pair[0] for pair in got])
        relay = jnp.stack([relay[0]] + [pair[1] for pair in got])
        return jnp.concatenate([direct, relay]).reshape(slot_count, width)

    columns = width // 2
    mine = lax.dynamic_slice_in_dim(qkv_weight, core * columns, columns, 2)
    mine = lax.all_gather(mine, "dp", axis=1, tiled=True)
    out_full = lax.all_gather(after(out_weight, mine), "dp", axis=0, tiled=True)
    other = swap(mine, 0, 1)
    first, second = jnp.where(core == 0, mine, other), jnp.where(core == 0, other, mine)
    qkv_full = jnp.concatenate([first, second], axis=-1)
    valid_rows = valid_mask.astype(f32)[:, None]
    valid_count = all_sum(jnp.broadcast_to(jnp.sum(valid_rows), (8, 128)))[0, 0]
    prefix_len = prefix[0]
    near = near_bias(position_bias_table, prefix_len, blocks)

    flat_routes = routes.reshape(-1)
    pair_count = length * top_count
    slot_count = sources * capacity
    route_hits = (flat_routes[:, None] == jnp.arange(expert_count, dtype=jnp.int32)[None, :]).astype(bf16)
    lower_ones = (
        lax.broadcasted_iota(jnp.int32, (pair_count, pair_count), 0)
        >= lax.broadcasted_iota(jnp.int32, (pair_count, pair_count), 1)
    ).astype(bf16)
    running = jnp.dot(lower_ones, route_hits, preferred_element_type=f32)
    pair_rank = jnp.sum((running - 1.0) * route_hits.astype(f32), axis=1).astype(jnp.int32)
    away = (flat_routes // 2) ^ here_group
    away = ((away % 2) * 2 + ((flat_routes % 2) ^ half)) * (groups // 2) + away // 2
    slot_of_pair = (away * capacity + pair_rank).reshape(length, top_count)
    slot_hot = (
        slot_of_pair[:, :, None] == lax.broadcasted_iota(jnp.int32, (1, 1, slot_count), 2)
    ).astype(bf16)

    resid = tokens.astype(f32)
    normed1 = norm_apply(resid, gain_attn).astype(bf16)
    qkv_rows = jnp.einsum("td,cde->cte", normed1, qkv_full, preferred_element_type=f32).astype(bf16)
    attended, probs = attention_forward(position_bias_table[:, bucket_far()], qkv_rows, near)
    middle = resid + jnp.dot(attended, out_full, preferred_element_type=f32)
    normed2 = norm_apply(middle, gain_moe).astype(bf16)
    logits = jnp.dot(normed2, router, preferred_element_type=f32)
    gate_vals = gate_values(logits, routes)

    send_rows = jnp.einsum("tks,td->sd", slot_hot, normed2, preferred_element_type=f32).astype(bf16)
    rows_in = send_out(send_rows)
    pick = half.reshape(1).astype(jnp.int32)
    hidden_t, slope, produced, rows_t = expert_forward(pick, rows_in, w_in, w_out)
    returned = collect(*send_back(produced))
    picked = jnp.einsum("tks,sd->tkd", slot_hot, returned, preferred_element_type=f32)
    output = middle + jnp.sum(gate_vals[:, :, None] * picked, axis=1)
    misfit = output - teacher.astype(f32)
    square_sum = jnp.sum(valid_rows * misfit * misfit)
    grad_y = cotangent.astype(f32) + valid_rows * misfit * (total_tokens / valid_count)
    grad_pairs = (gate_vals[:, :, None] * grad_y[:, None, :]).astype(bf16)
    send_grads = jnp.einsum("tks,tkd->sd", slot_hot, grad_pairs, preferred_element_type=f32).astype(bf16)
    grad_rows = send_out(send_grads)

    out_rows = inner // copies
    in_rows = width // copies
    far_bit = here_dp % 2
    slices = jnp.arange(rest, dtype=jnp.int32) * 4

    def pieces_of(left, right, rows, bit0, layout, tile):
        picks = jnp.concatenate([slices + ((half ^ other_half) * 2 + bit0) for other_half in (1, 0)])
        return weight_part(picks.astype(jnp.int32), left, right, rows, layout, tile)

    def add(left, right):
        return (left.astype(f32) + right.astype(f32)).astype(bf16)

    def fold(unit, bit):
        unit = unit.reshape((2, unit.shape[0] // 2) + unit.shape[1:])
        away_part = lax.dynamic_index_in_dim(unit, 1 - bit, 0, keepdims=False)
        return away_part, lax.dynamic_index_in_dim(unit, bit, 0, keepdims=False)

    far_masks = list(reversed(bits(copies)[2:]))

    def near_add(got, keep):
        away_part, stay_part = fold(add(got, keep), (here_dp // far_masks[0]) % 2)
        return away_part, stay_part

    def far_trade(away_part):
        return swap(away_part, far_masks[0], 0)

    def finish(got, stay):
        unit = add(got, stay)
        for mask in far_masks[1:]:
            away_part, stay_part = fold(unit, (here_dp // mask) % 2)
            unit = add(swap(away_part, mask, 0), stay_part)
        return unit[0]

    out_layout, in_layout = (2, 3, 1), (2, 1, 1, 2)
    send_a, send_b, send_c = pieces_of(hidden_t, grad_rows, out_rows, 1 - far_bit, out_layout, width)
    got_a = swap(send_a, 1, 0)
    grad_pre, grad_in_rows = expert_backward(pick, after(grad_rows, send_a), w_in, w_out, slope)
    own, traded, sent_back = send_back(after(grad_in_rows, got_a))
    got_b = swap(after(send_b, traded), 1, 0)
    grad_pre = after(grad_pre, traded)
    send_d, send_e, send_f, send_g = pieces_of(rows_t, grad_pre, in_rows, 1 - far_bit, in_layout, 512)
    keep_d, keep_e, keep_f, keep_g = pieces_of(rows_t, grad_pre, in_rows, far_bit, in_layout, 512)
    keep_a, keep_b, keep_c = pieces_of(hidden_t, after(grad_rows, keep_d), out_rows, far_bit, out_layout, width)
    away_a, stay_a = near_add(got_a, keep_a)
    far_a = far_trade(away_a)
    away_b, stay_b = near_add(got_b, keep_b)
    sent_back = collect(own, traded, [after(pair, away_b) for pair in sent_back])
    sent_back, send_c, send_d = lax.optimization_barrier((sent_back, send_c, send_d))
    far_b = far_trade(away_b)
    got_c = swap(send_c, 1, 0)
    got_d = swap(send_d, 1, 0)

    grad_gates = jnp.sum(grad_y[:, None, :] * picked, axis=-1)
    grad_normed2 = jnp.einsum("tks,sd->td", slot_hot, sent_back, preferred_element_type=f32)
    gate_out, gate_back = jax.vjp(lambda logit_vals: gate_values(logit_vals, routes), logits)
    grad_logits = gate_back(grad_gates)[0].astype(bf16)
    grad_router = jnp.einsum("td,te->de", normed2, grad_logits, preferred_element_type=f32)
    grad_normed2 = grad_normed2 + jnp.einsum("te,de->td", grad_logits, router, preferred_element_type=f32)
    norm_out, norm_back = jax.vjp(norm_apply, middle, gain_moe)
    grad_mid_norm, grad_gain_moe = norm_back(grad_normed2)
    grad_middle = grad_y + grad_mid_norm
    grad_attn_proj = grad_middle.astype(bf16)
    grad_attended = jnp.einsum("te,de->td", grad_attn_proj, out_full, preferred_element_type=f32).astype(bf16)
    grad_q, grad_k, grad_v, bands = attention_backward(qkv_rows, grad_attended, probs)
    grad_q, grad_k, grad_v, got_c, got_d = lax.optimization_barrier((grad_q, grad_k, grad_v, got_c, got_d))
    done_a = finish(after(far_a, grad_q), stay_a)

    away_c, stay_c = near_add(got_c, keep_c)
    far_c = far_trade(away_c)
    away_d, stay_d = near_add(got_d, keep_d)
    far_d = far_trade(away_d)
    got_e, got_f, got_g = [swap(after(send, away_d), 1, 0) for send in (send_e, send_f, send_g)]
    away_e, stay_e = near_add(got_e, keep_e)
    far_e = far_trade(away_e)
    away_f, stay_f = near_add(after(got_f, stay_e), keep_f)
    far_f = far_trade(away_f)
    away_g, stay_g = near_add(after(got_g, stay_f), keep_g)
    far_g = far_trade(away_g)
    done_b = finish(far_b, stay_b)
    done_c = finish(far_c, stay_c)
    done_d = finish(far_d, stay_d)
    done_e = finish(far_e, stay_e)
    done_f = finish(far_f, stay_f)
    done_g = finish(far_g, stay_g)
    due = [(stay_e,), (stay_g, done_b, done_c, done_d), (done_e, done_f), (done_g,)]

    def weight_gradient(left, right):
        return jnp.einsum("td,te->de", left, right, preferred_element_type=f32).astype(bf16)

    mats = [weight_gradient(normed1, part) for part in (grad_q, grad_k, grad_v)]
    mats.append(weight_gradient(attended, grad_attn_proj))
    group_bits = bits(groups)
    share = 4 * in_rows // groups
    if share == in_rows:
        total = jnp.stack([mats[0], mats[2], mats[1], mats[3]]).reshape((2,) * len(group_bits) + (copies, share, width))
    else:
        total = jnp.stack(mats).reshape(4, copies, in_rows, width).transpose(1, 0, 2, 3)
        total = total.reshape((copies,) + (2,) * len(group_bits) + (share, width))
        order = list(range(len(group_bits), 0, -1)) + [0, len(group_bits) + 1, len(group_bits) + 2]
        total = total.transpose(order)
    for mask in group_bits:
        bit = (here_group // mask) % 2
        away_part = lax.dynamic_index_in_dim(total, 1 - bit, 0, keepdims=False)
        stay_part = lax.dynamic_index_in_dim(total, bit, 0, keepdims=False)
        total = add(after(swap(away_part, 0, mask), *(due.pop(0) if due else ())), stay_part)
    for mask in reversed(bits(copies)):
        away_part, stay_part = fold(total, (here_dp // mask) % 2)
        total = add(after(swap(away_part, mask, 0), *(due.pop(0) if due else ())), stay_part)
    total = total[0]
    for mask in reversed(group_bits):
        bit = (here_group // mask) % 2
        other = swap(total, 0, mask)
        total = jnp.stack([jnp.where(bit == 0, total, other), jnp.where(bit == 0, other, total)])
    order = list(range(len(group_bits) - 1, -1, -1)) + [len(group_bits), len(group_bits) + 1]
    total = total.transpose(order).reshape(4, in_rows, width).astype(f32)
    grad_qkv, grad_out_weight = total[:3], total[3]

    grad_normed1 = sum(
        jnp.einsum("te,de->td", part, qkv_full[c], preferred_element_type=f32)
        for c, part in enumerate((grad_q, grad_k, grad_v))
    )
    first_out, first_back = jax.vjp(norm_apply, resid, gain_attn)
    grad_resid_norm, grad_gain_attn = first_back(grad_normed1)
    grad_input = grad_middle + grad_resid_norm
    grad_table = table_gradient(bands, position_bias_table.shape[1])

    out_theirs = swap(jnp.concatenate([done_a, done_b[:1]]), PAIR, 0)
    out_mine = jnp.concatenate([done_b[1:], done_c])
    in_theirs = swap(jnp.concatenate([done_d, done_e]), PAIR, 0)
    in_mine = jnp.concatenate([done_f, done_g])

    def both_experts(mine, theirs):
        mine, theirs = [part.reshape(-1, part.shape[-1]).astype(f32) for part in (mine, theirs)]
        return jnp.stack([jnp.where(half == 0, mine, theirs), jnp.where(half == 0, theirs, mine)])

    grad_w_out = both_experts(out_mine, out_theirs)
    grad_w_in = both_experts(in_mine, in_theirs)

    def sum_many(values):
        flat = jnp.concatenate([value.reshape(-1) for value in values])
        size = flat.shape[0]
        flat = jnp.pad(flat, (0, -size % 1024)).reshape(-1, 128)
        flat = all_sum(flat).reshape(-1)
        done, place = [], 0
        for value in values:
            done.append(flat[place : place + value.size].reshape(value.shape))
            place += value.size
        return done

    grad_gain_moe, grad_router, square_total, grad_gain_attn, grad_table = sum_many(
        (grad_gain_moe, grad_router, square_sum, grad_gain_attn, grad_table)
    )
    distill_loss = square_total / (width * valid_count)
    return (
        output.astype(bf16),
        distill_loss,
        grad_input,
        grad_qkv,
        grad_out_weight,
        grad_w_in,
        grad_w_out,
        grad_router,
        grad_table,
        grad_gain_attn,
        grad_gain_moe,
    )


def solution(mesh):
    rows = P(AXES, None)
    return jax.shard_map(
        on_device,
        mesh=mesh,
        in_specs=(
            rows,
            P(None, "dp", None),
            P("dp", None),
            P(),
            P(),
            P(),
            P(),
            P("expert", None, None),
            P("expert", None, None),
            rows,
            P(AXES),
            P(AXES),
            rows,
            rows,
        ),
        out_specs=(
            rows,
            P(),
            rows,
            P(None, "dp", None),
            P("dp", None),
            P("expert", "dp", None),
            P("expert", "dp", None),
            P(),
            P(),
            P(),
            P(),
        ),
        check_vma=False,
    )
```

```python
import math
import jax
import jax.numpy as jnp
from jax import lax
from jax.experimental import pallas as pl
from jax.experimental.pallas import tpu as pltpu
from jax.sharding import PartitionSpec as P

BLOCK = 128
THIRDS = 3
EPS = 1e-06
GELU_A = math.sqrt(2.0 / math.pi)
GELU_B = 0.044715
NT = (((1,), (1,)), ((), ()))
TN = (((0,), (0,)), ((), ()))
VMEM_BYTES = 56 * 1024 * 1024


def cost(micros):
    return pl.CostEstimate(flops=int(micros * 0.37e9), bytes_accessed=0, transcendentals=0)


def dot_f32(left, right, dims=(((1,), (0,)), ((), ()))):
    return lax.dot_general(left, right, dims, preferred_element_type=jnp.float32)


def assemble(rows, pieces, relayed):
    capacity = pieces[0].shape[0] // 2
    for place, piece in enumerate(pieces):
        rows[pl.ds(place * capacity, capacity), :] = piece[pl.ds(0, capacity), :]
    rows[pl.ds(len(pieces) * capacity, relayed.shape[0]), :] = relayed[...]


def whole(shape):
    return pl.BlockSpec(shape, lambda *step: (0,) * len(shape))


def expert_forward_kernel(pick, *refs, chunk, count):
    pieces, relayed, w_in, w_out = refs[:count], refs[count], refs[count + 1], refs[count + 2]
    hidden_t, slope, mine, theirs, rows_t, rows, total = refs[count + 3 :]
    step = pl.program_id(0)

    @pl.when(step == 0)
    def _():
        assemble(rows, pieces, relayed)
        total[...] = jnp.zeros_like(total)
        rows_t[...] = rows[...].T

    for start in range(0, rows.shape[0], chunk):
        part = pl.ds(start, chunk)
        pre = dot_f32(rows[part, :], w_in[0])
        square = pre * pre
        bend = jnp.tanh(pre * (GELU_A + (GELU_A * GELU_B) * square))
        half = 0.5 + 0.5 * bend
        act = (pre * half).astype(jnp.bfloat16)
        lift = pre * (0.5 * GELU_A + (1.5 * GELU_A * GELU_B) * square)
        slope[part, :] = (half + lift * (1.0 - bend * bend)).astype(jnp.bfloat16)
        hidden_t[:, part] = act.T
        total[part, :] += dot_f32(act, w_out[0])

    @pl.when(step == pl.num_programs(0) - 1)
    def _():
        half = mine.shape[0]
        mine[...] = total[pl.ds(0, half), :].astype(jnp.bfloat16)
        theirs[...] = total[pl.ds(half, half), :].astype(jnp.bfloat16)


def expert_forward(pick, pieces, relayed, w_in, w_out, tile=512, chunk=256):
    many, width = pieces[0].shape[0] * len(pieces), relayed.shape[1]
    inner = w_in.shape[2]
    bf16 = jnp.bfloat16
    return pl.pallas_call(
        lambda *refs: expert_forward_kernel(*refs, chunk=chunk, count=len(pieces)),
        grid_spec=pltpu.PrefetchScalarGridSpec(
            num_scalar_prefetch=1,
            grid=(inner // tile,),
            in_specs=[whole(piece.shape) for piece in pieces]
            + [
                whole(relayed.shape),
                pl.BlockSpec((1, width, tile), lambda f, pick: (pick[0], 0, f)),
                pl.BlockSpec((1, tile, width), lambda f, pick: (pick[0], f, 0)),
            ],
            out_specs=[
                pl.BlockSpec((tile, many), lambda f, pick: (f, 0)),
                pl.BlockSpec((many, tile), lambda f, pick: (0, f)),
                whole((many // 2, width)),
                whole((many // 2, width)),
                whole((width, many)),
            ],
            scratch_shapes=[pltpu.VMEM((many, width), bf16), pltpu.VMEM((many, width), jnp.float32)],
        ),
        out_shape=[
            jax.ShapeDtypeStruct((inner, many), bf16),
            jax.ShapeDtypeStruct((many, inner), bf16),
            jax.ShapeDtypeStruct((many // 2, width), bf16),
            jax.ShapeDtypeStruct((many // 2, width), bf16),
            jax.ShapeDtypeStruct((width, many), bf16),
        ],
        compiler_params=pltpu.CompilerParams(vmem_limit_bytes=VMEM_BYTES),
        cost_estimate=cost(22),
        name="expert_forward",
    )(pick, *pieces, relayed, w_in, w_out)


def expert_backward_kernel(pick, grads, w_in, w_out, slope, grad_pre, mine, theirs, total, *, chunk):
    step = pl.program_id(0)

    @pl.when(step == 0)
    def _():
        total[...] = jnp.zeros_like(total)

    for start in range(0, grads.shape[0], chunk):
        part = pl.ds(start, chunk)
        back = dot_f32(grads[part, :], w_out[0], NT) * slope[part, :].astype(jnp.float32)
        back = back.astype(jnp.bfloat16)
        grad_pre[part, :] = back
        total[part, :] += dot_f32(back, w_in[0], NT)

    @pl.when(step == pl.num_programs(0) - 1)
    def _():
        half = mine.shape[0]
        mine[...] = total[pl.ds(0, half), :].astype(jnp.bfloat16)
        theirs[...] = total[pl.ds(half, half), :].astype(jnp.bfloat16)


def expert_backward(pick, grads, w_in, w_out, slope, tile=512, chunk=640):
    many, width = grads.shape
    inner = w_in.shape[2]
    bf16 = jnp.bfloat16
    return pl.pallas_call(
        lambda *refs: expert_backward_kernel(*refs, chunk=chunk),
        grid_spec=pltpu.PrefetchScalarGridSpec(
            num_scalar_prefetch=1,
            grid=(inner // tile,),
            in_specs=[
                whole((many, width)),
                pl.BlockSpec((1, width, tile), lambda f, pick: (pick[0], 0, f)),
                pl.BlockSpec((1, tile, width), lambda f, pick: (pick[0], f, 0)),
                pl.BlockSpec((many, tile), lambda f, pick: (0, f)),
            ],
            out_specs=[
                pl.BlockSpec((many, tile), lambda f, pick: (0, f)),
                whole((many // 2, width)),
                whole((many // 2, width)),
            ],
            scratch_shapes=[pltpu.VMEM((many, width), jnp.float32)],
        ),
        out_shape=[
            jax.ShapeDtypeStruct((many, inner), bf16),
            jax.ShapeDtypeStruct((many // 2, width), bf16),
            jax.ShapeDtypeStruct((many // 2, width), bf16),
        ],
        compiler_params=pltpu.CompilerParams(vmem_limit_bytes=VMEM_BYTES),
        cost_estimate=cost(20),
        name="expert_backward",
    )(pick, grads, w_in, w_out, slope)


def seen_blocks(row_block, blocks):
    return max(row_block + 1, blocks // 2)


def attention_forward_kernel(far, queries, keys, values, near, attended, probs, *, heads, blocks):
    pair = pl.program_id(0)
    lane = lax.broadcasted_iota(jnp.int32, (BLOCK, 2 * heads), 1)
    for row_block in range(blocks):
        rows = pl.ds(row_block * BLOCK, BLOCK)
        span = seen_blocks(row_block, blocks)
        seen = pl.ds(0, span * BLOCK)
        outs = []
        for head in range(2):
            mine = (lane < heads) if head == 0 else (lane >= heads)
            query = jnp.where(mine, queries[rows, :] * 0.125, 0.0).astype(jnp.bfloat16)
            score = dot_f32(query, keys[seen, :], NT)
            far_bias = far[pair * 2 + head]
            pieces = []
            for key_block in range(span):
                piece = score[:, key_block * BLOCK : (key_block + 1) * BLOCK]
                slot = near_slot(row_block, key_block, blocks)
                pieces.append(piece + (far_bias if slot is None else near[head, slot]))
            peak = pieces[0]
            for piece in pieces[1:]:
                peak = jnp.maximum(peak, piece)
            peak = jnp.max(peak, axis=1, keepdims=True)
            pieces = [jnp.exp(piece - peak) for piece in pieces]
            mass = pieces[0]
            for piece in pieces[1:]:
                mass = mass + piece
            scale = 1.0 / jnp.sum(mass, axis=1, keepdims=True)
            weights = jnp.concatenate([(piece * scale).astype(jnp.bfloat16) for piece in pieces], axis=1)
            probs[head, rows, seen] = weights
            outs.append(dot_f32(weights, values[seen, :]))
        attended[rows, :] = jnp.where(lane < heads, outs[0], outs[1]).astype(jnp.bfloat16)


def near_slot(row_block, key_block, blocks):
    half = blocks // 2
    if key_block < row_block - 1:
        return None
    if key_block == row_block - 1:
        return 0
    if key_block == row_block:
        return 1 + min(row_block, half)
    count = 2 + half
    for row in range(half):
        for key in range(row + 1, half):
            if (row, key) == (row_block, key_block):
                return count
            count += 1
    raise ValueError


def near_pairs(blocks):
    half = blocks // 2
    pairs = [(1, 0)] + [(row, row) for row in range(half + 1)]
    return pairs + [(row, key) for row in range(half) for key in range(row + 1, half)]


def attention_forward(far, qk_rows, v_rows, near):
    length, width = v_rows.shape
    pairs = width // 128
    blocks = length // BLOCK
    slots = near.shape[1]
    return pl.pallas_call(
        lambda *refs: attention_forward_kernel(*refs, heads=64, blocks=blocks),
        grid_spec=pltpu.PrefetchScalarGridSpec(
            num_scalar_prefetch=1,
            grid=(pairs,),
            in_specs=[
                pl.BlockSpec((None, length, 128), lambda h, far: (0, 0, h)),
                pl.BlockSpec((None, length, 128), lambda h, far: (1, 0, h)),
                pl.BlockSpec((length, 128), lambda h, far: (0, h)),
                pl.BlockSpec((2, slots, BLOCK, BLOCK), lambda h, far: (h, 0, 0, 0)),
            ],
            out_specs=[
                pl.BlockSpec((length, 128), lambda h, far: (0, h)),
                pl.BlockSpec((2, length, length), lambda h, far: (h, 0, 0)),
            ],
        ),
        out_shape=[
            jax.ShapeDtypeStruct((length, width), jnp.bfloat16),
            jax.ShapeDtypeStruct((2 * pairs, length, length), jnp.bfloat16),
        ],
        compiler_params=pltpu.CompilerParams(vmem_limit_bytes=VMEM_BYTES),
        cost_estimate=cost(17),
        name="attention_forward",
    )(far, qk_rows, qk_rows, v_rows, near)


def attention_backward_kernel(queries, keys, values, grads, probs, grad_rows, bands, flow, *, heads, blocks):
    lane = lax.broadcasted_iota(jnp.int32, (BLOCK, 2 * heads), 1)
    query_t = (queries[...] * 0.125).astype(jnp.bfloat16).T
    grad_t = grads[...].T
    half = blocks // 2
    dk, dv = [], []
    dq = [[], []]
    for head in range(2):
        mine = (lane < heads) if head == 0 else (lane >= heads)
        sums = [None] * 4
        for row_block in range(blocks):
            rows = pl.ds(row_block * BLOCK, BLOCK)
            span = seen_blocks(row_block, blocks)
            seen = pl.ds(0, span * BLOCK)
            grad = jnp.where(mine, grads[rows, :], 0.0).astype(jnp.bfloat16)
            soft = probs[head, rows, seen].astype(jnp.float32)
            back = dot_f32(grad, values[seen, :], NT)
            inner = jnp.sum(soft * back, axis=1, keepdims=True)
            score_grad = (soft * (back - inner)).astype(jnp.bfloat16)
            flow[rows, seen] = score_grad
            dq[head].append(dot_f32(score_grad, keys[seen, :]) * 0.125)
            for key_block in range(span):
                band = max(key_block - row_block, -2)
                if band > 1:
                    continue
                tile = score_grad[:, key_block * BLOCK : (key_block + 1) * BLOCK].astype(jnp.float32)
                sums[band + 2] = tile if sums[band + 2] is None else sums[band + 2] + tile
        for band in range(4):
            bands[head, band] = sums[band]
        part = slice(head * heads, (head + 1) * heads)
        key_pieces, value_pieces = [], []
        for key_block in range(blocks):
            first = 0 if key_block < half else key_block
            rows = pl.ds(first * BLOCK, (blocks - first) * BLOCK)
            cols = pl.ds(key_block * BLOCK, BLOCK)
            key_pieces.append(dot_f32(query_t[part, first * BLOCK :], flow[rows, cols]))
            value_pieces.append(dot_f32(grad_t[part, first * BLOCK :], probs[head, rows, cols]))
        dk.append(jnp.concatenate(key_pieces, axis=1))
        dv.append(jnp.concatenate(value_pieces, axis=1))
    for row_block in range(blocks):
        rows = pl.ds(row_block * BLOCK, BLOCK)
        grad_rows[0, rows, :] = jnp.where(lane < heads, dq[0][row_block], dq[1][row_block]).astype(jnp.bfloat16)
    grad_rows[1] = jnp.concatenate(dk, axis=0).T.astype(jnp.bfloat16)
    grad_rows[2] = jnp.concatenate(dv, axis=0).T.astype(jnp.bfloat16)


def attention_backward(qk_rows, v_rows, grads, probs):
    length, width = grads.shape
    pairs = width // 128
    blocks = length // BLOCK
    block = pl.BlockSpec((length, 128), lambda h: (0, h))
    of_two = [pl.BlockSpec((None, length, 128), lambda h, c=c: (c, 0, h)) for c in range(2)]
    return pl.pallas_call(
        lambda *refs: attention_backward_kernel(*refs, heads=64, blocks=blocks),
        grid=(pairs,),
        in_specs=[*of_two, block, block, pl.BlockSpec((2, length, length), lambda h: (h, 0, 0))],
        out_specs=[pl.BlockSpec((3, length, 128), lambda h: (0, 0, h)), pl.BlockSpec((2, 4, BLOCK, BLOCK), lambda h: (h, 0, 0, 0))],
        out_shape=[jax.ShapeDtypeStruct((3, length, width), jnp.bfloat16)]
        + [jax.ShapeDtypeStruct((2 * pairs, 4, BLOCK, BLOCK), jnp.float32)],
        scratch_shapes=[pltpu.VMEM((length, length), jnp.bfloat16)],
        compiler_params=pltpu.CompilerParams(vmem_limit_bytes=VMEM_BYTES),
        cost_estimate=cost(17),
        name="attention_backward",
    )(qk_rows, qk_rows, v_rows, grads, probs)


def cut_slices(result, outs, count, layout):
    rows = result.shape[0] // count
    part, many = rows // THIRDS, count // 2
    place = 0
    for out, pieces in zip(outs, layout):
        for piece in range(pieces):
            half, third = divmod(place, THIRDS)
            for k in range(many):
                start = (half * many + k) * rows + third * part
                out[k, piece] = result[start : start + part]
            place += 1


def weight_part_kernel(picks, *refs, count, layout):
    lefts, right, outs = refs[:count], refs[count], refs[count + 1 :]
    left = jnp.concatenate([ref[...] for ref in lefts], axis=0)
    cut_slices(dot_f32(left, right[...]).astype(jnp.bfloat16), outs, count, layout)


def weight_first_kernel(picks, *refs, count, layout, pieces):
    lefts, parts, relayed, outs = refs[:count], refs[count : count + pieces], refs[count + pieces], refs[count + pieces + 1 :]
    assemble(outs[0], parts, relayed)
    left = jnp.concatenate([ref[...] for ref in lefts], axis=0)
    cut_slices(dot_f32(left, outs[0][...]).astype(jnp.bfloat16), outs[1:], count, layout)


def weight_part_plain(picks, left, right, rows, layout):
    depth, width = right.shape
    many, part = picks.shape[0] // 2, rows // THIRDS
    result = jnp.take(left.reshape(-1, rows, depth), picks, axis=0)
    result = jnp.einsum("srd,dw->srw", result, right, preferred_element_type=jnp.float32).astype(jnp.bfloat16)
    result = result.reshape(2, many, THIRDS, part, width).transpose(1, 0, 2, 3, 4).reshape(many, 2 * THIRDS, part, width)
    starts = [sum(layout[:place]) for place in range(len(layout))]
    return [result[:, start : start + pieces] for start, pieces in zip(starts, layout)]


def weight_part(picks, left, right, rows, layout, tile):
    depth, width = right.shape
    count = picks.shape[0]
    many, part = count // 2, rows // THIRDS
    if part % 16:
        return weight_part_plain(picks, left, right, rows, layout)
    return pl.pallas_call(
        lambda *refs: weight_part_kernel(*refs, count=count, layout=layout),
        grid_spec=pltpu.PrefetchScalarGridSpec(
            num_scalar_prefetch=1,
            grid=(width // tile,),
            in_specs=[pl.BlockSpec((rows, depth), lambda i, picks, k=k: (picks[k], 0)) for k in range(count)]
            + [pl.BlockSpec((depth, tile), lambda i, picks: (0, i))],
            out_specs=[pl.BlockSpec((many, pieces, part, tile), lambda i, picks: (0, 0, 0, i)) for pieces in layout],
        ),
        out_shape=[jax.ShapeDtypeStruct((many, pieces, part, width), jnp.bfloat16) for pieces in layout],
        compiler_params=pltpu.CompilerParams(vmem_limit_bytes=VMEM_BYTES),
        cost_estimate=cost(7),
        name="weight_part",
    )(picks, *([left] * count), right)


def weight_first(picks, left, pieces, relayed, rows, layout):
    depth, width = left.shape[1], relayed.shape[1]
    count = picks.shape[0]
    many, part = count // 2, rows // THIRDS
    if part % 16:
        capacity = pieces[0].shape[0] // 2
        right = jnp.concatenate([piece[:capacity] for piece in pieces] + [relayed])
        return [right, *weight_part_plain(picks, left, right, rows, layout)]
    return pl.pallas_call(
        lambda *refs: weight_first_kernel(*refs, count=count, layout=layout, pieces=len(pieces)),
        grid_spec=pltpu.PrefetchScalarGridSpec(
            num_scalar_prefetch=1,
            grid=(1,),
            in_specs=[pl.BlockSpec((rows, depth), lambda i, picks, k=k: (picks[k], 0)) for k in range(count)]
            + [whole(piece.shape) for piece in pieces]
            + [whole(relayed.shape)],
            out_specs=[whole((depth, width))] + [whole((many, pieces, part, width)) for pieces in layout],
        ),
        out_shape=[jax.ShapeDtypeStruct((depth, width), jnp.bfloat16)]
        + [jax.ShapeDtypeStruct((many, pieces, part, width), jnp.bfloat16) for pieces in layout],
        compiler_params=pltpu.CompilerParams(vmem_limit_bytes=VMEM_BYTES),
        cost_estimate=cost(7),
        name="weight_first",
    )(picks, *([left] * count), *pieces, relayed)


def hot_columns(slots, first, count):
    rows = first + lax.broadcasted_iota(jnp.int32, (count, slots.shape[1]), 0)
    return (rows == slots).astype(jnp.bfloat16)


def hot_rows(slots, first, count):
    cols = first + lax.broadcasted_iota(jnp.int32, (slots.shape[0], count), 1)
    return (cols == slots).astype(jnp.bfloat16)


def pack_kernel(slots, values, *outs):
    table = values[...]
    for place, out in enumerate(outs):
        count = out.shape[0]
        hot = hot_columns(slots[0:1, :], place * count, count) + hot_columns(slots[1:2, :], place * count, count)
        out[...] = dot_f32(hot, table).astype(jnp.bfloat16)


def pack(slots, values, pieces, count):
    return pl.pallas_call(
        pack_kernel,
        out_shape=[jax.ShapeDtypeStruct((count, values.shape[1]), jnp.bfloat16)] * pieces,
        compiler_params=pltpu.CompilerParams(vmem_limit_bytes=VMEM_BYTES),
        cost_estimate=cost(4),
        name="pack",
    )(slots, values)


def slot_pieces(near, passed, far):
    capacity = far[0].shape[0] // 2
    return [(near, capacity), (passed, capacity)] + [(ref, 2 * capacity) for ref in far]


def unpack(slots, refs):
    total, first = None, 0
    for ref, count in refs:
        part = dot_f32(hot_rows(slots, first, count), ref[pl.ds(0, count), :])
        total = part if total is None else total + part
        first += count
    return total


def combine_kernel(*refs, chips):
    slots, slots_t, scale, near, passed = refs[:5]
    far = refs[5 : 5 + chips - 1]
    middle, teacher, cotangent, valid, gates = refs[4 + chips : 9 + chips]
    output, grad_y, grad_gates, square = refs[9 + chips : 13 + chips]
    sends = refs[13 + chips :]
    f32 = jnp.float32
    order = slot_pieces(near, passed, far)
    picked = [unpack(slots[:, k : k + 1], order) for k in range(2)]
    result = middle[...] + (gates[:, 0:1] * picked[0] + gates[:, 1:2] * picked[1])
    output[...] = result.astype(jnp.bfloat16)
    misfit = valid[...] * (result - teacher[...].astype(f32))
    square[...] = jnp.sum((misfit * misfit).reshape(-1, 8, misfit.shape[1]), axis=0)
    grad = cotangent[...].astype(f32) + misfit * scale[0, 0]
    grad_y[...] = grad
    for k in range(2):
        grad_gates[:, k : k + 1] = jnp.sum(grad * picked[k], axis=1, keepdims=True)
    scaled = [(gates[:, k : k + 1] * grad).astype(jnp.bfloat16) for k in range(2)]
    for place, out in enumerate(sends):
        count = out.shape[0]
        rows = [dot_f32(hot_columns(slots_t[k : k + 1, :], place * count, count), scaled[k]) for k in range(2)]
        out[...] = (rows[0] + rows[1]).astype(jnp.bfloat16)


def combine(slots, scale, near, passed, far, middle, teacher, cotangent, valid, gates):
    length, width = middle.shape
    chips = len(far) + 1
    f32, bf16 = jnp.float32, jnp.bfloat16
    return pl.pallas_call(
        lambda *refs: combine_kernel(*refs, chips=chips),
        in_specs=[pl.BlockSpec(memory_space=pltpu.VMEM)] * 2
        + [pl.BlockSpec(memory_space=pltpu.SMEM)]
        + [pl.BlockSpec(memory_space=pltpu.VMEM)] * (6 + chips),
        out_shape=[
            jax.ShapeDtypeStruct((length, width), bf16),
            jax.ShapeDtypeStruct((length, width), f32),
            jax.ShapeDtypeStruct((length, 2), f32),
            jax.ShapeDtypeStruct((8, width), f32),
        ]
        + [jax.ShapeDtypeStruct(far[0].shape, bf16)] * chips,
        compiler_params=pltpu.CompilerParams(vmem_limit_bytes=VMEM_BYTES),
        cost_estimate=cost(8),
        name="combine",
    )(slots, slots.T, scale, near, passed, *far, middle, teacher, cotangent, valid, gates)


def collect_kernel(*refs, chips):
    slots, near, passed = refs[:3]
    far = refs[3 : 2 + chips]
    middle, gain, grad_logits, router, grad_y, weight = refs[2 + chips : 8 + chips]
    grad_middle, rounded, grad_attended, grad_gain = refs[8 + chips :]
    f32 = jnp.float32
    order = slot_pieces(near, passed, far)
    grad = dot_f32(grad_logits[...], router[...], NT)
    grad = grad + (unpack(slots[:, 0:1], order) + unpack(slots[:, 1:2], order))
    value = middle[...]
    root = lax.rsqrt(jnp.mean(value * value, axis=1, keepdims=True) + EPS)
    normed = value * root
    grad_gain[...] = jnp.sum((grad * normed).reshape(-1, 8, value.shape[1]), axis=0)
    scaled = grad * gain[...]
    inner = jnp.mean(scaled * normed, axis=1, keepdims=True)
    result = grad_y[...] + root * (scaled - normed * inner)
    grad_middle[...] = result
    low = result.astype(jnp.bfloat16)
    rounded[...] = low
    grad_attended[...] = dot_f32(low, weight[...], NT).astype(jnp.bfloat16)


def collect(slots, near, passed, far, middle, gain, grad_logits, router, grad_y, weight):
    length, width = middle.shape
    chips = len(far) + 1
    f32, bf16 = jnp.float32, jnp.bfloat16
    return pl.pallas_call(
        lambda *refs: collect_kernel(*refs, chips=chips),
        out_shape=[
            jax.ShapeDtypeStruct((length, width), f32),
            jax.ShapeDtypeStruct((length, width), bf16),
            jax.ShapeDtypeStruct((length, width), bf16),
            jax.ShapeDtypeStruct((8, width), f32),
        ],
        compiler_params=pltpu.CompilerParams(vmem_limit_bytes=VMEM_BYTES),
        cost_estimate=cost(7),
        name="collect",
    )(slots, near, passed, *far, middle, gain.reshape(1, -1), grad_logits, router, grad_y, weight)


def outer_halves_kernel(core, left, right, away, stay, left_t, *, count):
    step = pl.program_id(0)

    @pl.when(step == 0)
    def _():
        left_t[...] = left[...].T

    result = dot_f32(left_t[...], right[...]).astype(jnp.bfloat16)

    @pl.when(step < count)
    def _():
        away[...] = result

    @pl.when(step >= count)
    def _():
        stay[...] = result


def outer_halves(core, left, right):
    length, width = left.shape
    count, half = right.shape[0], right.shape[2] // 2
    shape = jax.ShapeDtypeStruct((count, width, half), jnp.bfloat16)
    return pl.pallas_call(
        lambda *refs: outer_halves_kernel(*refs, count=count),
        grid_spec=pltpu.PrefetchScalarGridSpec(
            num_scalar_prefetch=1,
            grid=(2 * count,),
            in_specs=[
                pl.BlockSpec((length, width), lambda i, core: (0, 0)),
                pl.BlockSpec((None, length, half), lambda i, core: (i % count, 0, jnp.where(i < count, 1 - core[0], core[0]))),
            ],
            out_specs=[
                pl.BlockSpec((None, width, half), lambda i, core: (jnp.minimum(i, count - 1), 0, 0)),
                pl.BlockSpec((None, width, half), lambda i, core: (jnp.maximum(i - count, 0), 0, 0)),
            ],
            scratch_shapes=[pltpu.VMEM((width, length), jnp.bfloat16)],
        ),
        out_shape=[shape, shape],
        compiler_params=pltpu.CompilerParams(vmem_limit_bytes=VMEM_BYTES),
        cost_estimate=cost(2 * count),
        name="outer_halves",
    )(core, left, right)


def project_kernel(core, rows, mine, other, result, joined, *, used):
    half = mine.shape[1]
    first = jnp.where(core[0] == 0, mine[...], other[...])
    second = jnp.where(core[0] == 0, other[...], mine[...])
    joined[:, :half] = first
    joined[:, half:] = second

    @pl.when(pl.program_id(0) < used)
    def _():
        result[:, :half] = dot_f32(rows[...], first).astype(jnp.bfloat16)
        result[:, half:] = dot_f32(rows[...], second).astype(jnp.bfloat16)


def project(core, rows, mine, other, used):
    count, width, half = mine.shape
    length = rows.shape[0]
    return pl.pallas_call(
        lambda *refs: project_kernel(*refs, used=used),
        grid_spec=pltpu.PrefetchScalarGridSpec(
            num_scalar_prefetch=1,
            grid=(count,),
            in_specs=[
                pl.BlockSpec((length, width), lambda i, core: (0, 0)),
                pl.BlockSpec((None, width, half), lambda i, core: (i, 0, 0)),
                pl.BlockSpec((None, width, half), lambda i, core: (i, 0, 0)),
            ],
            out_specs=[
                pl.BlockSpec((None, length, 2 * half), lambda i, core: (jnp.minimum(i, used - 1), 0, 0)),
                pl.BlockSpec((None, width, 2 * half), lambda i, core: (i, 0, 0)),
            ],
        ),
        out_shape=[
            jax.ShapeDtypeStruct((used, length, 2 * half), jnp.bfloat16),
            jax.ShapeDtypeStruct((count, width, 2 * half), jnp.bfloat16),
        ],
        compiler_params=pltpu.CompilerParams(vmem_limit_bytes=VMEM_BYTES),
        cost_estimate=cost(3),
        name="project",
    )(core, rows, mine, other)


BOUNDS = (12, 16, 23, 32, 46, 64, 91)
TOP_PRECISION = lax.Precision.HIGHEST
AXES = ("dp", "expert")
PAIR = 2


def after(value, *others):
    return lax.optimization_barrier((value, *others))[0] if others else value


def bucket_index(offset):
    distance = jnp.abs(offset)
    far_bucket = 8 + sum([(distance >= level).astype(jnp.int32) for level in BOUNDS])
    near_bucket = jnp.where(distance < 8, distance, far_bucket)
    return jnp.where(offset > 0, 16, 0) + near_bucket


def norm_apply(inputs, gain_vec):
    return inputs * lax.rsqrt(jnp.mean(inputs * inputs, axis=-1, keepdims=True) + EPS) * gain_vec


def gate_values(logits, routes):
    soft_probs = jax.nn.softmax(logits, axis=-1)
    picked_hot = (
        routes[:, :, None] == jnp.arange(logits.shape[1], dtype=jnp.int32)[None, None, :]
    ).astype(jnp.float32)
    chosen = jnp.sum(soft_probs[:, None, :] * picked_hot, axis=-1)
    return chosen / jnp.sum(chosen, axis=1, keepdims=True)


def tile_offsets(query_block, key_block):
    rows = query_block * BLOCK + lax.broadcasted_iota(jnp.int32, (BLOCK, BLOCK), 0)
    cols = key_block * BLOCK + lax.broadcasted_iota(jnp.int32, (BLOCK, BLOCK), 1)
    return rows, cols


def near_bias(table, prefix_len, blocks):
    buckets = table.shape[1]
    tiles = []
    for query_block, key_block in near_pairs(blocks):
        rows, cols = tile_offsets(query_block, key_block)
        hot = (bucket_index(cols - rows)[None] == jnp.arange(buckets, dtype=jnp.int32)[:, None, None]).astype(jnp.float32)
        tile = jnp.einsum("hb,bxy->hxy", table, hot, precision=TOP_PRECISION)
        if key_block >= query_block:
            tile = jnp.where(((cols <= rows) | (cols < prefix_len))[None], tile, -1e30)
        tiles.append(tile)
    return jnp.stack(tiles, axis=1)


def table_gradient(bands, buckets):
    rows, cols = tile_offsets(0, 0)
    ids = [jnp.full((BLOCK, BLOCK), bucket_far(), jnp.int32)]
    ids += [bucket_index(shift * BLOCK + cols - rows) for shift in (-1, 0, 1)]
    hot = (jnp.stack(ids)[..., None] == jnp.arange(buckets, dtype=jnp.int32)).astype(jnp.float32)
    return jnp.einsum("hdxy,dxyb->hb", bands, hot, precision=TOP_PRECISION)


def bucket_far():
    return 8 + len(BOUNDS)


def on_device(
    tokens,
    qkv_weight,
    out_weight,
    position_bias_table,
    gain_attn,
    gain_moe,
    router,
    w_in,
    w_out,
    routes,
    prefix,
    valid_mask,
    teacher,
    cotangent,
):
    length, width = tokens.shape
    bf16, f32 = jnp.bfloat16, jnp.float32
    expert_count = router.shape[1]
    top_count = routes.shape[1]
    groups = lax.axis_size("expert")
    copies = lax.axis_size("dp")
    inner = w_in.shape[2]
    capacity = 5 * length * top_count // (4 * expert_count)
    total_tokens = length * copies * groups
    sources = 2 * groups
    blocks = length // BLOCK
    here_dp, here_group = lax.axis_index("dp"), lax.axis_index("expert")
    half = (here_dp // PAIR) % 2
    core = here_group % 2
    rest = copies // 4

    def swap(value, dp_mask, group_mask):
        pairs = [
            (i, ((i // groups) ^ dp_mask) * groups + ((i % groups) ^ group_mask))
            for i in range(copies * groups)
        ]
        return lax.ppermute(value, AXES, pairs)

    def bits(count):
        return [1 << place for place in range(count.bit_length() - 1)]

    def partial_sums(value):
        sums = []
        for masks in [(0, mask) for mask in bits(groups)] + [(mask, 0) for mask in bits(copies)]:
            value = value + swap(value, *masks)
            sums.append(value)
        return sums

    chips = groups

    def across(value, place):
        return swap(value, PAIR * (place // (groups // 2)), 2 * (place % (groups // 2)))

    def send_out(pieces):
        got = [pieces[0]] + [across(pieces[place], place) for place in range(1, chips)]
        return got, swap(jnp.concatenate([piece[capacity:] for piece in got]), 0, 1)

    def send_back(mine, theirs):
        passed = swap(theirs, 0, 1)
        sends = []
        for place in range(1, chips):
            part = slice(place * capacity, (place + 1) * capacity)
            sends.append(jnp.concatenate([mine[part], passed[part]]))
        return passed, sends, [across(send, place) for place, send in enumerate(sends, 1)]

    def ring_place(device):
        return jnp.where(device % 2 == 0, device // 2, copies - 1 - device // 2)

    ring = list(range(0, copies, 2)) + list(range(copies - 1, 0, -2))

    def gather_ring(shard, due):
        if copies > 8:
            return lax.all_gather(shard, "dp", axis=1, tiled=True)
        count, rows, columns = shard.shape
        place = ring_place(here_dp)
        table = jnp.array(ring, jnp.int32)
        full = jnp.zeros((count, copies, rows, columns), bf16)
        full = lax.dynamic_update_index_in_dim(full, shard, here_dp, 1)
        for turn, steps in ((1, copies // 2), (-1, copies // 2 - 1)):
            held = shard
            pairs = [(ring[i], ring[(i + turn) % copies]) for i in range(copies)]
            for step in range(1, steps + 1):
                held = lax.ppermute(after(held, *due[step - 2 : step - 1]) if step > 1 else held, "dp", pairs)
                full = lax.dynamic_update_index_in_dim(full, held, table[(place - turn * step) % copies], 1)
        return full.reshape(count, copies * rows, columns)

    columns = width // 2
    core_index = core.reshape(1).astype(jnp.int32)
    shards = jnp.concatenate([qkv_weight, out_weight[None]])
    shards = lax.dynamic_slice_in_dim(shards, core * columns, columns, 2)
    valid_rows = valid_mask.astype(f32)[:, None]
    counts = partial_sums(jnp.broadcast_to(jnp.sum(valid_rows), (8, 128)))
    valid_count = counts[-1][0, 0]
    mine_qk, mine_vo = gather_ring(shards[:2], counts), gather_ring(shards[2:], ())
    other_qk, other_vo = swap(mine_qk, 0, 1), swap(mine_vo, 0, 1)
    prefix_len = prefix[0]
    near = near_bias(position_bias_table, prefix_len, blocks)

    flat_routes = routes.reshape(-1)
    pair_count = length * top_count
    slot_count = sources * capacity
    route_hits = (flat_routes[:, None] == jnp.arange(expert_count, dtype=jnp.int32)[None, :]).astype(bf16)
    lower_ones = (
        lax.broadcasted_iota(jnp.int32, (pair_count, pair_count), 0)
        >= lax.broadcasted_iota(jnp.int32, (pair_count, pair_count), 1)
    ).astype(bf16)
    running = jnp.dot(lower_ones, route_hits, preferred_element_type=f32)
    pair_rank = jnp.sum((running - 1.0) * route_hits.astype(f32), axis=1).astype(jnp.int32)
    away = (flat_routes // 2) ^ here_group
    chip = ((flat_routes % 2) ^ half) * (groups // 2) + away // 2
    slots = ((chip * 2 + away % 2) * capacity + pair_rank).reshape(length, top_count)
    slots_t = slots.T

    resid = tokens.astype(f32)
    normed1 = norm_apply(resid, gain_attn).astype(bf16)
    qk_rows, weight_qk = project(core_index, normed1, mine_qk, other_qk, 2)
    v_rows, weight_vo = project(core_index, normed1, mine_vo, other_vo, 1)
    v_rows = v_rows[0]
    near = after(near, valid_count)
    attended, probs = attention_forward(position_bias_table[:, bucket_far()], qk_rows, v_rows, near)
    middle = resid + jnp.dot(attended, weight_vo[1], preferred_element_type=f32)
    normed2 = norm_apply(middle, gain_moe).astype(bf16)
    sends = pack(slots_t, normed2, chips, 2 * capacity)
    logits = jnp.dot(normed2, router, preferred_element_type=f32)
    gate_vals = gate_values(logits, routes)

    rows_got, rows_passed = send_out(sends)
    pick = half.reshape(1).astype(jnp.int32)
    hidden_t, slope, mine, theirs, rows_t = expert_forward(pick, rows_got, rows_passed, w_in, w_out)
    passed, _, far = send_back(mine, theirs)
    scale = (total_tokens / valid_count).reshape(1, 1)
    output, grad_y, grad_gates, squares, *sends = combine(
        slots, scale, mine, passed, far, middle, teacher, cotangent, valid_rows, gate_vals
    )
    grads_got, grads_passed = send_out(sends)
    gate_back = jax.vjp(lambda logit_vals: gate_values(logit_vals, routes), logits)[1]
    grad_logits = gate_back(grad_gates)[0].astype(bf16)
    grad_router = jnp.einsum("td,te->de", normed2, grad_logits, preferred_element_type=f32)

    out_rows = inner // copies
    in_rows = width // copies
    far_bit = here_dp % 2
    slices = jnp.arange(rest, dtype=jnp.int32) * 4

    def picks(bit0):
        return jnp.concatenate([slices + ((half ^ other_half) * 2 + bit0) for other_half in (1, 0)]).astype(jnp.int32)

    sent, kept = picks(1 - far_bit), picks(far_bit)

    def add(left, right):
        return (left.astype(f32) + right.astype(f32)).astype(bf16)

    def fold(unit, bit, axis=0):
        unit = unit.reshape(unit.shape[:axis] + (2, unit.shape[axis] // 2) + unit.shape[axis + 1 :])
        away_part = lax.dynamic_index_in_dim(unit, 1 - bit, axis, keepdims=False)
        return away_part, lax.dynamic_index_in_dim(unit, bit, axis, keepdims=False)

    far_masks = list(reversed(bits(copies)[2:]))

    def near_add(got, keep):
        away_part, stay_part = fold(add(got, keep), (here_dp // far_masks[0]) % 2)
        return away_part, stay_part

    def far_trade(away_part):
        return swap(away_part, far_masks[0], 0)

    def finish(got, stay):
        unit = add(got, stay)
        for mask in far_masks[1:]:
            away_part, stay_part = fold(unit, (here_dp // mask) % 2)
            unit = add(swap(away_part, mask, 0), stay_part)
        return unit[0]

    out_layout, in_layout = (2, 3, 1), (2, 1, 1, 2)
    grad_rows, send_a, send_b, send_c = weight_first(sent, hidden_t, grads_got, grads_passed, out_rows, out_layout)
    got_a = swap(send_a, 1, 0)
    grad_pre, mine, theirs = expert_backward(pick, after(grad_rows, send_a), w_in, w_out, slope)
    passed, sends, far = send_back(mine, after(theirs, got_a))
    got_b = swap(after(send_b, passed), 1, 0)
    grad_pre = after(grad_pre, *sends)
    send_d, send_e, send_f, send_g = weight_part(sent, rows_t, grad_pre, in_rows, in_layout, inner // 2)
    keep_d, keep_e, keep_f, keep_g = weight_part(kept, rows_t, grad_pre, in_rows, in_layout, inner // 2)
    keep_a, keep_b, keep_c = weight_part(kept, hidden_t, after(grad_rows, keep_d), out_rows, out_layout, width)
    away_a, stay_a = near_add(got_a, keep_a)
    far_a = far_trade(away_a)
    away_b, stay_b = near_add(got_b, keep_b)
    far = [after(pair, away_b) for pair in far]
    far_b = far_trade(away_b)
    grad_middle, grad_attn_proj, grad_attended, gain_moe_parts = collect(
        slots, mine, passed, far, middle, gain_moe, grad_logits, router, grad_y, weight_vo[1]
    )
    grad_gain_moe = jnp.sum(gain_moe_parts, axis=0)
    send_c, send_d = after((send_c, send_d), *far)
    got_c = swap(send_c, 1, 0)
    got_d = swap(send_d, 1, 0)
    out_away, out_stay = outer_halves(core_index, attended, grad_attn_proj[None])
    out_got = swap(out_away, 0, 1)
    grad_attended = after(grad_attended, out_away)
    grad_qkv_rows, bands = attention_backward(qk_rows, v_rows, grad_attended, probs)
    grad_qkv_rows, got_c, got_d = lax.optimization_barrier((grad_qkv_rows, got_c, got_d))
    done_a = finish(after(far_a, grad_qkv_rows), stay_a)
    done_b = finish(after(far_b, grad_qkv_rows), stay_b)

    away_c, stay_c = near_add(got_c, keep_c)
    far_c = far_trade(away_c)
    away_d, stay_d = near_add(got_d, keep_d)
    far_d = far_trade(away_d)
    got_e, got_f, got_g = [swap(after(send, away_d), 1, 0) for send in (send_e, send_f, send_g)]

    qkv_away, qkv_stay = outer_halves(core_index, normed1, grad_qkv_rows)
    qkv_got = swap(qkv_away, 0, 1)
    away_e, stay_e = near_add(got_e, keep_e)
    far_e = far_trade(away_e)
    qkv_total = add(after(qkv_got, stay_e), qkv_stay)
    away_f, stay_f = near_add(after(got_f, qkv_total), keep_f)
    far_f = far_trade(away_f)
    group_masks = bits(groups)[1:]
    dp_masks = sorted(bits(copies), key=lambda mask: (mask != PAIR, mask))

    def owners(part):
        return part.reshape(part.shape[0], copies, in_rows, columns)

    def over_groups(total, due):
        for mask in group_masks:
            away_part, stay_part = fold(total, (here_group // mask) % 2, 2)
            total = add(after(swap(away_part, 0, mask), *due), stay_part)
        return total

    out_total = over_groups(owners(add(out_got, out_stay)), ())
    done_c = finish(after(far_c, qkv_total), stay_c)
    total = over_groups(owners(qkv_total), (stay_f, done_c))
    away_g, stay_g = near_add(after(got_g, total), keep_g)
    far_g = far_trade(away_g)
    far_d, far_e, far_f = [after(far, total) for far in (far_d, far_e, far_f)]
    done_d = finish(far_d, stay_d)
    done_e = finish(far_e, stay_e)
    done_f = finish(far_f, stay_f)
    done_g = finish(far_g, stay_g)
    due = [(done_d,), (done_e, done_f), (done_g,)]
    reduced = total
    total = jnp.concatenate([total, out_total])
    total = total.reshape((4,) + (2,) * len(dp_masks) + total.shape[2:])
    left_bits = sorted(dp_masks, reverse=True)
    for mask in dp_masks:
        axis = 1 + left_bits.index(mask)
        left_bits.remove(mask)
        bit = (here_dp // mask) % 2
        away_part = lax.dynamic_index_in_dim(total, 1 - bit, axis, keepdims=False)
        stay_part = lax.dynamic_index_in_dim(total, bit, axis, keepdims=False)
        total = add(after(swap(away_part, mask, 0), *(due.pop(0) if due else ())), stay_part)
    for mask in reversed(group_masks):
        bit = (here_group // mask) % 2
        other = swap(total, 0, mask)
        total = jnp.concatenate([jnp.where(bit == 0, total, other), jnp.where(bit == 0, other, total)], axis=1)
    other = swap(total, 0, 1)
    total = jnp.concatenate([jnp.where(core == 0, total, other), jnp.where(core == 0, other, total)], axis=2)
    total = total.astype(f32)
    grad_qkv, grad_out_weight = total[:3], total[3]

    later = after(grad_qkv_rows, qkv_total)
    grad_normed1 = jnp.einsum("cte,cde->td", later[:2], weight_qk, preferred_element_type=f32)
    grad_normed1 = grad_normed1 + jnp.einsum("te,de->td", later[2], weight_vo[0], preferred_element_type=f32)
    first_back = jax.vjp(norm_apply, resid, gain_attn)[1]
    grad_resid_norm, grad_gain_attn = first_back(grad_normed1)
    grad_input = grad_middle + grad_resid_norm
    grad_table = table_gradient(after(bands, qkv_total), position_bias_table.shape[1])
    square_sum = jnp.sum(squares)

    def sum_many(values):
        flat = jnp.concatenate([value.reshape(-1) for value in values])
        flat = after(flat, reduced)
        size = flat.shape[0]
        flat = jnp.pad(flat, (0, -size % 1024)).reshape(-1, 128)
        flat = partial_sums(flat)[-1].reshape(-1)
        done, place = [], 0
        for value in values:
            done.append(flat[place : place + value.size].reshape(value.shape))
            place += value.size
        return done

    out_theirs = swap(jnp.concatenate([done_a, done_b[:1]]), PAIR, 0)
    out_mine = jnp.concatenate([done_b[1:], done_c])
    in_theirs = swap(jnp.concatenate([done_d, done_e]), PAIR, 0)
    in_mine = jnp.concatenate([done_f, done_g])

    def both_experts(mine, theirs):
        mine, theirs = [part.reshape(-1, part.shape[-1]).astype(f32) for part in (mine, theirs)]
        return jnp.stack([jnp.where(half == 0, mine, theirs), jnp.where(half == 0, theirs, mine)])

    grad_w_out = both_experts(out_mine, out_theirs)
    grad_w_in = both_experts(in_mine, in_theirs)

    grad_gain_moe, grad_router, square_total, grad_gain_attn, grad_table = sum_many(
        (grad_gain_moe, grad_router, square_sum, grad_gain_attn, grad_table)
    )
    distill_loss = square_total / (width * valid_count)
    return (
        output.astype(bf16),
        distill_loss,
        grad_input,
        grad_qkv,
        grad_out_weight,
        grad_w_in,
        grad_w_out,
        grad_router,
        grad_table,
        grad_gain_attn,
        grad_gain_moe,
    )


def solution(mesh):
    rows = P(AXES, None)
    return jax.shard_map(
        on_device,
        mesh=mesh,
        in_specs=(
            rows,
            P(None, "dp", None),
            P("dp", None),
            P(),
            P(),
            P(),
            P(),
            P("expert", None, None),
            P("expert", None, None),
            rows,
            P(AXES),
            P(AXES),
            rows,
            rows,
        ),
        out_specs=(
            rows,
            P(),
            rows,
            P(None, "dp", None),
            P("dp", None),
            P("expert", "dp", None),
            P("expert", "dp", None),
            P(),
            P(),
            P(),
            P(),
        ),
        check_vma=False,
    )
```

```python
import math
import jax
import jax.numpy as jnp
from jax import lax
from jax.experimental import pallas as pl
from jax.experimental.pallas import tpu as pltpu
from jax.sharding import PartitionSpec as P

BLOCK = 128
THIRDS = 3
EPS = 1e-06
GELU_A = math.sqrt(2.0 / math.pi)
GELU_B = 0.044715
NT = (((1,), (1,)), ((), ()))
TN = (((0,), (0,)), ((), ()))
VMEM_BYTES = 56 * 1024 * 1024


def cost(micros):
    return pl.CostEstimate(flops=int(micros * 0.37e9), bytes_accessed=0, transcendentals=0)


def dot_f32(left, right, dims=(((1,), (0,)), ((), ()))):
    return lax.dot_general(left, right, dims, preferred_element_type=jnp.float32)


def assemble(rows, pieces, relayed):
    capacity = pieces[0].shape[0] // 2
    for place, piece in enumerate(pieces):
        rows[pl.ds(place * capacity, capacity), :] = piece[pl.ds(0, capacity), :]
    rows[pl.ds(len(pieces) * capacity, relayed.shape[0]), :] = relayed[...]


def whole(shape):
    return pl.BlockSpec(shape, lambda *step: (0,) * len(shape))


def expert_forward_kernel(pick, *refs, chunk, count):
    pieces, relayed, w_in, w_out = refs[:count], refs[count], refs[count + 1], refs[count + 2]
    hidden_t, slope, mine, theirs, rows_t, rows, total = refs[count + 3 :]
    step = pl.program_id(0)

    @pl.when(step == 0)
    def _():
        assemble(rows, pieces, relayed)
        total[...] = jnp.zeros_like(total)
        rows_t[...] = rows[...].T

    for start in range(0, rows.shape[0], chunk):
        part = pl.ds(start, chunk)
        pre = dot_f32(rows[part, :], w_in[0])
        square = pre * pre
        bend = jnp.tanh(pre * (GELU_A + (GELU_A * GELU_B) * square))
        half = 0.5 + 0.5 * bend
        act = (pre * half).astype(jnp.bfloat16)
        lift = pre * (0.5 * GELU_A + (1.5 * GELU_A * GELU_B) * square)
        slope[part, :] = (half + lift * (1.0 - bend * bend)).astype(jnp.bfloat16)
        hidden_t[:, part] = act.T
        total[part, :] += dot_f32(act, w_out[0])

    @pl.when(step == pl.num_programs(0) - 1)
    def _():
        half = mine.shape[0]
        mine[...] = total[pl.ds(0, half), :].astype(jnp.bfloat16)
        theirs[...] = total[pl.ds(half, half), :].astype(jnp.bfloat16)


def expert_forward(pick, pieces, relayed, w_in, w_out, tile=512, chunk=256):
    many, width = pieces[0].shape[0] * len(pieces), relayed.shape[1]
    inner = w_in.shape[2]
    bf16 = jnp.bfloat16
    return pl.pallas_call(
        lambda *refs: expert_forward_kernel(*refs, chunk=chunk, count=len(pieces)),
        grid_spec=pltpu.PrefetchScalarGridSpec(
            num_scalar_prefetch=1,
            grid=(inner // tile,),
            in_specs=[whole(piece.shape) for piece in pieces]
            + [
                whole(relayed.shape),
                pl.BlockSpec((1, width, tile), lambda f, pick: (pick[0], 0, f)),
                pl.BlockSpec((1, tile, width), lambda f, pick: (pick[0], f, 0)),
            ],
            out_specs=[
                pl.BlockSpec((tile, many), lambda f, pick: (f, 0)),
                pl.BlockSpec((many, tile), lambda f, pick: (0, f)),
                whole((many // 2, width)),
                whole((many // 2, width)),
                whole((width, many)),
            ],
            scratch_shapes=[pltpu.VMEM((many, width), bf16), pltpu.VMEM((many, width), jnp.float32)],
        ),
        out_shape=[
            jax.ShapeDtypeStruct((inner, many), bf16),
            jax.ShapeDtypeStruct((many, inner), bf16),
            jax.ShapeDtypeStruct((many // 2, width), bf16),
            jax.ShapeDtypeStruct((many // 2, width), bf16),
            jax.ShapeDtypeStruct((width, many), bf16),
        ],
        compiler_params=pltpu.CompilerParams(vmem_limit_bytes=VMEM_BYTES),
        cost_estimate=cost(22),
        name="expert_forward",
    )(pick, *pieces, relayed, w_in, w_out)


def expert_backward_kernel(pick, grads, w_in, w_out, slope, grad_pre, mine, theirs, total, *, chunk):
    step = pl.program_id(0)

    @pl.when(step == 0)
    def _():
        total[...] = jnp.zeros_like(total)

    for start in range(0, grads.shape[0], chunk):
        part = pl.ds(start, chunk)
        back = dot_f32(grads[part, :], w_out[0], NT) * slope[part, :].astype(jnp.float32)
        back = back.astype(jnp.bfloat16)
        grad_pre[part, :] = back
        total[part, :] += dot_f32(back, w_in[0], NT)

    @pl.when(step == pl.num_programs(0) - 1)
    def _():
        half = mine.shape[0]
        mine[...] = total[pl.ds(0, half), :].astype(jnp.bfloat16)
        theirs[...] = total[pl.ds(half, half), :].astype(jnp.bfloat16)


def expert_backward(pick, grads, w_in, w_out, slope, tile=512, chunk=640):
    many, width = grads.shape
    inner = w_in.shape[2]
    bf16 = jnp.bfloat16
    return pl.pallas_call(
        lambda *refs: expert_backward_kernel(*refs, chunk=chunk),
        grid_spec=pltpu.PrefetchScalarGridSpec(
            num_scalar_prefetch=1,
            grid=(inner // tile,),
            in_specs=[
                whole((many, width)),
                pl.BlockSpec((1, width, tile), lambda f, pick: (pick[0], 0, f)),
                pl.BlockSpec((1, tile, width), lambda f, pick: (pick[0], f, 0)),
                pl.BlockSpec((many, tile), lambda f, pick: (0, f)),
            ],
            out_specs=[
                pl.BlockSpec((many, tile), lambda f, pick: (0, f)),
                whole((many // 2, width)),
                whole((many // 2, width)),
            ],
            scratch_shapes=[pltpu.VMEM((many, width), jnp.float32)],
        ),
        out_shape=[
            jax.ShapeDtypeStruct((many, inner), bf16),
            jax.ShapeDtypeStruct((many // 2, width), bf16),
            jax.ShapeDtypeStruct((many // 2, width), bf16),
        ],
        compiler_params=pltpu.CompilerParams(vmem_limit_bytes=VMEM_BYTES),
        cost_estimate=cost(20),
        name="expert_backward",
    )(pick, grads, w_in, w_out, slope)


def seen_blocks(row_block, blocks):
    return max(row_block + 1, blocks // 2)


def attention_forward_kernel(far, prefix, queries, keys, values, offsets, attended, probs, *, heads, blocks):
    pair = pl.program_id(0)
    lane = lax.broadcasted_iota(jnp.int32, (BLOCK, 2 * heads), 1)
    row = lax.broadcasted_iota(jnp.int32, (BLOCK, BLOCK), 0)
    col = lax.broadcasted_iota(jnp.int32, (BLOCK, BLOCK), 1)
    turned = []
    for head in range(2):
        line = jnp.broadcast_to(offsets[head : head + 1, :], (BLOCK, 4 * BLOCK))
        turned.append(pltpu.roll(line, 0, 1, stride=1, stride_axis=0))
    for row_block in range(blocks):
        rows = pl.ds(row_block * BLOCK, BLOCK)
        span = seen_blocks(row_block, blocks)
        seen = pl.ds(0, span * BLOCK)
        outs = []
        for head in range(2):
            mine = (lane < heads) if head == 0 else (lane >= heads)
            query = jnp.where(mine, queries[rows, :] * 0.125, 0.0).astype(jnp.bfloat16)
            score = dot_f32(query, keys[seen, :], NT)
            far_bias = far[pair * 2 + head]
            pieces = []
            for key_block in range(span):
                piece = score[:, key_block * BLOCK : (key_block + 1) * BLOCK]
                shift = key_block - row_block
                if shift < -1:
                    piece = piece + far_bias
                elif shift < 2:
                    piece = piece + turned[head][:, (2 + shift) * BLOCK : (3 + shift) * BLOCK]
                else:
                    raise ValueError(shift)
                if shift >= 0:
                    shown = col + key_block * BLOCK < prefix[0]
                    piece = jnp.where((shown | (col <= row)) if shift == 0 else shown, piece, -1e30)
                pieces.append(piece)
            peak = pieces[0]
            for piece in pieces[1:]:
                peak = jnp.maximum(peak, piece)
            peak = jnp.max(peak, axis=1, keepdims=True)
            pieces = [jnp.exp(piece - peak) for piece in pieces]
            mass = pieces[0]
            for piece in pieces[1:]:
                mass = mass + piece
            scale = 1.0 / jnp.sum(mass, axis=1, keepdims=True)
            weights = jnp.concatenate([(piece * scale).astype(jnp.bfloat16) for piece in pieces], axis=1)
            probs[head, rows, seen] = weights
            outs.append(dot_f32(weights, values[seen, :]))
        attended[rows, :] = jnp.where(lane < heads, outs[0], outs[1]).astype(jnp.bfloat16)


def attention_forward(far, prefix, qkv_rows, offsets):
    length, width = qkv_rows.shape[1:]
    pairs = width // 128
    blocks = length // BLOCK
    return pl.pallas_call(
        lambda *refs: attention_forward_kernel(*refs, heads=64, blocks=blocks),
        grid_spec=pltpu.PrefetchScalarGridSpec(
            num_scalar_prefetch=2,
            grid=(pairs,),
            in_specs=[pl.BlockSpec((None, length, 128), lambda h, far, prefix, c=c: (c, 0, h)) for c in range(3)]
            + [pl.BlockSpec((None, 2, 4 * BLOCK), lambda h, far, prefix: (h, 0, 0))],
            out_specs=[
                pl.BlockSpec((length, 128), lambda h, far, prefix: (0, h)),
                pl.BlockSpec((2, length, length), lambda h, far, prefix: (h, 0, 0)),
            ],
        ),
        out_shape=[
            jax.ShapeDtypeStruct((length, width), jnp.bfloat16),
            jax.ShapeDtypeStruct((2 * pairs, length, length), jnp.bfloat16),
        ],
        compiler_params=pltpu.CompilerParams(vmem_limit_bytes=VMEM_BYTES),
        cost_estimate=cost(17),
        name="attention_forward",
    )(far, prefix, qkv_rows, qkv_rows, qkv_rows, offsets.reshape(pairs, 2, 4 * BLOCK))


def attention_backward_kernel(queries, keys, values, grads, probs, grad_rows, bands, flow, *, heads, blocks):
    lane = lax.broadcasted_iota(jnp.int32, (BLOCK, 2 * heads), 1)
    query_t = (queries[...] * 0.125).astype(jnp.bfloat16).T
    grad_t = grads[...].T
    half = blocks // 2
    dk, dv = [], []
    dq = [[], []]
    for head in range(2):
        mine = (lane < heads) if head == 0 else (lane >= heads)
        sums = [None] * 4
        for row_block in range(blocks):
            rows = pl.ds(row_block * BLOCK, BLOCK)
            span = seen_blocks(row_block, blocks)
            seen = pl.ds(0, span * BLOCK)
            grad = jnp.where(mine, grads[rows, :], 0.0).astype(jnp.bfloat16)
            soft = probs[head, rows, seen].astype(jnp.float32)
            back = dot_f32(grad, values[seen, :], NT)
            inner = jnp.sum(soft * back, axis=1, keepdims=True)
            score_grad = (soft * (back - inner)).astype(jnp.bfloat16)
            flow[rows, seen] = score_grad
            dq[head].append(dot_f32(score_grad, keys[seen, :]) * 0.125)
            for key_block in range(span):
                band = max(key_block - row_block, -2)
                if band > 1:
                    continue
                tile = score_grad[:, key_block * BLOCK : (key_block + 1) * BLOCK].astype(jnp.float32)
                sums[band + 2] = tile if sums[band + 2] is None else sums[band + 2] + tile
        for band in range(4):
            bands[head, band] = sums[band]
        part = slice(head * heads, (head + 1) * heads)
        key_pieces, value_pieces = [], []
        for key_block in range(blocks):
            first = 0 if key_block < half else key_block
            rows = pl.ds(first * BLOCK, (blocks - first) * BLOCK)
            cols = pl.ds(key_block * BLOCK, BLOCK)
            key_pieces.append(dot_f32(query_t[part, first * BLOCK :], flow[rows, cols]))
            value_pieces.append(dot_f32(grad_t[part, first * BLOCK :], probs[head, rows, cols]))
        dk.append(jnp.concatenate(key_pieces, axis=1))
        dv.append(jnp.concatenate(value_pieces, axis=1))
    for row_block in range(blocks):
        rows = pl.ds(row_block * BLOCK, BLOCK)
        grad_rows[0, rows, :] = jnp.where(lane < heads, dq[0][row_block], dq[1][row_block]).astype(jnp.bfloat16)
    grad_rows[1] = jnp.concatenate(dk, axis=0).T.astype(jnp.bfloat16)
    grad_rows[2] = jnp.concatenate(dv, axis=0).T.astype(jnp.bfloat16)


def attention_backward(qkv_rows, grads, probs):
    length, width = grads.shape
    pairs = width // 128
    blocks = length // BLOCK
    block = pl.BlockSpec((length, 128), lambda h: (0, h))
    of_three = [pl.BlockSpec((None, length, 128), lambda h, c=c: (c, 0, h)) for c in range(3)]
    return pl.pallas_call(
        lambda *refs: attention_backward_kernel(*refs, heads=64, blocks=blocks),
        grid=(pairs,),
        in_specs=[*of_three, block, pl.BlockSpec((2, length, length), lambda h: (h, 0, 0))],
        out_specs=[pl.BlockSpec((3, length, 128), lambda h: (0, 0, h)), pl.BlockSpec((2, 4, BLOCK, BLOCK), lambda h: (h, 0, 0, 0))],
        out_shape=[jax.ShapeDtypeStruct((3, length, width), jnp.bfloat16)]
        + [jax.ShapeDtypeStruct((2 * pairs, 4, BLOCK, BLOCK), jnp.float32)],
        scratch_shapes=[pltpu.VMEM((length, length), jnp.bfloat16)],
        compiler_params=pltpu.CompilerParams(vmem_limit_bytes=VMEM_BYTES),
        cost_estimate=cost(17),
        name="attention_backward",
    )(qkv_rows, qkv_rows, qkv_rows, grads, probs)


def pieces_left(lefts, plans):
    many = len(lefts) // (1 + max(group for plan in plans for group, _ in plan))
    part = lefts[0].shape[0] // THIRDS
    return jnp.concatenate(
        [
            lefts[group * many + k][pl.ds(third * part, part), :]
            for plan in plans
            for group, third in plan
            for k in range(many)
        ]
    )


def put_pieces(result, outs):
    place = 0
    for out in outs:
        many, pieces, part = out.shape[:3]
        for piece in range(pieces):
            for k in range(many):
                out[k, piece] = result[place : place + part]
                place += part


def weight_part_kernel(picks, *refs, count, plans):
    lefts, right, outs = refs[:count], refs[count], refs[count + 1 :]
    left = pieces_left(lefts, plans)
    put_pieces(dot_f32(left, right[...]).astype(jnp.bfloat16), outs)


def weight_first_kernel(picks, *refs, count, plans, pieces):
    lefts, parts, relayed, outs = refs[:count], refs[count : count + pieces], refs[count + pieces], refs[count + pieces + 1 :]
    assemble(outs[0], parts, relayed)
    left = pieces_left(lefts, plans)
    put_pieces(dot_f32(left, outs[0][...]).astype(jnp.bfloat16), outs[1:])


def weight_part_plain(picks, left, right, rows, plans, many):
    depth, width = right.shape
    part = rows // THIRDS
    result = jnp.take(left.reshape(-1, rows, depth), picks, axis=0)
    result = jnp.einsum("srd,dw->srw", result, right, preferred_element_type=jnp.float32).astype(jnp.bfloat16)
    result = result.reshape(-1, many, THIRDS, part, width)
    return [jnp.stack([result[group, :, third] for group, third in plan], axis=1) for plan in plans]


def weight_part(picks, left, right, rows, plans, many, tile):
    depth, width = right.shape
    count, part = picks.shape[0], rows // THIRDS
    if part % 16:
        return weight_part_plain(picks, left, right, rows, plans, many)
    return pl.pallas_call(
        lambda *refs: weight_part_kernel(*refs, count=count, plans=plans),
        grid_spec=pltpu.PrefetchScalarGridSpec(
            num_scalar_prefetch=1,
            grid=(width // tile,),
            in_specs=[pl.BlockSpec((rows, depth), lambda i, picks, k=k: (picks[k], 0)) for k in range(count)]
            + [pl.BlockSpec((depth, tile), lambda i, picks: (0, i))],
            out_specs=[pl.BlockSpec((many, len(plan), part, tile), lambda i, picks: (0, 0, 0, i)) for plan in plans],
        ),
        out_shape=[jax.ShapeDtypeStruct((many, len(plan), part, width), jnp.bfloat16) for plan in plans],
        compiler_params=pltpu.CompilerParams(vmem_limit_bytes=VMEM_BYTES),
        cost_estimate=cost(4),
        name="weight_part",
    )(picks, *([left] * count), right)


def weight_first(picks, left, pieces, relayed, rows, plans, many):
    depth, width = left.shape[1], relayed.shape[1]
    count, part = picks.shape[0], rows // THIRDS
    if part % 16:
        capacity = pieces[0].shape[0] // 2
        right = jnp.concatenate([piece[:capacity] for piece in pieces] + [relayed])
        return [right, *weight_part_plain(picks, left, right, rows, plans, many)]
    return pl.pallas_call(
        lambda *refs: weight_first_kernel(*refs, count=count, plans=plans, pieces=len(pieces)),
        grid_spec=pltpu.PrefetchScalarGridSpec(
            num_scalar_prefetch=1,
            grid=(1,),
            in_specs=[pl.BlockSpec((rows, depth), lambda i, picks, k=k: (picks[k], 0)) for k in range(count)]
            + [whole(piece.shape) for piece in pieces]
            + [whole(relayed.shape)],
            out_specs=[whole((depth, width))] + [whole((many, len(plan), part, width)) for plan in plans],
        ),
        out_shape=[jax.ShapeDtypeStruct((depth, width), jnp.bfloat16)]
        + [jax.ShapeDtypeStruct((many, len(plan), part, width), jnp.bfloat16) for plan in plans],
        compiler_params=pltpu.CompilerParams(vmem_limit_bytes=VMEM_BYTES),
        cost_estimate=cost(4),
        name="weight_first",
    )(picks, *([left] * count), *pieces, relayed)


def hot_columns(slots, first, count):
    rows = first + lax.broadcasted_iota(jnp.int32, (count, slots.shape[1]), 0)
    return (rows == slots).astype(jnp.bfloat16)


def hot_rows(slots, first, count):
    cols = first + lax.broadcasted_iota(jnp.int32, (slots.shape[0], count), 1)
    return (cols == slots).astype(jnp.bfloat16)


def halves(core, mine, other):
    return jnp.where(core == 0, mine, other), jnp.where(core == 0, other, mine)


def join_kernel(places, *refs):
    pieces, out = refs[:-1], refs[-1]
    rows = pieces[0].shape[1]
    count = pieces[0].shape[0]
    for chunk in range(out.shape[0] // count):
        for step in range(len(pieces) * count // out.shape[0]):
            piece = pieces[chunk * (len(pieces) * count // out.shape[0]) + step]
            start = pl.multiple_of(places[step] * rows, rows)
            out[pl.ds(chunk * count, count), pl.ds(start, rows), :] = piece[...]


def join(places, chunks):
    count, rows, columns = chunks[0][0].shape
    steps = len(chunks[0])
    return pl.pallas_call(
        join_kernel,
        in_specs=[pl.BlockSpec(memory_space=pltpu.SMEM)] + [pl.BlockSpec(memory_space=pltpu.VMEM)] * (steps * len(chunks)),
        out_shape=jax.ShapeDtypeStruct((count * len(chunks), steps * rows, columns), jnp.bfloat16),
        compiler_params=pltpu.CompilerParams(vmem_limit_bytes=VMEM_BYTES),
        cost_estimate=cost(3),
        name="join",
    )(places, *[piece for chunk in chunks for piece in chunk])


def project_kernel(core, rows, mine, other, result):
    half = mine.shape[1]
    first, second = halves(core[0], mine[...], other[...])
    result[:, :half] = dot_f32(rows[...], first).astype(jnp.bfloat16)
    result[:, half:] = dot_f32(rows[...], second).astype(jnp.bfloat16)


def project(core, rows, mine, other, used):
    width, half = mine.shape[1:]
    length = rows.shape[0]
    return pl.pallas_call(
        project_kernel,
        grid_spec=pltpu.PrefetchScalarGridSpec(
            num_scalar_prefetch=1,
            grid=(used,),
            in_specs=[
                whole((length, width)),
                pl.BlockSpec((None, width, half), lambda i, core: (i, 0, 0)),
                pl.BlockSpec((None, width, half), lambda i, core: (i, 0, 0)),
            ],
            out_specs=pl.BlockSpec((None, length, 2 * half), lambda i, core: (i, 0, 0)),
        ),
        out_shape=jax.ShapeDtypeStruct((used, length, 2 * half), jnp.bfloat16),
        compiler_params=pltpu.CompilerParams(vmem_limit_bytes=VMEM_BYTES),
        cost_estimate=cost(4),
        name="project",
    )(core, rows, mine, other)


def route_kernel(core, attended, tokens, mine, other, gain, router, routes, slots, middle, normed, gates, *outs):
    f32 = jnp.float32
    first, second = halves(core[0], mine[...], other[...])
    rows = attended[...]
    moved = jnp.concatenate([dot_f32(rows, first), dot_f32(rows, second)], axis=1)
    value = tokens[...].astype(f32) + moved
    middle[...] = value
    low = (value * lax.rsqrt(jnp.mean(value * value, axis=1, keepdims=True) + EPS) * gain[...]).astype(jnp.bfloat16)
    normed[...] = low
    for place, out in enumerate(outs):
        count = out.shape[0]
        hot = hot_columns(slots[0:1, :], place * count, count) + hot_columns(slots[1:2, :], place * count, count)
        out[...] = dot_f32(hot, low).astype(jnp.bfloat16)
    logits = dot_f32(low, router[...])
    soft = jnp.exp(logits - jnp.max(logits, axis=1, keepdims=True))
    soft = soft / jnp.sum(soft, axis=1, keepdims=True)
    expert = lax.broadcasted_iota(jnp.int32, soft.shape, 1)
    chosen = [jnp.sum(jnp.where(expert == routes[:, k : k + 1], soft, 0.0), axis=1, keepdims=True) for k in range(2)]
    for k in range(2):
        gates[:, k : k + 1] = chosen[k] / (chosen[0] + chosen[1])


def route(core, attended, tokens, mine, other, gain, router, routes, slots, pieces, count):
    length, width = tokens.shape
    last, half = mine.shape[0] - 1, mine.shape[2]
    f32, bf16 = jnp.float32, jnp.bfloat16
    weight = pl.BlockSpec((None, width, half), lambda i, core: (last, 0, 0))
    shapes = [((length, width), f32), ((length, width), bf16), ((length, 2), f32)] + [((count, width), bf16)] * pieces
    return pl.pallas_call(
        route_kernel,
        grid_spec=pltpu.PrefetchScalarGridSpec(
            num_scalar_prefetch=1,
            grid=(1,),
            in_specs=[whole((length, width)), whole((length, width)), weight, weight, whole((1, width)), whole(router.shape), whole(routes.shape), whole(slots.shape)],
            out_specs=[whole(shape) for shape, _ in shapes],
        ),
        out_shape=[jax.ShapeDtypeStruct(shape, kind) for shape, kind in shapes],
        compiler_params=pltpu.CompilerParams(vmem_limit_bytes=VMEM_BYTES),
        cost_estimate=cost(6),
        name="route",
    )(core, attended, tokens, mine, other, gain.reshape(1, -1), router, routes, slots)


def slot_pieces(near, passed, far):
    capacity = far[0].shape[0] // 2
    return [(near, capacity), (passed, capacity)] + [(ref, 2 * capacity) for ref in far]


def unpack(slots, refs):
    total, first = None, 0
    for ref, count in refs:
        part = dot_f32(hot_rows(slots, first, count), ref[pl.ds(0, count), :])
        total = part if total is None else total + part
        first += count
    return total


def combine_kernel(*refs, chips):
    slots, slots_t, scale, near, passed = refs[:5]
    far = refs[5 : 5 + chips - 1]
    middle, teacher, cotangent, valid, gates, routes = refs[4 + chips : 10 + chips]
    output, grad_y, grad_logits, square = refs[10 + chips : 14 + chips]
    sends = refs[14 + chips :]
    f32 = jnp.float32
    order = slot_pieces(near, passed, far)
    picked = [unpack(slots[:, k : k + 1], order) for k in range(2)]
    result = middle[...] + (gates[:, 0:1] * picked[0] + gates[:, 1:2] * picked[1])
    output[...] = result.astype(jnp.bfloat16)
    misfit = valid[...] * (result - teacher[...].astype(f32))
    square[...] = jnp.sum((misfit * misfit).reshape(-1, 8, misfit.shape[1]), axis=0)
    grad = cotangent[...].astype(f32) + misfit * scale[0, 0]
    grad_y[...] = grad
    steep = [jnp.sum(grad * picked[k], axis=1, keepdims=True) for k in range(2)]
    slack = gates[:, 0:1] * steep[0] + gates[:, 1:2] * steep[1]
    expert = lax.broadcasted_iota(jnp.int32, grad_logits.shape, 1)
    turn = [jnp.where(expert == routes[:, k : k + 1], gates[:, k : k + 1] * (steep[k] - slack), 0.0) for k in range(2)]
    grad_logits[...] = (turn[0] + turn[1]).astype(jnp.bfloat16)
    scaled = [(gates[:, k : k + 1] * grad).astype(jnp.bfloat16) for k in range(2)]
    for place, out in enumerate(sends):
        count = out.shape[0]
        rows = [dot_f32(hot_columns(slots_t[k : k + 1, :], place * count, count), scaled[k]) for k in range(2)]
        out[...] = (rows[0] + rows[1]).astype(jnp.bfloat16)


def combine(slots, slots_t, scale, near, passed, far, middle, teacher, cotangent, valid, gates, routes, experts):
    length, width = middle.shape
    chips = len(far) + 1
    f32, bf16 = jnp.float32, jnp.bfloat16
    return pl.pallas_call(
        lambda *refs: combine_kernel(*refs, chips=chips),
        in_specs=[pl.BlockSpec(memory_space=pltpu.VMEM)] * 2
        + [pl.BlockSpec(memory_space=pltpu.SMEM)]
        + [pl.BlockSpec(memory_space=pltpu.VMEM)] * (7 + chips),
        out_shape=[
            jax.ShapeDtypeStruct((length, width), bf16),
            jax.ShapeDtypeStruct((length, width), f32),
            jax.ShapeDtypeStruct((length, experts), bf16),
            jax.ShapeDtypeStruct((8, width), f32),
        ]
        + [jax.ShapeDtypeStruct(far[0].shape, bf16)] * chips,
        compiler_params=pltpu.CompilerParams(vmem_limit_bytes=VMEM_BYTES),
        cost_estimate=cost(8),
        name="combine",
    )(slots, slots_t, scale, near, passed, *far, middle, teacher, cotangent, valid, gates, routes)


def norm_back(value, gain, grad):
    root = lax.rsqrt(jnp.mean(value * value, axis=1, keepdims=True) + EPS)
    normed = value * root
    scaled = grad * gain
    inner = jnp.mean(scaled * normed, axis=1, keepdims=True)
    return root * (scaled - normed * inner), jnp.sum((grad * normed).reshape(-1, 8, value.shape[1]), axis=0)


def collect_kernel(core, *refs, chips):
    slots, near, passed = refs[:3]
    far = refs[3 : 2 + chips]
    middle, gain, grad_logits, router, grad_y, mine, other = refs[2 + chips : 9 + chips]
    grad_middle, rounded, grad_attended, grad_gain = refs[9 + chips :]
    order = slot_pieces(near, passed, far)
    grad = dot_f32(grad_logits[...], router[...], NT)
    grad = grad + (unpack(slots[:, 0:1], order) + unpack(slots[:, 1:2], order))
    turned, grad_gain[...] = norm_back(middle[...], gain[...], grad)
    result = grad_y[...] + turned
    grad_middle[...] = result
    low = result.astype(jnp.bfloat16)
    rounded[...] = low
    first, second = halves(core[0], mine[...], other[...])
    half = first.shape[1]
    grad_attended[...] = (dot_f32(low[:, :half], first, NT) + dot_f32(low[:, half:], second, NT)).astype(jnp.bfloat16)


def collect(core, slots, near, passed, far, middle, gain, grad_logits, router, grad_y, mine, other):
    length, width = middle.shape
    chips = len(far) + 1
    last, half = mine.shape[0] - 1, mine.shape[2]
    f32, bf16 = jnp.float32, jnp.bfloat16
    weight = pl.BlockSpec((None, width, half), lambda i, core: (last, 0, 0))
    plain = [slots, near, passed, *far, middle, gain.reshape(1, -1), grad_logits, router, grad_y]
    shapes = [((length, width), f32), ((length, width), bf16), ((length, width), bf16), ((8, width), f32)]
    return pl.pallas_call(
        lambda *refs: collect_kernel(*refs, chips=chips),
        grid_spec=pltpu.PrefetchScalarGridSpec(
            num_scalar_prefetch=1,
            grid=(1,),
            in_specs=[whole(array.shape) for array in plain] + [weight, weight],
            out_specs=[whole(shape) for shape, _ in shapes],
        ),
        out_shape=[jax.ShapeDtypeStruct(shape, kind) for shape, kind in shapes],
        compiler_params=pltpu.CompilerParams(vmem_limit_bytes=VMEM_BYTES),
        cost_estimate=cost(8),
        name="collect",
    )(core, *plain, mine, other)


def outer_halves_kernel(core, normed, attended, rights, last, away, stay, normed_t, attended_t, *, count):
    step = pl.program_id(0)
    half = away.shape[1]

    def put(result):
        result = result.astype(jnp.bfloat16)

        @pl.when(core[0] == 0)
        def _():
            stay[...] = result[:, :half]
            away[...] = result[:, half:]

        @pl.when(core[0] != 0)
        def _():
            away[...] = result[:, :half]
            stay[...] = result[:, half:]

    @pl.when(step == 0)
    def _():
        normed_t[...] = normed[...].T
        attended_t[...] = attended[...].T

    @pl.when(step < count)
    def _():
        put(dot_f32(normed_t[...], rights[...]))

    @pl.when(step == count)
    def _():
        put(dot_f32(attended_t[...], last[...]))


def outer_halves(core, normed, attended, rights, last):
    length, width = normed.shape
    count, half = rights.shape[0], width // 2
    shape = jax.ShapeDtypeStruct((count + 1, width, half), jnp.bfloat16)
    return pl.pallas_call(
        lambda *refs: outer_halves_kernel(*refs, count=count),
        grid_spec=pltpu.PrefetchScalarGridSpec(
            num_scalar_prefetch=1,
            grid=(count + 1,),
            in_specs=[
                whole((length, width)),
                whole((length, width)),
                pl.BlockSpec((None, length, width), lambda i, core: (jnp.minimum(i, count - 1), 0, 0)),
                whole((length, width)),
            ],
            out_specs=[pl.BlockSpec((None, width, half), lambda i, core: (i, 0, 0))] * 2,
            scratch_shapes=[pltpu.VMEM((width, length), jnp.bfloat16)] * 2,
        ),
        out_shape=[shape, shape],
        compiler_params=pltpu.CompilerParams(vmem_limit_bytes=VMEM_BYTES),
        cost_estimate=cost(6),
        name="outer_halves",
    )(core, normed, attended, rights, last)


def enter_kernel(core, grads, mine, other, tokens, gain, grad_middle, grad_input, grad_gain, total):
    step = pl.program_id(0)
    first, second = halves(core[0], mine[...], other[...])
    half = first.shape[1]
    rows = grads[...]
    part = dot_f32(rows[:, :half], first, NT) + dot_f32(rows[:, half:], second, NT)

    @pl.when(step == 0)
    def _():
        total[...] = part

    @pl.when(step > 0)
    def _():
        total[...] += part

    @pl.when(step == pl.num_programs(0) - 1)
    def _():
        turned, grad_gain[...] = norm_back(tokens[...].astype(jnp.float32), gain[...], total[...])
        grad_input[...] = grad_middle[...] + turned


def enter(core, grads, mine, other, tokens, gain, grad_middle):
    length, width = tokens.shape
    count, half = grads.shape[0], mine.shape[2]
    weight = pl.BlockSpec((None, width, half), lambda i, core: (i, 0, 0))
    return pl.pallas_call(
        enter_kernel,
        grid_spec=pltpu.PrefetchScalarGridSpec(
            num_scalar_prefetch=1,
            grid=(count,),
            in_specs=[pl.BlockSpec((None, length, width), lambda i, core: (i, 0, 0)), weight, weight, whole((length, width)), whole((1, width)), whole((length, width))],
            out_specs=[whole((length, width)), whole((8, width))],
            scratch_shapes=[pltpu.VMEM((length, width), jnp.float32)],
        ),
        out_shape=[jax.ShapeDtypeStruct((length, width), jnp.float32), jax.ShapeDtypeStruct((8, width), jnp.float32)],
        compiler_params=pltpu.CompilerParams(vmem_limit_bytes=VMEM_BYTES),
        cost_estimate=cost(6),
        name="enter",
    )(core, grads, mine, other, tokens, gain.reshape(1, -1), grad_middle)


BOUNDS = (12, 16, 23, 32, 46, 64, 91)
TOP_PRECISION = lax.Precision.HIGHEST
AXES = ("dp", "expert")
PAIR = 2


def after(value, *others):
    return lax.optimization_barrier((value, *others))[0] if others else value


def bucket_index(offset):
    distance = jnp.abs(offset)
    far_bucket = 8 + sum([(distance >= level).astype(jnp.int32) for level in BOUNDS])
    near_bucket = jnp.where(distance < 8, distance, far_bucket)
    return jnp.where(offset > 0, 16, 0) + near_bucket


def norm_apply(inputs, gain_vec):
    return inputs * lax.rsqrt(jnp.mean(inputs * inputs, axis=-1, keepdims=True) + EPS) * gain_vec


def tile_offsets(query_block, key_block):
    rows = query_block * BLOCK + lax.broadcasted_iota(jnp.int32, (BLOCK, BLOCK), 0)
    cols = key_block * BLOCK + lax.broadcasted_iota(jnp.int32, (BLOCK, BLOCK), 1)
    return rows, cols


def offset_bias(table):
    offsets = jnp.arange(4 * BLOCK, dtype=jnp.int32) - 2 * BLOCK
    hot = (bucket_index(offsets)[None] == jnp.arange(table.shape[1], dtype=jnp.int32)[:, None]).astype(jnp.float32)
    return jnp.dot(table, hot, precision=TOP_PRECISION)


def table_gradient(bands, buckets):
    rows, cols = tile_offsets(0, 0)
    ids = [jnp.full((BLOCK, BLOCK), bucket_far(), jnp.int32)]
    ids += [bucket_index(shift * BLOCK + cols - rows) for shift in (-1, 0, 1)]
    hot = (jnp.stack(ids)[..., None] == jnp.arange(buckets, dtype=jnp.int32)).astype(jnp.float32)
    return jnp.einsum("hdxy,dxyb->hb", bands, hot, precision=TOP_PRECISION)


def bucket_far():
    return 8 + len(BOUNDS)


def on_device(
    tokens,
    qkv_weight,
    out_weight,
    position_bias_table,
    gain_attn,
    gain_moe,
    router,
    w_in,
    w_out,
    routes,
    prefix,
    valid_mask,
    teacher,
    cotangent,
):
    length, width = tokens.shape
    bf16, f32 = jnp.bfloat16, jnp.float32
    expert_count = router.shape[1]
    top_count = routes.shape[1]
    groups = lax.axis_size("expert")
    copies = lax.axis_size("dp")
    inner = w_in.shape[2]
    capacity = 5 * length * top_count // (4 * expert_count)
    total_tokens = length * copies * groups
    sources = 2 * groups
    blocks = length // BLOCK
    here_dp, here_group = lax.axis_index("dp"), lax.axis_index("expert")
    half = (here_dp >> 1) & 1
    core = here_group & 1
    rest = copies // 4

    def swap(value, dp_mask, group_mask):
        pairs = [
            (i, ((i // groups) ^ dp_mask) * groups + ((i % groups) ^ group_mask))
            for i in range(copies * groups)
        ]
        return lax.ppermute(value, AXES, pairs)

    def bits(count):
        return [1 << place for place in range(count.bit_length() - 1)]

    def partial_sums(value):
        sums = []
        for masks in [(0, mask) for mask in bits(groups)] + [(mask, 0) for mask in bits(copies)]:
            value = value + swap(value, *masks)
            sums.append(value)
        return sums

    chips = groups

    def across(value, place):
        return swap(value, PAIR * (place // (groups // 2)), 2 * (place % (groups // 2)))

    def send_out(pieces):
        got = [pieces[0]] + [across(pieces[place], place) for place in range(1, chips)]
        return got, swap(jnp.concatenate([piece[capacity:] for piece in got]), 0, 1)

    def send_back(mine, theirs):
        passed = swap(theirs, 0, 1)
        sends = []
        for place in range(1, chips):
            part = slice(place * capacity, (place + 1) * capacity)
            sends.append(jnp.concatenate([mine[part], passed[part]]))
        return passed, sends, [across(send, place) for place, send in enumerate(sends, 1)]

    ring = list(range(0, copies, 2)) + list(range(copies - 1, 0, -2))
    turns = [(1, step) for step in range(1, copies // 2 + 1)] + [(-1, step) for step in range(1, copies // 2)]

    def gather_ring(shard, due):
        got = [shard]
        for turn in (1, -1):
            held = shard
            pairs = [(ring[i], ring[(i + turn) % copies]) for i in range(copies)]
            for step in [step for way, step in turns if way == turn]:
                held = lax.ppermute(after(held, *due[step - 2 : step - 1]) if step > 1 else held, "dp", pairs)
                got.append(held)
        return got

    def ring_places():
        place = jnp.where(here_dp & 1 == 0, here_dp >> 1, copies - 1 - (here_dp >> 1))
        shift = jnp.array([0] + [turn * step for turn, step in turns], jnp.int32)
        place = (place - shift) & (copies - 1)
        return jnp.where(place < copies // 2, 2 * place, 2 * (copies - 1 - place) + 1).astype(jnp.int32)

    columns = width // 2
    core_index = core.reshape(1).astype(jnp.int32)
    valid_rows = valid_mask.astype(f32)[:, None]
    counts = partial_sums(jnp.broadcast_to(jnp.sum(valid_rows), (8, 128)))
    valid_count = counts[-1][0, 0]
    shards = [
        lax.dynamic_slice_in_dim(part, core * columns, columns, 2)
        for part in (qkv_weight[:2], jnp.concatenate([qkv_weight[2:], out_weight[None]]))
    ]
    if copies > 8:
        mine = lax.all_gather(jnp.concatenate(shards), "dp", axis=1, tiled=True)
    else:
        mine = join(ring_places(), [gather_ring(shards[0], counts), gather_ring(shards[1], ())])
    other = swap(mine, 0, 1)
    offsets = offset_bias(position_bias_table)

    flat_routes = routes.reshape(-1)
    pair_count = length * top_count
    slot_count = sources * capacity
    route_hits = (flat_routes[:, None] == jnp.arange(expert_count, dtype=jnp.int32)[None, :]).astype(bf16)
    lower_ones = (
        lax.broadcasted_iota(jnp.int32, (pair_count, pair_count), 0)
        >= lax.broadcasted_iota(jnp.int32, (pair_count, pair_count), 1)
    ).astype(bf16)
    running = jnp.dot(lower_ones, route_hits, preferred_element_type=f32)
    pair_rank = jnp.sum((running - 1.0) * route_hits.astype(f32), axis=1).astype(jnp.int32)
    away = (flat_routes >> 1) ^ here_group
    chip = ((flat_routes & 1) ^ half) * (groups // 2) + (away >> 1)
    slots = ((chip * 2 + (away & 1)) * capacity + pair_rank).reshape(length, top_count)
    slots_t = slots.T

    resid = tokens.astype(f32)
    normed1 = norm_apply(resid, gain_attn).astype(bf16)
    qkv_rows = project(core_index, normed1, mine, other, 3)
    offsets = after(offsets, valid_count)
    attended, probs = attention_forward(position_bias_table[:, bucket_far()], prefix, qkv_rows, offsets)
    middle, normed2, gates, *sends = route(
        core_index, attended, tokens, mine, other, gain_moe, router, routes, slots_t, chips, 2 * capacity
    )

    rows_got, rows_passed = send_out(sends)
    pick = half.reshape(1).astype(jnp.int32)
    hidden_t, slope, near, theirs, rows_t = expert_forward(pick, rows_got, rows_passed, w_in, w_out)
    passed, _, far = send_back(near, theirs)
    scale = (total_tokens / valid_count).reshape(1, 1)
    output, grad_y, grad_logits, squares, *sends = combine(
        slots, slots_t, scale, near, passed, far, middle, teacher, cotangent, valid_rows, gates, routes, expert_count
    )
    grads_got, grads_passed = send_out(sends)
    grad_router = jnp.einsum("td,te->de", normed2, grad_logits, preferred_element_type=f32)

    out_rows = inner // copies
    in_rows = width // copies
    far_bit = here_dp % 2
    slices = jnp.arange(rest, dtype=jnp.int32) * 4

    def picks(bit0):
        return jnp.concatenate([slices + ((half ^ other_half) * 2 + bit0) for other_half in (1, 0)]).astype(jnp.int32)

    sent, kept = picks(1 - far_bit), picks(far_bit)
    every = jnp.concatenate([sent, kept])

    def add(left, right):
        return (left.astype(f32) + right.astype(f32)).astype(bf16)

    def fold(unit, bit, axis=0):
        unit = unit.reshape(unit.shape[:axis] + (2, unit.shape[axis] // 2) + unit.shape[axis + 1 :])
        away_part = lax.dynamic_index_in_dim(unit, 1 - bit, axis, keepdims=False)
        return away_part, lax.dynamic_index_in_dim(unit, bit, axis, keepdims=False)

    far_masks = list(reversed(bits(copies)[2:]))

    def near_add(got, keep):
        away_part, stay_part = fold(add(got, keep), (here_dp // far_masks[0]) % 2)
        return away_part, stay_part

    def far_trade(away_part):
        return swap(away_part, far_masks[0], 0)

    def finish(got, stay):
        unit = add(got, stay)
        for mask in far_masks[1:]:
            away_part, stay_part = fold(unit, (here_dp // mask) % 2)
            unit = add(swap(away_part, mask, 0), stay_part)
        return unit[0]

    plan_a, plan_b = ((0, 0), (0, 1)), ((0, 2), (1, 0), (1, 1), (1, 2))
    plan_c, plan_d, plan_e = ((0, 0), (0, 1), (0, 2)), ((1, 0),), ((1, 1), (1, 2))

    def keep(plan):
        return tuple((group + 2, third) for group, third in plan)

    grad_rows, send_a, send_b = weight_first(sent, hidden_t, grads_got, grads_passed, out_rows, (plan_a, plan_b), rest)
    got_a = swap(send_a, 1, 0)
    grad_pre, near, theirs = expert_backward(pick, after(grad_rows, send_a), w_in, w_out, slope)
    passed, sends, far = send_back(near, after(theirs, got_a))
    grad_rows, grad_pre = lax.optimization_barrier((grad_rows, grad_pre, *sends))[:2]
    got_b = swap(after(send_b, passed), 1, 0)
    keep_a, keep_b = weight_part(kept, hidden_t, grad_rows, out_rows, (plan_a, plan_b), rest, width)
    away_a, stay_a = near_add(got_a, keep_a)
    far_a = far_trade(away_a)
    send_c, send_d, send_e, keep_c, keep_d, keep_e = weight_part(
        every,
        rows_t,
        after(grad_pre, away_a),
        in_rows,
        (plan_c, plan_d, plan_e, keep(plan_c), keep(plan_d), keep(plan_e)),
        rest,
        inner // 2,
    )
    far = [after(part, send_c) for part in far]
    got_c = swap(after(send_c, *far), 1, 0)
    grad_middle, grad_attn_proj, grad_attended, gain_moe_parts = collect(
        core_index, slots, near, passed, far, middle, gain_moe, grad_logits, router, grad_y, mine, other
    )
    away_b, stay_b = near_add(after(got_b, grad_attended), keep_b)
    grad_attended, away_b, far_a = lax.optimization_barrier((grad_attended, away_b, far_a))
    far_b = [far_trade(away_b[:, :2]), far_trade(away_b[:, 2:])]
    grad_qkv_rows, bands = attention_backward(qkv_rows, grad_attended, probs)
    grad_qkv_rows, got_c, far_b[0] = lax.optimization_barrier((grad_qkv_rows, got_c, far_b[0]))
    done_a = finish(after(far_a, grad_qkv_rows), stay_a)

    away_c, stay_c = near_add(got_c, keep_c)
    far_c = far_trade(away_c)
    got_d, got_e = [swap(after(send, away_c), 1, 0) for send in (send_d, send_e)]
    weights_away, weights_stay = outer_halves(core_index, normed1, attended, grad_qkv_rows, grad_attn_proj)
    weights_got = swap(weights_away, 0, 1)
    away_d, stay_d = near_add(got_d, keep_d)
    far_d = far_trade(away_d)
    grad_input, gain_attn_parts = enter(core_index, grad_qkv_rows, mine, other, tokens, gain_attn, grad_middle)
    grad_table = table_gradient(after(bands, weights_away), position_bias_table.shape[1])
    weights_total = add(after(weights_got, stay_d, gain_attn_parts, grad_table), weights_stay)

    group_masks = bits(groups)[1:]
    dp_masks = sorted(bits(copies), key=lambda mask: (mask != PAIR, mask))
    total = weights_total.reshape(4, copies, in_rows, columns)
    for mask in group_masks:
        away_part, stay_part = fold(total, (here_group // mask) % 2, 2)
        total = add(swap(away_part, 0, mask), stay_part)
    away_e, stay_e = near_add(after(got_e, total), keep_e)
    far_e = far_trade(away_e)
    done_b = jnp.concatenate([finish(far_b[0], stay_b[:, :2]), finish(after(far_b[1], total), stay_b[:, 2:])])
    done_c = finish(after(far_c, total), stay_c)
    done_d = finish(after(far_d, total), stay_d)
    done_e = finish(far_e, stay_e)

    small = [
        jnp.sum(gain_moe_parts, axis=0),
        jnp.sum(gain_attn_parts, axis=0),
        grad_router,
        grad_table,
        jnp.sum(squares),
    ]
    sizes = [value.size for value in small]
    flat = jnp.concatenate([value.reshape(-1) for value in small])
    flat = jnp.pad(flat, (0, -sum(sizes) % 1024)).reshape(-1, 128)

    due = [(), (done_c, done_d), (done_e,)]
    total = total.reshape((4,) + (2,) * len(dp_masks) + total.shape[2:])
    left_bits = sorted(dp_masks, reverse=True)
    for mask in dp_masks:
        axis = 1 + left_bits.index(mask)
        left_bits.remove(mask)
        bit = (here_dp // mask) % 2
        away_part = lax.dynamic_index_in_dim(total, 1 - bit, axis, keepdims=False)
        stay_part = lax.dynamic_index_in_dim(total, bit, axis, keepdims=False)
        total = add(after(swap(away_part, mask, 0), *(due.pop(0) if due else ())), stay_part)
        flat = flat + swap(flat, mask, 0)
        total, flat = lax.optimization_barrier((total, flat))
    for mask in reversed(group_masks):
        bit = (here_group // mask) % 2
        other_part = swap(total, 0, mask)
        total = jnp.concatenate([jnp.where(bit == 0, total, other_part), jnp.where(bit == 0, other_part, total)], axis=1)
        flat = flat + swap(flat, 0, mask)
        total, flat = lax.optimization_barrier((total, flat))
    other_part = swap(total, 0, 1)
    flat = flat + swap(flat, 0, 1)
    total = jnp.concatenate([jnp.where(core == 0, total, other_part), jnp.where(core == 0, other_part, total)], axis=2)
    total = total.astype(f32)
    grad_qkv, grad_out_weight = total[:3], total[3]
    flat = flat.reshape(-1)
    starts = [sum(sizes[:place]) for place in range(len(sizes))]
    grad_gain_moe, grad_gain_attn, grad_router, grad_table, square_total = [
        flat[start : start + value.size].reshape(value.shape) for start, value in zip(starts, small)
    ]

    out_theirs = swap(jnp.concatenate([done_a, done_b[:1]]), PAIR, 0)
    out_mine = done_b[1:]
    in_theirs = swap(done_c, PAIR, 0)
    in_mine = jnp.concatenate([done_d, done_e])

    def both_experts(mine, theirs):
        mine, theirs = [part.reshape(-1, part.shape[-1]).astype(f32) for part in (mine, theirs)]
        return jnp.stack([jnp.where(half == 0, mine, theirs), jnp.where(half == 0, theirs, mine)])

    grad_w_out = both_experts(out_mine, out_theirs)
    grad_w_in = both_experts(in_mine, in_theirs)

    distill_loss = square_total / (width * valid_count)
    return (
        output.astype(bf16),
        distill_loss,
        grad_input,
        grad_qkv,
        grad_out_weight,
        grad_w_in,
        grad_w_out,
        grad_router,
        grad_table,
        grad_gain_attn,
        grad_gain_moe,
    )


def solution(mesh):
    rows = P(AXES, None)
    return jax.shard_map(
        on_device,
        mesh=mesh,
        in_specs=(
            rows,
            P(None, "dp", None),
            P("dp", None),
            P(),
            P(),
            P(),
            P(),
            P("expert", None, None),
            P("expert", None, None),
            rows,
            P(AXES),
            P(AXES),
            rows,
            rows,
        ),
        out_specs=(
            rows,
            P(),
            rows,
            P(None, "dp", None),
            P("dp", None),
            P("expert", "dp", None),
            P("expert", "dp", None),
            P(),
            P(),
            P(),
            P(),
        ),
        check_vma=False,
    )
```

```python
import math
import jax
import jax.numpy as jnp
from jax import lax
from jax.experimental import pallas as pl
from jax.experimental.pallas import tpu as pltpu
from jax.sharding import PartitionSpec as P

BLOCK = 128
THIRDS = 3
EPS = 1e-06
GELU_A = math.sqrt(2.0 / math.pi)
GELU_B = 0.044715
NT = (((1,), (1,)), ((), ()))
TN = (((0,), (0,)), ((), ()))
VMEM_BYTES = 56 * 1024 * 1024


def cost(micros):
    return pl.CostEstimate(flops=int(micros * 0.37e9), bytes_accessed=0, transcendentals=0)


def dot_f32(left, right, dims=(((1,), (0,)), ((), ()))):
    return lax.dot_general(left, right, dims, preferred_element_type=jnp.float32)


def assemble(rows, pieces):
    start = 0
    for piece in pieces:
        rows[pl.ds(start, piece.shape[0]), :] = piece[...]
        start += piece.shape[0]


def hand_out(total, outs):
    start = 0
    for out in outs:
        out[...] = total[pl.ds(start, out.shape[0]), :].astype(out.dtype)
        start += out.shape[0]


def whole(shape):
    return pl.BlockSpec(shape, lambda *step: (0,) * len(shape))


def expert_forward_kernel(pick, *refs, chunk, count):
    pieces, w_in, w_out = refs[:count], refs[count], refs[count + 1]
    hidden_t, slope, rows_t = refs[count + 2 : count + 5]
    outs, rows, total = refs[count + 5 : 2 * count + 5], refs[2 * count + 5], refs[2 * count + 6]
    step = pl.program_id(0)

    @pl.when(step == 0)
    def _():
        assemble(rows, pieces)
        total[...] = jnp.zeros_like(total)
        rows_t[...] = rows[...].T

    for start in range(0, rows.shape[0], chunk):
        part = pl.ds(start, chunk)
        pre = dot_f32(rows[part, :], w_in[0])
        square = pre * pre
        bend = jnp.tanh(pre * (GELU_A + (GELU_A * GELU_B) * square))
        half = 0.5 + 0.5 * bend
        act = (pre * half).astype(jnp.bfloat16)
        lift = pre * (0.5 * GELU_A + (1.5 * GELU_A * GELU_B) * square)
        slope[part, :] = (half + lift * (1.0 - bend * bend)).astype(jnp.bfloat16)
        hidden_t[:, part] = act.T
        total[part, :] += dot_f32(act, w_out[0])

    @pl.when(step == pl.num_programs(0) - 1)
    def _():
        hand_out(total, outs)


def expert_forward(pick, pieces, w_in, w_out, tile=512, chunk=128):
    many, width = sum(piece.shape[0] for piece in pieces), pieces[0].shape[1]
    inner = w_in.shape[2]
    bf16 = jnp.bfloat16
    return pl.pallas_call(
        lambda *refs: expert_forward_kernel(*refs, chunk=chunk, count=len(pieces)),
        grid_spec=pltpu.PrefetchScalarGridSpec(
            num_scalar_prefetch=1,
            grid=(inner // tile,),
            in_specs=[whole(piece.shape) for piece in pieces]
            + [
                pl.BlockSpec((1, width, tile), lambda f, pick: (pick[0], 0, f)),
                pl.BlockSpec((1, tile, width), lambda f, pick: (pick[0], f, 0)),
            ],
            out_specs=[
                pl.BlockSpec((tile, many), lambda f, pick: (f, 0)),
                pl.BlockSpec((many, tile), lambda f, pick: (0, f)),
                whole((width, many)),
            ]
            + [whole(piece.shape) for piece in pieces],
            scratch_shapes=[pltpu.VMEM((many, width), bf16), pltpu.VMEM((many, width), jnp.float32)],
        ),
        out_shape=[
            jax.ShapeDtypeStruct((inner, many), bf16),
            jax.ShapeDtypeStruct((many, inner), bf16),
            jax.ShapeDtypeStruct((width, many), bf16),
        ]
        + [jax.ShapeDtypeStruct(piece.shape, bf16) for piece in pieces],
        compiler_params=pltpu.CompilerParams(vmem_limit_bytes=VMEM_BYTES),
        cost_estimate=cost(13),
        name="expert_forward",
    )(pick, *pieces, w_in, w_out)


def expert_backward_kernel(pick, *refs, chunk, count):
    pieces, w_in, w_out, slope = refs[:count], refs[count], refs[count + 1], refs[count + 2]
    grad_pre, rows = refs[count + 3 : count + 5]
    outs, total = refs[count + 5 : 2 * count + 5], refs[2 * count + 5]
    step = pl.program_id(0)

    @pl.when(step == 0)
    def _():
        assemble(rows, pieces)
        total[...] = jnp.zeros_like(total)

    for start in range(0, rows.shape[0], chunk):
        part = pl.ds(start, chunk)
        back = dot_f32(rows[part, :], w_out[0], NT) * slope[part, :].astype(jnp.float32)
        back = back.astype(jnp.bfloat16)
        grad_pre[part, :] = back
        total[part, :] += dot_f32(back, w_in[0], NT)

    @pl.when(step == pl.num_programs(0) - 1)
    def _():
        hand_out(total, outs)


def expert_backward(pick, pieces, w_in, w_out, slope, tile=512, chunk=320):
    many, width = sum(piece.shape[0] for piece in pieces), pieces[0].shape[1]
    inner = w_in.shape[2]
    bf16 = jnp.bfloat16
    return pl.pallas_call(
        lambda *refs: expert_backward_kernel(*refs, chunk=chunk, count=len(pieces)),
        grid_spec=pltpu.PrefetchScalarGridSpec(
            num_scalar_prefetch=1,
            grid=(inner // tile,),
            in_specs=[whole(piece.shape) for piece in pieces]
            + [
                pl.BlockSpec((1, width, tile), lambda f, pick: (pick[0], 0, f)),
                pl.BlockSpec((1, tile, width), lambda f, pick: (pick[0], f, 0)),
                pl.BlockSpec((many, tile), lambda f, pick: (0, f)),
            ],
            out_specs=[pl.BlockSpec((many, tile), lambda f, pick: (0, f)), whole((many, width))]
            + [whole(piece.shape) for piece in pieces],
            scratch_shapes=[pltpu.VMEM((many, width), jnp.float32)],
        ),
        out_shape=[jax.ShapeDtypeStruct((many, inner), bf16), jax.ShapeDtypeStruct((many, width), bf16)]
        + [jax.ShapeDtypeStruct(piece.shape, bf16) for piece in pieces],
        compiler_params=pltpu.CompilerParams(vmem_limit_bytes=VMEM_BYTES),
        cost_estimate=cost(11),
        name="expert_backward",
    )(pick, *pieces, w_in, w_out, slope)


def seen_blocks(row_block, blocks):
    return max(row_block + 1, blocks // 2)


def attention_forward_kernel(far, prefix, queries, keys, values, offsets, attended, probs, *, heads, blocks):
    pair = pl.program_id(0)
    lane = lax.broadcasted_iota(jnp.int32, (BLOCK, 2 * heads), 1)
    row = lax.broadcasted_iota(jnp.int32, (BLOCK, BLOCK), 0)
    col = lax.broadcasted_iota(jnp.int32, (BLOCK, BLOCK), 1)
    turned = []
    for head in range(2):
        line = jnp.broadcast_to(offsets[head : head + 1, :], (BLOCK, 4 * BLOCK))
        turned.append(pltpu.roll(line, 0, 1, stride=1, stride_axis=0))
    for row_block in range(blocks):
        rows = pl.ds(row_block * BLOCK, BLOCK)
        span = seen_blocks(row_block, blocks)
        seen = pl.ds(0, span * BLOCK)
        outs = []
        for head in range(2):
            mine = (lane < heads) if head == 0 else (lane >= heads)
            query = jnp.where(mine, queries[rows, :] * 0.125, 0.0).astype(jnp.bfloat16)
            score = dot_f32(query, keys[seen, :], NT)
            far_bias = far[pair * 2 + head]
            pieces = []
            for key_block in range(span):
                piece = score[:, key_block * BLOCK : (key_block + 1) * BLOCK]
                shift = key_block - row_block
                if shift < -1:
                    piece = piece + far_bias
                elif shift < 2:
                    piece = piece + turned[head][:, (2 + shift) * BLOCK : (3 + shift) * BLOCK]
                else:
                    raise ValueError(shift)
                if shift >= 0:
                    shown = col + key_block * BLOCK < prefix[0]
                    piece = jnp.where((shown | (col <= row)) if shift == 0 else shown, piece, -1e30)
                pieces.append(piece)
            peak = pieces[0]
            for piece in pieces[1:]:
                peak = jnp.maximum(peak, piece)
            peak = jnp.max(peak, axis=1, keepdims=True)
            pieces = [jnp.exp(piece - peak) for piece in pieces]
            mass = pieces[0]
            for piece in pieces[1:]:
                mass = mass + piece
            scale = 1.0 / jnp.sum(mass, axis=1, keepdims=True)
            weights = jnp.concatenate([(piece * scale).astype(jnp.bfloat16) for piece in pieces], axis=1)
            probs[head, rows, seen] = weights
            outs.append(dot_f32(weights, values[seen, :]))
        attended[rows, :] = jnp.where(lane < heads, outs[0], outs[1]).astype(jnp.bfloat16)


def attention_forward(far, prefix, qkv_rows, offsets):
    length, width = qkv_rows.shape[1:]
    pairs = width // 128
    blocks = length // BLOCK
    return pl.pallas_call(
        lambda *refs: attention_forward_kernel(*refs, heads=64, blocks=blocks),
        grid_spec=pltpu.PrefetchScalarGridSpec(
            num_scalar_prefetch=2,
            grid=(pairs,),
            in_specs=[pl.BlockSpec((None, length, 128), lambda h, far, prefix, c=c: (c, 0, h)) for c in range(3)]
            + [pl.BlockSpec((None, 2, 4 * BLOCK), lambda h, far, prefix: (h, 0, 0))],
            out_specs=[
                pl.BlockSpec((length, 128), lambda h, far, prefix: (0, h)),
                pl.BlockSpec((2, length, length), lambda h, far, prefix: (h, 0, 0)),
            ],
        ),
        out_shape=[
            jax.ShapeDtypeStruct((length, width), jnp.bfloat16),
            jax.ShapeDtypeStruct((2 * pairs, length, length), jnp.bfloat16),
        ],
        compiler_params=pltpu.CompilerParams(vmem_limit_bytes=VMEM_BYTES),
        cost_estimate=cost(17),
        name="attention_forward",
    )(far, prefix, qkv_rows, qkv_rows, qkv_rows, offsets.reshape(pairs, 2, 4 * BLOCK))


def attention_backward_kernel(queries, keys, values, grads, probs, grad_rows, bands, flow, *, heads, blocks):
    lane = lax.broadcasted_iota(jnp.int32, (BLOCK, 2 * heads), 1)
    query_t = (queries[...] * 0.125).astype(jnp.bfloat16).T
    grad_t = grads[...].T
    half = blocks // 2
    dk, dv = [], []
    dq = [[], []]
    for head in range(2):
        mine = (lane < heads) if head == 0 else (lane >= heads)
        sums = [None] * 4
        for row_block in range(blocks):
            rows = pl.ds(row_block * BLOCK, BLOCK)
            span = seen_blocks(row_block, blocks)
            seen = pl.ds(0, span * BLOCK)
            grad = jnp.where(mine, grads[rows, :], 0.0).astype(jnp.bfloat16)
            soft = probs[head, rows, seen].astype(jnp.float32)
            back = dot_f32(grad, values[seen, :], NT)
            inner = jnp.sum(soft * back, axis=1, keepdims=True)
            score_grad = (soft * (back - inner)).astype(jnp.bfloat16)
            flow[rows, seen] = score_grad
            dq[head].append(dot_f32(score_grad, keys[seen, :]) * 0.125)
            for key_block in range(span):
                band = max(key_block - row_block, -2)
                if band > 1:
                    continue
                tile = score_grad[:, key_block * BLOCK : (key_block + 1) * BLOCK].astype(jnp.float32)
                sums[band + 2] = tile if sums[band + 2] is None else sums[band + 2] + tile
        for band in range(4):
            bands[head, band] = sums[band]
        part = slice(head * heads, (head + 1) * heads)
        key_pieces, value_pieces = [], []
        for key_block in range(blocks):
            first = 0 if key_block < half else key_block
            rows = pl.ds(first * BLOCK, (blocks - first) * BLOCK)
            cols = pl.ds(key_block * BLOCK, BLOCK)
            key_pieces.append(dot_f32(query_t[part, first * BLOCK :], flow[rows, cols]))
            value_pieces.append(dot_f32(grad_t[part, first * BLOCK :], probs[head, rows, cols]))
        dk.append(jnp.concatenate(key_pieces, axis=1))
        dv.append(jnp.concatenate(value_pieces, axis=1))
    for row_block in range(blocks):
        rows = pl.ds(row_block * BLOCK, BLOCK)
        grad_rows[0, rows, :] = jnp.where(lane < heads, dq[0][row_block], dq[1][row_block]).astype(jnp.bfloat16)
    grad_rows[1] = jnp.concatenate(dk, axis=0).T.astype(jnp.bfloat16)
    grad_rows[2] = jnp.concatenate(dv, axis=0).T.astype(jnp.bfloat16)


def attention_backward(qkv_rows, grads, probs):
    length, width = grads.shape
    pairs = width // 128
    blocks = length // BLOCK
    block = pl.BlockSpec((length, 128), lambda h: (0, h))
    of_three = [pl.BlockSpec((None, length, 128), lambda h, c=c: (c, 0, h)) for c in range(3)]
    return pl.pallas_call(
        lambda *refs: attention_backward_kernel(*refs, heads=64, blocks=blocks),
        grid=(pairs,),
        in_specs=[*of_three, block, pl.BlockSpec((2, length, length), lambda h: (h, 0, 0))],
        out_specs=[pl.BlockSpec((3, length, 128), lambda h: (0, 0, h)), pl.BlockSpec((2, 4, BLOCK, BLOCK), lambda h: (h, 0, 0, 0))],
        out_shape=[jax.ShapeDtypeStruct((3, length, width), jnp.bfloat16)]
        + [jax.ShapeDtypeStruct((2 * pairs, 4, BLOCK, BLOCK), jnp.float32)],
        scratch_shapes=[pltpu.VMEM((length, length), jnp.bfloat16)],
        compiler_params=pltpu.CompilerParams(vmem_limit_bytes=VMEM_BYTES),
        cost_estimate=cost(17),
        name="attention_backward",
    )(qkv_rows, qkv_rows, qkv_rows, grads, probs)


def pieces_left(lefts, plans, many):
    part = lefts[0][0].shape[0] // THIRDS
    return jnp.concatenate(
        [
            jnp.concatenate([ref[pl.ds(third * part, part), :] for ref in lefts[group * many + k]], axis=1)
            for plan in plans
            for group, third in plan
            for k in range(many)
        ]
    )


def put_pieces(result, outs):
    place = 0
    for out in outs:
        many, pieces, part = out.shape[:3]
        for piece in range(pieces):
            for k in range(many):
                out[k, piece] = result[place : place + part]
                place += part


def weight_part_kernel(picks, *refs, count, plans, many):
    lefts, rights, outs = refs[: 2 * count], refs[2 * count : 2 * count + 2], refs[2 * count + 2 :]
    left = pieces_left(list(zip(lefts[:count], lefts[count:])), plans, many)
    right = jnp.concatenate([ref[...] for ref in rights], axis=0)
    put_pieces(dot_f32(left, right).astype(jnp.bfloat16), outs)


def weight_part_plain(picks, lefts, rights, rows, plans, many):
    left, right = jnp.concatenate(lefts, axis=1), jnp.concatenate(rights, axis=0)
    depth, width = right.shape
    part = rows // THIRDS
    result = jnp.take(left.reshape(-1, rows, depth), picks, axis=0)
    result = jnp.einsum("srd,dw->srw", result, right, preferred_element_type=jnp.float32).astype(jnp.bfloat16)
    result = result.reshape(-1, many, THIRDS, part, width)
    return [jnp.stack([result[group, :, third] for group, third in plan], axis=1) for plan in plans]


def weight_part(picks, lefts, rights, rows, plans, many, tile):
    depth, width = rights[0].shape
    count, part = picks.shape[0], rows // THIRDS
    if part % 16:
        return weight_part_plain(picks, lefts, rights, rows, plans, many)
    return pl.pallas_call(
        lambda *refs: weight_part_kernel(*refs, count=count, plans=plans, many=many),
        grid_spec=pltpu.PrefetchScalarGridSpec(
            num_scalar_prefetch=1,
            grid=(width // tile,),
            in_specs=[pl.BlockSpec((rows, depth), lambda i, picks, k=k: (picks[k], 0)) for k in range(count)] * 2
            + [pl.BlockSpec((depth, tile), lambda i, picks: (0, i))] * 2,
            out_specs=[pl.BlockSpec((many, len(plan), part, tile), lambda i, picks: (0, 0, 0, i)) for plan in plans],
        ),
        out_shape=[jax.ShapeDtypeStruct((many, len(plan), part, width), jnp.bfloat16) for plan in plans],
        compiler_params=pltpu.CompilerParams(vmem_limit_bytes=VMEM_BYTES),
        cost_estimate=cost(4),
        name="weight_part",
    )(picks, *([lefts[0]] * count), *([lefts[1]] * count), *rights)


def hot_columns(slots, first, count):
    rows = first + lax.broadcasted_iota(jnp.int32, (count, slots.shape[1]), 0)
    return (rows == slots).astype(jnp.bfloat16)


def halves(core, mine, other):
    return jnp.where(core == 0, mine, other), jnp.where(core == 0, other, mine)


def join_kernel(places, *refs):
    pieces, out = refs[:-1], refs[-1]
    rows = pieces[0].shape[1]
    count = pieces[0].shape[0]
    for chunk in range(out.shape[0] // count):
        for step in range(len(pieces) * count // out.shape[0]):
            piece = pieces[chunk * (len(pieces) * count // out.shape[0]) + step]
            start = pl.multiple_of(places[step] * rows, rows)
            out[pl.ds(chunk * count, count), pl.ds(start, rows), :] = piece[...]


def join(places, chunks):
    count, rows, columns = chunks[0][0].shape
    steps = len(chunks[0])
    return pl.pallas_call(
        join_kernel,
        in_specs=[pl.BlockSpec(memory_space=pltpu.SMEM)] + [pl.BlockSpec(memory_space=pltpu.VMEM)] * (steps * len(chunks)),
        out_shape=jax.ShapeDtypeStruct((count * len(chunks), steps * rows, columns), jnp.bfloat16),
        compiler_params=pltpu.CompilerParams(vmem_limit_bytes=VMEM_BYTES),
        cost_estimate=cost(3),
        name="join",
    )(places, *[piece for chunk in chunks for piece in chunk])


def project_kernel(core, rows, mine, other, result):
    half = mine.shape[1]
    first, second = halves(core[0], mine[...], other[...])
    result[:, :half] = dot_f32(rows[...], first).astype(jnp.bfloat16)
    result[:, half:] = dot_f32(rows[...], second).astype(jnp.bfloat16)


def project(core, rows, mine, other, used):
    width, half = mine.shape[1:]
    length = rows.shape[0]
    return pl.pallas_call(
        project_kernel,
        grid_spec=pltpu.PrefetchScalarGridSpec(
            num_scalar_prefetch=1,
            grid=(used,),
            in_specs=[
                whole((length, width)),
                pl.BlockSpec((None, width, half), lambda i, core: (i, 0, 0)),
                pl.BlockSpec((None, width, half), lambda i, core: (i, 0, 0)),
            ],
            out_specs=pl.BlockSpec((None, length, 2 * half), lambda i, core: (i, 0, 0)),
        ),
        out_shape=jax.ShapeDtypeStruct((used, length, 2 * half), jnp.bfloat16),
        compiler_params=pltpu.CompilerParams(vmem_limit_bytes=VMEM_BYTES),
        cost_estimate=cost(4),
        name="project",
    )(core, rows, mine, other)


def route_kernel(core, attended, tokens, mine, other, gain, router, routes, slots, middle, normed, gates, *outs):
    f32 = jnp.float32
    first, second = halves(core[0], mine[...], other[...])
    rows = attended[...]
    moved = jnp.concatenate([dot_f32(rows, first), dot_f32(rows, second)], axis=1)
    value = tokens[...].astype(f32) + moved
    middle[...] = value
    low = (value * lax.rsqrt(jnp.mean(value * value, axis=1, keepdims=True) + EPS) * gain[...]).astype(jnp.bfloat16)
    normed[...] = low
    start = 0
    for first_out, second_out in zip(outs[::2], outs[1::2]):
        size = first_out.shape[0]
        hot = hot_columns(slots[0:1, :], start, 2 * size) + hot_columns(slots[1:2, :], start, 2 * size)
        part = dot_f32(hot, low).astype(jnp.bfloat16)
        first_out[...] = part[:size]
        second_out[...] = part[size:]
        start += 2 * size
    logits = dot_f32(low, router[...])
    soft = jnp.exp(logits - jnp.max(logits, axis=1, keepdims=True))
    soft = soft / jnp.sum(soft, axis=1, keepdims=True)
    expert = lax.broadcasted_iota(jnp.int32, soft.shape, 1)
    chosen = [jnp.sum(jnp.where(expert == routes[:, k : k + 1], soft, 0.0), axis=1, keepdims=True) for k in range(2)]
    for k in range(2):
        gates[:, k : k + 1] = chosen[k] / (chosen[0] + chosen[1])


def route(core, attended, tokens, mine, other, gain, router, routes, slots, pieces, count):
    length, width = tokens.shape
    last, half = mine.shape[0] - 1, mine.shape[2]
    f32, bf16 = jnp.float32, jnp.bfloat16
    weight = pl.BlockSpec((None, width, half), lambda i, core: (last, 0, 0))
    shapes = [((length, width), f32), ((length, width), bf16), ((length, 2), f32)] + [((count, width), bf16)] * pieces
    return pl.pallas_call(
        route_kernel,
        grid_spec=pltpu.PrefetchScalarGridSpec(
            num_scalar_prefetch=1,
            grid=(1,),
            in_specs=[whole((length, width)), whole((length, width)), weight, weight, whole((1, width)), whole(router.shape), whole(routes.shape), whole(slots.shape)],
            out_specs=[whole(shape) for shape, _ in shapes],
        ),
        out_shape=[jax.ShapeDtypeStruct(shape, kind) for shape, kind in shapes],
        compiler_params=pltpu.CompilerParams(vmem_limit_bytes=VMEM_BYTES),
        cost_estimate=cost(6),
        name="route",
    )(core, attended, tokens, mine, other, gain.reshape(1, -1), router, routes, slots)


def hot_route(slots, k, count):
    cols = lax.broadcasted_iota(jnp.int32, (slots.shape[0], count), 1)
    return cols == slots[:, k : k + 1]


def combine_kernel(*refs, count):
    slots, slots_t, scale = refs[:3]
    pieces = refs[3 : 3 + count]
    middle, teacher, cotangent, valid, gates, routes = refs[3 + count : 9 + count]
    output, grad_y, grad_logits, square = refs[9 + count : 13 + count]
    sends, rows = refs[13 + count : 13 + 2 * count], refs[13 + 2 * count]
    f32, bf16 = jnp.float32, jnp.bfloat16
    assemble(rows, pieces)
    table = rows[...]
    picked = [dot_f32(hot_route(slots, k, rows.shape[0]).astype(bf16), table) for k in range(2)]
    result = middle[...] + (gates[:, 0:1] * picked[0] + gates[:, 1:2] * picked[1])
    output[...] = result.astype(bf16)
    misfit = valid[...] * (result - teacher[...].astype(f32))
    square[...] = jnp.sum((misfit * misfit).reshape(-1, 8, misfit.shape[1]), axis=0)
    grad = cotangent[...].astype(f32) + misfit * scale[0, 0]
    grad_y[...] = grad
    steep = [jnp.sum(grad * picked[k], axis=1, keepdims=True) for k in range(2)]
    slack = gates[:, 0:1] * steep[0] + gates[:, 1:2] * steep[1]
    expert = lax.broadcasted_iota(jnp.int32, grad_logits.shape, 1)
    turn = [jnp.where(expert == routes[:, k : k + 1], gates[:, k : k + 1] * (steep[k] - slack), 0.0) for k in range(2)]
    grad_logits[...] = (turn[0] + turn[1]).astype(bf16)
    scaled = [(gates[:, k : k + 1] * grad).astype(bf16) for k in range(2)]
    start = 0
    for first, second in zip(sends[::2], sends[1::2]):
        size = first.shape[0]
        part = [dot_f32(hot_columns(slots_t[k : k + 1, :], start, 2 * size), scaled[k]) for k in range(2)]
        part = (part[0] + part[1]).astype(bf16)
        first[...] = part[:size]
        second[...] = part[size:]
        start += 2 * size


def combine(slots, slots_t, scale, pieces, middle, teacher, cotangent, valid, gates, routes, experts):
    length, width = middle.shape
    count = len(pieces)
    f32, bf16 = jnp.float32, jnp.bfloat16
    return pl.pallas_call(
        lambda *refs: combine_kernel(*refs, count=count),
        in_specs=[pl.BlockSpec(memory_space=pltpu.VMEM)] * 2
        + [pl.BlockSpec(memory_space=pltpu.SMEM)]
        + [pl.BlockSpec(memory_space=pltpu.VMEM)] * (6 + count),
        out_shape=[
            jax.ShapeDtypeStruct((length, width), bf16),
            jax.ShapeDtypeStruct((length, width), f32),
            jax.ShapeDtypeStruct((length, experts), bf16),
            jax.ShapeDtypeStruct((8, width), f32),
        ]
        + [jax.ShapeDtypeStruct(piece.shape, bf16) for piece in pieces],
        scratch_shapes=[pltpu.VMEM((sum(piece.shape[0] for piece in pieces), width), bf16)],
        compiler_params=pltpu.CompilerParams(vmem_limit_bytes=VMEM_BYTES),
        cost_estimate=cost(8),
        name="combine",
    )(slots, slots_t, scale, *pieces, middle, teacher, cotangent, valid, gates, routes)


def norm_back(value, gain, grad):
    root = lax.rsqrt(jnp.mean(value * value, axis=1, keepdims=True) + EPS)
    normed = value * root
    scaled = grad * gain
    inner = jnp.mean(scaled * normed, axis=1, keepdims=True)
    return root * (scaled - normed * inner), jnp.sum((grad * normed).reshape(-1, 8, value.shape[1]), axis=0)


def collect_kernel(core, *refs, count):
    slots, pieces = refs[0], refs[1 : 1 + count]
    middle, gain, grad_logits, router, grad_y, mine, other = refs[1 + count : 8 + count]
    grad_middle, rounded, grad_attended, grad_gain, rows = refs[8 + count :]
    assemble(rows, pieces)
    hot = (hot_route(slots, 0, rows.shape[0]) | hot_route(slots, 1, rows.shape[0])).astype(jnp.bfloat16)
    grad = dot_f32(grad_logits[...], router[...], NT) + dot_f32(hot, rows[...])
    turned, grad_gain[...] = norm_back(middle[...], gain[...], grad)
    result = grad_y[...] + turned
    grad_middle[...] = result
    low = result.astype(jnp.bfloat16)
    rounded[...] = low
    first, second = halves(core[0], mine[...], other[...])
    half = first.shape[1]
    grad_attended[...] = (dot_f32(low[:, :half], first, NT) + dot_f32(low[:, half:], second, NT)).astype(jnp.bfloat16)


def collect(core, slots, pieces, middle, gain, grad_logits, router, grad_y, mine, other):
    length, width = middle.shape
    last, half = mine.shape[0] - 1, mine.shape[2]
    f32, bf16 = jnp.float32, jnp.bfloat16
    weight = pl.BlockSpec((None, width, half), lambda i, core: (last, 0, 0))
    plain = [slots, *pieces, middle, gain.reshape(1, -1), grad_logits, router, grad_y]
    shapes = [((length, width), f32), ((length, width), bf16), ((length, width), bf16), ((8, width), f32)]
    return pl.pallas_call(
        lambda *refs: collect_kernel(*refs, count=len(pieces)),
        grid_spec=pltpu.PrefetchScalarGridSpec(
            num_scalar_prefetch=1,
            grid=(1,),
            in_specs=[whole(array.shape) for array in plain] + [weight, weight],
            out_specs=[whole(shape) for shape, _ in shapes],
            scratch_shapes=[pltpu.VMEM((sum(piece.shape[0] for piece in pieces), width), bf16)],
        ),
        out_shape=[jax.ShapeDtypeStruct(shape, kind) for shape, kind in shapes],
        compiler_params=pltpu.CompilerParams(vmem_limit_bytes=VMEM_BYTES),
        cost_estimate=cost(8),
        name="collect",
    )(core, *plain, mine, other)


def outer_halves_kernel(core, normed, attended, rights, last, away, stay, normed_t, attended_t, *, count):
    step = pl.program_id(0)
    half = away.shape[1]

    def put(result):
        result = result.astype(jnp.bfloat16)

        @pl.when(core[0] == 0)
        def _():
            stay[...] = result[:, :half]
            away[...] = result[:, half:]

        @pl.when(core[0] != 0)
        def _():
            away[...] = result[:, :half]
            stay[...] = result[:, half:]

    @pl.when(step == 0)
    def _():
        normed_t[...] = normed[...].T
        attended_t[...] = attended[...].T

    @pl.when(step < count)
    def _():
        put(dot_f32(normed_t[...], rights[...]))

    @pl.when(step == count)
    def _():
        put(dot_f32(attended_t[...], last[...]))


def outer_halves(core, normed, attended, rights, last):
    length, width = normed.shape
    count, half = rights.shape[0], width // 2
    shape = jax.ShapeDtypeStruct((count + 1, width, half), jnp.bfloat16)
    return pl.pallas_call(
        lambda *refs: outer_halves_kernel(*refs, count=count),
        grid_spec=pltpu.PrefetchScalarGridSpec(
            num_scalar_prefetch=1,
            grid=(count + 1,),
            in_specs=[
                whole((length, width)),
                whole((length, width)),
                pl.BlockSpec((None, length, width), lambda i, core: (jnp.minimum(i, count - 1), 0, 0)),
                whole((length, width)),
            ],
            out_specs=[pl.BlockSpec((None, width, half), lambda i, core: (i, 0, 0))] * 2,
            scratch_shapes=[pltpu.VMEM((width, length), jnp.bfloat16)] * 2,
        ),
        out_shape=[shape, shape],
        compiler_params=pltpu.CompilerParams(vmem_limit_bytes=VMEM_BYTES),
        cost_estimate=cost(6),
        name="outer_halves",
    )(core, normed, attended, rights, last)


def enter_kernel(core, grads, mine, other, tokens, gain, grad_middle, grad_input, grad_gain, total):
    step = pl.program_id(0)
    first, second = halves(core[0], mine[...], other[...])
    half = first.shape[1]
    rows = grads[...]
    part = dot_f32(rows[:, :half], first, NT) + dot_f32(rows[:, half:], second, NT)

    @pl.when(step == 0)
    def _():
        total[...] = part

    @pl.when(step > 0)
    def _():
        total[...] += part

    @pl.when(step == pl.num_programs(0) - 1)
    def _():
        turned, grad_gain[...] = norm_back(tokens[...].astype(jnp.float32), gain[...], total[...])
        grad_input[...] = grad_middle[...] + turned


def enter(core, grads, mine, other, tokens, gain, grad_middle):
    length, width = tokens.shape
    count, half = grads.shape[0], mine.shape[2]
    weight = pl.BlockSpec((None, width, half), lambda i, core: (i, 0, 0))
    return pl.pallas_call(
        enter_kernel,
        grid_spec=pltpu.PrefetchScalarGridSpec(
            num_scalar_prefetch=1,
            grid=(count,),
            in_specs=[pl.BlockSpec((None, length, width), lambda i, core: (i, 0, 0)), weight, weight, whole((length, width)), whole((1, width)), whole((length, width))],
            out_specs=[whole((length, width)), whole((8, width))],
            scratch_shapes=[pltpu.VMEM((length, width), jnp.float32)],
        ),
        out_shape=[jax.ShapeDtypeStruct((length, width), jnp.float32), jax.ShapeDtypeStruct((8, width), jnp.float32)],
        compiler_params=pltpu.CompilerParams(vmem_limit_bytes=VMEM_BYTES),
        cost_estimate=cost(6),
        name="enter",
    )(core, grads, mine, other, tokens, gain.reshape(1, -1), grad_middle)


BOUNDS = (12, 16, 23, 32, 46, 64, 91)
TOP_PRECISION = lax.Precision.HIGHEST
AXES = ("dp", "expert")
PAIR = 2


def after(value, *others):
    return lax.optimization_barrier((value, *others))[0] if others else value


def bucket_index(offset):
    distance = jnp.abs(offset)
    far_bucket = 8 + sum([(distance >= level).astype(jnp.int32) for level in BOUNDS])
    near_bucket = jnp.where(distance < 8, distance, far_bucket)
    return jnp.where(offset > 0, 16, 0) + near_bucket


def norm_apply(inputs, gain_vec):
    return inputs * lax.rsqrt(jnp.mean(inputs * inputs, axis=-1, keepdims=True) + EPS) * gain_vec


def tile_offsets(query_block, key_block):
    rows = query_block * BLOCK + lax.broadcasted_iota(jnp.int32, (BLOCK, BLOCK), 0)
    cols = key_block * BLOCK + lax.broadcasted_iota(jnp.int32, (BLOCK, BLOCK), 1)
    return rows, cols


def offset_bias(table):
    offsets = jnp.arange(4 * BLOCK, dtype=jnp.int32) - 2 * BLOCK
    hot = (bucket_index(offsets)[None] == jnp.arange(table.shape[1], dtype=jnp.int32)[:, None]).astype(jnp.float32)
    return jnp.dot(table, hot, precision=TOP_PRECISION)


def table_gradient(bands, buckets):
    rows, cols = tile_offsets(0, 0)
    ids = [jnp.full((BLOCK, BLOCK), bucket_far(), jnp.int32)]
    ids += [bucket_index(shift * BLOCK + cols - rows) for shift in (-1, 0, 1)]
    hot = (jnp.stack(ids)[..., None] == jnp.arange(buckets, dtype=jnp.int32)).astype(jnp.float32)
    return jnp.einsum("hdxy,dxyb->hb", bands, hot, precision=TOP_PRECISION)


def bucket_far():
    return 8 + len(BOUNDS)


def on_device(
    tokens,
    qkv_weight,
    out_weight,
    position_bias_table,
    gain_attn,
    gain_moe,
    router,
    w_in,
    w_out,
    routes,
    prefix,
    valid_mask,
    teacher,
    cotangent,
):
    length, width = tokens.shape
    bf16, f32 = jnp.bfloat16, jnp.float32
    expert_count = router.shape[1]
    top_count = routes.shape[1]
    groups = lax.axis_size("expert")
    copies = lax.axis_size("dp")
    inner = w_in.shape[2]
    capacity = 5 * length * top_count // (4 * expert_count)
    total_tokens = length * copies * groups
    sources = 2 * groups
    blocks = length // BLOCK
    here_dp, here_group = lax.axis_index("dp"), lax.axis_index("expert")
    half = (here_dp >> 1) & 1
    core = here_group & 1
    rest = copies // 4

    def swap(value, dp_mask, group_mask):
        pairs = [
            (i, ((i // groups) ^ dp_mask) * groups + ((i % groups) ^ group_mask))
            for i in range(copies * groups)
        ]
        return lax.ppermute(value, AXES, pairs)

    def bits(count):
        return [1 << place for place in range(count.bit_length() - 1)]

    def partial_sums(value):
        sums = []
        for masks in [(0, mask) for mask in bits(groups)] + [(mask, 0) for mask in bits(copies)]:
            value = value + swap(value, *masks)
            sums.append(value)
        return sums

    chips = groups

    def across(value, place):
        return swap(value, PAIR * (place // (groups // 2)), 2 * (place % (groups // 2)))

    def to_chips(pieces):
        return [pieces[0]] + [across(pieces[place], place) for place in range(1, chips)]

    def through(visit, sends):
        direct, relay = to_chips(sends[::2]), to_chips(sends[1::2])
        seen, direct = visit(direct)
        direct = to_chips(direct)
        relay = [after(part, seen) for part in relay]
        passed = visit(swap(jnp.concatenate(relay), 0, 1))
        passed = swap(after(passed, *direct), 0, 1)
        relay = [passed[place * capacity : (place + 1) * capacity] for place in range(chips)]
        return direct, relay

    def weave(direct, relay):
        return [part for pair in zip(direct, to_chips(relay)) for part in pair]

    ring = list(range(0, copies, 2)) + list(range(copies - 1, 0, -2))
    turns = [(1, step) for step in range(1, copies // 2 + 1)] + [(-1, step) for step in range(1, copies // 2)]

    def gather_ring(shard, due):
        got = [shard]
        for turn in (1, -1):
            held = shard
            pairs = [(ring[i], ring[(i + turn) % copies]) for i in range(copies)]
            for step in [step for way, step in turns if way == turn]:
                held = lax.ppermute(after(held, *due[step - 2 : step - 1]) if step > 1 else held, "dp", pairs)
                got.append(held)
        return got

    def ring_places():
        place = jnp.where(here_dp & 1 == 0, here_dp >> 1, copies - 1 - (here_dp >> 1))
        shift = jnp.array([0] + [turn * step for turn, step in turns], jnp.int32)
        place = (place - shift) & (copies - 1)
        return jnp.where(place < copies // 2, 2 * place, 2 * (copies - 1 - place) + 1).astype(jnp.int32)

    columns = width // 2
    core_index = core.reshape(1).astype(jnp.int32)
    valid_rows = valid_mask.astype(f32)[:, None]
    counts = partial_sums(jnp.broadcast_to(jnp.sum(valid_rows), (8, 128)))
    valid_count = counts[-1][0, 0]
    shards = [
        lax.dynamic_slice_in_dim(part, core * columns, columns, 2)
        for part in (qkv_weight[:2], jnp.concatenate([qkv_weight[2:], out_weight[None]]))
    ]
    if copies > 8:
        mine = lax.all_gather(jnp.concatenate(shards), "dp", axis=1, tiled=True)
    else:
        mine = join(ring_places(), [gather_ring(shards[0], counts), gather_ring(shards[1], ())])
    other = swap(mine, 0, 1)
    offsets = offset_bias(position_bias_table)

    flat_routes = routes.reshape(-1)
    pair_count = length * top_count
    slot_count = sources * capacity
    route_hits = (flat_routes[:, None] == jnp.arange(expert_count, dtype=jnp.int32)[None, :]).astype(bf16)
    lower_ones = (
        lax.broadcasted_iota(jnp.int32, (pair_count, pair_count), 0)
        >= lax.broadcasted_iota(jnp.int32, (pair_count, pair_count), 1)
    ).astype(bf16)
    running = jnp.dot(lower_ones, route_hits, preferred_element_type=f32)
    pair_rank = jnp.sum((running - 1.0) * route_hits.astype(f32), axis=1).astype(jnp.int32)
    away = (flat_routes >> 1) ^ here_group
    chip = ((flat_routes & 1) ^ half) * (groups // 2) + (away >> 1)
    slots = ((chip * 2 + (away & 1)) * capacity + pair_rank).reshape(length, top_count)
    slots_t = slots.T

    resid = tokens.astype(f32)
    normed1 = norm_apply(resid, gain_attn).astype(bf16)
    qkv_rows = project(core_index, normed1, mine, other, 3)
    offsets = after(offsets, valid_count)
    attended, probs = attention_forward(position_bias_table[:, bucket_far()], prefix, qkv_rows, offsets)
    middle, normed2, gates, *sends = route(
        core_index, attended, tokens, mine, other, gain_moe, router, routes, slots_t, 2 * chips, capacity
    )

    pick = half.reshape(1).astype(jnp.int32)
    hidden, slopes, rows_in = [], [], []

    def expert(pieces):
        one = not isinstance(pieces, list)
        hidden_t, slope, rows_t, *results = expert_forward(pick, [pieces] if one else pieces, w_in, w_out)
        for kept, value in zip((hidden, slopes, rows_in), (hidden_t, slope, rows_t)):
            kept.append(value)
        return results[0] if one else (hidden_t, results)

    back = weave(*through(expert, sends))
    scale = (total_tokens / valid_count).reshape(1, 1)
    output, grad_y, grad_logits, squares, *sends = combine(
        slots, slots_t, scale, back, middle, teacher, cotangent, valid_rows, gates, routes, expert_count
    )
    grad_router = jnp.einsum("td,te->de", normed2, grad_logits, preferred_element_type=f32)

    out_rows = inner // copies
    in_rows = width // copies
    far_bit = here_dp % 2
    slices = jnp.arange(rest, dtype=jnp.int32) * 4

    def picks(bit0):
        return jnp.concatenate([slices + ((half ^ other_half) * 2 + bit0) for other_half in (1, 0)]).astype(jnp.int32)

    sent, kept = picks(1 - far_bit), picks(far_bit)
    every = jnp.concatenate([sent, kept])

    def add(left, right):
        return (left.astype(f32) + right.astype(f32)).astype(bf16)

    def fold(unit, bit, axis=0):
        unit = unit.reshape(unit.shape[:axis] + (2, unit.shape[axis] // 2) + unit.shape[axis + 1 :])
        away_part = lax.dynamic_index_in_dim(unit, 1 - bit, axis, keepdims=False)
        return away_part, lax.dynamic_index_in_dim(unit, bit, axis, keepdims=False)

    far_masks = list(reversed(bits(copies)[2:]))

    def near_add(got, keep):
        away_part, stay_part = fold(add(got, keep), (here_dp // far_masks[0]) % 2)
        return away_part, stay_part

    def far_trade(away_part):
        return swap(away_part, far_masks[0], 0)

    def finish(got, stay):
        unit = add(got, stay)
        for mask in far_masks[1:]:
            away_part, stay_part = fold(unit, (here_dp // mask) % 2)
            unit = add(swap(away_part, mask, 0), stay_part)
        return unit[0]

    plan_a, plan_b, plan_c = ((0, 0),), ((0, 1), (0, 2)), ((1, 0), (1, 1), (1, 2))
    plan_d, plan_e, plan_f = ((0, 0), (0, 1)), ((0, 2), (1, 0), (1, 1)), ((1, 2),)
    out_plans, in_plans = (plan_a, plan_b, plan_c), (plan_d, plan_e, plan_f)

    def keep(plan):
        return tuple((group + 2, third) for group, third in plan)

    grad_rows, grad_pre, parts = [], [], []

    def expert_back(pieces):
        if isinstance(pieces, list):
            grad_pre_rows, grads, *results = expert_backward(pick, pieces, w_in, w_out, slopes[0])
            grad_rows.append(grads)
            grad_pre.append(grad_pre_rows)
            return grad_pre_rows, results
        grad_rows.append(pieces)
        parts.extend(weight_part(sent, hidden, grad_rows, out_rows, out_plans, rest, width))
        parts[0] = swap(parts[0], 1, 0)
        pieces = after(pieces, parts[1])
        grad_pre_rows, _, results = expert_backward(pick, [pieces], w_in, w_out, slopes[1])
        grad_pre.append(grad_pre_rows)
        return after(results, parts[0])

    direct, relay = through(expert_back, sends)
    got_a, send_b, send_c = parts
    got_b = swap(after(send_b, relay[0]), 1, 0)
    back = weave(direct, relay)
    grad_rows, grad_pre = lax.optimization_barrier((grad_rows, grad_pre, relay))[:2]
    keep_a, keep_b, keep_c = weight_part(kept, hidden, grad_rows, out_rows, out_plans, rest, width)
    away_a, stay_a = near_add(got_a, keep_a)
    far_a = far_trade(away_a)
    send_d, send_e, send_f, keep_d, keep_e, keep_f = weight_part(
        every, rows_in, after(grad_pre, away_a), in_rows, in_plans + tuple(keep(plan) for plan in in_plans), rest, inner // 2
    )
    back = [after(part, send_d) for part in back]
    got_c = swap(after(send_c, *back), 1, 0)
    grad_middle, grad_attn_proj, grad_attended, gain_moe_parts = collect(
        core_index, slots, back, middle, gain_moe, grad_logits, router, grad_y, mine, other
    )
    away_b, stay_b = near_add(after(got_b, grad_attended), keep_b)
    grad_attended, away_b, far_a = lax.optimization_barrier((grad_attended, away_b, far_a))
    far_b = far_trade(away_b)
    done_a = finish(far_a, stay_a)
    grad_qkv_rows, bands = attention_backward(qkv_rows, grad_attended, probs)
    grad_qkv_rows, got_c = lax.optimization_barrier((grad_qkv_rows, got_c))

    away_c, stay_c = near_add(got_c, keep_c)
    far_c = far_trade(away_c)
    got_d = swap(after(send_d, away_c), 1, 0)
    weights_away, weights_stay = outer_halves(
        core_index, normed1, attended, after(grad_qkv_rows, far_b, away_c), grad_attn_proj
    )
    done_b = finish(far_b, stay_b)
    weights_got = jnp.stack([swap(weights_away[place], 0, 1) for place in range(4)])
    grad_input, gain_attn_parts = enter(core_index, grad_qkv_rows, mine, other, tokens, gain_attn, grad_middle)
    away_d, stay_d = near_add(got_d, keep_d)
    far_d = far_trade(away_d)
    weights_total = add(after(weights_got, gain_attn_parts, away_d), weights_stay)
    got_e = swap(after(send_e, away_d), 1, 0)
    got_f = swap(after(send_f, away_d), 1, 0)

    group_masks = bits(groups)[1:]
    dp_masks = sorted(bits(copies), key=lambda mask: (mask != PAIR, mask))
    total = weights_total.reshape(4, copies, in_rows, columns)
    for mask in group_masks:
        away_part, stay_part = fold(total, (here_group // mask) % 2, 2)
        total = add(swap(away_part, 0, mask), stay_part)
    away_e, stay_e = near_add(after(got_e, total), keep_e)
    far_e = far_trade(away_e)
    away_f, stay_f = near_add(after(got_f, away_e), keep_f)
    far_f = far_trade(away_f)
    done_c = finish(after(far_c, total), stay_c)
    out_theirs = swap(after(jnp.concatenate([done_a, done_b]), total), PAIR, 0)

    grad_table = table_gradient(after(bands, weights_total), position_bias_table.shape[1])
    small = [
        jnp.sum(gain_moe_parts, axis=0),
        jnp.sum(gain_attn_parts, axis=0),
        grad_router,
        grad_table,
        jnp.sum(squares),
    ]
    sizes = [value.size for value in small]
    flat = jnp.concatenate([value.reshape(-1) for value in small])
    flat = after(jnp.pad(flat, (0, -sum(sizes) % 1024)).reshape(-1, 128), total)

    total = total.reshape((4,) + (2,) * len(dp_masks) + total.shape[2:])
    left_bits = sorted(dp_masks, reverse=True)
    for mask in dp_masks:
        axis = 1 + left_bits.index(mask)
        left_bits.remove(mask)
        bit = (here_dp // mask) % 2
        away_part = lax.dynamic_index_in_dim(total, 1 - bit, axis, keepdims=False)
        stay_part = lax.dynamic_index_in_dim(total, bit, axis, keepdims=False)
        got = swap(away_part, mask, 0)
        if mask == PAIR:
            total = add(after(got, done_c, away_f), stay_part)
            done_d = finish(after(far_d, total), stay_d)
        else:
            total = add(got, stay_part)
        flat = flat + swap(flat, mask, 0)
        total, flat = lax.optimization_barrier((total, flat))
    done_e = finish(after(far_e, total), stay_e)
    done_f = finish(after(far_f, total), stay_f)
    for mask in reversed(group_masks):
        bit = (here_group // mask) % 2
        other_part = swap(total, 0, mask)
        total = jnp.concatenate([jnp.where(bit == 0, total, other_part), jnp.where(bit == 0, other_part, total)], axis=1)
        flat = flat + swap(flat, 0, mask)
        total, flat = lax.optimization_barrier((total, flat))
    other_part = swap(total, 0, 1)
    flat = flat + swap(flat, 0, 1)
    total = jnp.concatenate([jnp.where(core == 0, total, other_part), jnp.where(core == 0, other_part, total)], axis=2)
    weights_done = total.astype(f32)
    grad_qkv, grad_out_weight = weights_done[:3], weights_done[3]
    flat = flat.reshape(-1)
    starts = [sum(sizes[:place]) for place in range(len(sizes))]
    grad_gain_moe, grad_gain_attn, grad_router, grad_table, square_total = [
        flat[start : start + value.size].reshape(value.shape) for start, value in zip(starts, small)
    ]

    in_theirs = jnp.concatenate([swap(done_d, PAIR, 0), swap(done_e[:1], PAIR, 0)])
    out_mine, in_mine = done_c, jnp.concatenate([done_e[1:], done_f])

    def both_experts(mine, theirs):
        mine, theirs = [part.reshape(-1, part.shape[-1]).astype(f32) for part in (mine, theirs)]
        return jnp.stack([jnp.where(half == 0, mine, theirs), jnp.where(half == 0, theirs, mine)])

    grad_w_out = both_experts(out_mine, out_theirs)
    grad_w_in = both_experts(in_mine, in_theirs)

    distill_loss = square_total / (width * valid_count)
    return (
        output.astype(bf16),
        distill_loss,
        grad_input,
        grad_qkv,
        grad_out_weight,
        grad_w_in,
        grad_w_out,
        grad_router,
        grad_table,
        grad_gain_attn,
        grad_gain_moe,
    )


def solution(mesh):
    rows = P(AXES, None)
    return jax.shard_map(
        on_device,
        mesh=mesh,
        in_specs=(
            rows,
            P(None, "dp", None),
            P("dp", None),
            P(),
            P(),
            P(),
            P(),
            P("expert", None, None),
            P("expert", None, None),
            rows,
            P(AXES),
            P(AXES),
            rows,
            rows,
        ),
        out_specs=(
            rows,
            P(),
            rows,
            P(None, "dp", None),
            P("dp", None),
            P("expert", "dp", None),
            P("expert", "dp", None),
            P(),
            P(),
            P(),
            P(),
        ),
        check_vma=False,
    )
```

```python
import math
import jax
import jax.numpy as jnp
from jax import lax
from jax.experimental import pallas as pl
from jax.experimental.pallas import tpu as pltpu
from jax.sharding import PartitionSpec as P

BLOCK = 128
THIRDS = 3
EPS = 1e-06
GELU_A = math.sqrt(2.0 / math.pi)
GELU_B = 0.044715
NT = (((1,), (1,)), ((), ()))
TN = (((0,), (0,)), ((), ()))
VMEM_BYTES = 56 * 1024 * 1024


def cost(micros):
    return pl.CostEstimate(flops=int(micros * 0.37e9), bytes_accessed=0, transcendentals=0)


def dot_f32(left, right, dims=(((1,), (0,)), ((), ()))):
    return lax.dot_general(left, right, dims, preferred_element_type=jnp.float32)


def assemble(rows, pieces):
    start = 0
    for piece in pieces:
        rows[pl.ds(start, piece.shape[0]), :] = piece[...]
        start += piece.shape[0]


def hand_out(total, outs):
    start = 0
    for out in outs:
        out[...] = total[pl.ds(start, out.shape[0]), :].astype(out.dtype)
        start += out.shape[0]


def whole(shape):
    return pl.BlockSpec(shape, lambda *step: (0,) * len(shape))


def expert_forward_kernel(pick, *refs, chunk, count):
    pieces, w_in, w_out = refs[:count], refs[count], refs[count + 1]
    hidden_t, slope, rows_t = refs[count + 2 : count + 5]
    outs, rows, total = refs[count + 5 : 2 * count + 5], refs[2 * count + 5], refs[2 * count + 6]
    step = pl.program_id(0)

    @pl.when(step == 0)
    def _():
        assemble(rows, pieces)
        total[...] = jnp.zeros_like(total)
        rows_t[...] = rows[...].T

    for start in range(0, rows.shape[0], chunk):
        part = pl.ds(start, chunk)
        pre = dot_f32(rows[part, :], w_in[0])
        square = pre * pre
        bend = jnp.tanh(pre * (GELU_A + (GELU_A * GELU_B) * square))
        half = 0.5 + 0.5 * bend
        act = (pre * half).astype(jnp.bfloat16)
        lift = pre * (0.5 * GELU_A + (1.5 * GELU_A * GELU_B) * square)
        slope[part, :] = (half + lift * (1.0 - bend * bend)).astype(jnp.bfloat16)
        hidden_t[:, part] = act.T
        total[part, :] += dot_f32(act, w_out[0])

    @pl.when(step == pl.num_programs(0) - 1)
    def _():
        hand_out(total, outs)


def expert_forward(pick, pieces, w_in, w_out, tile=768, chunk=320):
    many, width = sum(piece.shape[0] for piece in pieces), pieces[0].shape[1]
    inner = w_in.shape[2]
    bf16 = jnp.bfloat16
    return pl.pallas_call(
        lambda *refs: expert_forward_kernel(*refs, chunk=chunk, count=len(pieces)),
        grid_spec=pltpu.PrefetchScalarGridSpec(
            num_scalar_prefetch=1,
            grid=(inner // tile,),
            in_specs=[whole(piece.shape) for piece in pieces]
            + [
                pl.BlockSpec((1, width, tile), lambda f, pick: (pick[0], 0, f)),
                pl.BlockSpec((1, tile, width), lambda f, pick: (pick[0], f, 0)),
            ],
            out_specs=[
                pl.BlockSpec((tile, many), lambda f, pick: (f, 0)),
                pl.BlockSpec((many, tile), lambda f, pick: (0, f)),
                whole((width, many)),
            ]
            + [whole(piece.shape) for piece in pieces],
            scratch_shapes=[pltpu.VMEM((many, width), bf16), pltpu.VMEM((many, width), jnp.float32)],
        ),
        out_shape=[
            jax.ShapeDtypeStruct((inner, many), bf16),
            jax.ShapeDtypeStruct((many, inner), bf16),
            jax.ShapeDtypeStruct((width, many), bf16),
        ]
        + [jax.ShapeDtypeStruct(piece.shape, bf16) for piece in pieces],
        compiler_params=pltpu.CompilerParams(vmem_limit_bytes=VMEM_BYTES),
        cost_estimate=cost(13),
        name="expert_forward",
    )(pick, *pieces, w_in, w_out)


def expert_backward_kernel(pick, *refs, chunk, count):
    pieces, w_in, w_out, slope = refs[:count], refs[count], refs[count + 1], refs[count + 2]
    grad_pre, rows = refs[count + 3 : count + 5]
    outs, total = refs[count + 5 : 2 * count + 5], refs[2 * count + 5]
    step = pl.program_id(0)

    @pl.when(step == 0)
    def _():
        assemble(rows, pieces)
        total[...] = jnp.zeros_like(total)

    for start in range(0, rows.shape[0], chunk):
        part = pl.ds(start, chunk)
        back = dot_f32(rows[part, :], w_out[0], NT) * slope[part, :].astype(jnp.float32)
        back = back.astype(jnp.bfloat16)
        grad_pre[part, :] = back
        total[part, :] += dot_f32(back, w_in[0], NT)

    @pl.when(step == pl.num_programs(0) - 1)
    def _():
        hand_out(total, outs)


def expert_backward(pick, pieces, w_in, w_out, slope, tile=768, chunk=640):
    many, width = sum(piece.shape[0] for piece in pieces), pieces[0].shape[1]
    inner = w_in.shape[2]
    bf16 = jnp.bfloat16
    return pl.pallas_call(
        lambda *refs: expert_backward_kernel(*refs, chunk=chunk, count=len(pieces)),
        grid_spec=pltpu.PrefetchScalarGridSpec(
            num_scalar_prefetch=1,
            grid=(inner // tile,),
            in_specs=[whole(piece.shape) for piece in pieces]
            + [
                pl.BlockSpec((1, width, tile), lambda f, pick: (pick[0], 0, f)),
                pl.BlockSpec((1, tile, width), lambda f, pick: (pick[0], f, 0)),
                pl.BlockSpec((many, tile), lambda f, pick: (0, f)),
            ],
            out_specs=[pl.BlockSpec((many, tile), lambda f, pick: (0, f)), whole((many, width))]
            + [whole(piece.shape) for piece in pieces],
            scratch_shapes=[pltpu.VMEM((many, width), jnp.float32)],
        ),
        out_shape=[jax.ShapeDtypeStruct((many, inner), bf16), jax.ShapeDtypeStruct((many, width), bf16)]
        + [jax.ShapeDtypeStruct(piece.shape, bf16) for piece in pieces],
        compiler_params=pltpu.CompilerParams(vmem_limit_bytes=VMEM_BYTES),
        cost_estimate=cost(11),
        name="expert_backward",
    )(pick, *pieces, w_in, w_out, slope)


def seen_blocks(row_block, blocks):
    return max(row_block + 1, blocks // 2)


def attention_forward_kernel(far, prefix, queries, keys, values, offsets, attended, probs, *, heads, blocks):
    pair = pl.program_id(0)
    lane = lax.broadcasted_iota(jnp.int32, (BLOCK, 2 * heads), 1)
    row = lax.broadcasted_iota(jnp.int32, (BLOCK, BLOCK), 0)
    col = lax.broadcasted_iota(jnp.int32, (BLOCK, BLOCK), 1)
    turned = []
    for head in range(2):
        line = jnp.broadcast_to(offsets[head : head + 1, :], (BLOCK, 4 * BLOCK))
        turned.append(pltpu.roll(line, 0, 1, stride=1, stride_axis=0))
    for row_block in range(blocks):
        rows = pl.ds(row_block * BLOCK, BLOCK)
        span = seen_blocks(row_block, blocks)
        seen = pl.ds(0, span * BLOCK)
        outs = []
        for head in range(2):
            mine = (lane < heads) if head == 0 else (lane >= heads)
            query = jnp.where(mine, queries[rows, :] * 0.125, 0.0).astype(jnp.bfloat16)
            score = dot_f32(query, keys[seen, :], NT)
            far_bias = far[pair * 2 + head]
            pieces = []
            for key_block in range(span):
                piece = score[:, key_block * BLOCK : (key_block + 1) * BLOCK]
                shift = key_block - row_block
                if shift < -1:
                    piece = piece + far_bias
                elif shift < 2:
                    piece = piece + turned[head][:, (2 + shift) * BLOCK : (3 + shift) * BLOCK]
                else:
                    raise ValueError(shift)
                if shift >= 0:
                    shown = col + key_block * BLOCK < prefix[0]
                    piece = jnp.where((shown | (col <= row)) if shift == 0 else shown, piece, -1e30)
                pieces.append(piece)
            peak = pieces[0]
            for piece in pieces[1:]:
                peak = jnp.maximum(peak, piece)
            peak = jnp.max(peak, axis=1, keepdims=True)
            pieces = [jnp.exp(piece - peak) for piece in pieces]
            mass = pieces[0]
            for piece in pieces[1:]:
                mass = mass + piece
            scale = 1.0 / jnp.sum(mass, axis=1, keepdims=True)
            weights = jnp.concatenate([(piece * scale).astype(jnp.bfloat16) for piece in pieces], axis=1)
            probs[head, rows, seen] = weights
            outs.append(dot_f32(weights, values[seen, :]))
        attended[rows, :] = jnp.where(lane < heads, outs[0], outs[1]).astype(jnp.bfloat16)


def attention_forward(far, prefix, qkv_rows, offsets):
    length, width = qkv_rows.shape[1:]
    pairs = width // 128
    blocks = length // BLOCK
    return pl.pallas_call(
        lambda *refs: attention_forward_kernel(*refs, heads=64, blocks=blocks),
        grid_spec=pltpu.PrefetchScalarGridSpec(
            num_scalar_prefetch=2,
            grid=(pairs,),
            in_specs=[pl.BlockSpec((None, length, 128), lambda h, far, prefix, c=c: (c, 0, h)) for c in range(3)]
            + [pl.BlockSpec((None, 2, 4 * BLOCK), lambda h, far, prefix: (h, 0, 0))],
            out_specs=[
                pl.BlockSpec((length, 128), lambda h, far, prefix: (0, h)),
                pl.BlockSpec((2, length, length), lambda h, far, prefix: (h, 0, 0)),
            ],
        ),
        out_shape=[
            jax.ShapeDtypeStruct((length, width), jnp.bfloat16),
            jax.ShapeDtypeStruct((2 * pairs, length, length), jnp.bfloat16),
        ],
        compiler_params=pltpu.CompilerParams(vmem_limit_bytes=VMEM_BYTES),
        cost_estimate=cost(17),
        name="attention_forward",
    )(far, prefix, qkv_rows, qkv_rows, qkv_rows, offsets.reshape(pairs, 2, 4 * BLOCK))


def attention_backward_kernel(queries, keys, values, grads, probs, grad_rows, bands, flow, *, heads, blocks):
    lane = lax.broadcasted_iota(jnp.int32, (BLOCK, 2 * heads), 1)
    query_t = (queries[...] * 0.125).astype(jnp.bfloat16).T
    grad_t = grads[...].T
    half = blocks // 2
    dk, dv = [], []
    dq = [[], []]
    for head in range(2):
        mine = (lane < heads) if head == 0 else (lane >= heads)
        sums = [None] * 4
        for row_block in range(blocks):
            rows = pl.ds(row_block * BLOCK, BLOCK)
            span = seen_blocks(row_block, blocks)
            seen = pl.ds(0, span * BLOCK)
            grad = jnp.where(mine, grads[rows, :], 0.0).astype(jnp.bfloat16)
            soft = probs[head, rows, seen].astype(jnp.float32)
            back = dot_f32(grad, values[seen, :], NT)
            inner = jnp.sum(soft * back, axis=1, keepdims=True)
            score_grad = (soft * (back - inner)).astype(jnp.bfloat16)
            flow[rows, seen] = score_grad
            dq[head].append(dot_f32(score_grad, keys[seen, :]) * 0.125)
            for key_block in range(span):
                band = max(key_block - row_block, -2)
                if band > 1:
                    continue
                tile = score_grad[:, key_block * BLOCK : (key_block + 1) * BLOCK].astype(jnp.float32)
                sums[band + 2] = tile if sums[band + 2] is None else sums[band + 2] + tile
        for band in range(4):
            bands[head, band] = sums[band]
        part = slice(head * heads, (head + 1) * heads)
        key_pieces, value_pieces = [], []
        for key_block in range(blocks):
            first = 0 if key_block < half else key_block
            rows = pl.ds(first * BLOCK, (blocks - first) * BLOCK)
            cols = pl.ds(key_block * BLOCK, BLOCK)
            key_pieces.append(dot_f32(query_t[part, first * BLOCK :], flow[rows, cols]))
            value_pieces.append(dot_f32(grad_t[part, first * BLOCK :], probs[head, rows, cols]))
        dk.append(jnp.concatenate(key_pieces, axis=1))
        dv.append(jnp.concatenate(value_pieces, axis=1))
    for row_block in range(blocks):
        rows = pl.ds(row_block * BLOCK, BLOCK)
        grad_rows[0, rows, :] = jnp.where(lane < heads, dq[0][row_block], dq[1][row_block]).astype(jnp.bfloat16)
    grad_rows[1] = jnp.concatenate(dk, axis=0).T.astype(jnp.bfloat16)
    grad_rows[2] = jnp.concatenate(dv, axis=0).T.astype(jnp.bfloat16)


def attention_backward(qkv_rows, grads, probs):
    length, width = grads.shape
    pairs = width // 128
    blocks = length // BLOCK
    block = pl.BlockSpec((length, 128), lambda h: (0, h))
    of_three = [pl.BlockSpec((None, length, 128), lambda h, c=c: (c, 0, h)) for c in range(3)]
    return pl.pallas_call(
        lambda *refs: attention_backward_kernel(*refs, heads=64, blocks=blocks),
        grid=(pairs,),
        in_specs=[*of_three, block, pl.BlockSpec((2, length, length), lambda h: (h, 0, 0))],
        out_specs=[pl.BlockSpec((3, length, 128), lambda h: (0, 0, h)), pl.BlockSpec((2, 4, BLOCK, BLOCK), lambda h: (h, 0, 0, 0))],
        out_shape=[jax.ShapeDtypeStruct((3, length, width), jnp.bfloat16)]
        + [jax.ShapeDtypeStruct((2 * pairs, 4, BLOCK, BLOCK), jnp.float32)],
        scratch_shapes=[pltpu.VMEM((length, length), jnp.bfloat16)],
        compiler_params=pltpu.CompilerParams(vmem_limit_bytes=VMEM_BYTES),
        cost_estimate=cost(17),
        name="attention_backward",
    )(qkv_rows, qkv_rows, qkv_rows, grads, probs)


def pieces_left(lefts, plans, many):
    part = lefts[0][0].shape[0] // THIRDS
    return jnp.concatenate(
        [
            jnp.concatenate([ref[pl.ds(third * part, part), :] for ref in lefts[group * many + k]], axis=1)
            for plan in plans
            for group, third in plan
            for k in range(many)
        ]
    )


def put_pieces(result, outs):
    place = 0
    for out in outs:
        many, pieces, part = out.shape[:3]
        for piece in range(pieces):
            for k in range(many):
                out[k, piece] = result[place : place + part]
                place += part


def weight_part_kernel(picks, *refs, count, plans, many):
    lefts, rights, outs = refs[: 2 * count], refs[2 * count : 2 * count + 2], refs[2 * count + 2 :]
    left = pieces_left(list(zip(lefts[:count], lefts[count:])), plans, many)
    right = jnp.concatenate([ref[...] for ref in rights], axis=0)
    put_pieces(dot_f32(left, right).astype(jnp.bfloat16), outs)


def weight_part_plain(picks, lefts, rights, rows, plans, many):
    left, right = jnp.concatenate(lefts, axis=1), jnp.concatenate(rights, axis=0)
    depth, width = right.shape
    part = rows // THIRDS
    result = jnp.take(left.reshape(-1, rows, depth), picks, axis=0)
    result = jnp.einsum("srd,dw->srw", result, right, preferred_element_type=jnp.float32).astype(jnp.bfloat16)
    result = result.reshape(-1, many, THIRDS, part, width)
    return [jnp.stack([result[group, :, third] for group, third in plan], axis=1) for plan in plans]


def weight_part(picks, lefts, rights, rows, plans, many, tile):
    depth, width = rights[0].shape
    count, part = picks.shape[0], rows // THIRDS
    if part % 16:
        return weight_part_plain(picks, lefts, rights, rows, plans, many)
    return pl.pallas_call(
        lambda *refs: weight_part_kernel(*refs, count=count, plans=plans, many=many),
        grid_spec=pltpu.PrefetchScalarGridSpec(
            num_scalar_prefetch=1,
            grid=(width // tile,),
            in_specs=[pl.BlockSpec((rows, depth), lambda i, picks, k=k: (picks[k], 0)) for k in range(count)] * 2
            + [pl.BlockSpec((depth, tile), lambda i, picks: (0, i))] * 2,
            out_specs=[pl.BlockSpec((many, len(plan), part, tile), lambda i, picks: (0, 0, 0, i)) for plan in plans],
        ),
        out_shape=[jax.ShapeDtypeStruct((many, len(plan), part, width), jnp.bfloat16) for plan in plans],
        compiler_params=pltpu.CompilerParams(vmem_limit_bytes=VMEM_BYTES),
        cost_estimate=cost(4),
        name="weight_part",
    )(picks, *([lefts[0]] * count), *([lefts[1]] * count), *rights)


def hot_columns(slots, first, count):
    rows = first + lax.broadcasted_iota(jnp.int32, (count, slots.shape[1]), 0)
    return (rows == slots).astype(jnp.bfloat16)


def halves(core, mine, other):
    return jnp.where(core == 0, mine, other), jnp.where(core == 0, other, mine)


def join_kernel(places, *refs):
    pieces, out = refs[:-1], refs[-1]
    rows = pieces[0].shape[1]
    count = pieces[0].shape[0]
    for chunk in range(out.shape[0] // count):
        for step in range(len(pieces) * count // out.shape[0]):
            piece = pieces[chunk * (len(pieces) * count // out.shape[0]) + step]
            start = pl.multiple_of(places[step] * rows, rows)
            out[pl.ds(chunk * count, count), pl.ds(start, rows), :] = piece[...]


def join(places, chunks):
    count, rows, columns = chunks[0][0].shape
    steps = len(chunks[0])
    return pl.pallas_call(
        join_kernel,
        in_specs=[pl.BlockSpec(memory_space=pltpu.SMEM)] + [pl.BlockSpec(memory_space=pltpu.VMEM)] * (steps * len(chunks)),
        out_shape=jax.ShapeDtypeStruct((count * len(chunks), steps * rows, columns), jnp.bfloat16),
        compiler_params=pltpu.CompilerParams(vmem_limit_bytes=VMEM_BYTES),
        cost_estimate=cost(3),
        name="join",
    )(places, *[piece for chunk in chunks for piece in chunk])


def project_kernel(core, rows, mine, other, result):
    half = mine.shape[1]
    first, second = halves(core[0], mine[...], other[...])
    result[:, :half] = dot_f32(rows[...], first).astype(jnp.bfloat16)
    result[:, half:] = dot_f32(rows[...], second).astype(jnp.bfloat16)


def project(core, rows, mine, other, used):
    width, half = mine.shape[1:]
    length = rows.shape[0]
    return pl.pallas_call(
        project_kernel,
        grid_spec=pltpu.PrefetchScalarGridSpec(
            num_scalar_prefetch=1,
            grid=(used,),
            in_specs=[
                whole((length, width)),
                pl.BlockSpec((None, width, half), lambda i, core: (i, 0, 0)),
                pl.BlockSpec((None, width, half), lambda i, core: (i, 0, 0)),
            ],
            out_specs=pl.BlockSpec((None, length, 2 * half), lambda i, core: (i, 0, 0)),
        ),
        out_shape=jax.ShapeDtypeStruct((used, length, 2 * half), jnp.bfloat16),
        compiler_params=pltpu.CompilerParams(vmem_limit_bytes=VMEM_BYTES),
        cost_estimate=cost(4),
        name="project",
    )(core, rows, mine, other)


def route_kernel(core, attended, tokens, mine, other, gain, router, routes, slots, middle, normed, gates, *outs):
    f32 = jnp.float32
    first, second = halves(core[0], mine[...], other[...])
    rows = attended[...]
    moved = jnp.concatenate([dot_f32(rows, first), dot_f32(rows, second)], axis=1)
    value = tokens[...].astype(f32) + moved
    middle[...] = value
    low = (value * lax.rsqrt(jnp.mean(value * value, axis=1, keepdims=True) + EPS) * gain[...]).astype(jnp.bfloat16)
    normed[...] = low
    start = 0
    for first_out, second_out in zip(outs[::2], outs[1::2]):
        size = first_out.shape[0]
        hot = hot_columns(slots[0:1, :], start, 2 * size) + hot_columns(slots[1:2, :], start, 2 * size)
        part = dot_f32(hot, low).astype(jnp.bfloat16)
        first_out[...] = part[:size]
        second_out[...] = part[size:]
        start += 2 * size
    logits = dot_f32(low, router[...])
    soft = jnp.exp(logits - jnp.max(logits, axis=1, keepdims=True))
    soft = soft / jnp.sum(soft, axis=1, keepdims=True)
    expert = lax.broadcasted_iota(jnp.int32, soft.shape, 1)
    chosen = [jnp.sum(jnp.where(expert == routes[:, k : k + 1], soft, 0.0), axis=1, keepdims=True) for k in range(2)]
    for k in range(2):
        gates[:, k : k + 1] = chosen[k] / (chosen[0] + chosen[1])


def route(core, attended, tokens, mine, other, gain, router, routes, slots, pieces, count):
    length, width = tokens.shape
    last, half = mine.shape[0] - 1, mine.shape[2]
    f32, bf16 = jnp.float32, jnp.bfloat16
    weight = pl.BlockSpec((None, width, half), lambda i, core: (last, 0, 0))
    shapes = [((length, width), f32), ((length, width), bf16), ((length, 2), f32)] + [((count, width), bf16)] * pieces
    return pl.pallas_call(
        route_kernel,
        grid_spec=pltpu.PrefetchScalarGridSpec(
            num_scalar_prefetch=1,
            grid=(1,),
            in_specs=[whole((length, width)), whole((length, width)), weight, weight, whole((1, width)), whole(router.shape), whole(routes.shape), whole(slots.shape)],
            out_specs=[whole(shape) for shape, _ in shapes],
        ),
        out_shape=[jax.ShapeDtypeStruct(shape, kind) for shape, kind in shapes],
        compiler_params=pltpu.CompilerParams(vmem_limit_bytes=VMEM_BYTES),
        cost_estimate=cost(6),
        name="route",
    )(core, attended, tokens, mine, other, gain.reshape(1, -1), router, routes, slots)


def hot_route(slots, k, count):
    cols = lax.broadcasted_iota(jnp.int32, (slots.shape[0], count), 1)
    return cols == slots[:, k : k + 1]


def combine_kernel(*refs, count):
    slots, slots_t, scale = refs[:3]
    pieces = refs[3 : 3 + count]
    middle, teacher, cotangent, valid, gates, routes = refs[3 + count : 9 + count]
    output, grad_y, grad_logits, square = refs[9 + count : 13 + count]
    sends, rows = refs[13 + count : 13 + 2 * count], refs[13 + 2 * count]
    f32, bf16 = jnp.float32, jnp.bfloat16
    assemble(rows, pieces)
    table = rows[...]
    picked = [dot_f32(hot_route(slots, k, rows.shape[0]).astype(bf16), table) for k in range(2)]
    result = middle[...] + (gates[:, 0:1] * picked[0] + gates[:, 1:2] * picked[1])
    output[...] = result.astype(bf16)
    misfit = valid[...] * (result - teacher[...].astype(f32))
    square[...] = jnp.sum((misfit * misfit).reshape(-1, 8, misfit.shape[1]), axis=0)
    grad = cotangent[...].astype(f32) + misfit * scale[0, 0]
    grad_y[...] = grad
    steep = [jnp.sum(grad * picked[k], axis=1, keepdims=True) for k in range(2)]
    slack = gates[:, 0:1] * steep[0] + gates[:, 1:2] * steep[1]
    expert = lax.broadcasted_iota(jnp.int32, grad_logits.shape, 1)
    turn = [jnp.where(expert == routes[:, k : k + 1], gates[:, k : k + 1] * (steep[k] - slack), 0.0) for k in range(2)]
    grad_logits[...] = (turn[0] + turn[1]).astype(bf16)
    scaled = [(gates[:, k : k + 1] * grad).astype(bf16) for k in range(2)]
    start = 0
    for first, second in zip(sends[::2], sends[1::2]):
        size = first.shape[0]
        part = [dot_f32(hot_columns(slots_t[k : k + 1, :], start, 2 * size), scaled[k]) for k in range(2)]
        part = (part[0] + part[1]).astype(bf16)
        first[...] = part[:size]
        second[...] = part[size:]
        start += 2 * size


def combine(slots, slots_t, scale, pieces, middle, teacher, cotangent, valid, gates, routes, experts):
    length, width = middle.shape
    count = len(pieces)
    f32, bf16 = jnp.float32, jnp.bfloat16
    return pl.pallas_call(
        lambda *refs: combine_kernel(*refs, count=count),
        in_specs=[pl.BlockSpec(memory_space=pltpu.VMEM)] * 2
        + [pl.BlockSpec(memory_space=pltpu.SMEM)]
        + [pl.BlockSpec(memory_space=pltpu.VMEM)] * (6 + count),
        out_shape=[
            jax.ShapeDtypeStruct((length, width), bf16),
            jax.ShapeDtypeStruct((length, width), f32),
            jax.ShapeDtypeStruct((length, experts), bf16),
            jax.ShapeDtypeStruct((8, width), f32),
        ]
        + [jax.ShapeDtypeStruct(piece.shape, bf16) for piece in pieces],
        scratch_shapes=[pltpu.VMEM((sum(piece.shape[0] for piece in pieces), width), bf16)],
        compiler_params=pltpu.CompilerParams(vmem_limit_bytes=VMEM_BYTES),
        cost_estimate=cost(8),
        name="combine",
    )(slots, slots_t, scale, *pieces, middle, teacher, cotangent, valid, gates, routes)


def norm_back(value, gain, grad):
    root = lax.rsqrt(jnp.mean(value * value, axis=1, keepdims=True) + EPS)
    normed = value * root
    scaled = grad * gain
    inner = jnp.mean(scaled * normed, axis=1, keepdims=True)
    return root * (scaled - normed * inner), jnp.sum((grad * normed).reshape(-1, 8, value.shape[1]), axis=0)


def collect_kernel(core, *refs, count):
    slots, pieces = refs[0], refs[1 : 1 + count]
    middle, gain, grad_logits, router, grad_y, mine, other = refs[1 + count : 8 + count]
    grad_middle, rounded, grad_attended, grad_gain, rows = refs[8 + count :]
    assemble(rows, pieces)
    hot = (hot_route(slots, 0, rows.shape[0]) | hot_route(slots, 1, rows.shape[0])).astype(jnp.bfloat16)
    grad = dot_f32(grad_logits[...], router[...], NT) + dot_f32(hot, rows[...])
    turned, grad_gain[...] = norm_back(middle[...], gain[...], grad)
    result = grad_y[...] + turned
    grad_middle[...] = result
    low = result.astype(jnp.bfloat16)
    rounded[...] = low
    first, second = halves(core[0], mine[...], other[...])
    half = first.shape[1]
    grad_attended[...] = (dot_f32(low[:, :half], first, NT) + dot_f32(low[:, half:], second, NT)).astype(jnp.bfloat16)


def collect(core, slots, pieces, middle, gain, grad_logits, router, grad_y, mine, other):
    length, width = middle.shape
    last, half = mine.shape[0] - 1, mine.shape[2]
    f32, bf16 = jnp.float32, jnp.bfloat16
    weight = pl.BlockSpec((None, width, half), lambda i, core: (last, 0, 0))
    plain = [slots, *pieces, middle, gain.reshape(1, -1), grad_logits, router, grad_y]
    shapes = [((length, width), f32), ((length, width), bf16), ((length, width), bf16), ((8, width), f32)]
    return pl.pallas_call(
        lambda *refs: collect_kernel(*refs, count=len(pieces)),
        grid_spec=pltpu.PrefetchScalarGridSpec(
            num_scalar_prefetch=1,
            grid=(1,),
            in_specs=[whole(array.shape) for array in plain] + [weight, weight],
            out_specs=[whole(shape) for shape, _ in shapes],
            scratch_shapes=[pltpu.VMEM((sum(piece.shape[0] for piece in pieces), width), bf16)],
        ),
        out_shape=[jax.ShapeDtypeStruct(shape, kind) for shape, kind in shapes],
        compiler_params=pltpu.CompilerParams(vmem_limit_bytes=VMEM_BYTES),
        cost_estimate=cost(8),
        name="collect",
    )(core, *plain, mine, other)


def outer_halves_kernel(core, normed, attended, rights, last, *refs, count):
    aways, stays, normed_t, attended_t = refs[:2], refs[2:4], refs[4], refs[5]
    step = pl.program_id(0)

    @pl.when(step == 0)
    def _():
        normed_t[...] = normed[...].T
        attended_t[...] = attended[...].T

    for place in range(count + 1):

        @pl.when(step == place)
        def _():
            result = dot_f32(normed_t[...], rights[...]) if place < count else dot_f32(attended_t[...], last[...])
            result = result.astype(jnp.bfloat16)
            half = result.shape[1] // 2
            away, stay = aways[place // 2], stays[place // 2]
            slot = place % 2

            @pl.when(core[0] == 0)
            def _():
                stay[slot] = result[:, :half]
                away[slot] = result[:, half:]

            @pl.when(core[0] != 0)
            def _():
                away[slot] = result[:, :half]
                stay[slot] = result[:, half:]


def outer_halves(core, normed, attended, rights, last):
    length, width = normed.shape
    count, half = rights.shape[0], width // 2
    shape = jax.ShapeDtypeStruct((2, width, half), jnp.bfloat16)
    return pl.pallas_call(
        lambda *refs: outer_halves_kernel(*refs, count=count),
        grid_spec=pltpu.PrefetchScalarGridSpec(
            num_scalar_prefetch=1,
            grid=(count + 1,),
            in_specs=[
                whole((length, width)),
                whole((length, width)),
                pl.BlockSpec((None, length, width), lambda i, core: (jnp.minimum(i, count - 1), 0, 0)),
                whole((length, width)),
            ],
            out_specs=[whole(shape.shape)] * 4,
            scratch_shapes=[pltpu.VMEM((width, length), jnp.bfloat16)] * 2,
        ),
        out_shape=[shape] * 4,
        compiler_params=pltpu.CompilerParams(vmem_limit_bytes=VMEM_BYTES),
        cost_estimate=cost(6),
        name="outer_halves",
    )(core, normed, attended, rights, last)


def enter_kernel(core, grads, mine, other, tokens, gain, grad_middle, grad_input, grad_gain, total):
    step = pl.program_id(0)
    first, second = halves(core[0], mine[...], other[...])
    half = first.shape[1]
    rows = grads[...]
    part = dot_f32(rows[:, :half], first, NT) + dot_f32(rows[:, half:], second, NT)

    @pl.when(step == 0)
    def _():
        total[...] = part

    @pl.when(step > 0)
    def _():
        total[...] += part

    @pl.when(step == pl.num_programs(0) - 1)
    def _():
        turned, grad_gain[...] = norm_back(tokens[...].astype(jnp.float32), gain[...], total[...])
        grad_input[...] = grad_middle[...] + turned


def enter(core, grads, mine, other, tokens, gain, grad_middle):
    length, width = tokens.shape
    count, half = grads.shape[0], mine.shape[2]
    weight = pl.BlockSpec((None, width, half), lambda i, core: (i, 0, 0))
    return pl.pallas_call(
        enter_kernel,
        grid_spec=pltpu.PrefetchScalarGridSpec(
            num_scalar_prefetch=1,
            grid=(count,),
            in_specs=[pl.BlockSpec((None, length, width), lambda i, core: (i, 0, 0)), weight, weight, whole((length, width)), whole((1, width)), whole((length, width))],
            out_specs=[whole((length, width)), whole((8, width))],
            scratch_shapes=[pltpu.VMEM((length, width), jnp.float32)],
        ),
        out_shape=[jax.ShapeDtypeStruct((length, width), jnp.float32), jax.ShapeDtypeStruct((8, width), jnp.float32)],
        compiler_params=pltpu.CompilerParams(vmem_limit_bytes=VMEM_BYTES),
        cost_estimate=cost(6),
        name="enter",
    )(core, grads, mine, other, tokens, gain.reshape(1, -1), grad_middle)


BOUNDS = (12, 16, 23, 32, 46, 64, 91)
TOP_PRECISION = lax.Precision.HIGHEST
AXES = ("dp", "expert")
PAIR = 2


def after(value, *others):
    return lax.optimization_barrier((value, *others))[0] if others else value


def bucket_index(offset):
    distance = jnp.abs(offset)
    far_bucket = 8 + sum([(distance >= level).astype(jnp.int32) for level in BOUNDS])
    near_bucket = jnp.where(distance < 8, distance, far_bucket)
    return jnp.where(offset > 0, 16, 0) + near_bucket


def norm_apply(inputs, gain_vec):
    return inputs * lax.rsqrt(jnp.mean(inputs * inputs, axis=-1, keepdims=True) + EPS) * gain_vec


def tile_offsets(query_block, key_block):
    rows = query_block * BLOCK + lax.broadcasted_iota(jnp.int32, (BLOCK, BLOCK), 0)
    cols = key_block * BLOCK + lax.broadcasted_iota(jnp.int32, (BLOCK, BLOCK), 1)
    return rows, cols


def offset_bias(table):
    offsets = jnp.arange(4 * BLOCK, dtype=jnp.int32) - 2 * BLOCK
    hot = (bucket_index(offsets)[None] == jnp.arange(table.shape[1], dtype=jnp.int32)[:, None]).astype(jnp.float32)
    return jnp.dot(table, hot, precision=TOP_PRECISION)


def table_gradient(bands, buckets):
    rows, cols = tile_offsets(0, 0)
    ids = [jnp.full((BLOCK, BLOCK), bucket_far(), jnp.int32)]
    ids += [bucket_index(shift * BLOCK + cols - rows) for shift in (-1, 0, 1)]
    hot = (jnp.stack(ids)[..., None] == jnp.arange(buckets, dtype=jnp.int32)).astype(jnp.float32)
    return jnp.einsum("hdxy,dxyb->hb", bands, hot, precision=TOP_PRECISION)


def bucket_far():
    return 8 + len(BOUNDS)


def on_device(
    tokens,
    qkv_weight,
    out_weight,
    position_bias_table,
    gain_attn,
    gain_moe,
    router,
    w_in,
    w_out,
    routes,
    prefix,
    valid_mask,
    teacher,
    cotangent,
):
    length, width = tokens.shape
    bf16, f32 = jnp.bfloat16, jnp.float32
    expert_count = router.shape[1]
    top_count = routes.shape[1]
    groups = lax.axis_size("expert")
    copies = lax.axis_size("dp")
    inner = w_in.shape[2]
    capacity = 5 * length * top_count // (4 * expert_count)
    total_tokens = length * copies * groups
    sources = 2 * groups
    blocks = length // BLOCK
    here_dp, here_group = lax.axis_index("dp"), lax.axis_index("expert")
    half = (here_dp >> 1) & 1
    core = here_group & 1
    rest = copies // 4

    def swap(value, dp_mask, group_mask):
        pairs = [
            (i, ((i // groups) ^ dp_mask) * groups + ((i % groups) ^ group_mask))
            for i in range(copies * groups)
        ]
        return lax.ppermute(value, AXES, pairs)

    def bits(count):
        return [1 << place for place in range(count.bit_length() - 1)]

    def partial_sums(value):
        sums = []
        for masks in [(0, mask) for mask in bits(groups)] + [(mask, 0) for mask in bits(copies)]:
            value = value + swap(value, *masks)
            sums.append(value)
        return sums

    chips = groups

    def across(value, place):
        return swap(value, PAIR * (place // (groups // 2)), 2 * (place % (groups // 2)))

    def to_chips(pieces):
        return [pieces[0]] + [across(pieces[place], place) for place in range(1, chips)]

    def through(visit, sends):
        direct, relay = to_chips(sends[::2]), to_chips(sends[1::2])
        seen, direct = visit(direct)
        direct = to_chips(direct)
        relay = [after(part, seen) for part in relay]
        passed = visit(swap(jnp.concatenate(relay), 0, 1))
        passed = swap(after(passed, *direct), 0, 1)
        relay = [passed[place * capacity : (place + 1) * capacity] for place in range(chips)]
        return direct, relay

    def weave(direct, relay):
        return [part for pair in zip(direct, to_chips(relay)) for part in pair]

    ring = list(range(0, copies, 2)) + list(range(copies - 1, 0, -2))
    turns = [(1, step) for step in range(1, copies // 2 + 1)] + [(-1, step) for step in range(1, copies // 2)]

    def gather_ring(shard, due):
        got = [shard]
        for turn in (1, -1):
            held = shard
            pairs = [(ring[i], ring[(i + turn) % copies]) for i in range(copies)]
            for step in [step for way, step in turns if way == turn]:
                held = lax.ppermute(after(held, *due[step - 2 : step - 1]) if step > 1 else held, "dp", pairs)
                got.append(held)
        return got

    def ring_places():
        place = jnp.where(here_dp & 1 == 0, here_dp >> 1, copies - 1 - (here_dp >> 1))
        shift = jnp.array([0] + [turn * step for turn, step in turns], jnp.int32)
        place = (place - shift) & (copies - 1)
        return jnp.where(place < copies // 2, 2 * place, 2 * (copies - 1 - place) + 1).astype(jnp.int32)


    flat_routes = routes.reshape(-1)
    pair_count = length * top_count
    slot_count = sources * capacity
    route_hits = (flat_routes[:, None] == jnp.arange(expert_count, dtype=jnp.int32)[None, :]).astype(bf16)
    lower_ones = (
        lax.broadcasted_iota(jnp.int32, (pair_count, pair_count), 0)
        >= lax.broadcasted_iota(jnp.int32, (pair_count, pair_count), 1)
    ).astype(bf16)
    running = jnp.dot(lower_ones, route_hits, preferred_element_type=f32)
    pair_rank = jnp.sum((running - 1.0) * route_hits.astype(f32), axis=1).astype(jnp.int32)
    away = (flat_routes >> 1) ^ here_group
    chip = ((flat_routes & 1) ^ half) * (groups // 2) + (away >> 1)
    slots = ((chip * 2 + (away & 1)) * capacity + pair_rank).reshape(length, top_count)
    slots_t = slots.T

    resid = tokens.astype(f32)
    normed1 = norm_apply(resid, gain_attn).astype(bf16)
    columns = width // 2
    core_index = core.reshape(1).astype(jnp.int32)
    valid_rows = valid_mask.astype(f32)[:, None]
    counts = partial_sums(jnp.broadcast_to(jnp.sum(valid_rows), (8, 128)))
    valid_count = counts[-1][0, 0]
    shards = [
        lax.dynamic_slice_in_dim(part, core * columns, columns, 2)
        for part in (qkv_weight[:2], jnp.concatenate([qkv_weight[2:], out_weight[None]]))
    ]
    if copies > 8:
        mine = lax.all_gather(jnp.concatenate(shards), "dp", axis=1, tiled=True)
    else:
        mine = join(ring_places(), [gather_ring(shards[0], counts[:3]), gather_ring(shards[1], (slots_t, normed1, counts[3]))])
    other = swap(mine, 0, 1)
    qkv_rows = project(core_index, normed1, mine, other, 3)
    offsets = after(offset_bias(position_bias_table), valid_count)
    attended, probs = attention_forward(position_bias_table[:, bucket_far()], prefix, qkv_rows, offsets)
    middle, normed2, gates, *sends = route(
        core_index, attended, tokens, mine, other, gain_moe, router, routes, slots_t, 2 * chips, capacity
    )

    pick = half.reshape(1).astype(jnp.int32)
    hidden, slopes, rows_in = [], [], []

    def expert(pieces):
        one = not isinstance(pieces, list)
        hidden_t, slope, rows_t, *results = expert_forward(pick, [pieces] if one else pieces, w_in, w_out)
        for kept, value in zip((hidden, slopes, rows_in), (hidden_t, slope, rows_t)):
            kept.append(value)
        return results[0] if one else (hidden_t, results)

    back = weave(*through(expert, sends))
    scale = (total_tokens / valid_count).reshape(1, 1)
    output, grad_y, grad_logits, squares, *sends = combine(
        slots, slots_t, scale, back, middle, teacher, cotangent, valid_rows, gates, routes, expert_count
    )
    grad_router = jnp.einsum("td,te->de", normed2, grad_logits, preferred_element_type=f32)

    out_rows = inner // copies
    in_rows = width // copies
    far_bit = here_dp % 2
    slices = jnp.arange(rest, dtype=jnp.int32) * 4

    def picks(bit0):
        return jnp.concatenate([slices + ((half ^ other_half) * 2 + bit0) for other_half in (1, 0)]).astype(jnp.int32)

    sent, kept = picks(1 - far_bit), picks(far_bit)

    def add(left, right):
        return (left.astype(f32) + right.astype(f32)).astype(bf16)

    def fold(unit, bit, axis=0):
        unit = unit.reshape(unit.shape[:axis] + (2, unit.shape[axis] // 2) + unit.shape[axis + 1 :])
        away_part = lax.dynamic_index_in_dim(unit, 1 - bit, axis, keepdims=False)
        return away_part, lax.dynamic_index_in_dim(unit, bit, axis, keepdims=False)

    far_masks = list(reversed(bits(copies)[2:]))

    def near_add(got, keep):
        away_part, stay_part = fold(add(got, keep), (here_dp // far_masks[0]) % 2)
        return away_part, stay_part

    def far_trade(away_part):
        return swap(away_part, far_masks[0], 0)

    def finish(got, stay):
        unit = add(got, stay)
        for mask in far_masks[1:]:
            away_part, stay_part = fold(unit, (here_dp // mask) % 2)
            unit = add(swap(away_part, mask, 0), stay_part)
        return unit[0]

    plan_a, plan_b, plan_c = ((0, 0),), ((0, 1), (0, 2)), ((1, 0), (1, 1), (1, 2))
    plan_d, plan_e, plan_f = ((0, 0), (0, 1)), ((0, 2), (1, 0), (1, 1)), ((1, 2),)
    out_plans, in_plans = (plan_a, plan_b, plan_c), (plan_d, plan_e, plan_f)

    grad_rows, grad_pre, parts = [], [], []

    def expert_back(pieces):
        if isinstance(pieces, list):
            grad_pre_rows, grads, *results = expert_backward(pick, pieces, w_in, w_out, slopes[0])
            grad_rows.append(grads)
            grad_pre.append(grad_pre_rows)
            return grad_pre_rows, results
        grad_rows.append(pieces)
        parts.extend(weight_part(sent, hidden, grad_rows, out_rows, out_plans, rest, width))
        parts[0] = swap(parts[0], 1, 0)
        pieces = after(pieces, parts[1])
        grad_pre_rows, _, results = expert_backward(pick, [pieces], w_in, w_out, slopes[1])
        grad_pre.append(grad_pre_rows)
        return after(results, parts[0])

    direct, relay = through(expert_back, sends)
    got_a, send_b, send_c = parts
    got_b = swap(after(send_b, relay[0]), 1, 0)
    back = weave(direct, relay)
    grad_rows, grad_pre = lax.optimization_barrier((grad_rows, grad_pre, relay))[:2]
    keep_a, keep_b, keep_c = weight_part(kept, hidden, grad_rows, out_rows, out_plans, rest, width)
    away_a, stay_a = near_add(got_a, keep_a)
    far_a = far_trade(away_a)
    grad_pre = after(grad_pre, away_a)
    send_d, send_e, send_f = weight_part(sent, rows_in, grad_pre, in_rows, in_plans, rest, inner // 2)
    back = [after(part, send_d) for part in back]
    got_c = swap(after(send_c, *back), 1, 0)
    grad_middle, grad_attn_proj, grad_attended, gain_moe_parts = collect(
        core_index, slots, back, middle, gain_moe, grad_logits, router, grad_y, mine, other
    )
    away_b, stay_b = near_add(after(got_b, grad_attended), keep_b)
    grad_attended, away_b, far_a = lax.optimization_barrier((grad_attended, away_b, far_a))
    far_b = far_trade(away_b)
    done_a = finish(far_a, stay_a)
    grad_qkv_rows, bands = attention_backward(qkv_rows, grad_attended, probs)
    grad_qkv_rows, got_c = lax.optimization_barrier((grad_qkv_rows, got_c))

    away_c, stay_c = near_add(got_c, keep_c)
    far_c = far_trade(away_c)
    got_d = swap(after(send_d, away_c), 1, 0)
    *weights_away, stay_1, stay_2 = outer_halves(
        core_index, normed1, attended, after(grad_qkv_rows, far_b, away_c), grad_attn_proj
    )
    done_b = finish(far_b, stay_b)
    keep_d, keep_e, keep_f = weight_part(
        kept, rows_in, after(grad_pre, *weights_away), in_rows, in_plans, rest, inner // 2
    )
    group_masks = bits(groups)[1:]
    dp_masks = sorted(bits(copies), key=lambda mask: (mask != PAIR, mask))

    def over_groups(got, stay, *due):
        got = add(after(got, *due), stay).reshape(2, copies, in_rows, columns)
        for mask in group_masks[:-1]:
            away_part, stay_part = fold(got, (here_group // mask) % 2, 2)
            got = add(swap(away_part, 0, mask), stay_part)
        away_part, stay_part = fold(got, (here_group // group_masks[-1]) % 2, 2)
        return swap(away_part, 0, group_masks[-1]), stay_part

    def over_dp(total, mask, passed):
        axis = 1 + sorted([other for other in dp_masks if other not in passed], reverse=True).index(mask)
        bit = (here_dp // mask) % 2
        away_part = lax.dynamic_index_in_dim(total, 1 - bit, axis, keepdims=False)
        stay_part = lax.dynamic_index_in_dim(total, bit, axis, keepdims=False)
        return swap(away_part, mask, 0), stay_part

    weights_got = [swap(part, 0, 1) for part in weights_away]
    first = over_groups(weights_got[0], stay_1, keep_d)
    second = over_groups(weights_got[1], stay_2, first[1])
    grad_input, gain_attn_parts = enter(
        core_index, after(grad_qkv_rows, second[1]), mine, other, tokens, gain_attn, grad_middle
    )
    away_d, stay_d = near_add(after(got_d, second[1]), keep_d)
    far_d = far_trade(away_d)
    got_e = swap(after(send_e, away_c), 1, 0)
    done_c = finish(after(far_c, away_d), stay_c)
    grad_table = table_gradient(after(bands, second[1]), position_bias_table.shape[1])

    chains = [add(after(first[0], away_d, gain_attn_parts), first[1]).reshape((2,) + (2,) * len(dp_masks) + (-1, columns)), None]
    trades = [over_dp(chains[0], dp_masks[0], ()), None]
    away_e, stay_e = near_add(after(got_e, trades[0][1]), keep_e)
    far_e = far_trade(away_e)
    got_f = swap(after(send_f, away_e), 1, 0)
    chains[1] = add(after(second[0], done_c, grad_table, away_e), second[1]).reshape(chains[0].shape)
    trades[1] = over_dp(chains[1], dp_masks[0], ())
    trades[0] = (after(trades[0][0], trades[1][1]), trades[0][1])
    total = trades[1][1]
    out_theirs = swap(after(jnp.concatenate([done_a, done_b]), total), PAIR, 0)
    away_f, stay_f = near_add(after(got_f, total), keep_f)
    trades[1] = (after(trades[1][0], away_f), trades[1][1])

    small = [
        jnp.sum(gain_moe_parts, axis=0),
        jnp.sum(gain_attn_parts, axis=0),
        grad_router,
        grad_table,
        jnp.sum(squares),
    ]
    sizes = [value.size for value in small]
    flat = jnp.concatenate([value.reshape(-1) for value in small])
    flat = after(jnp.pad(flat, (0, -sum(sizes) % 1024)).reshape(-1, 128), total)

    for place, mask in enumerate(dp_masks):
        flat_got = swap(flat, mask, 0)
        chains = [add(*trades[0]), None]
        if place + 1 < len(dp_masks):
            trades_next = [over_dp(chains[0], dp_masks[place + 1], dp_masks[: place + 1]), None]
        chains[1] = add(after(trades[1][0], chains[0]), trades[1][1])
        flat = flat + flat_got
        if place + 1 < len(dp_masks):
            trades_next[1] = over_dp(chains[1], dp_masks[place + 1], dp_masks[: place + 1])
            trades = trades_next
        if mask == PAIR:
            done_d = finish(after(far_d, chains[1]), stay_d)
            in_first = swap(done_d, PAIR, 0)
        flat = after(flat, chains[1])
    total = jnp.concatenate(chains)
    far_f = far_trade(after(away_f, total))
    done_e = finish(after(far_e, total), stay_e)
    in_theirs = jnp.concatenate([in_first, swap(done_e[:1], PAIR, 0)])
    for mask in reversed(group_masks):
        bit = (here_group // mask) % 2
        other_part = swap(total, 0, mask)
        total = jnp.concatenate([jnp.where(bit == 0, total, other_part), jnp.where(bit == 0, other_part, total)], axis=1)
        flat = flat + swap(flat, 0, mask)
        total, flat = lax.optimization_barrier((total, flat))
    other_part = swap(total, 0, 1)
    flat = flat + swap(flat, 0, 1)
    total = jnp.concatenate([jnp.where(core == 0, total, other_part), jnp.where(core == 0, other_part, total)], axis=2)
    weights_done = total.astype(f32)
    grad_qkv, grad_out_weight = weights_done[:3], weights_done[3]
    done_f = finish(far_f, stay_f)
    flat = flat.reshape(-1)
    starts = [sum(sizes[:place]) for place in range(len(sizes))]
    grad_gain_moe, grad_gain_attn, grad_router, grad_table, square_total = [
        flat[start : start + value.size].reshape(value.shape) for start, value in zip(starts, small)
    ]

    out_mine, in_mine = done_c, jnp.concatenate([done_e[1:], done_f])

    def both_experts(mine, theirs):
        mine, theirs = [part.reshape(-1, part.shape[-1]).astype(f32) for part in (mine, theirs)]
        return jnp.stack([jnp.where(half == 0, mine, theirs), jnp.where(half == 0, theirs, mine)])

    grad_w_out = both_experts(out_mine, out_theirs)
    grad_w_in = both_experts(in_mine, in_theirs)

    distill_loss = square_total / (width * valid_count)
    return (
        output.astype(bf16),
        distill_loss,
        grad_input,
        grad_qkv,
        grad_out_weight,
        grad_w_in,
        grad_w_out,
        grad_router,
        grad_table,
        grad_gain_attn,
        grad_gain_moe,
    )


def solution(mesh):
    rows = P(AXES, None)
    return jax.shard_map(
        on_device,
        mesh=mesh,
        in_specs=(
            rows,
            P(None, "dp", None),
            P("dp", None),
            P(),
            P(),
            P(),
            P(),
            P("expert", None, None),
            P("expert", None, None),
            rows,
            P(AXES),
            P(AXES),
            rows,
            rows,
        ),
        out_specs=(
            rows,
            P(),
            rows,
            P(None, "dp", None),
            P("dp", None),
            P("expert", "dp", None),
            P("expert", "dp", None),
            P(),
            P(),
            P(),
            P(),
        ),
        check_vma=False,
    )
```

```python
import math
import jax
import jax.numpy as jnp
from jax import lax
from jax.experimental import pallas as pl
from jax.experimental.pallas import tpu as pltpu
from jax.sharding import PartitionSpec as P

BLOCK = 128
THIRDS = 3
EPS = 1e-06
GELU_A = math.sqrt(2.0 / math.pi)
GELU_B = 0.044715
NT = (((1,), (1,)), ((), ()))
TN = (((0,), (0,)), ((), ()))
VMEM_BYTES = 56 * 1024 * 1024


def cost(micros):
    return pl.CostEstimate(flops=int(micros * 0.37e9), bytes_accessed=0, transcendentals=0)


def dot_f32(left, right, dims=(((1,), (0,)), ((), ()))):
    return lax.dot_general(left, right, dims, preferred_element_type=jnp.float32)


def assemble(rows, pieces):
    start = 0
    for piece in pieces:
        rows[pl.ds(start, piece.shape[0]), :] = piece[...]
        start += piece.shape[0]


def hand_out(total, outs):
    start = 0
    for out in outs:
        out[...] = total[pl.ds(start, out.shape[0]), :].astype(out.dtype)
        start += out.shape[0]


def whole(shape):
    return pl.BlockSpec(shape, lambda *step: (0,) * len(shape))


def expert_forward_kernel(pick, *refs, chunk, count):
    pieces, w_in, w_out = refs[:count], refs[count], refs[count + 1]
    hidden_t, slope, rows_t = refs[count + 2 : count + 5]
    outs, rows, total = refs[count + 5 : 2 * count + 5], refs[2 * count + 5], refs[2 * count + 6]
    step = pl.program_id(0)

    @pl.when(step == 0)
    def _():
        assemble(rows, pieces)
        total[...] = jnp.zeros_like(total)
        rows_t[...] = rows[...].T

    for start in range(0, rows.shape[0], chunk):
        part = pl.ds(start, chunk)
        pre = dot_f32(rows[part, :], w_in[0])
        square = pre * pre
        bend = jnp.tanh(pre * (GELU_A + (GELU_A * GELU_B) * square))
        half = 0.5 + 0.5 * bend
        act = (pre * half).astype(jnp.bfloat16)
        lift = pre * (0.5 * GELU_A + (1.5 * GELU_A * GELU_B) * square)
        slope[part, :] = (half + lift * (1.0 - bend * bend)).astype(jnp.bfloat16)
        hidden_t[:, part] = act.T
        total[part, :] += dot_f32(act, w_out[0])

    @pl.when(step == pl.num_programs(0) - 1)
    def _():
        hand_out(total, outs)


def expert_forward(pick, pieces, w_in, w_out, tile=768, chunk=320):
    many, width = sum(piece.shape[0] for piece in pieces), pieces[0].shape[1]
    inner = w_in.shape[2]
    bf16 = jnp.bfloat16
    return pl.pallas_call(
        lambda *refs: expert_forward_kernel(*refs, chunk=chunk, count=len(pieces)),
        grid_spec=pltpu.PrefetchScalarGridSpec(
            num_scalar_prefetch=1,
            grid=(inner // tile,),
            in_specs=[whole(piece.shape) for piece in pieces]
            + [
                pl.BlockSpec((1, width, tile), lambda f, pick: (pick[0], 0, f)),
                pl.BlockSpec((1, tile, width), lambda f, pick: (pick[0], f, 0)),
            ],
            out_specs=[
                pl.BlockSpec((tile, many), lambda f, pick: (f, 0)),
                pl.BlockSpec((many, tile), lambda f, pick: (0, f)),
                whole((width, many)),
            ]
            + [whole(piece.shape) for piece in pieces],
            scratch_shapes=[pltpu.VMEM((many, width), bf16), pltpu.VMEM((many, width), jnp.float32)],
        ),
        out_shape=[
            jax.ShapeDtypeStruct((inner, many), bf16),
            jax.ShapeDtypeStruct((many, inner), bf16),
            jax.ShapeDtypeStruct((width, many), bf16),
        ]
        + [jax.ShapeDtypeStruct(piece.shape, bf16) for piece in pieces],
        compiler_params=pltpu.CompilerParams(vmem_limit_bytes=VMEM_BYTES),
        cost_estimate=cost(13),
        name="expert_forward",
    )(pick, *pieces, w_in, w_out)


def expert_backward_kernel(pick, *refs, chunk, count):
    pieces, w_in, w_out, slope = refs[:count], refs[count], refs[count + 1], refs[count + 2]
    grad_pre, rows = refs[count + 3 : count + 5]
    outs, total = refs[count + 5 : 2 * count + 5], refs[2 * count + 5]
    step = pl.program_id(0)

    @pl.when(step == 0)
    def _():
        assemble(rows, pieces)
        total[...] = jnp.zeros_like(total)

    for start in range(0, rows.shape[0], chunk):
        part = pl.ds(start, chunk)
        back = dot_f32(rows[part, :], w_out[0], NT) * slope[part, :].astype(jnp.float32)
        back = back.astype(jnp.bfloat16)
        grad_pre[part, :] = back
        total[part, :] += dot_f32(back, w_in[0], NT)

    @pl.when(step == pl.num_programs(0) - 1)
    def _():
        hand_out(total, outs)


def expert_backward(pick, pieces, w_in, w_out, slope, tile=768, chunk=640):
    many, width = sum(piece.shape[0] for piece in pieces), pieces[0].shape[1]
    inner = w_in.shape[2]
    bf16 = jnp.bfloat16
    return pl.pallas_call(
        lambda *refs: expert_backward_kernel(*refs, chunk=chunk, count=len(pieces)),
        grid_spec=pltpu.PrefetchScalarGridSpec(
            num_scalar_prefetch=1,
            grid=(inner // tile,),
            in_specs=[whole(piece.shape) for piece in pieces]
            + [
                pl.BlockSpec((1, width, tile), lambda f, pick: (pick[0], 0, f)),
                pl.BlockSpec((1, tile, width), lambda f, pick: (pick[0], f, 0)),
                pl.BlockSpec((many, tile), lambda f, pick: (0, f)),
            ],
            out_specs=[pl.BlockSpec((many, tile), lambda f, pick: (0, f)), whole((many, width))]
            + [whole(piece.shape) for piece in pieces],
            scratch_shapes=[pltpu.VMEM((many, width), jnp.float32)],
        ),
        out_shape=[jax.ShapeDtypeStruct((many, inner), bf16), jax.ShapeDtypeStruct((many, width), bf16)]
        + [jax.ShapeDtypeStruct(piece.shape, bf16) for piece in pieces],
        compiler_params=pltpu.CompilerParams(vmem_limit_bytes=VMEM_BYTES),
        cost_estimate=cost(11),
        name="expert_backward",
    )(pick, *pieces, w_in, w_out, slope)


def seen_blocks(row_block, blocks):
    return max(row_block + 1, blocks // 2)


def attention_forward_kernel(far, prefix, queries, keys, values, offsets, attended, probs, *, heads, blocks):
    pair = pl.program_id(0)
    lane = lax.broadcasted_iota(jnp.int32, queries.shape, 1)
    row = lax.broadcasted_iota(jnp.int32, (BLOCK, BLOCK), 0)
    col = lax.broadcasted_iota(jnp.int32, (BLOCK, BLOCK), 1)
    outs = []
    for head in range(2):
        line = jnp.broadcast_to(offsets[head : head + 1, :], (BLOCK, 4 * BLOCK))
        turned = pltpu.roll(line, 0, 1, stride=1, stride_axis=0)
        far_bias = far[pair * 2 + head]
        mine = (lane < heads) if head == 0 else (lane >= heads)
        query = jnp.where(mine, queries[...] * 0.125, 0.0).astype(jnp.bfloat16)
        score = dot_f32(query, keys[...], NT)
        strips = []
        for row_block in range(blocks):
            span = seen_blocks(row_block, blocks)
            pieces = []
            for key_block in range(span):
                piece = score[row_block * BLOCK : (row_block + 1) * BLOCK, key_block * BLOCK : (key_block + 1) * BLOCK]
                shift = key_block - row_block
                if shift < -1:
                    piece = piece + far_bias
                elif shift < 2:
                    piece = piece + turned[:, (2 + shift) * BLOCK : (3 + shift) * BLOCK]
                else:
                    raise ValueError(shift)
                if shift >= 0:
                    shown = col + key_block * BLOCK < prefix[0]
                    piece = jnp.where((shown | (col <= row)) if shift == 0 else shown, piece, -1e30)
                pieces.append(piece)
            peak = pieces[0]
            for piece in pieces[1:]:
                peak = jnp.maximum(peak, piece)
            peak = jnp.max(peak, axis=1, keepdims=True)
            pieces = [jnp.exp(piece - peak) for piece in pieces]
            mass = pieces[0]
            for piece in pieces[1:]:
                mass = mass + piece
            scale = 1.0 / jnp.sum(mass, axis=1, keepdims=True)
            pieces = [(piece * scale).astype(jnp.bfloat16) for piece in pieces]
            pieces += [jnp.zeros((BLOCK, BLOCK), jnp.bfloat16)] * (blocks - span)
            strips.append(jnp.concatenate(pieces, axis=1))
        weights = jnp.concatenate(strips, axis=0)
        probs[head] = weights
        outs.append(dot_f32(weights, values[...]))
    attended[...] = jnp.where(lane < heads, outs[0], outs[1]).astype(jnp.bfloat16)


def attention_forward(far, prefix, qkv_rows, offsets):
    length, width = qkv_rows.shape[1:]
    pairs = width // 128
    blocks = length // BLOCK
    return pl.pallas_call(
        lambda *refs: attention_forward_kernel(*refs, heads=64, blocks=blocks),
        grid_spec=pltpu.PrefetchScalarGridSpec(
            num_scalar_prefetch=2,
            grid=(pairs,),
            in_specs=[pl.BlockSpec((None, length, 128), lambda h, far, prefix, c=c: (c, 0, h)) for c in range(3)]
            + [pl.BlockSpec((None, 2, 4 * BLOCK), lambda h, far, prefix: (h, 0, 0))],
            out_specs=[
                pl.BlockSpec((length, 128), lambda h, far, prefix: (0, h)),
                pl.BlockSpec((2, length, length), lambda h, far, prefix: (h, 0, 0)),
            ],
        ),
        out_shape=[
            jax.ShapeDtypeStruct((length, width), jnp.bfloat16),
            jax.ShapeDtypeStruct((2 * pairs, length, length), jnp.bfloat16),
        ],
        compiler_params=pltpu.CompilerParams(vmem_limit_bytes=VMEM_BYTES),
        cost_estimate=cost(13),
        name="attention_forward",
    )(far, prefix, qkv_rows, qkv_rows, qkv_rows, offsets.reshape(pairs, 2, 4 * BLOCK))


def attention_backward_kernel(queries, keys, values, grads, probs, grad_rows, bands, *, heads, blocks):
    lane = lax.broadcasted_iota(jnp.int32, queries.shape, 1)
    query_t = (queries[...] * 0.125).astype(jnp.bfloat16).T
    grad_t = grads[...].T
    dq, dk, dv = [], [], []
    for head in range(2):
        mine = (lane < heads) if head == 0 else (lane >= heads)
        sums = [None] * 4
        grad = jnp.where(mine, grads[...], 0.0).astype(jnp.bfloat16)
        back = dot_f32(grad, values[...], NT)
        strips = []
        for row_block in range(blocks):
            span = seen_blocks(row_block, blocks)
            rows = slice(row_block * BLOCK, (row_block + 1) * BLOCK)
            soft = probs[head, pl.ds(row_block * BLOCK, BLOCK), pl.ds(0, span * BLOCK)].astype(jnp.float32)
            part = back[rows, : span * BLOCK]
            inner = jnp.sum(soft * part, axis=1, keepdims=True)
            score_grad = (soft * (part - inner)).astype(jnp.bfloat16)
            for key_block in range(span):
                band = max(key_block - row_block, -2)
                tile = score_grad[:, key_block * BLOCK : (key_block + 1) * BLOCK].astype(jnp.float32)
                sums[band + 2] = tile if sums[band + 2] is None else sums[band + 2] + tile
            if span < blocks:
                rest = jnp.zeros((BLOCK, (blocks - span) * BLOCK), jnp.bfloat16)
                score_grad = jnp.concatenate([score_grad, rest], axis=1)
            strips.append(score_grad)
        flow = jnp.concatenate(strips, axis=0)
        for band in range(4):
            bands[head, band] = sums[band]
        part = slice(head * heads, (head + 1) * heads)
        dq.append(dot_f32(flow, keys[...]) * 0.125)
        dk.append(dot_f32(query_t[part], flow))
        dv.append(dot_f32(grad_t[part], probs[head]))
    grad_rows[0] = jnp.where(lane < heads, dq[0], dq[1]).astype(jnp.bfloat16)
    grad_rows[1] = jnp.concatenate(dk, axis=0).T.astype(jnp.bfloat16)
    grad_rows[2] = jnp.concatenate(dv, axis=0).T.astype(jnp.bfloat16)


def attention_backward(qkv_rows, grads, probs):
    length, width = grads.shape
    pairs = width // 128
    blocks = length // BLOCK
    block = pl.BlockSpec((length, 128), lambda h: (0, h))
    of_three = [pl.BlockSpec((None, length, 128), lambda h, c=c: (c, 0, h)) for c in range(3)]
    return pl.pallas_call(
        lambda *refs: attention_backward_kernel(*refs, heads=64, blocks=blocks),
        grid=(pairs,),
        in_specs=[*of_three, block, pl.BlockSpec((2, length, length), lambda h: (h, 0, 0))],
        out_specs=[pl.BlockSpec((3, length, 128), lambda h: (0, 0, h)), pl.BlockSpec((2, 4, BLOCK, BLOCK), lambda h: (h, 0, 0, 0))],
        out_shape=[jax.ShapeDtypeStruct((3, length, width), jnp.bfloat16)]
        + [jax.ShapeDtypeStruct((2 * pairs, 4, BLOCK, BLOCK), jnp.float32)],
        compiler_params=pltpu.CompilerParams(vmem_limit_bytes=VMEM_BYTES),
        cost_estimate=cost(12),
        name="attention_backward",
    )(qkv_rows, qkv_rows, qkv_rows, grads, probs)


def pieces_left(lefts, plans, many):
    part = lefts[0][0].shape[0] // THIRDS
    return jnp.concatenate(
        [
            jnp.concatenate([ref[pl.ds(third * part, part), :] for ref in lefts[group * many + k]], axis=1)
            for plan in plans
            for group, third in plan
            for k in range(many)
        ]
    )


def put_pieces(result, outs):
    place = 0
    for out in outs:
        many, pieces, part = out.shape[:3]
        for piece in range(pieces):
            for k in range(many):
                out[k, piece] = result[place : place + part]
                place += part


def weight_part_kernel(picks, *refs, count, plans, many):
    lefts, rights, outs = refs[: 2 * count], refs[2 * count : 2 * count + 2], refs[2 * count + 2 :]
    left = pieces_left(list(zip(lefts[:count], lefts[count:])), plans, many)
    right = jnp.concatenate([ref[...] for ref in rights], axis=0)
    put_pieces(dot_f32(left, right).astype(jnp.bfloat16), outs)


def weight_part_plain(picks, lefts, rights, rows, plans, many):
    left, right = jnp.concatenate(lefts, axis=1), jnp.concatenate(rights, axis=0)
    depth, width = right.shape
    part = rows // THIRDS
    result = jnp.take(left.reshape(-1, rows, depth), picks, axis=0)
    result = jnp.einsum("srd,dw->srw", result, right, preferred_element_type=jnp.float32).astype(jnp.bfloat16)
    result = result.reshape(-1, many, THIRDS, part, width)
    return [jnp.stack([result[group, :, third] for group, third in plan], axis=1) for plan in plans]


def weight_part(picks, lefts, rights, rows, plans, many, tile):
    depth, width = rights[0].shape
    count, part = picks.shape[0], rows // THIRDS
    if part % 16:
        return weight_part_plain(picks, lefts, rights, rows, plans, many)
    return pl.pallas_call(
        lambda *refs: weight_part_kernel(*refs, count=count, plans=plans, many=many),
        grid_spec=pltpu.PrefetchScalarGridSpec(
            num_scalar_prefetch=1,
            grid=(width // tile,),
            in_specs=[pl.BlockSpec((rows, depth), lambda i, picks, k=k: (picks[k], 0)) for k in range(count)] * 2
            + [pl.BlockSpec((depth, tile), lambda i, picks: (0, i))] * 2,
            out_specs=[pl.BlockSpec((many, len(plan), part, tile), lambda i, picks: (0, 0, 0, i)) for plan in plans],
        ),
        out_shape=[jax.ShapeDtypeStruct((many, len(plan), part, width), jnp.bfloat16) for plan in plans],
        compiler_params=pltpu.CompilerParams(vmem_limit_bytes=VMEM_BYTES),
        cost_estimate=cost(4),
        name="weight_part",
    )(picks, *([lefts[0]] * count), *([lefts[1]] * count), *rights)


def hot_columns(slots, first, count):
    rows = first + lax.broadcasted_iota(jnp.int32, (count, slots.shape[1]), 0)
    return (rows == slots).astype(jnp.bfloat16)


def halves(core, mine, other):
    return jnp.where(core == 0, mine, other), jnp.where(core == 0, other, mine)


def join_kernel(places, *refs):
    pieces, out = refs[:-1], refs[-1]
    rows = pieces[0].shape[1]
    count = pieces[0].shape[0]
    for chunk in range(out.shape[0] // count):
        for step in range(len(pieces) * count // out.shape[0]):
            piece = pieces[chunk * (len(pieces) * count // out.shape[0]) + step]
            start = pl.multiple_of(places[step] * rows, rows)
            out[pl.ds(chunk * count, count), pl.ds(start, rows), :] = piece[...]


def join(places, chunks):
    count, rows, columns = chunks[0][0].shape
    steps = len(chunks[0])
    return pl.pallas_call(
        join_kernel,
        in_specs=[pl.BlockSpec(memory_space=pltpu.SMEM)] + [pl.BlockSpec(memory_space=pltpu.VMEM)] * (steps * len(chunks)),
        out_shape=jax.ShapeDtypeStruct((count * len(chunks), steps * rows, columns), jnp.bfloat16),
        compiler_params=pltpu.CompilerParams(vmem_limit_bytes=VMEM_BYTES),
        cost_estimate=cost(3),
        name="join",
    )(places, *[piece for chunk in chunks for piece in chunk])


def project_kernel(core, rows, mine, other, result):
    half = mine.shape[1]
    first, second = halves(core[0], mine[...], other[...])
    result[:, :half] = dot_f32(rows[...], first).astype(jnp.bfloat16)
    result[:, half:] = dot_f32(rows[...], second).astype(jnp.bfloat16)


def project(core, rows, mine, other, used):
    width, half = mine.shape[1:]
    length = rows.shape[0]
    return pl.pallas_call(
        project_kernel,
        grid_spec=pltpu.PrefetchScalarGridSpec(
            num_scalar_prefetch=1,
            grid=(used,),
            in_specs=[
                whole((length, width)),
                pl.BlockSpec((None, width, half), lambda i, core: (i, 0, 0)),
                pl.BlockSpec((None, width, half), lambda i, core: (i, 0, 0)),
            ],
            out_specs=pl.BlockSpec((None, length, 2 * half), lambda i, core: (i, 0, 0)),
        ),
        out_shape=jax.ShapeDtypeStruct((used, length, 2 * half), jnp.bfloat16),
        compiler_params=pltpu.CompilerParams(vmem_limit_bytes=VMEM_BYTES),
        cost_estimate=cost(4),
        name="project",
    )(core, rows, mine, other)


def route_kernel(core, attended, tokens, mine, other, gain, router, routes, slots, middle, normed, gates, *outs):
    f32 = jnp.float32
    first, second = halves(core[0], mine[...], other[...])
    rows = attended[...]
    moved = jnp.concatenate([dot_f32(rows, first), dot_f32(rows, second)], axis=1)
    value = tokens[...].astype(f32) + moved
    middle[...] = value
    low = (value * lax.rsqrt(jnp.mean(value * value, axis=1, keepdims=True) + EPS) * gain[...]).astype(jnp.bfloat16)
    normed[...] = low
    start = 0
    for first_out, second_out in zip(outs[::2], outs[1::2]):
        size = first_out.shape[0]
        hot = hot_columns(slots[0:1, :], start, 2 * size) + hot_columns(slots[1:2, :], start, 2 * size)
        part = dot_f32(hot, low).astype(jnp.bfloat16)
        first_out[...] = part[:size]
        second_out[...] = part[size:]
        start += 2 * size
    logits = dot_f32(low, router[...])
    soft = jnp.exp(logits - jnp.max(logits, axis=1, keepdims=True))
    soft = soft / jnp.sum(soft, axis=1, keepdims=True)
    expert = lax.broadcasted_iota(jnp.int32, soft.shape, 1)
    chosen = [jnp.sum(jnp.where(expert == routes[:, k : k + 1], soft, 0.0), axis=1, keepdims=True) for k in range(2)]
    for k in range(2):
        gates[:, k : k + 1] = chosen[k] / (chosen[0] + chosen[1])


def route(core, attended, tokens, mine, other, gain, router, routes, slots, pieces, count):
    length, width = tokens.shape
    last, half = mine.shape[0] - 1, mine.shape[2]
    f32, bf16 = jnp.float32, jnp.bfloat16
    weight = pl.BlockSpec((None, width, half), lambda i, core: (last, 0, 0))
    shapes = [((length, width), f32), ((length, width), bf16), ((length, 2), f32)] + [((count, width), bf16)] * pieces
    return pl.pallas_call(
        route_kernel,
        grid_spec=pltpu.PrefetchScalarGridSpec(
            num_scalar_prefetch=1,
            grid=(1,),
            in_specs=[whole((length, width)), whole((length, width)), weight, weight, whole((1, width)), whole(router.shape), whole(routes.shape), whole(slots.shape)],
            out_specs=[whole(shape) for shape, _ in shapes],
        ),
        out_shape=[jax.ShapeDtypeStruct(shape, kind) for shape, kind in shapes],
        compiler_params=pltpu.CompilerParams(vmem_limit_bytes=VMEM_BYTES),
        cost_estimate=cost(6),
        name="route",
    )(core, attended, tokens, mine, other, gain.reshape(1, -1), router, routes, slots)


def hot_route(slots, k, count):
    cols = lax.broadcasted_iota(jnp.int32, (slots.shape[0], count), 1)
    return cols == slots[:, k : k + 1]


def combine_kernel(*refs, count):
    slots, slots_t, scale = refs[:3]
    pieces = refs[3 : 3 + count]
    middle, teacher, cotangent, valid, gates, routes = refs[3 + count : 9 + count]
    output, grad_y, grad_logits, square = refs[9 + count : 13 + count]
    sends, rows = refs[13 + count : 13 + 2 * count], refs[13 + 2 * count]
    f32, bf16 = jnp.float32, jnp.bfloat16
    assemble(rows, pieces)
    table = rows[...]
    picked = [dot_f32(hot_route(slots, k, rows.shape[0]).astype(bf16), table) for k in range(2)]
    result = middle[...] + (gates[:, 0:1] * picked[0] + gates[:, 1:2] * picked[1])
    output[...] = result.astype(bf16)
    misfit = valid[...] * (result - teacher[...].astype(f32))
    square[...] = jnp.sum((misfit * misfit).reshape(-1, 8, misfit.shape[1]), axis=0)
    grad = cotangent[...].astype(f32) + misfit * scale[0, 0]
    grad_y[...] = grad
    steep = [jnp.sum(grad * picked[k], axis=1, keepdims=True) for k in range(2)]
    slack = gates[:, 0:1] * steep[0] + gates[:, 1:2] * steep[1]
    expert = lax.broadcasted_iota(jnp.int32, grad_logits.shape, 1)
    turn = [jnp.where(expert == routes[:, k : k + 1], gates[:, k : k + 1] * (steep[k] - slack), 0.0) for k in range(2)]
    grad_logits[...] = (turn[0] + turn[1]).astype(bf16)
    scaled = [(gates[:, k : k + 1] * grad).astype(bf16) for k in range(2)]
    start = 0
    for first, second in zip(sends[::2], sends[1::2]):
        size = first.shape[0]
        part = [dot_f32(hot_columns(slots_t[k : k + 1, :], start, 2 * size), scaled[k]) for k in range(2)]
        part = (part[0] + part[1]).astype(bf16)
        first[...] = part[:size]
        second[...] = part[size:]
        start += 2 * size


def combine(slots, slots_t, scale, pieces, middle, teacher, cotangent, valid, gates, routes, experts):
    length, width = middle.shape
    count = len(pieces)
    f32, bf16 = jnp.float32, jnp.bfloat16
    return pl.pallas_call(
        lambda *refs: combine_kernel(*refs, count=count),
        in_specs=[pl.BlockSpec(memory_space=pltpu.VMEM)] * 2
        + [pl.BlockSpec(memory_space=pltpu.SMEM)]
        + [pl.BlockSpec(memory_space=pltpu.VMEM)] * (6 + count),
        out_shape=[
            jax.ShapeDtypeStruct((length, width), bf16),
            jax.ShapeDtypeStruct((length, width), f32),
            jax.ShapeDtypeStruct((length, experts), bf16),
            jax.ShapeDtypeStruct((8, width), f32),
        ]
        + [jax.ShapeDtypeStruct(piece.shape, bf16) for piece in pieces],
        scratch_shapes=[pltpu.VMEM((sum(piece.shape[0] for piece in pieces), width), bf16)],
        compiler_params=pltpu.CompilerParams(vmem_limit_bytes=VMEM_BYTES),
        cost_estimate=cost(8),
        name="combine",
    )(slots, slots_t, scale, *pieces, middle, teacher, cotangent, valid, gates, routes)


def norm_back(value, gain, grad):
    root = lax.rsqrt(jnp.mean(value * value, axis=1, keepdims=True) + EPS)
    normed = value * root
    scaled = grad * gain
    inner = jnp.mean(scaled * normed, axis=1, keepdims=True)
    return root * (scaled - normed * inner), jnp.sum((grad * normed).reshape(-1, 8, value.shape[1]), axis=0)


def collect_kernel(core, *refs, count):
    slots, pieces = refs[0], refs[1 : 1 + count]
    middle, gain, grad_logits, router, grad_y, mine, other = refs[1 + count : 8 + count]
    grad_middle, rounded, grad_attended, grad_gain, rows = refs[8 + count :]
    assemble(rows, pieces)
    hot = (hot_route(slots, 0, rows.shape[0]) | hot_route(slots, 1, rows.shape[0])).astype(jnp.bfloat16)
    grad = dot_f32(grad_logits[...], router[...], NT) + dot_f32(hot, rows[...])
    turned, grad_gain[...] = norm_back(middle[...], gain[...], grad)
    result = grad_y[...] + turned
    grad_middle[...] = result
    low = result.astype(jnp.bfloat16)
    rounded[...] = low
    first, second = halves(core[0], mine[...], other[...])
    half = first.shape[1]
    grad_attended[...] = (dot_f32(low[:, :half], first, NT) + dot_f32(low[:, half:], second, NT)).astype(jnp.bfloat16)


def collect(core, slots, pieces, middle, gain, grad_logits, router, grad_y, mine, other):
    length, width = middle.shape
    last, half = mine.shape[0] - 1, mine.shape[2]
    f32, bf16 = jnp.float32, jnp.bfloat16
    weight = pl.BlockSpec((None, width, half), lambda i, core: (last, 0, 0))
    plain = [slots, *pieces, middle, gain.reshape(1, -1), grad_logits, router, grad_y]
    shapes = [((length, width), f32), ((length, width), bf16), ((length, width), bf16), ((8, width), f32)]
    return pl.pallas_call(
        lambda *refs: collect_kernel(*refs, count=len(pieces)),
        grid_spec=pltpu.PrefetchScalarGridSpec(
            num_scalar_prefetch=1,
            grid=(1,),
            in_specs=[whole(array.shape) for array in plain] + [weight, weight],
            out_specs=[whole(shape) for shape, _ in shapes],
            scratch_shapes=[pltpu.VMEM((sum(piece.shape[0] for piece in pieces), width), bf16)],
        ),
        out_shape=[jax.ShapeDtypeStruct(shape, kind) for shape, kind in shapes],
        compiler_params=pltpu.CompilerParams(vmem_limit_bytes=VMEM_BYTES),
        cost_estimate=cost(8),
        name="collect",
    )(core, *plain, mine, other)


def outer_halves_kernel(core, normed, attended, rights, last, *refs, count):
    aways, stays, normed_t, attended_t = refs[:2], refs[2:4], refs[4], refs[5]
    step = pl.program_id(0)

    @pl.when(step == 0)
    def _():
        normed_t[...] = normed[...].T
        attended_t[...] = attended[...].T

    for place in range(count + 1):

        @pl.when(step == place)
        def _():
            result = dot_f32(normed_t[...], rights[...]) if place < count else dot_f32(attended_t[...], last[...])
            result = result.astype(jnp.bfloat16)
            half = result.shape[1] // 2
            away, stay = aways[place // 2], stays[place // 2]
            slot = place % 2

            @pl.when(core[0] == 0)
            def _():
                stay[slot] = result[:, :half]
                away[slot] = result[:, half:]

            @pl.when(core[0] != 0)
            def _():
                away[slot] = result[:, :half]
                stay[slot] = result[:, half:]


def outer_halves(core, normed, attended, rights, last):
    length, width = normed.shape
    count, half = rights.shape[0], width // 2
    shape = jax.ShapeDtypeStruct((2, width, half), jnp.bfloat16)
    return pl.pallas_call(
        lambda *refs: outer_halves_kernel(*refs, count=count),
        grid_spec=pltpu.PrefetchScalarGridSpec(
            num_scalar_prefetch=1,
            grid=(count + 1,),
            in_specs=[
                whole((length, width)),
                whole((length, width)),
                pl.BlockSpec((None, length, width), lambda i, core: (jnp.minimum(i, count - 1), 0, 0)),
                whole((length, width)),
            ],
            out_specs=[whole(shape.shape)] * 4,
            scratch_shapes=[pltpu.VMEM((width, length), jnp.bfloat16)] * 2,
        ),
        out_shape=[shape] * 4,
        compiler_params=pltpu.CompilerParams(vmem_limit_bytes=VMEM_BYTES),
        cost_estimate=cost(6),
        name="outer_halves",
    )(core, normed, attended, rights, last)


def enter_kernel(core, grads, mine, other, tokens, gain, grad_middle, grad_input, grad_gain, total):
    step = pl.program_id(0)
    first, second = halves(core[0], mine[...], other[...])
    half = first.shape[1]
    rows = grads[...]
    part = dot_f32(rows[:, :half], first, NT) + dot_f32(rows[:, half:], second, NT)

    @pl.when(step == 0)
    def _():
        total[...] = part

    @pl.when(step > 0)
    def _():
        total[...] += part

    @pl.when(step == pl.num_programs(0) - 1)
    def _():
        turned, grad_gain[...] = norm_back(tokens[...].astype(jnp.float32), gain[...], total[...])
        grad_input[...] = grad_middle[...] + turned


def enter(core, grads, mine, other, tokens, gain, grad_middle):
    length, width = tokens.shape
    count, half = grads.shape[0], mine.shape[2]
    weight = pl.BlockSpec((None, width, half), lambda i, core: (i, 0, 0))
    return pl.pallas_call(
        enter_kernel,
        grid_spec=pltpu.PrefetchScalarGridSpec(
            num_scalar_prefetch=1,
            grid=(count,),
            in_specs=[pl.BlockSpec((None, length, width), lambda i, core: (i, 0, 0)), weight, weight, whole((length, width)), whole((1, width)), whole((length, width))],
            out_specs=[whole((length, width)), whole((8, width))],
            scratch_shapes=[pltpu.VMEM((length, width), jnp.float32)],
        ),
        out_shape=[jax.ShapeDtypeStruct((length, width), jnp.float32), jax.ShapeDtypeStruct((8, width), jnp.float32)],
        compiler_params=pltpu.CompilerParams(vmem_limit_bytes=VMEM_BYTES),
        cost_estimate=cost(6),
        name="enter",
    )(core, grads, mine, other, tokens, gain.reshape(1, -1), grad_middle)


BOUNDS = (12, 16, 23, 32, 46, 64, 91)
TOP_PRECISION = lax.Precision.HIGHEST
AXES = ("dp", "expert")
PAIR = 2


def after(value, *others):
    return lax.optimization_barrier((value, *others))[0] if others else value


def bucket_index(offset):
    distance = jnp.abs(offset)
    far_bucket = 8 + sum([(distance >= level).astype(jnp.int32) for level in BOUNDS])
    near_bucket = jnp.where(distance < 8, distance, far_bucket)
    return jnp.where(offset > 0, 16, 0) + near_bucket


def norm_apply(inputs, gain_vec):
    return inputs * lax.rsqrt(jnp.mean(inputs * inputs, axis=-1, keepdims=True) + EPS) * gain_vec


def tile_offsets(query_block, key_block):
    rows = query_block * BLOCK + lax.broadcasted_iota(jnp.int32, (BLOCK, BLOCK), 0)
    cols = key_block * BLOCK + lax.broadcasted_iota(jnp.int32, (BLOCK, BLOCK), 1)
    return rows, cols


def offset_bias(table):
    offsets = jnp.arange(4 * BLOCK, dtype=jnp.int32) - 2 * BLOCK
    hot = (bucket_index(offsets)[None] == jnp.arange(table.shape[1], dtype=jnp.int32)[:, None]).astype(jnp.float32)
    return jnp.dot(table, hot, precision=TOP_PRECISION)


def table_gradient(bands, buckets):
    rows, cols = tile_offsets(0, 0)
    ids = [jnp.full((BLOCK, BLOCK), bucket_far(), jnp.int32)]
    ids += [bucket_index(shift * BLOCK + cols - rows) for shift in (-1, 0, 1)]
    hot = (jnp.stack(ids)[..., None] == jnp.arange(buckets, dtype=jnp.int32)).astype(jnp.float32)
    return jnp.einsum("hdxy,dxyb->hb", bands, hot, precision=TOP_PRECISION)


def bucket_far():
    return 8 + len(BOUNDS)


def on_device(
    tokens,
    qkv_weight,
    out_weight,
    position_bias_table,
    gain_attn,
    gain_moe,
    router,
    w_in,
    w_out,
    routes,
    prefix,
    valid_mask,
    teacher,
    cotangent,
):
    length, width = tokens.shape
    bf16, f32 = jnp.bfloat16, jnp.float32
    expert_count = router.shape[1]
    top_count = routes.shape[1]
    groups = lax.axis_size("expert")
    copies = lax.axis_size("dp")
    inner = w_in.shape[2]
    capacity = 5 * length * top_count // (4 * expert_count)
    total_tokens = length * copies * groups
    sources = 2 * groups
    blocks = length // BLOCK
    here_dp, here_group = lax.axis_index("dp"), lax.axis_index("expert")
    half = (here_dp >> 1) & 1
    core = here_group & 1
    rest = copies // 4

    def swap(value, dp_mask, group_mask):
        pairs = [
            (i, ((i // groups) ^ dp_mask) * groups + ((i % groups) ^ group_mask))
            for i in range(copies * groups)
        ]
        return lax.ppermute(value, AXES, pairs)

    def bits(count):
        return [1 << place for place in range(count.bit_length() - 1)]

    def partial_sums(value):
        sums = []
        for masks in [(0, mask) for mask in bits(groups)] + [(mask, 0) for mask in bits(copies)]:
            value = value + swap(value, *masks)
            sums.append(value)
        return sums

    chips = groups

    def across(value, place):
        return swap(value, PAIR * (place // (groups // 2)), 2 * (place % (groups // 2)))

    def to_chips(pieces):
        return [pieces[0]] + [across(pieces[place], place) for place in range(1, chips)]

    def through(visit, sends):
        direct, relay = to_chips(sends[::2]), to_chips(sends[1::2])
        seen, direct = visit(direct)
        direct = to_chips(direct)
        relay = [after(part, seen) for part in relay]
        passed = visit(swap(jnp.concatenate(relay), 0, 1))
        passed = swap(after(passed, *direct), 0, 1)
        relay = [passed[place * capacity : (place + 1) * capacity] for place in range(chips)]
        return direct, relay

    def weave(direct, relay):
        return [part for pair in zip(direct, to_chips(relay)) for part in pair]

    ring = list(range(0, copies, 2)) + list(range(copies - 1, 0, -2))
    turns = [(1, step) for step in range(1, copies // 2 + 1)] + [(-1, step) for step in range(1, copies // 2)]

    def gather_ring(shard, due):
        got = [shard]
        for turn in (1, -1):
            held = shard
            pairs = [(ring[i], ring[(i + turn) % copies]) for i in range(copies)]
            for step in [step for way, step in turns if way == turn]:
                held = lax.ppermute(after(held, *due[step - 2 : step - 1]) if step > 1 else held, "dp", pairs)
                got.append(held)
        return got

    def ring_places():
        place = jnp.where(here_dp & 1 == 0, here_dp >> 1, copies - 1 - (here_dp >> 1))
        shift = jnp.array([0] + [turn * step for turn, step in turns], jnp.int32)
        place = (place - shift) & (copies - 1)
        return jnp.where(place < copies // 2, 2 * place, 2 * (copies - 1 - place) + 1).astype(jnp.int32)


    flat_routes = routes.reshape(-1)
    pair_count = length * top_count
    slot_count = sources * capacity
    route_hits = (flat_routes[:, None] == jnp.arange(expert_count, dtype=jnp.int32)[None, :]).astype(bf16)
    lower_ones = (
        lax.broadcasted_iota(jnp.int32, (pair_count, pair_count), 0)
        >= lax.broadcasted_iota(jnp.int32, (pair_count, pair_count), 1)
    ).astype(bf16)
    running = jnp.dot(lower_ones, route_hits, preferred_element_type=f32)
    pair_rank = jnp.sum((running - 1.0) * route_hits.astype(f32), axis=1).astype(jnp.int32)
    away = (flat_routes >> 1) ^ here_group
    chip = ((flat_routes & 1) ^ half) * (groups // 2) + (away >> 1)
    slots = ((chip * 2 + (away & 1)) * capacity + pair_rank).reshape(length, top_count)
    slots_t = slots.T

    resid = tokens.astype(f32)
    normed1 = norm_apply(resid, gain_attn).astype(bf16)
    columns = width // 2
    core_index = core.reshape(1).astype(jnp.int32)
    valid_rows = valid_mask.astype(f32)[:, None]
    counts = [jnp.broadcast_to(jnp.sum(valid_rows), (8, 128))]
    count_trades = [(0, mask) for mask in bits(groups)] + [(mask, 0) for mask in bits(copies)]

    def count_beside(before, value):
        if len(counts) > len(count_trades):
            return value
        counts.append(counts[-1] + swap(after(counts[-1], before), *count_trades[len(counts) - 1]))
        return after(value, counts[-1])

    shards = [
        lax.dynamic_slice_in_dim(part, core * columns, columns, 2)
        for part in (qkv_weight[:2], jnp.concatenate([qkv_weight[2:], out_weight[None]]))
    ]
    if copies > 8:
        mine = lax.all_gather(jnp.concatenate(shards), "dp", axis=1, tiled=True)
    else:
        mine = join(ring_places(), [gather_ring(shards[0], ()), gather_ring(shards[1], (slots_t, normed1))])
    other = count_beside(mine, swap(mine, 0, 1))
    qkv_rows = count_beside(other, project(core_index, normed1, mine, other, 3))
    offsets = offset_bias(position_bias_table)
    attended, probs = attention_forward(position_bias_table[:, bucket_far()], prefix, qkv_rows, offsets)
    middle, normed2, gates, *sends = route(
        core_index, count_beside(qkv_rows, attended), tokens, mine, other, gain_moe, router, routes, slots_t, 2 * chips, capacity
    )

    pick = half.reshape(1).astype(jnp.int32)
    hidden, slopes, rows_in = [], [], []

    def expert(pieces):
        one = not isinstance(pieces, list)
        pieces = [pieces] if one else pieces
        hidden_t, slope, rows_t, *results = expert_forward(pick, pieces, w_in, w_out)
        hidden_t = count_beside(pieces[-1], hidden_t)
        for kept, value in zip((hidden, slopes, rows_in), (hidden_t, slope, rows_t)):
            kept.append(value)
        return results[0] if one else (hidden_t, results)

    back = weave(*through(expert, sends))
    while len(counts) <= len(count_trades):
        back[0] = count_beside(back[0], back[0])
    valid_count = counts[-1][0, 0]
    scale = (total_tokens / valid_count).reshape(1, 1)
    output, grad_y, grad_logits, squares, *sends = combine(
        slots, slots_t, scale, back, middle, teacher, cotangent, valid_rows, gates, routes, expert_count
    )

    out_rows = inner // copies
    in_rows = width // copies
    far_bit = here_dp % 2
    slices = jnp.arange(rest, dtype=jnp.int32) * 4

    def picks(bit0):
        return jnp.concatenate([slices + ((half ^ other_half) * 2 + bit0) for other_half in (1, 0)]).astype(jnp.int32)

    sent, kept = picks(1 - far_bit), picks(far_bit)

    def add(left, right):
        return (left.astype(f32) + right.astype(f32)).astype(bf16)

    def fold(unit, bit, axis=0):
        unit = unit.reshape(unit.shape[:axis] + (2, unit.shape[axis] // 2) + unit.shape[axis + 1 :])
        away_part = lax.dynamic_index_in_dim(unit, 1 - bit, axis, keepdims=False)
        return away_part, lax.dynamic_index_in_dim(unit, bit, axis, keepdims=False)

    far_masks = list(reversed(bits(copies)[2:]))

    def near_add(got, keep):
        away_part, stay_part = fold(add(got, keep), (here_dp // far_masks[0]) % 2)
        return away_part, stay_part

    def far_trade(away_part):
        return swap(away_part, far_masks[0], 0)

    def finish(got, stay):
        unit = add(got, stay)
        for mask in far_masks[1:]:
            away_part, stay_part = fold(unit, (here_dp // mask) % 2)
            unit = add(swap(away_part, mask, 0), stay_part)
        return unit[0]

    plan_a, plan_b, plan_c = ((0, 0),), ((0, 1), (0, 2)), ((1, 0), (1, 1), (1, 2))
    plan_d, plan_e, plan_f = ((0, 0), (0, 1)), ((0, 2), (1, 0), (1, 1)), ((1, 2),)
    out_plans, in_plans = (plan_a, plan_b, plan_c), (plan_d, plan_e, plan_f)

    grad_rows, grad_pre, parts = [], [], []

    def expert_back(pieces):
        if isinstance(pieces, list):
            grad_pre_rows, grads, *results = expert_backward(pick, pieces, w_in, w_out, slopes[0])
            grad_rows.append(grads)
            grad_pre.append(grad_pre_rows)
            return grad_pre_rows, results
        grad_rows.append(pieces)
        parts.extend(weight_part(sent, hidden, grad_rows, out_rows, out_plans, rest, width))
        parts[0] = swap(parts[0], 1, 0)
        pieces = after(pieces, parts[1])
        grad_pre_rows, _, results = expert_backward(pick, [pieces], w_in, w_out, slopes[1])
        grad_pre.append(grad_pre_rows)
        return after(results, parts[0])

    direct, relay = through(expert_back, sends)
    got_a, send_b, send_c = parts
    got_b = swap(after(send_b, relay[0]), 1, 0)
    back = weave(direct, relay)
    grad_rows, grad_pre = lax.optimization_barrier((grad_rows, grad_pre, relay))[:2]
    keep_a, keep_b, keep_c = weight_part(kept, hidden, grad_rows, out_rows, out_plans, rest, width)
    away_a, stay_a = near_add(got_a, keep_a)
    far_a = far_trade(away_a)
    grad_pre = after(grad_pre, away_a)
    send_d, send_e, send_f = weight_part(sent, rows_in, grad_pre, in_rows, in_plans, rest, inner // 2)
    back = [after(part, send_d) for part in back]
    got_c = swap(after(send_c, *back), 1, 0)
    grad_middle, grad_attn_proj, grad_attended, gain_moe_parts = collect(
        core_index, slots, back, middle, gain_moe, grad_logits, router, grad_y, mine, other
    )
    away_b, stay_b = near_add(after(got_b, grad_attended), keep_b)
    grad_attended, away_b, far_a = lax.optimization_barrier((grad_attended, away_b, far_a))
    far_b = far_trade(away_b)
    done_a = finish(far_a, stay_a)
    grad_qkv_rows, bands = attention_backward(qkv_rows, grad_attended, probs)
    grad_qkv_rows, got_c = lax.optimization_barrier((grad_qkv_rows, got_c))

    away_c, stay_c = near_add(got_c, keep_c)
    far_c = far_trade(away_c)
    got_d = swap(after(send_d, away_c), 1, 0)
    *weights_away, stay_1, stay_2 = outer_halves(
        core_index, normed1, attended, after(grad_qkv_rows, far_b, away_c), grad_attn_proj
    )
    done_b = finish(far_b, stay_b)
    keep_d, keep_e, keep_f = weight_part(
        kept, rows_in, after(grad_pre, *weights_away), in_rows, in_plans, rest, inner // 2
    )
    group_masks = bits(groups)[1:]
    dp_masks = sorted(bits(copies), key=lambda mask: (mask != PAIR, mask))

    def over_groups(got, stay, *due):
        got = add(after(got, *due), stay).reshape(2, copies, in_rows, columns)
        for mask in group_masks[:-1]:
            away_part, stay_part = fold(got, (here_group // mask) % 2, 2)
            got = add(swap(away_part, 0, mask), stay_part)
        away_part, stay_part = fold(got, (here_group // group_masks[-1]) % 2, 2)
        return swap(away_part, 0, group_masks[-1]), stay_part

    def over_dp(total, mask, passed):
        axis = 1 + sorted([other for other in dp_masks if other not in passed], reverse=True).index(mask)
        bit = (here_dp // mask) % 2
        away_part = lax.dynamic_index_in_dim(total, 1 - bit, axis, keepdims=False)
        stay_part = lax.dynamic_index_in_dim(total, bit, axis, keepdims=False)
        return swap(away_part, mask, 0), stay_part

    weights_got = [swap(part, 0, 1) for part in weights_away]
    first = over_groups(weights_got[0], stay_1, keep_d)
    second = over_groups(weights_got[1], stay_2, first[1])
    grad_input, gain_attn_parts = enter(
        core_index, after(grad_qkv_rows, second[1]), mine, other, tokens, gain_attn, grad_middle
    )
    away_d, stay_d = near_add(after(got_d, second[1]), keep_d)
    far_d = far_trade(away_d)
    got_e = swap(after(send_e, got_d), 1, 0)
    done_c = finish(after(far_c, away_d), stay_c)
    grad_table = table_gradient(after(bands, second[1]), position_bias_table.shape[1])

    chains = [add(after(first[0], away_d, gain_attn_parts), first[1]).reshape((2,) + (2,) * len(dp_masks) + (-1, columns)), None]
    trades = [over_dp(chains[0], dp_masks[0], ()), None]
    chains[1] = add(after(second[0], done_c, grad_table), second[1]).reshape(chains[0].shape)
    trades[1] = over_dp(chains[1], dp_masks[0], ())
    trades[0] = (after(trades[0][0], trades[1][1]), trades[0][1])
    total = trades[1][1]
    away_e, stay_e = near_add(after(got_e, total), keep_e)
    far_e = far_trade(away_e)
    got_f = swap(after(send_f, away_e), 1, 0)
    trades[1] = (after(trades[1][0], away_e), trades[1][1])

    normed2, squares, gain_moe_parts = after((normed2, squares, gain_moe_parts), second[1])
    grad_router = jnp.einsum("td,te->de", normed2, grad_logits, preferred_element_type=f32)
    small = [
        jnp.sum(gain_moe_parts, axis=0),
        jnp.sum(gain_attn_parts, axis=0),
        grad_router,
        grad_table,
        jnp.sum(squares),
    ]
    sizes = [value.size for value in small]
    flat = jnp.concatenate([value.reshape(-1) for value in small])
    flat = after(jnp.pad(flat, (0, -sum(sizes) % 1024)).reshape(-1, 128), total)

    for place, mask in enumerate(dp_masks):
        flat_got = swap(flat, mask, 0)
        chains = [add(*trades[0]), None]
        if place + 1 < len(dp_masks):
            trades_next = [over_dp(chains[0], dp_masks[place + 1], dp_masks[: place + 1]), None]
        chains[1] = add(after(trades[1][0], chains[0]), trades[1][1])
        flat = flat + flat_got
        if place + 1 < len(dp_masks):
            trades_next[1] = over_dp(chains[1], dp_masks[place + 1], dp_masks[: place + 1])
            trades = trades_next
        if mask == PAIR:
            done_d = finish(after(far_d, chains[1]), stay_d)
            in_first = swap(done_d, PAIR, 0)
            out_theirs = swap(after(jnp.concatenate([done_a, done_b]), chains[1]), PAIR, 0)
            away_f, stay_f = near_add(after(got_f, chains[1]), keep_f)
            far_f = far_trade(away_f)
        flat = after(flat, chains[1])
    total = jnp.concatenate(chains)
    done_e = finish(after(far_e, total), stay_e)
    in_theirs = jnp.concatenate([in_first, swap(done_e[:1], PAIR, 0)])
    for mask in reversed(group_masks):
        bit = (here_group // mask) % 2
        other_part = swap(total, 0, mask)
        total = jnp.concatenate([jnp.where(bit == 0, total, other_part), jnp.where(bit == 0, other_part, total)], axis=1)
        if mask == group_masks[0]:
            done_f = finish(after(far_f, total), stay_f)
            total = after(total, done_f)
        flat = flat + swap(flat, 0, mask)
        total, flat = lax.optimization_barrier((total, flat))
    other_part = swap(total, 0, 1)
    flat = flat + swap(flat, 0, 1)
    total = jnp.concatenate([jnp.where(core == 0, total, other_part), jnp.where(core == 0, other_part, total)], axis=2)
    weights_done = total.astype(f32)
    grad_qkv, grad_out_weight = weights_done[:3], weights_done[3]
    flat = flat.reshape(-1)
    starts = [sum(sizes[:place]) for place in range(len(sizes))]
    grad_gain_moe, grad_gain_attn, grad_router, grad_table, square_total = [
        flat[start : start + value.size].reshape(value.shape) for start, value in zip(starts, small)
    ]

    out_mine, in_mine = done_c, jnp.concatenate([done_e[1:], done_f])

    def both_experts(mine, theirs):
        mine, theirs = [part.reshape(-1, part.shape[-1]).astype(f32) for part in (mine, theirs)]
        return jnp.stack([jnp.where(half == 0, mine, theirs), jnp.where(half == 0, theirs, mine)])

    grad_w_out = both_experts(out_mine, out_theirs)
    grad_w_in = both_experts(in_mine, in_theirs)

    distill_loss = square_total / (width * valid_count)
    return (
        output.astype(bf16),
        distill_loss,
        grad_input,
        grad_qkv,
        grad_out_weight,
        grad_w_in,
        grad_w_out,
        grad_router,
        grad_table,
        grad_gain_attn,
        grad_gain_moe,
    )


def solution(mesh):
    rows = P(AXES, None)
    return jax.shard_map(
        on_device,
        mesh=mesh,
        in_specs=(
            rows,
            P(None, "dp", None),
            P("dp", None),
            P(),
            P(),
            P(),
            P(),
            P("expert", None, None),
            P("expert", None, None),
            rows,
            P(AXES),
            P(AXES),
            rows,
            rows,
        ),
        out_specs=(
            rows,
            P(),
            rows,
            P(None, "dp", None),
            P("dp", None),
            P("expert", "dp", None),
            P("expert", "dp", None),
            P(),
            P(),
            P(),
            P(),
        ),
        check_vma=False,
    )
```

```python
import math
import jax
import jax.numpy as jnp
from jax import lax
from jax.experimental import pallas as pl
from jax.experimental.pallas import tpu as pltpu
from jax.sharding import PartitionSpec as P

BLOCK = 128
THIRDS = 3
EPS = 1e-06
GELU_A = math.sqrt(2.0 / math.pi)
GELU_B = 0.044715
NT = (((1,), (1,)), ((), ()))
TN = (((0,), (0,)), ((), ()))
VMEM_BYTES = 56 * 1024 * 1024


def cost(micros):
    return pl.CostEstimate(flops=int(micros * 0.37e9), bytes_accessed=0, transcendentals=0)


def dot_f32(left, right, dims=(((1,), (0,)), ((), ()))):
    return lax.dot_general(left, right, dims, preferred_element_type=jnp.float32)


def assemble(rows, pieces):
    start = 0
    for piece in pieces:
        rows[pl.ds(start, piece.shape[0]), :] = piece[...]
        start += piece.shape[0]


def hand_out(total, outs):
    start = 0
    for out in outs:
        out[...] = total[pl.ds(start, out.shape[0]), :].astype(out.dtype)
        start += out.shape[0]


def whole(shape):
    return pl.BlockSpec(shape, lambda *step: (0,) * len(shape))


def expert_forward_kernel(pick, *refs, chunk, count):
    pieces, w_in, w_out = refs[:count], refs[count], refs[count + 1]
    hidden_t, slope, rows_t = refs[count + 2 : count + 5]
    outs, rows, total = refs[count + 5 : 2 * count + 5], refs[2 * count + 5], refs[2 * count + 6]
    step = pl.program_id(0)

    @pl.when(step == 0)
    def _():
        assemble(rows, pieces)
        total[...] = jnp.zeros_like(total)
        rows_t[...] = rows[...].T

    for start in range(0, rows.shape[0], chunk):
        part = pl.ds(start, chunk)
        pre = dot_f32(rows[part, :], w_in[0])
        square = pre * pre
        bend = jnp.tanh(pre * (GELU_A + (GELU_A * GELU_B) * square))
        half = 0.5 + 0.5 * bend
        act = (pre * half).astype(jnp.bfloat16)
        lift = pre * (0.5 * GELU_A + (1.5 * GELU_A * GELU_B) * square)
        slope[part, :] = (half + lift * (1.0 - bend * bend)).astype(jnp.bfloat16)
        hidden_t[:, part] = act.T
        total[part, :] += dot_f32(act, w_out[0])

    @pl.when(step == pl.num_programs(0) - 1)
    def _():
        hand_out(total, outs)


def expert_forward(pick, pieces, w_in, w_out, tile=768, chunk=320):
    many, width = sum(piece.shape[0] for piece in pieces), pieces[0].shape[1]
    inner = w_in.shape[2]
    bf16 = jnp.bfloat16
    return pl.pallas_call(
        lambda *refs: expert_forward_kernel(*refs, chunk=chunk, count=len(pieces)),
        grid_spec=pltpu.PrefetchScalarGridSpec(
            num_scalar_prefetch=1,
            grid=(inner // tile,),
            in_specs=[whole(piece.shape) for piece in pieces]
            + [
                pl.BlockSpec((1, width, tile), lambda f, pick: (pick[0], 0, f)),
                pl.BlockSpec((1, tile, width), lambda f, pick: (pick[0], f, 0)),
            ],
            out_specs=[
                pl.BlockSpec((tile, many), lambda f, pick: (f, 0)),
                pl.BlockSpec((many, tile), lambda f, pick: (0, f)),
                whole((width, many)),
            ]
            + [whole(piece.shape) for piece in pieces],
            scratch_shapes=[pltpu.VMEM((many, width), bf16), pltpu.VMEM((many, width), jnp.float32)],
        ),
        out_shape=[
            jax.ShapeDtypeStruct((inner, many), bf16),
            jax.ShapeDtypeStruct((many, inner), bf16),
            jax.ShapeDtypeStruct((width, many), bf16),
        ]
        + [jax.ShapeDtypeStruct(piece.shape, bf16) for piece in pieces],
        compiler_params=pltpu.CompilerParams(vmem_limit_bytes=VMEM_BYTES),
        cost_estimate=cost(13),
        name="expert_forward",
    )(pick, *pieces, w_in, w_out)


def expert_backward_kernel(pick, *refs, chunk, count):
    pieces, w_in, w_out, slope = refs[:count], refs[count], refs[count + 1], refs[count + 2]
    grad_pre, rows = refs[count + 3 : count + 5]
    outs, total = refs[count + 5 : 2 * count + 5], refs[2 * count + 5]
    step = pl.program_id(0)

    @pl.when(step == 0)
    def _():
        assemble(rows, pieces)
        total[...] = jnp.zeros_like(total)

    for start in range(0, rows.shape[0], chunk):
        part = pl.ds(start, chunk)
        back = dot_f32(rows[part, :], w_out[0], NT) * slope[part, :].astype(jnp.float32)
        back = back.astype(jnp.bfloat16)
        grad_pre[part, :] = back
        total[part, :] += dot_f32(back, w_in[0], NT)

    @pl.when(step == pl.num_programs(0) - 1)
    def _():
        hand_out(total, outs)


def expert_backward(pick, pieces, w_in, w_out, slope, tile=768, chunk=640):
    many, width = sum(piece.shape[0] for piece in pieces), pieces[0].shape[1]
    inner = w_in.shape[2]
    bf16 = jnp.bfloat16
    return pl.pallas_call(
        lambda *refs: expert_backward_kernel(*refs, chunk=chunk, count=len(pieces)),
        grid_spec=pltpu.PrefetchScalarGridSpec(
            num_scalar_prefetch=1,
            grid=(inner // tile,),
            in_specs=[whole(piece.shape) for piece in pieces]
            + [
                pl.BlockSpec((1, width, tile), lambda f, pick: (pick[0], 0, f)),
                pl.BlockSpec((1, tile, width), lambda f, pick: (pick[0], f, 0)),
                pl.BlockSpec((many, tile), lambda f, pick: (0, f)),
            ],
            out_specs=[pl.BlockSpec((many, tile), lambda f, pick: (0, f)), whole((many, width))]
            + [whole(piece.shape) for piece in pieces],
            scratch_shapes=[pltpu.VMEM((many, width), jnp.float32)],
        ),
        out_shape=[jax.ShapeDtypeStruct((many, inner), bf16), jax.ShapeDtypeStruct((many, width), bf16)]
        + [jax.ShapeDtypeStruct(piece.shape, bf16) for piece in pieces],
        compiler_params=pltpu.CompilerParams(vmem_limit_bytes=VMEM_BYTES),
        cost_estimate=cost(11),
        name="expert_backward",
    )(pick, *pieces, w_in, w_out, slope)


def seen_blocks(row_block, blocks):
    return max(row_block + 1, blocks // 2)


def attention_forward_kernel(far, prefix, queries, keys, values, offsets, attended, probs, *, heads, blocks):
    pair = pl.program_id(0)
    lane = lax.broadcasted_iota(jnp.int32, queries.shape, 1)
    row = lax.broadcasted_iota(jnp.int32, (BLOCK, BLOCK), 0)
    col = lax.broadcasted_iota(jnp.int32, (BLOCK, BLOCK), 1)
    outs = []
    for head in range(2):
        line = jnp.broadcast_to(offsets[head : head + 1, :], (BLOCK, 4 * BLOCK))
        turned = pltpu.roll(line, 0, 1, stride=1, stride_axis=0)
        far_bias = far[pair * 2 + head]
        mine = (lane < heads) if head == 0 else (lane >= heads)
        query = jnp.where(mine, queries[...] * 0.125, 0.0).astype(jnp.bfloat16)
        score = dot_f32(query, keys[...], NT)
        strips = []
        for row_block in range(blocks):
            span = seen_blocks(row_block, blocks)
            pieces = []
            for key_block in range(span):
                piece = score[row_block * BLOCK : (row_block + 1) * BLOCK, key_block * BLOCK : (key_block + 1) * BLOCK]
                shift = key_block - row_block
                if shift < -1:
                    piece = piece + far_bias
                elif shift < 2:
                    piece = piece + turned[:, (2 + shift) * BLOCK : (3 + shift) * BLOCK]
                else:
                    raise ValueError(shift)
                if shift >= 0:
                    shown = col + key_block * BLOCK < prefix[0]
                    piece = jnp.where((shown | (col <= row)) if shift == 0 else shown, piece, -1e30)
                pieces.append(piece)
            peak = pieces[0]
            for piece in pieces[1:]:
                peak = jnp.maximum(peak, piece)
            peak = jnp.max(peak, axis=1, keepdims=True)
            pieces = [jnp.exp(piece - peak) for piece in pieces]
            mass = pieces[0]
            for piece in pieces[1:]:
                mass = mass + piece
            scale = 1.0 / jnp.sum(mass, axis=1, keepdims=True)
            pieces = [(piece * scale).astype(jnp.bfloat16) for piece in pieces]
            pieces += [jnp.zeros((BLOCK, BLOCK), jnp.bfloat16)] * (blocks - span)
            strips.append(jnp.concatenate(pieces, axis=1))
        weights = jnp.concatenate(strips, axis=0)
        probs[head] = weights
        outs.append(dot_f32(weights, values[...]))
    attended[...] = jnp.where(lane < heads, outs[0], outs[1]).astype(jnp.bfloat16)


def attention_forward(far, prefix, qkv_rows, offsets):
    length, width = qkv_rows.shape[1:]
    pairs = width // 128
    blocks = length // BLOCK
    return pl.pallas_call(
        lambda *refs: attention_forward_kernel(*refs, heads=64, blocks=blocks),
        grid_spec=pltpu.PrefetchScalarGridSpec(
            num_scalar_prefetch=2,
            grid=(pairs,),
            in_specs=[pl.BlockSpec((None, length, 128), lambda h, far, prefix, c=c: (c, 0, h)) for c in range(3)]
            + [pl.BlockSpec((None, 2, 4 * BLOCK), lambda h, far, prefix: (h, 0, 0))],
            out_specs=[
                pl.BlockSpec((length, 128), lambda h, far, prefix: (0, h)),
                pl.BlockSpec((2, length, length), lambda h, far, prefix: (h, 0, 0)),
            ],
        ),
        out_shape=[
            jax.ShapeDtypeStruct((length, width), jnp.bfloat16),
            jax.ShapeDtypeStruct((2 * pairs, length, length), jnp.bfloat16),
        ],
        compiler_params=pltpu.CompilerParams(vmem_limit_bytes=VMEM_BYTES),
        cost_estimate=cost(13),
        name="attention_forward",
    )(far, prefix, qkv_rows, qkv_rows, qkv_rows, offsets.reshape(pairs, 2, 4 * BLOCK))


def attention_backward_kernel(queries, keys, values, grads, probs, grad_rows, bands, *, heads, blocks):
    lane = lax.broadcasted_iota(jnp.int32, queries.shape, 1)
    query_t = (queries[...] * 0.125).astype(jnp.bfloat16).T
    grad_t = grads[...].T
    dq, dk, dv = [], [], []
    for head in range(2):
        mine = (lane < heads) if head == 0 else (lane >= heads)
        sums = [None] * 4
        grad = jnp.where(mine, grads[...], 0.0).astype(jnp.bfloat16)
        back = dot_f32(grad, values[...], NT)
        strips = []
        for row_block in range(blocks):
            span = seen_blocks(row_block, blocks)
            rows = slice(row_block * BLOCK, (row_block + 1) * BLOCK)
            soft = probs[head, pl.ds(row_block * BLOCK, BLOCK), pl.ds(0, span * BLOCK)].astype(jnp.float32)
            part = back[rows, : span * BLOCK]
            inner = jnp.sum(soft * part, axis=1, keepdims=True)
            score_grad = (soft * (part - inner)).astype(jnp.bfloat16)
            for key_block in range(span):
                band = max(key_block - row_block, -2)
                tile = score_grad[:, key_block * BLOCK : (key_block + 1) * BLOCK].astype(jnp.float32)
                sums[band + 2] = tile if sums[band + 2] is None else sums[band + 2] + tile
            if span < blocks:
                rest = jnp.zeros((BLOCK, (blocks - span) * BLOCK), jnp.bfloat16)
                score_grad = jnp.concatenate([score_grad, rest], axis=1)
            strips.append(score_grad)
        flow = jnp.concatenate(strips, axis=0)
        for band in range(4):
            bands[head, band] = sums[band]
        part = slice(head * heads, (head + 1) * heads)
        dq.append(dot_f32(flow, keys[...]) * 0.125)
        dk.append(dot_f32(query_t[part], flow))
        dv.append(dot_f32(grad_t[part], probs[head]))
    grad_rows[0] = jnp.where(lane < heads, dq[0], dq[1]).astype(jnp.bfloat16)
    grad_rows[1] = jnp.concatenate(dk, axis=0).T.astype(jnp.bfloat16)
    grad_rows[2] = jnp.concatenate(dv, axis=0).T.astype(jnp.bfloat16)


def attention_backward(qkv_rows, grads, probs):
    length, width = grads.shape
    pairs = width // 128
    blocks = length // BLOCK
    block = pl.BlockSpec((length, 128), lambda h: (0, h))
    of_three = [pl.BlockSpec((None, length, 128), lambda h, c=c: (c, 0, h)) for c in range(3)]
    return pl.pallas_call(
        lambda *refs: attention_backward_kernel(*refs, heads=64, blocks=blocks),
        grid=(pairs,),
        in_specs=[*of_three, block, pl.BlockSpec((2, length, length), lambda h: (h, 0, 0))],
        out_specs=[pl.BlockSpec((3, length, 128), lambda h: (0, 0, h)), pl.BlockSpec((2, 4, BLOCK, BLOCK), lambda h: (h, 0, 0, 0))],
        out_shape=[jax.ShapeDtypeStruct((3, length, width), jnp.bfloat16)]
        + [jax.ShapeDtypeStruct((2 * pairs, 4, BLOCK, BLOCK), jnp.float32)],
        compiler_params=pltpu.CompilerParams(vmem_limit_bytes=VMEM_BYTES),
        cost_estimate=cost(12),
        name="attention_backward",
    )(qkv_rows, qkv_rows, qkv_rows, grads, probs)


def pieces_left(lefts, plans, many):
    part = lefts[0][0].shape[0] // THIRDS
    return jnp.concatenate(
        [
            jnp.concatenate([ref[pl.ds(third * part, part), :] for ref in lefts[group * many + k]], axis=1)
            for plan in plans
            for group, third in plan
            for k in range(many)
        ]
    )


def put_pieces(result, outs):
    place = 0
    for out in outs:
        many, pieces, part = out.shape[:3]
        for piece in range(pieces):
            for k in range(many):
                out[k, piece] = result[place : place + part]
                place += part


def weight_part_kernel(picks, *refs, count, plans, many):
    lefts, rights, outs = refs[: 2 * count], refs[2 * count : 2 * count + 2], refs[2 * count + 2 :]
    left = pieces_left(list(zip(lefts[:count], lefts[count:])), plans, many)
    right = jnp.concatenate([ref[...] for ref in rights], axis=0)
    put_pieces(dot_f32(left, right).astype(jnp.bfloat16), outs)


def weight_part_plain(picks, lefts, rights, rows, plans, many):
    left, right = jnp.concatenate(lefts, axis=1), jnp.concatenate(rights, axis=0)
    depth, width = right.shape
    part = rows // THIRDS
    result = jnp.take(left.reshape(-1, rows, depth), picks, axis=0)
    result = jnp.einsum("srd,dw->srw", result, right, preferred_element_type=jnp.float32).astype(jnp.bfloat16)
    result = result.reshape(-1, many, THIRDS, part, width)
    return [jnp.stack([result[group, :, third] for group, third in plan], axis=1) for plan in plans]


def weight_part(picks, lefts, rights, rows, plans, many, tile):
    depth, width = rights[0].shape
    count, part = picks.shape[0], rows // THIRDS
    if part % 16:
        return weight_part_plain(picks, lefts, rights, rows, plans, many)
    return pl.pallas_call(
        lambda *refs: weight_part_kernel(*refs, count=count, plans=plans, many=many),
        grid_spec=pltpu.PrefetchScalarGridSpec(
            num_scalar_prefetch=1,
            grid=(width // tile,),
            in_specs=[pl.BlockSpec((rows, depth), lambda i, picks, k=k: (picks[k], 0)) for k in range(count)] * 2
            + [pl.BlockSpec((depth, tile), lambda i, picks: (0, i))] * 2,
            out_specs=[pl.BlockSpec((many, len(plan), part, tile), lambda i, picks: (0, 0, 0, i)) for plan in plans],
        ),
        out_shape=[jax.ShapeDtypeStruct((many, len(plan), part, width), jnp.bfloat16) for plan in plans],
        compiler_params=pltpu.CompilerParams(vmem_limit_bytes=VMEM_BYTES),
        cost_estimate=cost(4),
        name="weight_part",
    )(picks, *([lefts[0]] * count), *([lefts[1]] * count), *rights)


def hot_columns(slots, first, count):
    rows = first + lax.broadcasted_iota(jnp.int32, (count, slots.shape[1]), 0)
    return (rows == slots).astype(jnp.bfloat16)


def halves(core, mine, other):
    return jnp.where(core == 0, mine, other), jnp.where(core == 0, other, mine)


def join_kernel(places, *refs):
    pieces, out = refs[:-1], refs[-1]
    rows = pieces[0].shape[1]
    count = pieces[0].shape[0]
    for chunk in range(out.shape[0] // count):
        for step in range(len(pieces) * count // out.shape[0]):
            piece = pieces[chunk * (len(pieces) * count // out.shape[0]) + step]
            start = pl.multiple_of(places[step] * rows, rows)
            out[pl.ds(chunk * count, count), pl.ds(start, rows), :] = piece[...]


def join(places, chunks):
    count, rows, columns = chunks[0][0].shape
    steps = len(chunks[0])
    return pl.pallas_call(
        join_kernel,
        in_specs=[pl.BlockSpec(memory_space=pltpu.SMEM)] + [pl.BlockSpec(memory_space=pltpu.VMEM)] * (steps * len(chunks)),
        out_shape=jax.ShapeDtypeStruct((count * len(chunks), steps * rows, columns), jnp.bfloat16),
        compiler_params=pltpu.CompilerParams(vmem_limit_bytes=VMEM_BYTES),
        cost_estimate=cost(3),
        name="join",
    )(places, *[piece for chunk in chunks for piece in chunk])


def project_kernel(core, rows, mine, other, result):
    half = mine.shape[1]
    first, second = halves(core[0], mine[...], other[...])
    result[:, :half] = dot_f32(rows[...], first).astype(jnp.bfloat16)
    result[:, half:] = dot_f32(rows[...], second).astype(jnp.bfloat16)


def project(core, rows, mine, other, used):
    width, half = mine.shape[1:]
    length = rows.shape[0]
    return pl.pallas_call(
        project_kernel,
        grid_spec=pltpu.PrefetchScalarGridSpec(
            num_scalar_prefetch=1,
            grid=(used,),
            in_specs=[
                whole((length, width)),
                pl.BlockSpec((None, width, half), lambda i, core: (i, 0, 0)),
                pl.BlockSpec((None, width, half), lambda i, core: (i, 0, 0)),
            ],
            out_specs=pl.BlockSpec((None, length, 2 * half), lambda i, core: (i, 0, 0)),
        ),
        out_shape=jax.ShapeDtypeStruct((used, length, 2 * half), jnp.bfloat16),
        compiler_params=pltpu.CompilerParams(vmem_limit_bytes=VMEM_BYTES),
        cost_estimate=cost(4),
        name="project",
    )(core, rows, mine, other)


def route_kernel(core, attended, tokens, mine, other, gain, router, routes, slots, middle, normed, gates, *outs):
    f32 = jnp.float32
    first, second = halves(core[0], mine[...], other[...])
    rows = attended[...]
    moved = jnp.concatenate([dot_f32(rows, first), dot_f32(rows, second)], axis=1)
    value = tokens[...].astype(f32) + moved
    middle[...] = value
    low = (value * lax.rsqrt(jnp.mean(value * value, axis=1, keepdims=True) + EPS) * gain[...]).astype(jnp.bfloat16)
    normed[...] = low
    start = 0
    for first_out, second_out in zip(outs[::2], outs[1::2]):
        size = first_out.shape[0]
        hot = hot_columns(slots[0:1, :], start, 2 * size) + hot_columns(slots[1:2, :], start, 2 * size)
        part = dot_f32(hot, low).astype(jnp.bfloat16)
        first_out[...] = part[:size]
        second_out[...] = part[size:]
        start += 2 * size
    logits = dot_f32(low, router[...])
    soft = jnp.exp(logits - jnp.max(logits, axis=1, keepdims=True))
    soft = soft / jnp.sum(soft, axis=1, keepdims=True)
    expert = lax.broadcasted_iota(jnp.int32, soft.shape, 1)
    chosen = [jnp.sum(jnp.where(expert == routes[:, k : k + 1], soft, 0.0), axis=1, keepdims=True) for k in range(2)]
    for k in range(2):
        gates[:, k : k + 1] = chosen[k] / (chosen[0] + chosen[1])


def route(core, attended, tokens, mine, other, gain, router, routes, slots, pieces, count):
    length, width = tokens.shape
    last, half = mine.shape[0] - 1, mine.shape[2]
    f32, bf16 = jnp.float32, jnp.bfloat16
    weight = pl.BlockSpec((None, width, half), lambda i, core: (last, 0, 0))
    shapes = [((length, width), f32), ((length, width), bf16), ((length, 2), f32)] + [((count, width), bf16)] * pieces
    return pl.pallas_call(
        route_kernel,
        grid_spec=pltpu.PrefetchScalarGridSpec(
            num_scalar_prefetch=1,
            grid=(1,),
            in_specs=[whole((length, width)), whole((length, width)), weight, weight, whole((1, width)), whole(router.shape), whole(routes.shape), whole(slots.shape)],
            out_specs=[whole(shape) for shape, _ in shapes],
        ),
        out_shape=[jax.ShapeDtypeStruct(shape, kind) for shape, kind in shapes],
        compiler_params=pltpu.CompilerParams(vmem_limit_bytes=VMEM_BYTES),
        cost_estimate=cost(6),
        name="route",
    )(core, attended, tokens, mine, other, gain.reshape(1, -1), router, routes, slots)


def hot_route(slots, k, count):
    cols = lax.broadcasted_iota(jnp.int32, (slots.shape[0], count), 1)
    return cols == slots[:, k : k + 1]


def combine_kernel(*refs, count):
    slots, slots_t, scale = refs[:3]
    pieces = refs[3 : 3 + count]
    middle, teacher, cotangent, valid, gates, routes = refs[3 + count : 9 + count]
    output, grad_y, grad_logits, square = refs[9 + count : 13 + count]
    sends, rows = refs[13 + count : 13 + 2 * count], refs[13 + 2 * count]
    f32, bf16 = jnp.float32, jnp.bfloat16
    assemble(rows, pieces)
    table = rows[...]
    picked = [dot_f32(hot_route(slots, k, rows.shape[0]).astype(bf16), table) for k in range(2)]
    result = middle[...] + (gates[:, 0:1] * picked[0] + gates[:, 1:2] * picked[1])
    output[...] = result.astype(bf16)
    misfit = valid[...] * (result - teacher[...].astype(f32))
    square[...] = jnp.sum((misfit * misfit).reshape(-1, 8, misfit.shape[1]), axis=0)
    grad = cotangent[...].astype(f32) + misfit * scale[0, 0]
    grad_y[...] = grad
    steep = [jnp.sum(grad * picked[k], axis=1, keepdims=True) for k in range(2)]
    slack = gates[:, 0:1] * steep[0] + gates[:, 1:2] * steep[1]
    expert = lax.broadcasted_iota(jnp.int32, grad_logits.shape, 1)
    turn = [jnp.where(expert == routes[:, k : k + 1], gates[:, k : k + 1] * (steep[k] - slack), 0.0) for k in range(2)]
    grad_logits[...] = (turn[0] + turn[1]).astype(bf16)
    scaled = [(gates[:, k : k + 1] * grad).astype(bf16) for k in range(2)]
    start = 0
    for first, second in zip(sends[::2], sends[1::2]):
        size = first.shape[0]
        part = [dot_f32(hot_columns(slots_t[k : k + 1, :], start, 2 * size), scaled[k]) for k in range(2)]
        part = (part[0] + part[1]).astype(bf16)
        first[...] = part[:size]
        second[...] = part[size:]
        start += 2 * size


def combine(slots, slots_t, scale, pieces, middle, teacher, cotangent, valid, gates, routes, experts):
    length, width = middle.shape
    count = len(pieces)
    f32, bf16 = jnp.float32, jnp.bfloat16
    return pl.pallas_call(
        lambda *refs: combine_kernel(*refs, count=count),
        in_specs=[pl.BlockSpec(memory_space=pltpu.VMEM)] * 2
        + [pl.BlockSpec(memory_space=pltpu.SMEM)]
        + [pl.BlockSpec(memory_space=pltpu.VMEM)] * (6 + count),
        out_shape=[
            jax.ShapeDtypeStruct((length, width), bf16),
            jax.ShapeDtypeStruct((length, width), f32),
            jax.ShapeDtypeStruct((length, experts), bf16),
            jax.ShapeDtypeStruct((8, width), f32),
        ]
        + [jax.ShapeDtypeStruct(piece.shape, bf16) for piece in pieces],
        scratch_shapes=[pltpu.VMEM((sum(piece.shape[0] for piece in pieces), width), bf16)],
        compiler_params=pltpu.CompilerParams(vmem_limit_bytes=VMEM_BYTES),
        cost_estimate=cost(8),
        name="combine",
    )(slots, slots_t, scale, *pieces, middle, teacher, cotangent, valid, gates, routes)


def norm_back(value, gain, grad):
    root = lax.rsqrt(jnp.mean(value * value, axis=1, keepdims=True) + EPS)
    normed = value * root
    scaled = grad * gain
    inner = jnp.mean(scaled * normed, axis=1, keepdims=True)
    return root * (scaled - normed * inner), jnp.sum((grad * normed).reshape(-1, 8, value.shape[1]), axis=0)


def collect_kernel(core, *refs, count):
    slots, pieces = refs[0], refs[1 : 1 + count]
    middle, gain, grad_logits, router, grad_y, mine, other = refs[1 + count : 8 + count]
    grad_middle, rounded, grad_attended, grad_gain, rows = refs[8 + count :]
    assemble(rows, pieces)
    hot = (hot_route(slots, 0, rows.shape[0]) | hot_route(slots, 1, rows.shape[0])).astype(jnp.bfloat16)
    grad = dot_f32(grad_logits[...], router[...], NT) + dot_f32(hot, rows[...])
    turned, grad_gain[...] = norm_back(middle[...], gain[...], grad)
    result = grad_y[...] + turned
    grad_middle[...] = result
    low = result.astype(jnp.bfloat16)
    rounded[...] = low
    first, second = halves(core[0], mine[...], other[...])
    half = first.shape[1]
    grad_attended[...] = (dot_f32(low[:, :half], first, NT) + dot_f32(low[:, half:], second, NT)).astype(jnp.bfloat16)


def collect(core, slots, pieces, middle, gain, grad_logits, router, grad_y, mine, other):
    length, width = middle.shape
    last, half = mine.shape[0] - 1, mine.shape[2]
    f32, bf16 = jnp.float32, jnp.bfloat16
    weight = pl.BlockSpec((None, width, half), lambda i, core: (last, 0, 0))
    plain = [slots, *pieces, middle, gain.reshape(1, -1), grad_logits, router, grad_y]
    shapes = [((length, width), f32), ((length, width), bf16), ((length, width), bf16), ((8, width), f32)]
    return pl.pallas_call(
        lambda *refs: collect_kernel(*refs, count=len(pieces)),
        grid_spec=pltpu.PrefetchScalarGridSpec(
            num_scalar_prefetch=1,
            grid=(1,),
            in_specs=[whole(array.shape) for array in plain] + [weight, weight],
            out_specs=[whole(shape) for shape, _ in shapes],
            scratch_shapes=[pltpu.VMEM((sum(piece.shape[0] for piece in pieces), width), bf16)],
        ),
        out_shape=[jax.ShapeDtypeStruct(shape, kind) for shape, kind in shapes],
        compiler_params=pltpu.CompilerParams(vmem_limit_bytes=VMEM_BYTES),
        cost_estimate=cost(8),
        name="collect",
    )(core, *plain, mine, other)


def outer_halves_kernel(core, normed, attended, rights, last, *refs, count):
    aways, stays, normed_t, attended_t = refs[:2], refs[2:4], refs[4], refs[5]
    step = pl.program_id(0)

    @pl.when(step == 0)
    def _():
        normed_t[...] = normed[...].T
        attended_t[...] = attended[...].T

    for place in range(count + 1):

        @pl.when(step == place)
        def _():
            result = dot_f32(normed_t[...], rights[...]) if place < count else dot_f32(attended_t[...], last[...])
            result = result.astype(jnp.bfloat16)
            half = result.shape[1] // 2
            away, stay = aways[place // 2], stays[place // 2]
            slot = place % 2

            @pl.when(core[0] == 0)
            def _():
                stay[slot] = result[:, :half]
                away[slot] = result[:, half:]

            @pl.when(core[0] != 0)
            def _():
                away[slot] = result[:, :half]
                stay[slot] = result[:, half:]


def outer_halves(core, normed, attended, rights, last):
    length, width = normed.shape
    count, half = rights.shape[0], width // 2
    shape = jax.ShapeDtypeStruct((2, width, half), jnp.bfloat16)
    return pl.pallas_call(
        lambda *refs: outer_halves_kernel(*refs, count=count),
        grid_spec=pltpu.PrefetchScalarGridSpec(
            num_scalar_prefetch=1,
            grid=(count + 1,),
            in_specs=[
                whole((length, width)),
                whole((length, width)),
                pl.BlockSpec((None, length, width), lambda i, core: (jnp.minimum(i, count - 1), 0, 0)),
                whole((length, width)),
            ],
            out_specs=[whole(shape.shape)] * 4,
            scratch_shapes=[pltpu.VMEM((width, length), jnp.bfloat16)] * 2,
        ),
        out_shape=[shape] * 4,
        compiler_params=pltpu.CompilerParams(vmem_limit_bytes=VMEM_BYTES),
        cost_estimate=cost(6),
        name="outer_halves",
    )(core, normed, attended, rights, last)


def enter_kernel(core, grads, mine, other, tokens, gain, grad_middle, grad_input, grad_gain, total):
    step = pl.program_id(0)
    first, second = halves(core[0], mine[...], other[...])
    half = first.shape[1]
    rows = grads[...]
    part = dot_f32(rows[:, :half], first, NT) + dot_f32(rows[:, half:], second, NT)

    @pl.when(step == 0)
    def _():
        total[...] = part

    @pl.when(step > 0)
    def _():
        total[...] += part

    @pl.when(step == pl.num_programs(0) - 1)
    def _():
        turned, grad_gain[...] = norm_back(tokens[...].astype(jnp.float32), gain[...], total[...])
        grad_input[...] = grad_middle[...] + turned


def enter(core, grads, mine, other, tokens, gain, grad_middle):
    length, width = tokens.shape
    count, half = grads.shape[0], mine.shape[2]
    weight = pl.BlockSpec((None, width, half), lambda i, core: (i, 0, 0))
    return pl.pallas_call(
        enter_kernel,
        grid_spec=pltpu.PrefetchScalarGridSpec(
            num_scalar_prefetch=1,
            grid=(count,),
            in_specs=[pl.BlockSpec((None, length, width), lambda i, core: (i, 0, 0)), weight, weight, whole((length, width)), whole((1, width)), whole((length, width))],
            out_specs=[whole((length, width)), whole((8, width))],
            scratch_shapes=[pltpu.VMEM((length, width), jnp.float32)],
        ),
        out_shape=[jax.ShapeDtypeStruct((length, width), jnp.float32), jax.ShapeDtypeStruct((8, width), jnp.float32)],
        compiler_params=pltpu.CompilerParams(vmem_limit_bytes=VMEM_BYTES),
        cost_estimate=cost(6),
        name="enter",
    )(core, grads, mine, other, tokens, gain.reshape(1, -1), grad_middle)


BOUNDS = (12, 16, 23, 32, 46, 64, 91)
TOP_PRECISION = lax.Precision.HIGHEST
AXES = ("dp", "expert")
PAIR = 2


def after(value, *others):
    return lax.optimization_barrier((value, *others))[0] if others else value


def bucket_index(offset):
    distance = jnp.abs(offset)
    far_bucket = 8 + sum([(distance >= level).astype(jnp.int32) for level in BOUNDS])
    near_bucket = jnp.where(distance < 8, distance, far_bucket)
    return jnp.where(offset > 0, 16, 0) + near_bucket


def norm_apply(inputs, gain_vec):
    return inputs * lax.rsqrt(jnp.mean(inputs * inputs, axis=-1, keepdims=True) + EPS) * gain_vec


def tile_offsets(query_block, key_block):
    rows = query_block * BLOCK + lax.broadcasted_iota(jnp.int32, (BLOCK, BLOCK), 0)
    cols = key_block * BLOCK + lax.broadcasted_iota(jnp.int32, (BLOCK, BLOCK), 1)
    return rows, cols


def offset_bias(table):
    offsets = jnp.arange(4 * BLOCK, dtype=jnp.int32) - 2 * BLOCK
    hot = (bucket_index(offsets)[None] == jnp.arange(table.shape[1], dtype=jnp.int32)[:, None]).astype(jnp.float32)
    return jnp.dot(table, hot, precision=TOP_PRECISION)


def table_gradient(bands, buckets):
    rows, cols = tile_offsets(0, 0)
    ids = [jnp.full((BLOCK, BLOCK), bucket_far(), jnp.int32)]
    ids += [bucket_index(shift * BLOCK + cols - rows) for shift in (-1, 0, 1)]
    hot = (jnp.stack(ids)[..., None] == jnp.arange(buckets, dtype=jnp.int32)).astype(jnp.float32)
    return jnp.einsum("hdxy,dxyb->hb", bands, hot, precision=TOP_PRECISION)


def bucket_far():
    return 8 + len(BOUNDS)


def on_device(
    tokens,
    qkv_weight,
    out_weight,
    position_bias_table,
    gain_attn,
    gain_moe,
    router,
    w_in,
    w_out,
    routes,
    prefix,
    valid_mask,
    teacher,
    cotangent,
):
    length, width = tokens.shape
    bf16, f32 = jnp.bfloat16, jnp.float32
    expert_count = router.shape[1]
    top_count = routes.shape[1]
    groups = lax.axis_size("expert")
    copies = lax.axis_size("dp")
    inner = w_in.shape[2]
    capacity = 5 * length * top_count // (4 * expert_count)
    total_tokens = length * copies * groups
    sources = 2 * groups
    blocks = length // BLOCK
    here_dp, here_group = lax.axis_index("dp"), lax.axis_index("expert")
    half = (here_dp >> 1) & 1
    core = here_group & 1
    rest = copies // 4

    def swap(value, dp_mask, group_mask):
        pairs = [
            (i, ((i // groups) ^ dp_mask) * groups + ((i % groups) ^ group_mask))
            for i in range(copies * groups)
        ]
        return lax.ppermute(value, AXES, pairs)

    def bits(count):
        return [1 << place for place in range(count.bit_length() - 1)]

    def partial_sums(value):
        sums = []
        for masks in [(0, mask) for mask in bits(groups)] + [(mask, 0) for mask in bits(copies)]:
            value = value + swap(value, *masks)
            sums.append(value)
        return sums

    chips = groups

    def across(value, place):
        return swap(value, PAIR * (place // (groups // 2)), 2 * (place % (groups // 2)))

    def to_chips(pieces):
        return [pieces[0]] + [across(pieces[place], place) for place in range(1, chips)]

    def through(visit, sends):
        direct, relay = to_chips(sends[::2]), to_chips(sends[1::2])
        seen, direct = visit(direct)
        direct = to_chips(direct)
        relay = [after(part, seen) for part in relay]
        passed = visit(swap(jnp.concatenate(relay), 0, 1))
        passed = swap(after(passed, *direct), 0, 1)
        relay = [passed[place * capacity : (place + 1) * capacity] for place in range(chips)]
        return direct, relay

    def weave(direct, relay):
        return [part for pair in zip(direct, to_chips(relay)) for part in pair]

    ring = list(range(0, copies, 2)) + list(range(copies - 1, 0, -2))
    turns = [(1, step) for step in range(1, copies // 2 + 1)] + [(-1, step) for step in range(1, copies // 2)]

    def gather_ring(shard, due):
        got = [shard]
        for turn in (1, -1):
            held = shard
            pairs = [(ring[i], ring[(i + turn) % copies]) for i in range(copies)]
            for step in [step for way, step in turns if way == turn]:
                held = lax.ppermute(after(held, *due[step - 2 : step - 1]) if step > 1 else held, "dp", pairs)
                got.append(held)
        return got

    def ring_places():
        place = jnp.where(here_dp & 1 == 0, here_dp >> 1, copies - 1 - (here_dp >> 1))
        shift = jnp.array([0] + [turn * step for turn, step in turns], jnp.int32)
        place = (place - shift) & (copies - 1)
        return jnp.where(place < copies // 2, 2 * place, 2 * (copies - 1 - place) + 1).astype(jnp.int32)


    flat_routes = routes.reshape(-1)
    pair_count = length * top_count
    slot_count = sources * capacity
    route_hits = (flat_routes[:, None] == jnp.arange(expert_count, dtype=jnp.int32)[None, :]).astype(bf16)
    lower_ones = (
        lax.broadcasted_iota(jnp.int32, (pair_count, pair_count), 0)
        >= lax.broadcasted_iota(jnp.int32, (pair_count, pair_count), 1)
    ).astype(bf16)
    running = jnp.dot(lower_ones, route_hits, preferred_element_type=f32)
    pair_rank = jnp.sum((running - 1.0) * route_hits.astype(f32), axis=1).astype(jnp.int32)
    away = (flat_routes >> 1) ^ here_group
    chip = ((flat_routes & 1) ^ half) * (groups // 2) + (away >> 1)
    slots = ((chip * 2 + (away & 1)) * capacity + pair_rank).reshape(length, top_count)
    slots_t = slots.T

    resid = tokens.astype(f32)
    normed1 = norm_apply(resid, gain_attn).astype(bf16)
    columns = width // 2
    core_index = core.reshape(1).astype(jnp.int32)
    valid_rows = valid_mask.astype(f32)[:, None]
    counts = [jnp.broadcast_to(jnp.sum(valid_rows), (8, 128))]
    count_trades = [(0, mask) for mask in bits(groups)] + [(mask, 0) for mask in bits(copies)]

    def count_beside(before, value):
        if len(counts) > len(count_trades):
            return value
        counts.append(counts[-1] + swap(after(counts[-1], before), *count_trades[len(counts) - 1]))
        return after(value, counts[-1])

    shards = [
        lax.dynamic_slice_in_dim(part, core * columns, columns, 2)
        for part in (qkv_weight[:2], jnp.concatenate([qkv_weight[2:], out_weight[None]]))
    ]
    if copies > 8:
        mine = lax.all_gather(jnp.concatenate(shards), "dp", axis=1, tiled=True)
    else:
        mine = join(ring_places(), [gather_ring(shards[0], ()), gather_ring(shards[1], (slots_t, normed1))])
    other = count_beside(mine, swap(mine, 0, 1))
    qkv_rows = count_beside(other, project(core_index, normed1, mine, other, 3))
    offsets = offset_bias(position_bias_table)
    attended, probs = attention_forward(position_bias_table[:, bucket_far()], prefix, qkv_rows, offsets)
    middle, normed2, gates, *sends = route(
        core_index, count_beside(qkv_rows, attended), tokens, mine, other, gain_moe, router, routes, slots_t, 2 * chips, capacity
    )

    pick = half.reshape(1).astype(jnp.int32)
    hidden, slopes, rows_in = [], [], []

    def expert(pieces):
        one = not isinstance(pieces, list)
        pieces = [pieces] if one else pieces
        hidden_t, slope, rows_t, *results = expert_forward(pick, pieces, w_in, w_out)
        hidden_t = count_beside(pieces[-1], hidden_t)
        for kept, value in zip((hidden, slopes, rows_in), (hidden_t, slope, rows_t)):
            kept.append(value)
        return results[0] if one else (hidden_t, results)

    back = weave(*through(expert, sends))
    while len(counts) <= len(count_trades):
        back[0] = count_beside(back[0], back[0])
    valid_count = counts[-1][0, 0]
    scale = (total_tokens / valid_count).reshape(1, 1)
    output, grad_y, grad_logits, squares, *sends = combine(
        slots, slots_t, scale, back, middle, teacher, cotangent, valid_rows, gates, routes, expert_count
    )

    out_rows = inner // copies
    in_rows = width // copies
    far_bit = here_dp % 2
    slices = jnp.arange(rest, dtype=jnp.int32) * 4

    def picks(bit0):
        return jnp.concatenate([slices + ((half ^ other_half) * 2 + bit0) for other_half in (1, 0)]).astype(jnp.int32)

    sent, kept = picks(1 - far_bit), picks(far_bit)

    def add(left, right):
        return (left.astype(f32) + right.astype(f32)).astype(bf16)

    def fold(unit, bit, axis=0):
        unit = unit.reshape(unit.shape[:axis] + (2, unit.shape[axis] // 2) + unit.shape[axis + 1 :])
        away_part = lax.dynamic_index_in_dim(unit, 1 - bit, axis, keepdims=False)
        return away_part, lax.dynamic_index_in_dim(unit, bit, axis, keepdims=False)

    far_masks = list(reversed(bits(copies)[2:]))

    def near_add(got, keep):
        away_part, stay_part = fold(add(got, keep), (here_dp // far_masks[0]) % 2)
        return away_part, stay_part

    def far_trade(away_part):
        return swap(away_part, far_masks[0], 0)

    def finish(got, stay):
        unit = add(got, stay)
        for mask in far_masks[1:]:
            away_part, stay_part = fold(unit, (here_dp // mask) % 2)
            unit = add(swap(away_part, mask, 0), stay_part)
        return unit[0]

    plan_a, plan_b, plan_c = ((0, 0),), ((0, 1), (0, 2)), ((1, 0), (1, 1), (1, 2))
    plan_d, plan_e, plan_f = ((0, 0), (0, 1)), ((0, 2), (1, 0)), ((1, 1), (1, 2))
    out_plans, in_plans = (plan_a, plan_b, plan_c), (plan_d, plan_e, plan_f)

    grad_rows, grad_pre = [], []

    def expert_back(pieces):
        if isinstance(pieces, list):
            grad_pre_rows, grads, *results = expert_backward(pick, pieces, w_in, w_out, slopes[0])
            grad_rows.append(grads)
            grad_pre.append(grad_pre_rows)
            return grad_pre_rows, results
        grad_rows.append(pieces)
        grad_pre_rows, _, results = expert_backward(pick, [pieces], w_in, w_out, slopes[1])
        grad_pre.append(grad_pre_rows)
        return results

    direct, relay = through(expert_back, sends)
    back = weave(direct, relay)
    grad_rows = lax.optimization_barrier((grad_rows, relay))[0]
    send_a, send_b, send_c = weight_part(sent, hidden, grad_rows, out_rows, out_plans, rest, width)
    got_a = swap(send_a, 1, 0)
    keep_a, keep_b, keep_c = weight_part(kept, hidden, after(grad_rows, send_a), out_rows, out_plans, rest, width)
    back = [after(part, keep_a) for part in back]
    got_b = swap(after(send_b, keep_a), 1, 0)
    grad_middle, grad_attn_proj, grad_attended, gain_moe_parts = collect(
        core_index, slots, back, middle, gain_moe, grad_logits, router, grad_y, mine, other
    )
    got_c = swap(after(send_c, grad_attended), 1, 0)
    away_a, stay_a = near_add(after(got_a, grad_attended), keep_a)
    far_a = far_trade(away_a)
    grad_qkv_rows, bands = attention_backward(qkv_rows, after(grad_attended, away_a), probs)
    grad_qkv_rows, got_b = lax.optimization_barrier((grad_qkv_rows, got_b))

    away_b, stay_b = near_add(got_b, keep_b)
    far_b = far_trade(away_b)
    *weights_away, stay_1, stay_2 = outer_halves(
        core_index, normed1, attended, after(grad_qkv_rows, away_b), grad_attn_proj
    )
    weights_away = lax.optimization_barrier((weights_away, far_a))[0]
    done_a = finish(far_a, stay_a)
    send_d, send_e, send_f = weight_part(sent, rows_in, after(grad_pre, *weights_away), in_rows, in_plans, rest, inner // 2)
    away_c, stay_c = near_add(after(got_c, send_d), keep_c)
    far_c = far_trade(away_c)
    got_d = swap(send_d, 1, 0)
    got_e = swap(after(send_e, away_c), 1, 0)
    group_masks = bits(groups)[1:]
    dp_masks = sorted(bits(copies), key=lambda mask: (mask != PAIR, mask))

    def over_groups(got, stay, *due):
        got = add(after(got, *due), stay).reshape(2, copies, in_rows, columns)
        for mask in group_masks[:-1]:
            away_part, stay_part = fold(got, (here_group // mask) % 2, 2)
            got = add(swap(away_part, 0, mask), stay_part)
        away_part, stay_part = fold(got, (here_group // group_masks[-1]) % 2, 2)
        return swap(away_part, 0, group_masks[-1]), stay_part

    def over_dp(total, mask, passed):
        axis = 1 + sorted([other for other in dp_masks if other not in passed], reverse=True).index(mask)
        bit = (here_dp // mask) % 2
        away_part = lax.dynamic_index_in_dim(total, 1 - bit, axis, keepdims=False)
        stay_part = lax.dynamic_index_in_dim(total, bit, axis, keepdims=False)
        return swap(away_part, mask, 0), stay_part

    weights_got = [swap(part, 0, 1) for part in weights_away]
    first = over_groups(weights_got[0], stay_1, away_c)
    second = over_groups(weights_got[1], stay_2, first[1])
    keep_d, keep_e, keep_f = weight_part(
        kept, rows_in, after(grad_pre, second[1]), in_rows, in_plans, rest, inner // 2
    )
    grad_input, gain_attn_parts = enter(
        core_index, after(grad_qkv_rows, keep_d), mine, other, tokens, gain_attn, grad_middle
    )
    away_d, stay_d = near_add(after(got_d, gain_attn_parts), keep_d)
    far_d = far_trade(away_d)
    got_f = swap(after(send_f, away_d, gain_attn_parts), 1, 0)
    done_b = finish(after(far_b, second[1]), stay_b)
    grad_table = table_gradient(after(bands, second[1]), position_bias_table.shape[1])

    chains = [add(after(first[0], away_d, gain_attn_parts), first[1]).reshape((2,) + (2,) * len(dp_masks) + (-1, columns)), None]
    trades = [over_dp(chains[0], dp_masks[0], ()), None]
    chains[1] = add(after(second[0], done_b, grad_table), second[1]).reshape(chains[0].shape)
    trades[1] = over_dp(chains[1], dp_masks[0], ())
    trades[0] = (after(trades[0][0], trades[1][1]), trades[0][1])
    total = trades[1][1]
    away_e, stay_e = near_add(after(got_e, total), keep_e)
    far_e = far_trade(away_e)
    trades[1] = (after(trades[1][0], away_e), trades[1][1])

    normed2, squares, gain_moe_parts = after((normed2, squares, gain_moe_parts), second[1])
    grad_router = jnp.einsum("td,te->de", normed2, grad_logits, preferred_element_type=f32)
    small = [
        jnp.sum(gain_moe_parts, axis=0),
        jnp.sum(gain_attn_parts, axis=0),
        grad_router,
        grad_table,
        jnp.sum(squares),
    ]
    sizes = [value.size for value in small]
    flat = jnp.concatenate([value.reshape(-1) for value in small])
    flat = after(jnp.pad(flat, (0, -sum(sizes) % 1024)).reshape(-1, 128), total)

    flat = flat + swap(flat, 0, 1)
    for place, mask in enumerate(dp_masks):
        flat_got = swap(flat, 0, group_masks[0]) if mask == PAIR else swap(flat, mask, 0)
        chains = [add(*trades[0]), None]
        if place + 1 < len(dp_masks):
            trades_next = [over_dp(chains[0], dp_masks[place + 1], dp_masks[: place + 1]), None]
        chains[1] = add(after(trades[1][0], chains[0]), trades[1][1])
        flat = flat + flat_got
        if place + 1 < len(dp_masks):
            trades_next[1] = over_dp(chains[1], dp_masks[place + 1], dp_masks[: place + 1])
            trades = trades_next
        if mask == PAIR:
            done_c = finish(after(far_c, chains[1]), stay_c)
            done_d = finish(after(far_d, chains[1]), stay_d)
            in_first = swap(done_d, PAIR, 0)
            out_theirs = swap(after(jnp.concatenate([done_a, done_b]), chains[1]), PAIR, 0)
            away_f, stay_f = near_add(after(got_f, chains[1]), keep_f)
            far_f = far_trade(away_f)
        flat = after(flat, chains[1])
    total = jnp.concatenate(chains)
    done_e = finish(after(far_e, total), stay_e)
    in_theirs = jnp.concatenate([in_first, swap(done_e[:1], PAIR, 0)])
    for mask in reversed(group_masks):
        bit = (here_group // mask) % 2
        other_part = swap(total, 0, mask)
        total = jnp.concatenate([jnp.where(bit == 0, total, other_part), jnp.where(bit == 0, other_part, total)], axis=1)
        if mask == group_masks[0]:
            done_f = finish(after(far_f, total), stay_f)
            total = after(total, done_f)
            flat = flat + swap(flat, PAIR, 0)
        else:
            flat = flat + swap(flat, 0, mask)
        total, flat = lax.optimization_barrier((total, flat))
    other_part = swap(total, 0, 1)
    total = jnp.concatenate([jnp.where(core == 0, total, other_part), jnp.where(core == 0, other_part, total)], axis=2)
    weights_done = total.astype(f32)
    grad_qkv, grad_out_weight = weights_done[:3], weights_done[3]
    flat = flat.reshape(-1)
    starts = [sum(sizes[:place]) for place in range(len(sizes))]
    grad_gain_moe, grad_gain_attn, grad_router, grad_table, square_total = [
        flat[start : start + value.size].reshape(value.shape) for start, value in zip(starts, small)
    ]

    out_mine, in_mine = done_c, jnp.concatenate([done_e[1:], done_f])

    def both_experts(mine, theirs):
        mine, theirs = [part.reshape(-1, part.shape[-1]).astype(f32) for part in (mine, theirs)]
        return jnp.stack([jnp.where(half == 0, mine, theirs), jnp.where(half == 0, theirs, mine)])

    grad_w_out = both_experts(out_mine, out_theirs)
    grad_w_in = both_experts(in_mine, in_theirs)

    distill_loss = square_total / (width * valid_count)
    return (
        output.astype(bf16),
        distill_loss,
        grad_input,
        grad_qkv,
        grad_out_weight,
        grad_w_in,
        grad_w_out,
        grad_router,
        grad_table,
        grad_gain_attn,
        grad_gain_moe,
    )


def solution(mesh):
    rows = P(AXES, None)
    return jax.shard_map(
        on_device,
        mesh=mesh,
        in_specs=(
            rows,
            P(None, "dp", None),
            P("dp", None),
            P(),
            P(),
            P(),
            P(),
            P("expert", None, None),
            P("expert", None, None),
            rows,
            P(AXES),
            P(AXES),
            rows,
            rows,
        ),
        out_specs=(
            rows,
            P(),
            rows,
            P(None, "dp", None),
            P("dp", None),
            P("expert", "dp", None),
            P("expert", "dp", None),
            P(),
            P(),
            P(),
            P(),
        ),
        check_vma=False,
    )
```

```python
import math
import jax
import jax.numpy as jnp
from jax import lax
from jax.experimental import pallas as pl
from jax.experimental.pallas import tpu as pltpu
from jax.sharding import PartitionSpec as P

BLOCK = 128
THIRDS = 3
EPS = 1e-06
GELU_A = math.sqrt(2.0 / math.pi)
GELU_B = 0.044715
NT = (((1,), (1,)), ((), ()))
TN = (((0,), (0,)), ((), ()))
VMEM_BYTES = 56 * 1024 * 1024


def cost(micros):
    return pl.CostEstimate(flops=int(micros * 0.37e9), bytes_accessed=0, transcendentals=0)


def dot_f32(left, right, dims=(((1,), (0,)), ((), ()))):
    return lax.dot_general(left, right, dims, preferred_element_type=jnp.float32)


def assemble(rows, pieces):
    start = 0
    for piece in pieces:
        rows[pl.ds(start, piece.shape[0]), :] = piece[...]
        start += piece.shape[0]


def hand_out(total, outs):
    start = 0
    for out in outs:
        out[...] = total[pl.ds(start, out.shape[0]), :].astype(out.dtype)
        start += out.shape[0]


def whole(shape):
    return pl.BlockSpec(shape, lambda *step: (0,) * len(shape))


def expert_forward_kernel(pick, *refs, chunk, count):
    pieces, w_in, w_out = refs[:count], refs[count], refs[count + 1]
    hidden_t, slope, rows_t = refs[count + 2 : count + 5]
    outs, rows, total = refs[count + 5 : -2], refs[-2], refs[-1]
    step = pl.program_id(0)

    @pl.when(step == 0)
    def _():
        assemble(rows, pieces)
        total[...] = jnp.zeros_like(total)
        rows_t[...] = rows[...].T

    for start in range(0, rows.shape[0], chunk):
        part = pl.ds(start, chunk)
        pre = dot_f32(rows[part, :], w_in[0])
        square = pre * pre
        bend = jnp.tanh(pre * (GELU_A + (GELU_A * GELU_B) * square))
        half = 0.5 + 0.5 * bend
        act = (pre * half).astype(jnp.bfloat16)
        lift = pre * (0.5 * GELU_A + (1.5 * GELU_A * GELU_B) * square)
        slope[part, :] = (half + lift * (1.0 - bend * bend)).astype(jnp.bfloat16)
        hidden_t[:, part] = act.T
        total[part, :] += dot_f32(act, w_out[0])

    @pl.when(step == pl.num_programs(0) - 1)
    def _():
        hand_out(total, outs)


def expert_forward(pick, pieces, results, w_in, w_out, tile=768, chunk=320):
    many, width = sum(piece.shape[0] for piece in pieces), pieces[0].shape[1]
    inner = w_in.shape[2]
    bf16 = jnp.bfloat16
    return pl.pallas_call(
        lambda *refs: expert_forward_kernel(*refs, chunk=chunk, count=len(pieces)),
        grid_spec=pltpu.PrefetchScalarGridSpec(
            num_scalar_prefetch=1,
            grid=(inner // tile,),
            in_specs=[whole(piece.shape) for piece in pieces]
            + [
                pl.BlockSpec((1, width, tile), lambda f, pick: (pick[0], 0, f)),
                pl.BlockSpec((1, tile, width), lambda f, pick: (pick[0], f, 0)),
            ],
            out_specs=[
                pl.BlockSpec((tile, many), lambda f, pick: (f, 0)),
                pl.BlockSpec((many, tile), lambda f, pick: (0, f)),
                whole((width, many)),
            ]
            + [whole((many // results, width))] * results,
            scratch_shapes=[pltpu.VMEM((many, width), bf16), pltpu.VMEM((many, width), jnp.float32)],
        ),
        out_shape=[
            jax.ShapeDtypeStruct((inner, many), bf16),
            jax.ShapeDtypeStruct((many, inner), bf16),
            jax.ShapeDtypeStruct((width, many), bf16),
        ]
        + [jax.ShapeDtypeStruct((many // results, width), bf16)] * results,
        compiler_params=pltpu.CompilerParams(vmem_limit_bytes=VMEM_BYTES),
        cost_estimate=cost(13),
        name="expert_forward",
    )(pick, *pieces, w_in, w_out)


def expert_backward_kernel(pick, *refs, chunk, count):
    pieces, w_in, w_out, slope = refs[:count], refs[count], refs[count + 1], refs[count + 2]
    grad_pre, rows = refs[count + 3 : count + 5]
    outs, total = refs[count + 5 : -1], refs[-1]
    step = pl.program_id(0)

    @pl.when(step == 0)
    def _():
        assemble(rows, pieces)
        total[...] = jnp.zeros_like(total)

    for start in range(0, rows.shape[0], chunk):
        part = pl.ds(start, chunk)
        back = dot_f32(rows[part, :], w_out[0], NT) * slope[part, :].astype(jnp.float32)
        back = back.astype(jnp.bfloat16)
        grad_pre[part, :] = back
        total[part, :] += dot_f32(back, w_in[0], NT)

    @pl.when(step == pl.num_programs(0) - 1)
    def _():
        hand_out(total, outs)


def expert_backward(pick, pieces, results, w_in, w_out, slope, tile=768, chunk=640):
    many, width = sum(piece.shape[0] for piece in pieces), pieces[0].shape[1]
    inner = w_in.shape[2]
    bf16 = jnp.bfloat16
    return pl.pallas_call(
        lambda *refs: expert_backward_kernel(*refs, chunk=chunk, count=len(pieces)),
        grid_spec=pltpu.PrefetchScalarGridSpec(
            num_scalar_prefetch=1,
            grid=(inner // tile,),
            in_specs=[whole(piece.shape) for piece in pieces]
            + [
                pl.BlockSpec((1, width, tile), lambda f, pick: (pick[0], 0, f)),
                pl.BlockSpec((1, tile, width), lambda f, pick: (pick[0], f, 0)),
                pl.BlockSpec((many, tile), lambda f, pick: (0, f)),
            ],
            out_specs=[pl.BlockSpec((many, tile), lambda f, pick: (0, f)), whole((many, width))]
            + [whole((many // results, width))] * results,
            scratch_shapes=[pltpu.VMEM((many, width), jnp.float32)],
        ),
        out_shape=[jax.ShapeDtypeStruct((many, inner), bf16), jax.ShapeDtypeStruct((many, width), bf16)]
        + [jax.ShapeDtypeStruct((many // results, width), bf16)] * results,
        compiler_params=pltpu.CompilerParams(vmem_limit_bytes=VMEM_BYTES),
        cost_estimate=cost(11),
        name="expert_backward",
    )(pick, *pieces, w_in, w_out, slope)


def seen_blocks(row_block, blocks):
    return max(row_block + 1, blocks // 2)


def attention_forward_kernel(far, prefix, queries, keys, values, offsets, attended, probs, *, heads, blocks):
    pair = pl.program_id(0)
    lane = lax.broadcasted_iota(jnp.int32, queries.shape, 1)
    row = lax.broadcasted_iota(jnp.int32, (BLOCK, BLOCK), 0)
    col = lax.broadcasted_iota(jnp.int32, (BLOCK, BLOCK), 1)
    outs = []
    for head in range(2):
        line = jnp.broadcast_to(offsets[head : head + 1, :], (BLOCK, 4 * BLOCK))
        turned = pltpu.roll(line, 0, 1, stride=1, stride_axis=0)
        far_bias = far[pair * 2 + head]
        mine = (lane < heads) if head == 0 else (lane >= heads)
        query = jnp.where(mine, queries[...] * 0.125, 0.0).astype(jnp.bfloat16)
        score = dot_f32(query, keys[...], NT)
        strips = []
        for row_block in range(blocks):
            span = seen_blocks(row_block, blocks)
            pieces = []
            for key_block in range(span):
                piece = score[row_block * BLOCK : (row_block + 1) * BLOCK, key_block * BLOCK : (key_block + 1) * BLOCK]
                shift = key_block - row_block
                if shift < -1:
                    piece = piece + far_bias
                elif shift < 2:
                    piece = piece + turned[:, (2 + shift) * BLOCK : (3 + shift) * BLOCK]
                else:
                    raise ValueError(shift)
                if shift >= 0:
                    shown = col + key_block * BLOCK < prefix[0]
                    piece = jnp.where((shown | (col <= row)) if shift == 0 else shown, piece, -1e30)
                pieces.append(piece)
            peak = pieces[0]
            for piece in pieces[1:]:
                peak = jnp.maximum(peak, piece)
            peak = jnp.max(peak, axis=1, keepdims=True)
            pieces = [jnp.exp(piece - peak) for piece in pieces]
            mass = pieces[0]
            for piece in pieces[1:]:
                mass = mass + piece
            scale = 1.0 / jnp.sum(mass, axis=1, keepdims=True)
            pieces = [(piece * scale).astype(jnp.bfloat16) for piece in pieces]
            pieces += [jnp.zeros((BLOCK, BLOCK), jnp.bfloat16)] * (blocks - span)
            strips.append(jnp.concatenate(pieces, axis=1))
        weights = jnp.concatenate(strips, axis=0)
        probs[head] = weights
        outs.append(dot_f32(weights, values[...]))
    attended[...] = jnp.where(lane < heads, outs[0], outs[1]).astype(jnp.bfloat16)


def attention_forward(far, prefix, qkv_rows, offsets):
    length, width = qkv_rows.shape[1:]
    pairs = width // 128
    blocks = length // BLOCK
    return pl.pallas_call(
        lambda *refs: attention_forward_kernel(*refs, heads=64, blocks=blocks),
        grid_spec=pltpu.PrefetchScalarGridSpec(
            num_scalar_prefetch=2,
            grid=(pairs,),
            in_specs=[pl.BlockSpec((None, length, 128), lambda h, far, prefix, c=c: (c, 0, h)) for c in range(3)]
            + [pl.BlockSpec((None, 2, 4 * BLOCK), lambda h, far, prefix: (h, 0, 0))],
            out_specs=[
                pl.BlockSpec((length, 128), lambda h, far, prefix: (0, h)),
                pl.BlockSpec((2, length, length), lambda h, far, prefix: (h, 0, 0)),
            ],
        ),
        out_shape=[
            jax.ShapeDtypeStruct((length, width), jnp.bfloat16),
            jax.ShapeDtypeStruct((2 * pairs, length, length), jnp.bfloat16),
        ],
        compiler_params=pltpu.CompilerParams(vmem_limit_bytes=VMEM_BYTES),
        cost_estimate=cost(13),
        name="attention_forward",
    )(far, prefix, qkv_rows, qkv_rows, qkv_rows, offsets.reshape(pairs, 2, 4 * BLOCK))


def attention_backward_kernel(queries, keys, values, grads, probs, grad_rows, bands, *, heads, blocks):
    lane = lax.broadcasted_iota(jnp.int32, queries.shape, 1)
    query_t = (queries[...] * 0.125).astype(jnp.bfloat16).T
    grad_t = grads[...].T
    dq, dk, dv = [], [], []
    for head in range(2):
        mine = (lane < heads) if head == 0 else (lane >= heads)
        sums = [None] * 4
        grad = jnp.where(mine, grads[...], 0.0).astype(jnp.bfloat16)
        back = dot_f32(grad, values[...], NT)
        strips = []
        for row_block in range(blocks):
            span = seen_blocks(row_block, blocks)
            rows = slice(row_block * BLOCK, (row_block + 1) * BLOCK)
            soft = probs[head, pl.ds(row_block * BLOCK, BLOCK), pl.ds(0, span * BLOCK)].astype(jnp.float32)
            part = back[rows, : span * BLOCK]
            inner = jnp.sum(soft * part, axis=1, keepdims=True)
            score_grad = (soft * (part - inner)).astype(jnp.bfloat16)
            for key_block in range(span):
                band = max(key_block - row_block, -2)
                tile = score_grad[:, key_block * BLOCK : (key_block + 1) * BLOCK].astype(jnp.float32)
                sums[band + 2] = tile if sums[band + 2] is None else sums[band + 2] + tile
            if span < blocks:
                rest = jnp.zeros((BLOCK, (blocks - span) * BLOCK), jnp.bfloat16)
                score_grad = jnp.concatenate([score_grad, rest], axis=1)
            strips.append(score_grad)
        flow = jnp.concatenate(strips, axis=0)
        for band in range(4):
            bands[head, band] = sums[band]
        part = slice(head * heads, (head + 1) * heads)
        dq.append(dot_f32(flow, keys[...]) * 0.125)
        dk.append(dot_f32(query_t[part], flow))
        dv.append(dot_f32(grad_t[part], probs[head]))
    grad_rows[0] = jnp.where(lane < heads, dq[0], dq[1]).astype(jnp.bfloat16)
    grad_rows[1] = jnp.concatenate(dk, axis=0).T.astype(jnp.bfloat16)
    grad_rows[2] = jnp.concatenate(dv, axis=0).T.astype(jnp.bfloat16)


def attention_backward(qkv_rows, grads, probs):
    length, width = grads.shape
    pairs = width // 128
    blocks = length // BLOCK
    block = pl.BlockSpec((length, 128), lambda h: (0, h))
    of_three = [pl.BlockSpec((None, length, 128), lambda h, c=c: (c, 0, h)) for c in range(3)]
    return pl.pallas_call(
        lambda *refs: attention_backward_kernel(*refs, heads=64, blocks=blocks),
        grid=(pairs,),
        in_specs=[*of_three, block, pl.BlockSpec((2, length, length), lambda h: (h, 0, 0))],
        out_specs=[pl.BlockSpec((3, length, 128), lambda h: (0, 0, h)), pl.BlockSpec((2, 4, BLOCK, BLOCK), lambda h: (h, 0, 0, 0))],
        out_shape=[jax.ShapeDtypeStruct((3, length, width), jnp.bfloat16)]
        + [jax.ShapeDtypeStruct((2 * pairs, 4, BLOCK, BLOCK), jnp.float32)],
        compiler_params=pltpu.CompilerParams(vmem_limit_bytes=VMEM_BYTES),
        cost_estimate=cost(12),
        name="attention_backward",
    )(qkv_rows, qkv_rows, qkv_rows, grads, probs)


def pieces_left(lefts, plans, many):
    part = lefts[0][0].shape[0] // THIRDS
    return jnp.concatenate(
        [
            jnp.concatenate([ref[pl.ds(third * part, part), :] for ref in lefts[group * many + k]], axis=1)
            for plan in plans
            for group, third in plan
            for k in range(many)
        ]
    )


def put_pieces(result, outs):
    place = 0
    for out in outs:
        many, pieces, part = out.shape[:3]
        for piece in range(pieces):
            for k in range(many):
                out[k, piece] = result[place : place + part]
                place += part


def weight_part_kernel(picks, *refs, count, plans, many):
    lefts, rights, outs = refs[: 2 * count], refs[2 * count : 2 * count + 2], refs[2 * count + 2 :]
    left = pieces_left(list(zip(lefts[:count], lefts[count:])), plans, many)
    right = jnp.concatenate([ref[...] for ref in rights], axis=0)
    put_pieces(dot_f32(left, right).astype(jnp.bfloat16), outs)


def weight_part_plain(picks, lefts, rights, rows, plans, many):
    left, right = jnp.concatenate(lefts, axis=1), jnp.concatenate(rights, axis=0)
    depth, width = right.shape
    part = rows // THIRDS
    result = jnp.take(left.reshape(-1, rows, depth), picks, axis=0)
    result = jnp.einsum("srd,dw->srw", result, right, preferred_element_type=jnp.float32).astype(jnp.bfloat16)
    result = result.reshape(-1, many, THIRDS, part, width)
    return [jnp.stack([result[group, :, third] for group, third in plan], axis=1) for plan in plans]


def weight_part(picks, lefts, rights, rows, plans, many, tile):
    depth, width = rights[0].shape
    count, part = picks.shape[0], rows // THIRDS
    if part % 16:
        return weight_part_plain(picks, lefts, rights, rows, plans, many)
    return pl.pallas_call(
        lambda *refs: weight_part_kernel(*refs, count=count, plans=plans, many=many),
        grid_spec=pltpu.PrefetchScalarGridSpec(
            num_scalar_prefetch=1,
            grid=(width // tile,),
            in_specs=[pl.BlockSpec((rows, depth), lambda i, picks, k=k: (picks[k], 0)) for k in range(count)] * 2
            + [pl.BlockSpec((depth, tile), lambda i, picks: (0, i))] * 2,
            out_specs=[pl.BlockSpec((many, len(plan), part, tile), lambda i, picks: (0, 0, 0, i)) for plan in plans],
        ),
        out_shape=[jax.ShapeDtypeStruct((many, len(plan), part, width), jnp.bfloat16) for plan in plans],
        compiler_params=pltpu.CompilerParams(vmem_limit_bytes=VMEM_BYTES),
        cost_estimate=cost(4),
        name="weight_part",
    )(picks, *([lefts[0]] * count), *([lefts[1]] * count), *rights)


def hot_columns(slots, first, count):
    rows = first + lax.broadcasted_iota(jnp.int32, (count, slots.shape[1]), 0)
    return (rows == slots).astype(jnp.bfloat16)


def halves(core, mine, other):
    return jnp.where(core == 0, mine, other), jnp.where(core == 0, other, mine)


def join_kernel(places, *refs):
    pieces, out = refs[:-1], refs[-1]
    rows = pieces[0].shape[1]
    count = pieces[0].shape[0]
    for chunk in range(out.shape[0] // count):
        for step in range(len(pieces) * count // out.shape[0]):
            piece = pieces[chunk * (len(pieces) * count // out.shape[0]) + step]
            start = pl.multiple_of(places[step] * rows, rows)
            out[pl.ds(chunk * count, count), pl.ds(start, rows), :] = piece[...]


def join(places, chunks):
    count, rows, columns = chunks[0][0].shape
    steps = len(chunks[0])
    return pl.pallas_call(
        join_kernel,
        in_specs=[pl.BlockSpec(memory_space=pltpu.SMEM)] + [pl.BlockSpec(memory_space=pltpu.VMEM)] * (steps * len(chunks)),
        out_shape=jax.ShapeDtypeStruct((count * len(chunks), steps * rows, columns), jnp.bfloat16),
        compiler_params=pltpu.CompilerParams(vmem_limit_bytes=VMEM_BYTES),
        cost_estimate=cost(3),
        name="join",
    )(places, *[piece for chunk in chunks for piece in chunk])


def project_kernel(core, rows, mine, other, result):
    half = mine.shape[1]
    first, second = halves(core[0], mine[...], other[...])
    result[:, :half] = dot_f32(rows[...], first).astype(jnp.bfloat16)
    result[:, half:] = dot_f32(rows[...], second).astype(jnp.bfloat16)


def project(core, rows, mine, other, used):
    width, half = mine.shape[1:]
    length = rows.shape[0]
    return pl.pallas_call(
        project_kernel,
        grid_spec=pltpu.PrefetchScalarGridSpec(
            num_scalar_prefetch=1,
            grid=(used,),
            in_specs=[
                whole((length, width)),
                pl.BlockSpec((None, width, half), lambda i, core: (i, 0, 0)),
                pl.BlockSpec((None, width, half), lambda i, core: (i, 0, 0)),
            ],
            out_specs=pl.BlockSpec((None, length, 2 * half), lambda i, core: (i, 0, 0)),
        ),
        out_shape=jax.ShapeDtypeStruct((used, length, 2 * half), jnp.bfloat16),
        compiler_params=pltpu.CompilerParams(vmem_limit_bytes=VMEM_BYTES),
        cost_estimate=cost(4),
        name="project",
    )(core, rows, mine, other)


def route_kernel(core, attended, tokens, mine, other, gain, router, routes, slots, middle, normed, gates, *outs):
    f32 = jnp.float32
    first, second = halves(core[0], mine[...], other[...])
    rows = attended[...]
    moved = jnp.concatenate([dot_f32(rows, first), dot_f32(rows, second)], axis=1)
    value = tokens[...].astype(f32) + moved
    middle[...] = value
    low = (value * lax.rsqrt(jnp.mean(value * value, axis=1, keepdims=True) + EPS) * gain[...]).astype(jnp.bfloat16)
    normed[...] = low
    start = 0
    for first_out, second_out in zip(outs[::2], outs[1::2]):
        size = first_out.shape[0]
        hot = hot_columns(slots[0:1, :], start, 2 * size) + hot_columns(slots[1:2, :], start, 2 * size)
        part = dot_f32(hot, low).astype(jnp.bfloat16)
        first_out[...] = part[:size]
        second_out[...] = part[size:]
        start += 2 * size
    logits = dot_f32(low, router[...])
    soft = jnp.exp(logits - jnp.max(logits, axis=1, keepdims=True))
    soft = soft / jnp.sum(soft, axis=1, keepdims=True)
    expert = lax.broadcasted_iota(jnp.int32, soft.shape, 1)
    chosen = [jnp.sum(jnp.where(expert == routes[:, k : k + 1], soft, 0.0), axis=1, keepdims=True) for k in range(2)]
    for k in range(2):
        gates[:, k : k + 1] = chosen[k] / (chosen[0] + chosen[1])


def route(core, attended, tokens, mine, other, gain, router, routes, slots, pieces, count):
    length, width = tokens.shape
    last, half = mine.shape[0] - 1, mine.shape[2]
    f32, bf16 = jnp.float32, jnp.bfloat16
    weight = pl.BlockSpec((None, width, half), lambda i, core: (last, 0, 0))
    shapes = [((length, width), f32), ((length, width), bf16), ((length, 2), f32)] + [((count, width), bf16)] * pieces
    return pl.pallas_call(
        route_kernel,
        grid_spec=pltpu.PrefetchScalarGridSpec(
            num_scalar_prefetch=1,
            grid=(1,),
            in_specs=[whole((length, width)), whole((length, width)), weight, weight, whole((1, width)), whole(router.shape), whole(routes.shape), whole(slots.shape)],
            out_specs=[whole(shape) for shape, _ in shapes],
        ),
        out_shape=[jax.ShapeDtypeStruct(shape, kind) for shape, kind in shapes],
        compiler_params=pltpu.CompilerParams(vmem_limit_bytes=VMEM_BYTES),
        cost_estimate=cost(6),
        name="route",
    )(core, attended, tokens, mine, other, gain.reshape(1, -1), router, routes, slots)


def hot_route(slots, k, count):
    cols = lax.broadcasted_iota(jnp.int32, (slots.shape[0], count), 1)
    return cols == slots[:, k : k + 1]


def combine_kernel(*refs, count):
    slots, slots_t, scale = refs[:3]
    pieces = refs[3 : 3 + count]
    middle, teacher, cotangent, valid, gates, routes = refs[3 + count : 9 + count]
    output, grad_y, grad_logits, square = refs[9 + count : 13 + count]
    sends, rows = refs[13 + count : 13 + 2 * count], refs[13 + 2 * count]
    f32, bf16 = jnp.float32, jnp.bfloat16
    assemble(rows, pieces)
    table = rows[...]
    picked = [dot_f32(hot_route(slots, k, rows.shape[0]).astype(bf16), table) for k in range(2)]
    result = middle[...] + (gates[:, 0:1] * picked[0] + gates[:, 1:2] * picked[1])
    output[...] = result.astype(bf16)
    misfit = valid[...] * (result - teacher[...].astype(f32))
    square[...] = jnp.sum((misfit * misfit).reshape(-1, 8, misfit.shape[1]), axis=0)
    grad = cotangent[...].astype(f32) + misfit * scale[0, 0]
    grad_y[...] = grad
    steep = [jnp.sum(grad * picked[k], axis=1, keepdims=True) for k in range(2)]
    slack = gates[:, 0:1] * steep[0] + gates[:, 1:2] * steep[1]
    expert = lax.broadcasted_iota(jnp.int32, grad_logits.shape, 1)
    turn = [jnp.where(expert == routes[:, k : k + 1], gates[:, k : k + 1] * (steep[k] - slack), 0.0) for k in range(2)]
    grad_logits[...] = (turn[0] + turn[1]).astype(bf16)
    scaled = [(gates[:, k : k + 1] * grad).astype(bf16) for k in range(2)]
    start = 0
    for first, second in zip(sends[::2], sends[1::2]):
        size = first.shape[0]
        part = [dot_f32(hot_columns(slots_t[k : k + 1, :], start, 2 * size), scaled[k]) for k in range(2)]
        part = (part[0] + part[1]).astype(bf16)
        first[...] = part[:size]
        second[...] = part[size:]
        start += 2 * size


def combine(slots, slots_t, scale, pieces, middle, teacher, cotangent, valid, gates, routes, experts):
    length, width = middle.shape
    count = len(pieces)
    f32, bf16 = jnp.float32, jnp.bfloat16
    return pl.pallas_call(
        lambda *refs: combine_kernel(*refs, count=count),
        in_specs=[pl.BlockSpec(memory_space=pltpu.VMEM)] * 2
        + [pl.BlockSpec(memory_space=pltpu.SMEM)]
        + [pl.BlockSpec(memory_space=pltpu.VMEM)] * (6 + count),
        out_shape=[
            jax.ShapeDtypeStruct((length, width), bf16),
            jax.ShapeDtypeStruct((length, width), f32),
            jax.ShapeDtypeStruct((length, experts), bf16),
            jax.ShapeDtypeStruct((8, width), f32),
        ]
        + [jax.ShapeDtypeStruct(piece.shape, bf16) for piece in pieces],
        scratch_shapes=[pltpu.VMEM((sum(piece.shape[0] for piece in pieces), width), bf16)],
        compiler_params=pltpu.CompilerParams(vmem_limit_bytes=VMEM_BYTES),
        cost_estimate=cost(8),
        name="combine",
    )(slots, slots_t, scale, *pieces, middle, teacher, cotangent, valid, gates, routes)


def norm_back(value, gain, grad):
    root = lax.rsqrt(jnp.mean(value * value, axis=1, keepdims=True) + EPS)
    normed = value * root
    scaled = grad * gain
    inner = jnp.mean(scaled * normed, axis=1, keepdims=True)
    return root * (scaled - normed * inner), jnp.sum((grad * normed).reshape(-1, 8, value.shape[1]), axis=0)


def collect_kernel(core, *refs, count):
    slots, pieces = refs[0], refs[1 : 1 + count]
    middle, gain, grad_logits, router, grad_y, mine, other = refs[1 + count : 8 + count]
    grad_middle, rounded, grad_attended, grad_gain, rows = refs[8 + count :]
    assemble(rows, pieces)
    hot = (hot_route(slots, 0, rows.shape[0]) | hot_route(slots, 1, rows.shape[0])).astype(jnp.bfloat16)
    grad = dot_f32(grad_logits[...], router[...], NT) + dot_f32(hot, rows[...])
    turned, grad_gain[...] = norm_back(middle[...], gain[...], grad)
    result = grad_y[...] + turned
    grad_middle[...] = result
    low = result.astype(jnp.bfloat16)
    rounded[...] = low
    first, second = halves(core[0], mine[...], other[...])
    half = first.shape[1]
    grad_attended[...] = (dot_f32(low[:, :half], first, NT) + dot_f32(low[:, half:], second, NT)).astype(jnp.bfloat16)


def collect(core, slots, pieces, middle, gain, grad_logits, router, grad_y, mine, other):
    length, width = middle.shape
    last, half = mine.shape[0] - 1, mine.shape[2]
    f32, bf16 = jnp.float32, jnp.bfloat16
    weight = pl.BlockSpec((None, width, half), lambda i, core: (last, 0, 0))
    plain = [slots, *pieces, middle, gain.reshape(1, -1), grad_logits, router, grad_y]
    shapes = [((length, width), f32), ((length, width), bf16), ((length, width), bf16), ((8, width), f32)]
    return pl.pallas_call(
        lambda *refs: collect_kernel(*refs, count=len(pieces)),
        grid_spec=pltpu.PrefetchScalarGridSpec(
            num_scalar_prefetch=1,
            grid=(1,),
            in_specs=[whole(array.shape) for array in plain] + [weight, weight],
            out_specs=[whole(shape) for shape, _ in shapes],
            scratch_shapes=[pltpu.VMEM((sum(piece.shape[0] for piece in pieces), width), bf16)],
        ),
        out_shape=[jax.ShapeDtypeStruct(shape, kind) for shape, kind in shapes],
        compiler_params=pltpu.CompilerParams(vmem_limit_bytes=VMEM_BYTES),
        cost_estimate=cost(8),
        name="collect",
    )(core, *plain, mine, other)


def outer_halves_kernel(core, normed, attended, rights, last, *refs, count):
    aways, stays, normed_t, attended_t = refs[:2], refs[2:4], refs[4], refs[5]
    step = pl.program_id(0)

    @pl.when(step == 0)
    def _():
        normed_t[...] = normed[...].T
        attended_t[...] = attended[...].T

    for place in range(count + 1):

        @pl.when(step == place)
        def _():
            result = dot_f32(normed_t[...], rights[...]) if place < count else dot_f32(attended_t[...], last[...])
            result = result.astype(jnp.bfloat16)
            half = result.shape[1] // 2
            away, stay = aways[place // 2], stays[place // 2]
            slot = place % 2

            @pl.when(core[0] == 0)
            def _():
                stay[slot] = result[:, :half]
                away[slot] = result[:, half:]

            @pl.when(core[0] != 0)
            def _():
                away[slot] = result[:, :half]
                stay[slot] = result[:, half:]


def outer_halves(core, normed, attended, rights, last):
    length, width = normed.shape
    count, half = rights.shape[0], width // 2
    shape = jax.ShapeDtypeStruct((2, width, half), jnp.bfloat16)
    return pl.pallas_call(
        lambda *refs: outer_halves_kernel(*refs, count=count),
        grid_spec=pltpu.PrefetchScalarGridSpec(
            num_scalar_prefetch=1,
            grid=(count + 1,),
            in_specs=[
                whole((length, width)),
                whole((length, width)),
                pl.BlockSpec((None, length, width), lambda i, core: (jnp.minimum(i, count - 1), 0, 0)),
                whole((length, width)),
            ],
            out_specs=[whole(shape.shape)] * 4,
            scratch_shapes=[pltpu.VMEM((width, length), jnp.bfloat16)] * 2,
        ),
        out_shape=[shape] * 4,
        compiler_params=pltpu.CompilerParams(vmem_limit_bytes=VMEM_BYTES),
        cost_estimate=cost(6),
        name="outer_halves",
    )(core, normed, attended, rights, last)


def enter_kernel(core, grads, mine, other, tokens, gain, grad_middle, grad_input, grad_gain, total):
    step = pl.program_id(0)
    first, second = halves(core[0], mine[...], other[...])
    half = first.shape[1]
    rows = grads[...]
    part = dot_f32(rows[:, :half], first, NT) + dot_f32(rows[:, half:], second, NT)

    @pl.when(step == 0)
    def _():
        total[...] = part

    @pl.when(step > 0)
    def _():
        total[...] += part

    @pl.when(step == pl.num_programs(0) - 1)
    def _():
        turned, grad_gain[...] = norm_back(tokens[...].astype(jnp.float32), gain[...], total[...])
        grad_input[...] = grad_middle[...] + turned


def enter(core, grads, mine, other, tokens, gain, grad_middle):
    length, width = tokens.shape
    count, half = grads.shape[0], mine.shape[2]
    weight = pl.BlockSpec((None, width, half), lambda i, core: (i, 0, 0))
    return pl.pallas_call(
        enter_kernel,
        grid_spec=pltpu.PrefetchScalarGridSpec(
            num_scalar_prefetch=1,
            grid=(count,),
            in_specs=[pl.BlockSpec((None, length, width), lambda i, core: (i, 0, 0)), weight, weight, whole((length, width)), whole((1, width)), whole((length, width))],
            out_specs=[whole((length, width)), whole((8, width))],
            scratch_shapes=[pltpu.VMEM((length, width), jnp.float32)],
        ),
        out_shape=[jax.ShapeDtypeStruct((length, width), jnp.float32), jax.ShapeDtypeStruct((8, width), jnp.float32)],
        compiler_params=pltpu.CompilerParams(vmem_limit_bytes=VMEM_BYTES),
        cost_estimate=cost(6),
        name="enter",
    )(core, grads, mine, other, tokens, gain.reshape(1, -1), grad_middle)


BOUNDS = (12, 16, 23, 32, 46, 64, 91)
TOP_PRECISION = lax.Precision.HIGHEST
AXES = ("dp", "expert")
PAIR = 2


def after(value, *others):
    return lax.optimization_barrier((value, *others))[0] if others else value


def bucket_index(offset):
    distance = jnp.abs(offset)
    far_bucket = 8 + sum([(distance >= level).astype(jnp.int32) for level in BOUNDS])
    near_bucket = jnp.where(distance < 8, distance, far_bucket)
    return jnp.where(offset > 0, 16, 0) + near_bucket


def norm_apply(inputs, gain_vec):
    return inputs * lax.rsqrt(jnp.mean(inputs * inputs, axis=-1, keepdims=True) + EPS) * gain_vec


def tile_offsets(query_block, key_block):
    rows = query_block * BLOCK + lax.broadcasted_iota(jnp.int32, (BLOCK, BLOCK), 0)
    cols = key_block * BLOCK + lax.broadcasted_iota(jnp.int32, (BLOCK, BLOCK), 1)
    return rows, cols


def offset_bias(table):
    offsets = jnp.arange(4 * BLOCK, dtype=jnp.int32) - 2 * BLOCK
    hot = (bucket_index(offsets)[None] == jnp.arange(table.shape[1], dtype=jnp.int32)[:, None]).astype(jnp.float32)
    return jnp.dot(table, hot, precision=TOP_PRECISION)


def table_gradient(bands, buckets):
    rows, cols = tile_offsets(0, 0)
    ids = [jnp.full((BLOCK, BLOCK), bucket_far(), jnp.int32)]
    ids += [bucket_index(shift * BLOCK + cols - rows) for shift in (-1, 0, 1)]
    hot = (jnp.stack(ids)[..., None] == jnp.arange(buckets, dtype=jnp.int32)).astype(jnp.float32)
    return jnp.einsum("hdxy,dxyb->hb", bands, hot, precision=TOP_PRECISION)


def bucket_far():
    return 8 + len(BOUNDS)


def on_device(
    tokens,
    qkv_weight,
    out_weight,
    position_bias_table,
    gain_attn,
    gain_moe,
    router,
    w_in,
    w_out,
    routes,
    prefix,
    valid_mask,
    teacher,
    cotangent,
):
    length, width = tokens.shape
    bf16, f32 = jnp.bfloat16, jnp.float32
    expert_count = router.shape[1]
    top_count = routes.shape[1]
    groups = lax.axis_size("expert")
    copies = lax.axis_size("dp")
    inner = w_in.shape[2]
    capacity = 5 * length * top_count // (4 * expert_count)
    total_tokens = length * copies * groups
    sources = 2 * groups
    blocks = length // BLOCK
    here_dp, here_group = lax.axis_index("dp"), lax.axis_index("expert")
    half = (here_dp >> 1) & 1
    core = here_group & 1
    rest = copies // 4

    def swap(value, dp_mask, group_mask):
        pairs = [
            (i, ((i // groups) ^ dp_mask) * groups + ((i % groups) ^ group_mask))
            for i in range(copies * groups)
        ]
        return lax.ppermute(value, AXES, pairs)

    def bits(count):
        return [1 << place for place in range(count.bit_length() - 1)]

    def partial_sums(value):
        sums = []
        for masks in [(0, mask) for mask in bits(groups)] + [(mask, 0) for mask in bits(copies)]:
            value = value + swap(value, *masks)
            sums.append(value)
        return sums

    chips = groups

    def across(value, place):
        return swap(value, PAIR * (place // (groups // 2)), 2 * (place % (groups // 2)))

    def to_chips(pieces):
        return [pieces[0]] + [across(pieces[place], place) for place in range(1, chips)]

    def through(visit, sends):
        direct, relay = to_chips(sends[::2]), to_chips(sends[1::2])
        seen, direct = visit(direct)
        direct = to_chips(direct)
        relay = [after(part, seen) for part in relay]
        passed = visit(swap(jnp.concatenate(relay), 0, 1))
        return direct, [swap(after(part, *direct), 0, 1) for part in passed]

    def weave(direct, relay):
        return [part for pair in zip(direct, to_chips(relay)) for part in pair]

    ring = list(range(0, copies, 2)) + list(range(copies - 1, 0, -2))
    turns = [(1, step) for step in range(1, copies // 2 + 1)] + [(-1, step) for step in range(1, copies // 2)]

    def gather_ring(shard, due):
        got = [shard]
        for turn in (1, -1):
            held = shard
            pairs = [(ring[i], ring[(i + turn) % copies]) for i in range(copies)]
            for step in [step for way, step in turns if way == turn]:
                held = lax.ppermute(after(held, *due[step - 2 : step - 1]) if step > 1 else held, "dp", pairs)
                got.append(held)
        return got

    def ring_places():
        place = jnp.where(here_dp & 1 == 0, here_dp >> 1, copies - 1 - (here_dp >> 1))
        shift = jnp.array([0] + [turn * step for turn, step in turns], jnp.int32)
        place = (place - shift) & (copies - 1)
        return jnp.where(place < copies // 2, 2 * place, 2 * (copies - 1 - place) + 1).astype(jnp.int32)


    flat_routes = routes.reshape(-1)
    pair_count = length * top_count
    slot_count = sources * capacity
    route_hits = (flat_routes[:, None] == jnp.arange(expert_count, dtype=jnp.int32)[None, :]).astype(bf16)
    lower_ones = (
        lax.broadcasted_iota(jnp.int32, (pair_count, pair_count), 0)
        >= lax.broadcasted_iota(jnp.int32, (pair_count, pair_count), 1)
    ).astype(bf16)
    running = jnp.dot(lower_ones, route_hits, preferred_element_type=f32)
    pair_rank = jnp.sum((running - 1.0) * route_hits.astype(f32), axis=1).astype(jnp.int32)
    away = (flat_routes >> 1) ^ here_group
    chip = ((flat_routes & 1) ^ half) * (groups // 2) + (away >> 1)
    slots = ((chip * 2 + (away & 1)) * capacity + pair_rank).reshape(length, top_count)
    slots_t = slots.T

    resid = tokens.astype(f32)
    normed1 = norm_apply(resid, gain_attn).astype(bf16)
    columns = width // 2
    core_index = core.reshape(1).astype(jnp.int32)
    valid_rows = valid_mask.astype(f32)[:, None]
    counts = [jnp.broadcast_to(jnp.sum(valid_rows), (8, 128))]
    count_trades = [(0, mask) for mask in bits(groups)] + [(mask, 0) for mask in bits(copies)]

    def count_beside(before, value):
        if len(counts) > len(count_trades):
            return value
        counts.append(counts[-1] + swap(after(counts[-1], before), *count_trades[len(counts) - 1]))
        return after(value, counts[-1])

    shards = [
        lax.dynamic_slice_in_dim(part, core * columns, columns, 2)
        for part in (qkv_weight[:2], jnp.concatenate([qkv_weight[2:], out_weight[None]]))
    ]
    if copies > 8:
        mine = lax.all_gather(jnp.concatenate(shards), "dp", axis=1, tiled=True)
    else:
        mine = join(ring_places(), [gather_ring(shards[0], ()), gather_ring(shards[1], (slots_t, normed1))])
    other = count_beside(mine, swap(mine, 0, 1))
    qkv_rows = count_beside(other, project(core_index, normed1, mine, other, 3))
    offsets = offset_bias(position_bias_table)
    attended, probs = attention_forward(position_bias_table[:, bucket_far()], prefix, qkv_rows, offsets)
    middle, normed2, gates, *sends = route(
        core_index, count_beside(qkv_rows, attended), tokens, mine, other, gain_moe, router, routes, slots_t, 2 * chips, capacity
    )

    pick = half.reshape(1).astype(jnp.int32)
    hidden, slopes, rows_in = [], [], []

    def expert(pieces):
        one = not isinstance(pieces, list)
        pieces = [pieces] if one else pieces
        hidden_t, slope, rows_t, *results = expert_forward(pick, pieces, chips, w_in, w_out)
        hidden_t = count_beside(pieces[-1], hidden_t)
        for kept, value in zip((hidden, slopes, rows_in), (hidden_t, slope, rows_t)):
            kept.append(value)
        return results if one else (hidden_t, results)

    back = weave(*through(expert, sends))
    while len(counts) <= len(count_trades):
        back[0] = count_beside(back[0], back[0])
    valid_count = counts[-1][0, 0]
    scale = (total_tokens / valid_count).reshape(1, 1)
    output, grad_y, grad_logits, squares, *sends = combine(
        slots, slots_t, scale, back, middle, teacher, cotangent, valid_rows, gates, routes, expert_count
    )

    out_rows = inner // copies
    in_rows = width // copies
    far_bit = here_dp % 2
    slices = jnp.arange(rest, dtype=jnp.int32) * 4

    def picks(bit0):
        return jnp.concatenate([slices + ((half ^ other_half) * 2 + bit0) for other_half in (1, 0)]).astype(jnp.int32)

    sent, kept = picks(1 - far_bit), picks(far_bit)

    def add(left, right):
        return (left.astype(f32) + right.astype(f32)).astype(bf16)

    def fold(unit, bit, axis=0):
        unit = unit.reshape(unit.shape[:axis] + (2, unit.shape[axis] // 2) + unit.shape[axis + 1 :])
        away_part = lax.dynamic_index_in_dim(unit, 1 - bit, axis, keepdims=False)
        return away_part, lax.dynamic_index_in_dim(unit, bit, axis, keepdims=False)

    far_masks = list(reversed(bits(copies)[2:]))

    def near_add(got, keep):
        away_part, stay_part = fold(add(got, keep), (here_dp // far_masks[0]) % 2)
        return away_part, stay_part

    def far_trade(away_part):
        return swap(away_part, far_masks[0], 0)

    def finish(got, stay):
        unit = add(got, stay)
        for mask in far_masks[1:]:
            away_part, stay_part = fold(unit, (here_dp // mask) % 2)
            unit = add(swap(away_part, mask, 0), stay_part)
        return unit[0]

    plan_a, plan_b, plan_c = ((0, 0), (0, 1)), ((0, 2), (1, 0)), ((1, 1), (1, 2))
    plan_d, plan_e, plan_f = plan_a, plan_b, plan_c
    out_plans, in_plans = (plan_a, plan_b, plan_c), (plan_d, plan_e, plan_f)

    grad_rows, grad_pre, parts = [], [], []

    def expert_back(pieces):
        if isinstance(pieces, list):
            grad_pre_rows, grads, *results = expert_backward(pick, pieces, chips, w_in, w_out, slopes[0])
            grad_rows.append(grads)
            grad_pre.append(grad_pre_rows)
            return grad_pre_rows, results
        grad_rows.append(pieces)
        parts.extend(weight_part(sent, hidden, grad_rows, out_rows, out_plans, rest, width))
        parts[0] = swap(parts[0], 1, 0)
        pieces = after(pieces, parts[1])
        grad_pre_rows, _, *results = expert_backward(pick, [pieces], chips, w_in, w_out, slopes[1])
        grad_pre.append(grad_pre_rows)
        return results

    direct, relay = through(expert_back, sends)
    got_a, send_b, send_c = parts
    relay = [after(part, got_a) for part in relay]
    got_b = swap(after(send_b, relay[0]), 1, 0)
    back = weave(direct, relay)
    grad_rows, grad_pre = lax.optimization_barrier((grad_rows, grad_pre, relay))[:2]
    keep_a, keep_b, keep_c = weight_part(kept, hidden, grad_rows, out_rows, out_plans, rest, width)
    away_a, stay_a = near_add(got_a, keep_a)
    far_a = far_trade(away_a)
    send_d, send_e, send_f = weight_part(sent, rows_in, after(grad_pre, away_a), in_rows, in_plans, rest, inner // 2)
    back = [after(part, send_d) for part in back]
    got_c = swap(after(send_c, send_d), 1, 0)
    grad_middle, grad_attn_proj, grad_attended, gain_moe_parts = collect(
        core_index, slots, back, middle, gain_moe, grad_logits, router, grad_y, mine, other
    )
    away_b, stay_b = near_add(after(got_b, grad_attended), keep_b)
    got_d = swap(after(send_d, grad_attended), 1, 0)
    grad_attended, away_b, far_a = lax.optimization_barrier((grad_attended, away_b, far_a))
    far_b = far_trade(away_b)
    done_a = finish(far_a, stay_a)
    grad_qkv_rows, bands = attention_backward(qkv_rows, grad_attended, probs)
    grad_qkv_rows, got_c = lax.optimization_barrier((grad_qkv_rows, got_c))

    away_c, stay_c = near_add(got_c, keep_c)
    far_c = far_trade(away_c)
    *weights_away, stay_1, stay_2 = outer_halves(
        core_index, normed1, attended, after(grad_qkv_rows, away_c), grad_attn_proj
    )
    weights_away, far_b, got_d = lax.optimization_barrier((weights_away, far_b, got_d))
    done_b = finish(far_b, stay_b)
    got_e = swap(after(send_e, got_d), 1, 0)
    keep_d, keep_e, keep_f = weight_part(
        kept, rows_in, after(grad_pre, *weights_away), in_rows, in_plans, rest, inner // 2
    )
    group_masks = bits(groups)[1:]
    dp_masks = sorted(bits(copies), key=lambda mask: (mask != PAIR, mask))

    def over_groups(got, stay, *due):
        got = add(after(got, *due), stay).reshape(2, copies, in_rows, columns)
        for mask in group_masks[:-1]:
            away_part, stay_part = fold(got, (here_group // mask) % 2, 2)
            got = add(swap(away_part, 0, mask), stay_part)
        away_part, stay_part = fold(got, (here_group // group_masks[-1]) % 2, 2)
        return swap(away_part, 0, group_masks[-1]), stay_part

    def over_dp(total, mask, passed):
        axis = 1 + sorted([other for other in dp_masks if other not in passed], reverse=True).index(mask)
        bit = (here_dp // mask) % 2
        away_part = lax.dynamic_index_in_dim(total, 1 - bit, axis, keepdims=False)
        stay_part = lax.dynamic_index_in_dim(total, bit, axis, keepdims=False)
        return swap(away_part, mask, 0), stay_part

    weights_got = [swap(part, 0, 1) for part in weights_away]
    first = over_groups(weights_got[0], stay_1, keep_d)
    second = over_groups(weights_got[1], stay_2, first[1])
    away_d, stay_d = near_add(after(got_d, second[1]), keep_d)
    far_d = far_trade(away_d)
    grad_input, gain_attn_parts = enter(
        core_index, after(grad_qkv_rows, away_d), mine, other, tokens, gain_attn, grad_middle
    )
    done_c = finish(after(far_c, gain_attn_parts), stay_c)
    grad_table = table_gradient(after(bands, second[1]), position_bias_table.shape[1])

    chains = [add(after(first[0], away_d, gain_attn_parts), first[1]).reshape((2,) + (2,) * len(dp_masks) + (-1, columns)), None]
    trades = [over_dp(chains[0], dp_masks[0], ()), None]
    away_e, stay_e = near_add(after(got_e, chains[0]), keep_e)
    far_e = far_trade(away_e)
    got_f = swap(after(send_f, away_e), 1, 0)
    chains[1] = add(after(second[0], done_c, grad_table, away_e), second[1]).reshape(chains[0].shape)
    trades[1] = over_dp(chains[1], dp_masks[0], ())
    total = trades[1][1]
    done_d = finish(after(far_d, chains[0]), stay_d)
    away_f, stay_f = near_add(after(got_f, total), keep_f)
    far_f = far_trade(away_f)
    trades = [(after(trades[0][0], total, done_d), trades[0][1]), (after(trades[1][0], away_f), trades[1][1])]

    normed2, squares, gain_moe_parts = after((normed2, squares, gain_moe_parts), second[1])
    grad_router = jnp.einsum("td,te->de", normed2, grad_logits, preferred_element_type=f32)
    small = [
        jnp.sum(gain_moe_parts, axis=0),
        jnp.sum(gain_attn_parts, axis=0),
        grad_router,
        grad_table,
        jnp.sum(squares),
    ]
    sizes = [value.size for value in small]
    flat = jnp.concatenate([value.reshape(-1) for value in small])
    flat = after(jnp.pad(flat, (0, -sum(sizes) % 1024)).reshape(-1, 128), total)

    flat = flat + swap(flat, 0, 1)
    for place, mask in enumerate(dp_masks):
        flat_got = swap(flat, 0, group_masks[0]) if mask == PAIR else swap(flat, mask, 0)
        if place == 1:
            done_e = finish(far_e, stay_e)
            trades[1] = (after(trades[1][0], done_e), trades[1][1])
        chains = [add(*trades[0]), None]
        if place + 1 < len(dp_masks):
            trades_next = [over_dp(chains[0], dp_masks[place + 1], dp_masks[: place + 1]), None]
        chains[1] = add(after(trades[1][0], chains[0]), trades[1][1])
        flat = flat + flat_got
        if place + 1 < len(dp_masks):
            trades_next[1] = over_dp(chains[1], dp_masks[place + 1], dp_masks[: place + 1])
            trades = trades_next
        if mask == PAIR:
            in_first = swap(done_d, PAIR, 0)
            out_theirs = swap(after(jnp.concatenate([done_a, done_b[:1]]), chains[1]), PAIR, 0)
        flat = after(flat, chains[1])
    total = jnp.concatenate(chains)
    in_theirs = jnp.concatenate([in_first, swap(done_e[:1], PAIR, 0)])
    for mask in reversed(group_masks):
        bit = (here_group // mask) % 2
        other_part = swap(total, 0, mask)
        total = jnp.concatenate([jnp.where(bit == 0, total, other_part), jnp.where(bit == 0, other_part, total)], axis=1)
        if mask == group_masks[0]:
            done_f = finish(after(far_f, total), stay_f)
            total = after(total, done_f)
            flat = flat + swap(flat, PAIR, 0)
        else:
            flat = flat + swap(flat, 0, mask)
        total, flat = lax.optimization_barrier((total, flat))
    other_part = swap(total, 0, 1)
    total = jnp.concatenate([jnp.where(core == 0, total, other_part), jnp.where(core == 0, other_part, total)], axis=2)
    weights_done = total.astype(f32)
    grad_qkv, grad_out_weight = weights_done[:3], weights_done[3]
    flat = flat.reshape(-1)
    starts = [sum(sizes[:place]) for place in range(len(sizes))]
    grad_gain_moe, grad_gain_attn, grad_router, grad_table, square_total = [
        flat[start : start + value.size].reshape(value.shape) for start, value in zip(starts, small)
    ]

    out_mine, in_mine = jnp.concatenate([done_b[1:], done_c]), jnp.concatenate([done_e[1:], done_f])

    def both_experts(mine, theirs):
        mine, theirs = [part.reshape(-1, part.shape[-1]).astype(f32) for part in (mine, theirs)]
        return jnp.stack([jnp.where(half == 0, mine, theirs), jnp.where(half == 0, theirs, mine)])

    grad_w_out = both_experts(out_mine, out_theirs)
    grad_w_in = both_experts(in_mine, in_theirs)

    distill_loss = square_total / (width * valid_count)
    return (
        output.astype(bf16),
        distill_loss,
        grad_input,
        grad_qkv,
        grad_out_weight,
        grad_w_in,
        grad_w_out,
        grad_router,
        grad_table,
        grad_gain_attn,
        grad_gain_moe,
    )


def solution(mesh):
    rows = P(AXES, None)
    return jax.shard_map(
        on_device,
        mesh=mesh,
        in_specs=(
            rows,
            P(None, "dp", None),
            P("dp", None),
            P(),
            P(),
            P(),
            P(),
            P("expert", None, None),
            P("expert", None, None),
            rows,
            P(AXES),
            P(AXES),
            rows,
            rows,
        ),
        out_specs=(
            rows,
            P(),
            rows,
            P(None, "dp", None),
            P("dp", None),
            P("expert", "dp", None),
            P("expert", "dp", None),
            P(),
            P(),
            P(),
            P(),
        ),
        check_vma=False,
    )
```

```python
import math
import jax
import jax.numpy as jnp
from jax import lax
from jax.experimental import pallas as pl
from jax.experimental.pallas import tpu as pltpu
from jax.sharding import PartitionSpec as P

BLOCK = 128
THIRDS = 3
EPS = 1e-06
GELU_A = math.sqrt(2.0 / math.pi)
GELU_B = 0.044715
NT = (((1,), (1,)), ((), ()))
TN = (((0,), (0,)), ((), ()))
VMEM_BYTES = 56 * 1024 * 1024


def cost(micros):
    return pl.CostEstimate(flops=int(micros * 0.37e9), bytes_accessed=0, transcendentals=0)


def dot_f32(left, right, dims=(((1,), (0,)), ((), ()))):
    return lax.dot_general(left, right, dims, preferred_element_type=jnp.float32)


def assemble(rows, pieces):
    start = 0
    for piece in pieces:
        rows[pl.ds(start, piece.shape[0]), :] = piece[...]
        start += piece.shape[0]


def hand_out(total, outs):
    start = 0
    for out in outs:
        out[...] = total[pl.ds(start, out.shape[0]), :].astype(out.dtype)
        start += out.shape[0]


def whole(shape):
    return pl.BlockSpec(shape, lambda *step: (0,) * len(shape))


def expert_forward_kernel(pick, *refs, chunk, count):
    pieces, w_in, w_out = refs[:count], refs[count], refs[count + 1]
    hidden_t, slope, rows_t = refs[count + 2 : count + 5]
    outs, rows, total = refs[count + 5 : -2], refs[-2], refs[-1]
    step = pl.program_id(0)

    @pl.when(step == 0)
    def _():
        assemble(rows, pieces)
        total[...] = jnp.zeros_like(total)
        rows_t[...] = rows[...].T

    for start in range(0, rows.shape[0], chunk):
        part = pl.ds(start, chunk)
        pre = dot_f32(rows[part, :], w_in[0])
        square = pre * pre
        bend = jnp.tanh(pre * (GELU_A + (GELU_A * GELU_B) * square))
        half = 0.5 + 0.5 * bend
        act = (pre * half).astype(jnp.bfloat16)
        lift = pre * (0.5 * GELU_A + (1.5 * GELU_A * GELU_B) * square)
        slope[part, :] = (half + lift * (1.0 - bend * bend)).astype(jnp.bfloat16)
        hidden_t[:, part] = act.T
        total[part, :] += dot_f32(act, w_out[0])

    @pl.when(step == pl.num_programs(0) - 1)
    def _():
        hand_out(total, outs)


def expert_forward(pick, pieces, results, w_in, w_out, tile=768, chunk=320):
    many, width = sum(piece.shape[0] for piece in pieces), pieces[0].shape[1]
    inner = w_in.shape[2]
    bf16 = jnp.bfloat16
    return pl.pallas_call(
        lambda *refs: expert_forward_kernel(*refs, chunk=chunk, count=len(pieces)),
        grid_spec=pltpu.PrefetchScalarGridSpec(
            num_scalar_prefetch=1,
            grid=(inner // tile,),
            in_specs=[whole(piece.shape) for piece in pieces]
            + [
                pl.BlockSpec((1, width, tile), lambda f, pick: (pick[0], 0, f)),
                pl.BlockSpec((1, tile, width), lambda f, pick: (pick[0], f, 0)),
            ],
            out_specs=[
                pl.BlockSpec((tile, many), lambda f, pick: (f, 0)),
                pl.BlockSpec((many, tile), lambda f, pick: (0, f)),
                whole((width, many)),
            ]
            + [whole((many // results, width))] * results,
            scratch_shapes=[pltpu.VMEM((many, width), bf16), pltpu.VMEM((many, width), jnp.float32)],
        ),
        out_shape=[
            jax.ShapeDtypeStruct((inner, many), bf16),
            jax.ShapeDtypeStruct((many, inner), bf16),
            jax.ShapeDtypeStruct((width, many), bf16),
        ]
        + [jax.ShapeDtypeStruct((many // results, width), bf16)] * results,
        compiler_params=pltpu.CompilerParams(vmem_limit_bytes=VMEM_BYTES),
        cost_estimate=cost(13),
        name="expert_forward",
    )(pick, *pieces, w_in, w_out)


def expert_backward_kernel(pick, *refs, chunk, count):
    pieces, w_in, w_out, slope = refs[:count], refs[count], refs[count + 1], refs[count + 2]
    grad_pre, rows = refs[count + 3 : count + 5]
    outs, total = refs[count + 5 : -1], refs[-1]
    step = pl.program_id(0)

    @pl.when(step == 0)
    def _():
        assemble(rows, pieces)
        total[...] = jnp.zeros_like(total)

    for start in range(0, rows.shape[0], chunk):
        part = pl.ds(start, chunk)
        back = dot_f32(rows[part, :], w_out[0], NT) * slope[part, :].astype(jnp.float32)
        back = back.astype(jnp.bfloat16)
        grad_pre[part, :] = back
        total[part, :] += dot_f32(back, w_in[0], NT)

    @pl.when(step == pl.num_programs(0) - 1)
    def _():
        hand_out(total, outs)


def expert_backward(pick, pieces, results, w_in, w_out, slope, tile=768, chunk=640):
    many, width = sum(piece.shape[0] for piece in pieces), pieces[0].shape[1]
    inner = w_in.shape[2]
    bf16 = jnp.bfloat16
    return pl.pallas_call(
        lambda *refs: expert_backward_kernel(*refs, chunk=chunk, count=len(pieces)),
        grid_spec=pltpu.PrefetchScalarGridSpec(
            num_scalar_prefetch=1,
            grid=(inner // tile,),
            in_specs=[whole(piece.shape) for piece in pieces]
            + [
                pl.BlockSpec((1, width, tile), lambda f, pick: (pick[0], 0, f)),
                pl.BlockSpec((1, tile, width), lambda f, pick: (pick[0], f, 0)),
                pl.BlockSpec((many, tile), lambda f, pick: (0, f)),
            ],
            out_specs=[pl.BlockSpec((many, tile), lambda f, pick: (0, f)), whole((many, width))]
            + [whole((many // results, width))] * results,
            scratch_shapes=[pltpu.VMEM((many, width), jnp.float32)],
        ),
        out_shape=[jax.ShapeDtypeStruct((many, inner), bf16), jax.ShapeDtypeStruct((many, width), bf16)]
        + [jax.ShapeDtypeStruct((many // results, width), bf16)] * results,
        compiler_params=pltpu.CompilerParams(vmem_limit_bytes=VMEM_BYTES),
        cost_estimate=cost(11),
        name="expert_backward",
    )(pick, *pieces, w_in, w_out, slope)


def seen_blocks(row_block, blocks):
    return max(row_block + 1, blocks // 2)


def attention_forward_kernel(far, prefix, queries, keys, values, offsets, attended, probs, *, heads, blocks):
    pair = pl.program_id(0)
    lane = lax.broadcasted_iota(jnp.int32, queries.shape, 1)
    row = lax.broadcasted_iota(jnp.int32, (BLOCK, BLOCK), 0)
    col = lax.broadcasted_iota(jnp.int32, (BLOCK, BLOCK), 1)
    outs = []
    for head in range(2):
        line = jnp.broadcast_to(offsets[head : head + 1, :], (BLOCK, 4 * BLOCK))
        turned = pltpu.roll(line, 0, 1, stride=1, stride_axis=0)
        far_bias = far[pair * 2 + head]
        mine = (lane < heads) if head == 0 else (lane >= heads)
        query = jnp.where(mine, queries[...] * 0.125, 0.0).astype(jnp.bfloat16)
        score = dot_f32(query, keys[...], NT)
        strips = []
        for row_block in range(blocks):
            span = seen_blocks(row_block, blocks)
            pieces = []
            for key_block in range(span):
                piece = score[row_block * BLOCK : (row_block + 1) * BLOCK, key_block * BLOCK : (key_block + 1) * BLOCK]
                shift = key_block - row_block
                if shift < -1:
                    piece = piece + far_bias
                elif shift < 2:
                    piece = piece + turned[:, (2 + shift) * BLOCK : (3 + shift) * BLOCK]
                else:
                    raise ValueError(shift)
                if shift >= 0:
                    shown = col + key_block * BLOCK < prefix[0]
                    piece = jnp.where((shown | (col <= row)) if shift == 0 else shown, piece, -1e30)
                pieces.append(piece)
            peak = pieces[0]
            for piece in pieces[1:]:
                peak = jnp.maximum(peak, piece)
            peak = jnp.max(peak, axis=1, keepdims=True)
            pieces = [jnp.exp(piece - peak) for piece in pieces]
            mass = pieces[0]
            for piece in pieces[1:]:
                mass = mass + piece
            scale = 1.0 / jnp.sum(mass, axis=1, keepdims=True)
            pieces = [(piece * scale).astype(jnp.bfloat16) for piece in pieces]
            pieces += [jnp.zeros((BLOCK, BLOCK), jnp.bfloat16)] * (blocks - span)
            strips.append(jnp.concatenate(pieces, axis=1))
        weights = jnp.concatenate(strips, axis=0)
        probs[head] = weights
        outs.append(dot_f32(weights, values[...]))
    attended[...] = jnp.where(lane < heads, outs[0], outs[1]).astype(jnp.bfloat16)


def attention_forward(far, prefix, qkv_rows, offsets):
    length, width = qkv_rows.shape[1:]
    pairs = width // 128
    blocks = length // BLOCK
    return pl.pallas_call(
        lambda *refs: attention_forward_kernel(*refs, heads=64, blocks=blocks),
        grid_spec=pltpu.PrefetchScalarGridSpec(
            num_scalar_prefetch=2,
            grid=(pairs,),
            in_specs=[pl.BlockSpec((None, length, 128), lambda h, far, prefix, c=c: (c, 0, h)) for c in range(3)]
            + [pl.BlockSpec((None, 2, 4 * BLOCK), lambda h, far, prefix: (h, 0, 0))],
            out_specs=[
                pl.BlockSpec((length, 128), lambda h, far, prefix: (0, h)),
                pl.BlockSpec((2, length, length), lambda h, far, prefix: (h, 0, 0)),
            ],
        ),
        out_shape=[
            jax.ShapeDtypeStruct((length, width), jnp.bfloat16),
            jax.ShapeDtypeStruct((2 * pairs, length, length), jnp.bfloat16),
        ],
        compiler_params=pltpu.CompilerParams(vmem_limit_bytes=VMEM_BYTES),
        cost_estimate=cost(13),
        name="attention_forward",
    )(far, prefix, qkv_rows, qkv_rows, qkv_rows, offsets.reshape(pairs, 2, 4 * BLOCK))


def attention_backward_kernel(queries, keys, values, grads, probs, grad_rows, bands, *, heads, blocks):
    lane = lax.broadcasted_iota(jnp.int32, queries.shape, 1)
    query_t = (queries[...] * 0.125).astype(jnp.bfloat16).T
    grad_t = grads[...].T
    dq, dk, dv = [], [], []
    for head in range(2):
        mine = (lane < heads) if head == 0 else (lane >= heads)
        sums = [None] * 4
        grad = jnp.where(mine, grads[...], 0.0).astype(jnp.bfloat16)
        back = dot_f32(grad, values[...], NT)
        strips = []
        for row_block in range(blocks):
            span = seen_blocks(row_block, blocks)
            rows = slice(row_block * BLOCK, (row_block + 1) * BLOCK)
            soft = probs[head, pl.ds(row_block * BLOCK, BLOCK), pl.ds(0, span * BLOCK)].astype(jnp.float32)
            part = back[rows, : span * BLOCK]
            inner = jnp.sum(soft * part, axis=1, keepdims=True)
            score_grad = (soft * (part - inner)).astype(jnp.bfloat16)
            for key_block in range(span):
                band = max(key_block - row_block, -2)
                tile = score_grad[:, key_block * BLOCK : (key_block + 1) * BLOCK].astype(jnp.float32)
                sums[band + 2] = tile if sums[band + 2] is None else sums[band + 2] + tile
            if span < blocks:
                rest = jnp.zeros((BLOCK, (blocks - span) * BLOCK), jnp.bfloat16)
                score_grad = jnp.concatenate([score_grad, rest], axis=1)
            strips.append(score_grad)
        flow = jnp.concatenate(strips, axis=0)
        for band in range(4):
            bands[head, band] = sums[band]
        part = slice(head * heads, (head + 1) * heads)
        dq.append(dot_f32(flow, keys[...]) * 0.125)
        dk.append(dot_f32(query_t[part], flow))
        dv.append(dot_f32(grad_t[part], probs[head]))
    grad_rows[0] = jnp.where(lane < heads, dq[0], dq[1]).astype(jnp.bfloat16)
    grad_rows[1] = jnp.concatenate(dk, axis=0).T.astype(jnp.bfloat16)
    grad_rows[2] = jnp.concatenate(dv, axis=0).T.astype(jnp.bfloat16)


def attention_backward(qkv_rows, grads, probs):
    length, width = grads.shape
    pairs = width // 128
    blocks = length // BLOCK
    block = pl.BlockSpec((length, 128), lambda h: (0, h))
    of_three = [pl.BlockSpec((None, length, 128), lambda h, c=c: (c, 0, h)) for c in range(3)]
    return pl.pallas_call(
        lambda *refs: attention_backward_kernel(*refs, heads=64, blocks=blocks),
        grid=(pairs,),
        in_specs=[*of_three, block, pl.BlockSpec((2, length, length), lambda h: (h, 0, 0))],
        out_specs=[pl.BlockSpec((3, length, 128), lambda h: (0, 0, h)), pl.BlockSpec((2, 4, BLOCK, BLOCK), lambda h: (h, 0, 0, 0))],
        out_shape=[jax.ShapeDtypeStruct((3, length, width), jnp.bfloat16)]
        + [jax.ShapeDtypeStruct((2 * pairs, 4, BLOCK, BLOCK), jnp.float32)],
        compiler_params=pltpu.CompilerParams(vmem_limit_bytes=VMEM_BYTES),
        cost_estimate=cost(4),
        name="attention_backward",
    )(qkv_rows, qkv_rows, qkv_rows, grads, probs)


def pieces_left(lefts, plans, many):
    part = lefts[0][0].shape[0] // THIRDS
    return jnp.concatenate(
        [
            jnp.concatenate([ref[pl.ds(third * part, part), :] for ref in lefts[group * many + k]], axis=1)
            for plan in plans
            for group, third in plan
            for k in range(many)
        ]
    )


def put_pieces(result, outs):
    place = 0
    for out in outs:
        many, pieces, part = out.shape[:3]
        for piece in range(pieces):
            for k in range(many):
                out[k, piece] = result[place : place + part]
                place += part


def weight_part_kernel(picks, *refs, count, plans, many):
    lefts, rights, outs = refs[: 2 * count], refs[2 * count : 2 * count + 2], refs[2 * count + 2 :]
    left = pieces_left(list(zip(lefts[:count], lefts[count:])), plans, many)
    right = jnp.concatenate([ref[...] for ref in rights], axis=0)
    put_pieces(dot_f32(left, right).astype(jnp.bfloat16), outs)


def weight_part_plain(picks, lefts, rights, rows, plans, many):
    left, right = jnp.concatenate(lefts, axis=1), jnp.concatenate(rights, axis=0)
    depth, width = right.shape
    part = rows // THIRDS
    result = jnp.take(left.reshape(-1, rows, depth), picks, axis=0)
    result = jnp.einsum("srd,dw->srw", result, right, preferred_element_type=jnp.float32).astype(jnp.bfloat16)
    result = result.reshape(-1, many, THIRDS, part, width)
    return [jnp.stack([result[group, :, third] for group, third in plan], axis=1) for plan in plans]


def weight_part(picks, lefts, rights, rows, plans, many, tile):
    depth, width = rights[0].shape
    count, part = picks.shape[0], rows // THIRDS
    if part % 16:
        return weight_part_plain(picks, lefts, rights, rows, plans, many)
    return pl.pallas_call(
        lambda *refs: weight_part_kernel(*refs, count=count, plans=plans, many=many),
        grid_spec=pltpu.PrefetchScalarGridSpec(
            num_scalar_prefetch=1,
            grid=(width // tile,),
            in_specs=[pl.BlockSpec((rows, depth), lambda i, picks, k=k: (picks[k], 0)) for k in range(count)] * 2
            + [pl.BlockSpec((depth, tile), lambda i, picks: (0, i))] * 2,
            out_specs=[pl.BlockSpec((many, len(plan), part, tile), lambda i, picks: (0, 0, 0, i)) for plan in plans],
        ),
        out_shape=[jax.ShapeDtypeStruct((many, len(plan), part, width), jnp.bfloat16) for plan in plans],
        compiler_params=pltpu.CompilerParams(vmem_limit_bytes=VMEM_BYTES),
        cost_estimate=cost(4),
        name="weight_part",
    )(picks, *([lefts[0]] * count), *([lefts[1]] * count), *rights)


def hot_columns(slots, first, count):
    rows = first + lax.broadcasted_iota(jnp.int32, (count, slots.shape[1]), 0)
    return (rows == slots).astype(jnp.bfloat16)


def halves(core, mine, other):
    return jnp.where(core == 0, mine, other), jnp.where(core == 0, other, mine)


def join_kernel(places, *refs):
    pieces, out = refs[:-1], refs[-1]
    rows = pieces[0].shape[1]
    count = pieces[0].shape[0]
    for chunk in range(out.shape[0] // count):
        for step in range(len(pieces) * count // out.shape[0]):
            piece = pieces[chunk * (len(pieces) * count // out.shape[0]) + step]
            start = pl.multiple_of(places[step] * rows, rows)
            out[pl.ds(chunk * count, count), pl.ds(start, rows), :] = piece[...]


def join(places, chunks):
    count, rows, columns = chunks[0][0].shape
    steps = len(chunks[0])
    return pl.pallas_call(
        join_kernel,
        in_specs=[pl.BlockSpec(memory_space=pltpu.SMEM)] + [pl.BlockSpec(memory_space=pltpu.VMEM)] * (steps * len(chunks)),
        out_shape=jax.ShapeDtypeStruct((count * len(chunks), steps * rows, columns), jnp.bfloat16),
        compiler_params=pltpu.CompilerParams(vmem_limit_bytes=VMEM_BYTES),
        cost_estimate=cost(3),
        name="join",
    )(places, *[piece for chunk in chunks for piece in chunk])


def project_kernel(core, rows, mine, other, result):
    half = mine.shape[1]
    first, second = halves(core[0], mine[...], other[...])
    result[:, :half] = dot_f32(rows[...], first).astype(jnp.bfloat16)
    result[:, half:] = dot_f32(rows[...], second).astype(jnp.bfloat16)


def project(core, rows, mine, other, used):
    width, half = mine.shape[1:]
    length = rows.shape[0]
    return pl.pallas_call(
        project_kernel,
        grid_spec=pltpu.PrefetchScalarGridSpec(
            num_scalar_prefetch=1,
            grid=(used,),
            in_specs=[
                whole((length, width)),
                pl.BlockSpec((None, width, half), lambda i, core: (i, 0, 0)),
                pl.BlockSpec((None, width, half), lambda i, core: (i, 0, 0)),
            ],
            out_specs=pl.BlockSpec((None, length, 2 * half), lambda i, core: (i, 0, 0)),
        ),
        out_shape=jax.ShapeDtypeStruct((used, length, 2 * half), jnp.bfloat16),
        compiler_params=pltpu.CompilerParams(vmem_limit_bytes=VMEM_BYTES),
        cost_estimate=cost(4),
        name="project",
    )(core, rows, mine, other)


def route_kernel(core, attended, tokens, mine, other, gain, router, routes, slots, middle, normed, gates, *outs):
    f32 = jnp.float32
    first, second = halves(core[0], mine[...], other[...])
    rows = attended[...]
    moved = jnp.concatenate([dot_f32(rows, first), dot_f32(rows, second)], axis=1)
    value = tokens[...].astype(f32) + moved
    middle[...] = value
    low = (value * lax.rsqrt(jnp.mean(value * value, axis=1, keepdims=True) + EPS) * gain[...]).astype(jnp.bfloat16)
    normed[...] = low
    start = 0
    for first_out, second_out in zip(outs[::2], outs[1::2]):
        size = first_out.shape[0]
        hot = hot_columns(slots[0:1, :], start, 2 * size) + hot_columns(slots[1:2, :], start, 2 * size)
        part = dot_f32(hot, low).astype(jnp.bfloat16)
        first_out[...] = part[:size]
        second_out[...] = part[size:]
        start += 2 * size
    logits = dot_f32(low, router[...])
    soft = jnp.exp(logits - jnp.max(logits, axis=1, keepdims=True))
    soft = soft / jnp.sum(soft, axis=1, keepdims=True)
    expert = lax.broadcasted_iota(jnp.int32, soft.shape, 1)
    chosen = [jnp.sum(jnp.where(expert == routes[:, k : k + 1], soft, 0.0), axis=1, keepdims=True) for k in range(2)]
    for k in range(2):
        gates[:, k : k + 1] = chosen[k] / (chosen[0] + chosen[1])


def route(core, attended, tokens, mine, other, gain, router, routes, slots, pieces, count):
    length, width = tokens.shape
    last, half = mine.shape[0] - 1, mine.shape[2]
    f32, bf16 = jnp.float32, jnp.bfloat16
    weight = pl.BlockSpec((None, width, half), lambda i, core: (last, 0, 0))
    shapes = [((length, width), f32), ((length, width), bf16), ((length, 2), f32)] + [((count, width), bf16)] * pieces
    return pl.pallas_call(
        route_kernel,
        grid_spec=pltpu.PrefetchScalarGridSpec(
            num_scalar_prefetch=1,
            grid=(1,),
            in_specs=[whole((length, width)), whole((length, width)), weight, weight, whole((1, width)), whole(router.shape), whole(routes.shape), whole(slots.shape)],
            out_specs=[whole(shape) for shape, _ in shapes],
        ),
        out_shape=[jax.ShapeDtypeStruct(shape, kind) for shape, kind in shapes],
        compiler_params=pltpu.CompilerParams(vmem_limit_bytes=VMEM_BYTES),
        cost_estimate=cost(6),
        name="route",
    )(core, attended, tokens, mine, other, gain.reshape(1, -1), router, routes, slots)


def hot_route(slots, k, count):
    cols = lax.broadcasted_iota(jnp.int32, (slots.shape[0], count), 1)
    return cols == slots[:, k : k + 1]


def combine_kernel(*refs, count):
    slots, slots_t, scale = refs[:3]
    pieces = refs[3 : 3 + count]
    middle, teacher, cotangent, valid, gates, routes = refs[3 + count : 9 + count]
    output, grad_y, grad_logits, square = refs[9 + count : 13 + count]
    sends, rows = refs[13 + count : 13 + 2 * count], refs[13 + 2 * count]
    f32, bf16 = jnp.float32, jnp.bfloat16
    assemble(rows, pieces)
    table = rows[...]
    picked = [dot_f32(hot_route(slots, k, rows.shape[0]).astype(bf16), table) for k in range(2)]
    result = middle[...] + (gates[:, 0:1] * picked[0] + gates[:, 1:2] * picked[1])
    output[...] = result.astype(bf16)
    misfit = valid[...] * (result - teacher[...].astype(f32))
    square[...] = jnp.sum((misfit * misfit).reshape(-1, 8, misfit.shape[1]), axis=0)
    grad = cotangent[...].astype(f32) + misfit * scale[0, 0]
    grad_y[...] = grad
    steep = [jnp.sum(grad * picked[k], axis=1, keepdims=True) for k in range(2)]
    slack = gates[:, 0:1] * steep[0] + gates[:, 1:2] * steep[1]
    expert = lax.broadcasted_iota(jnp.int32, grad_logits.shape, 1)
    turn = [jnp.where(expert == routes[:, k : k + 1], gates[:, k : k + 1] * (steep[k] - slack), 0.0) for k in range(2)]
    grad_logits[...] = (turn[0] + turn[1]).astype(bf16)
    scaled = [(gates[:, k : k + 1] * grad).astype(bf16) for k in range(2)]
    start = 0
    for first, second in zip(sends[::2], sends[1::2]):
        size = first.shape[0]
        part = [dot_f32(hot_columns(slots_t[k : k + 1, :], start, 2 * size), scaled[k]) for k in range(2)]
        part = (part[0] + part[1]).astype(bf16)
        first[...] = part[:size]
        second[...] = part[size:]
        start += 2 * size


def combine(slots, slots_t, scale, pieces, middle, teacher, cotangent, valid, gates, routes, experts):
    length, width = middle.shape
    count = len(pieces)
    f32, bf16 = jnp.float32, jnp.bfloat16
    return pl.pallas_call(
        lambda *refs: combine_kernel(*refs, count=count),
        in_specs=[pl.BlockSpec(memory_space=pltpu.VMEM)] * 2
        + [pl.BlockSpec(memory_space=pltpu.SMEM)]
        + [pl.BlockSpec(memory_space=pltpu.VMEM)] * (6 + count),
        out_shape=[
            jax.ShapeDtypeStruct((length, width), bf16),
            jax.ShapeDtypeStruct((length, width), f32),
            jax.ShapeDtypeStruct((length, experts), bf16),
            jax.ShapeDtypeStruct((8, width), f32),
        ]
        + [jax.ShapeDtypeStruct(piece.shape, bf16) for piece in pieces],
        scratch_shapes=[pltpu.VMEM((sum(piece.shape[0] for piece in pieces), width), bf16)],
        compiler_params=pltpu.CompilerParams(vmem_limit_bytes=VMEM_BYTES),
        cost_estimate=cost(8),
        name="combine",
    )(slots, slots_t, scale, *pieces, middle, teacher, cotangent, valid, gates, routes)


def norm_back(value, gain, grad):
    root = lax.rsqrt(jnp.mean(value * value, axis=1, keepdims=True) + EPS)
    normed = value * root
    scaled = grad * gain
    inner = jnp.mean(scaled * normed, axis=1, keepdims=True)
    return root * (scaled - normed * inner), jnp.sum((grad * normed).reshape(-1, 8, value.shape[1]), axis=0)


def collect_kernel(core, *refs, count):
    slots, pieces = refs[0], refs[1 : 1 + count]
    middle, gain, grad_logits, router, grad_y, mine, other = refs[1 + count : 8 + count]
    grad_middle, rounded, grad_attended, grad_gain, rows = refs[8 + count :]
    assemble(rows, pieces)
    hot = (hot_route(slots, 0, rows.shape[0]) | hot_route(slots, 1, rows.shape[0])).astype(jnp.bfloat16)
    grad = dot_f32(grad_logits[...], router[...], NT) + dot_f32(hot, rows[...])
    turned, grad_gain[...] = norm_back(middle[...], gain[...], grad)
    result = grad_y[...] + turned
    grad_middle[...] = result
    low = result.astype(jnp.bfloat16)
    rounded[...] = low
    first, second = halves(core[0], mine[...], other[...])
    half = first.shape[1]
    grad_attended[...] = (dot_f32(low[:, :half], first, NT) + dot_f32(low[:, half:], second, NT)).astype(jnp.bfloat16)


def collect(core, slots, pieces, middle, gain, grad_logits, router, grad_y, mine, other):
    length, width = middle.shape
    last, half = mine.shape[0] - 1, mine.shape[2]
    f32, bf16 = jnp.float32, jnp.bfloat16
    weight = pl.BlockSpec((None, width, half), lambda i, core: (last, 0, 0))
    plain = [slots, *pieces, middle, gain.reshape(1, -1), grad_logits, router, grad_y]
    shapes = [((length, width), f32), ((length, width), bf16), ((length, width), bf16), ((8, width), f32)]
    return pl.pallas_call(
        lambda *refs: collect_kernel(*refs, count=len(pieces)),
        grid_spec=pltpu.PrefetchScalarGridSpec(
            num_scalar_prefetch=1,
            grid=(1,),
            in_specs=[whole(array.shape) for array in plain] + [weight, weight],
            out_specs=[whole(shape) for shape, _ in shapes],
            scratch_shapes=[pltpu.VMEM((sum(piece.shape[0] for piece in pieces), width), bf16)],
        ),
        out_shape=[jax.ShapeDtypeStruct(shape, kind) for shape, kind in shapes],
        compiler_params=pltpu.CompilerParams(vmem_limit_bytes=VMEM_BYTES),
        cost_estimate=cost(8),
        name="collect",
    )(core, *plain, mine, other)


def outer_halves_kernel(core, normed, attended, rights, last, *refs, count):
    aways, stays, normed_t, attended_t = refs[:2], refs[2:4], refs[4], refs[5]
    step = pl.program_id(0)

    @pl.when(step == 0)
    def _():
        normed_t[...] = normed[...].T
        attended_t[...] = attended[...].T

    for place in range(count + 1):

        @pl.when(step == place)
        def _():
            result = dot_f32(normed_t[...], rights[...]) if place < count else dot_f32(attended_t[...], last[...])
            result = result.astype(jnp.bfloat16)
            half = result.shape[1] // 2
            away, stay = aways[place // 2], stays[place // 2]
            slot = place % 2

            @pl.when(core[0] == 0)
            def _():
                stay[slot] = result[:, :half]
                away[slot] = result[:, half:]

            @pl.when(core[0] != 0)
            def _():
                away[slot] = result[:, :half]
                stay[slot] = result[:, half:]


def outer_halves(core, normed, attended, rights, last):
    length, width = normed.shape
    count, half = rights.shape[0], width // 2
    shape = jax.ShapeDtypeStruct((2, width, half), jnp.bfloat16)
    return pl.pallas_call(
        lambda *refs: outer_halves_kernel(*refs, count=count),
        grid_spec=pltpu.PrefetchScalarGridSpec(
            num_scalar_prefetch=1,
            grid=(count + 1,),
            in_specs=[
                whole((length, width)),
                whole((length, width)),
                pl.BlockSpec((None, length, width), lambda i, core: (jnp.minimum(i, count - 1), 0, 0)),
                whole((length, width)),
            ],
            out_specs=[whole(shape.shape)] * 4,
            scratch_shapes=[pltpu.VMEM((width, length), jnp.bfloat16)] * 2,
        ),
        out_shape=[shape] * 4,
        compiler_params=pltpu.CompilerParams(vmem_limit_bytes=VMEM_BYTES),
        cost_estimate=cost(2),
        name="outer_halves",
    )(core, normed, attended, rights, last)


def enter_kernel(core, grads, mine, other, tokens, gain, grad_middle, grad_input, grad_gain, total):
    step = pl.program_id(0)
    first, second = halves(core[0], mine[...], other[...])
    half = first.shape[1]
    rows = grads[...]
    part = dot_f32(rows[:, :half], first, NT) + dot_f32(rows[:, half:], second, NT)

    @pl.when(step == 0)
    def _():
        total[...] = part

    @pl.when(step > 0)
    def _():
        total[...] += part

    @pl.when(step == pl.num_programs(0) - 1)
    def _():
        turned, grad_gain[...] = norm_back(tokens[...].astype(jnp.float32), gain[...], total[...])
        grad_input[...] = grad_middle[...] + turned


def enter(core, grads, mine, other, tokens, gain, grad_middle):
    length, width = tokens.shape
    count, half = grads.shape[0], mine.shape[2]
    weight = pl.BlockSpec((None, width, half), lambda i, core: (i, 0, 0))
    return pl.pallas_call(
        enter_kernel,
        grid_spec=pltpu.PrefetchScalarGridSpec(
            num_scalar_prefetch=1,
            grid=(count,),
            in_specs=[pl.BlockSpec((None, length, width), lambda i, core: (i, 0, 0)), weight, weight, whole((length, width)), whole((1, width)), whole((length, width))],
            out_specs=[whole((length, width)), whole((8, width))],
            scratch_shapes=[pltpu.VMEM((length, width), jnp.float32)],
        ),
        out_shape=[jax.ShapeDtypeStruct((length, width), jnp.float32), jax.ShapeDtypeStruct((8, width), jnp.float32)],
        compiler_params=pltpu.CompilerParams(vmem_limit_bytes=VMEM_BYTES),
        cost_estimate=cost(6),
        name="enter",
    )(core, grads, mine, other, tokens, gain.reshape(1, -1), grad_middle)


BOUNDS = (12, 16, 23, 32, 46, 64, 91)
TOP_PRECISION = lax.Precision.HIGHEST
AXES = ("dp", "expert")
PAIR = 2


def after(value, *others):
    return lax.optimization_barrier((value, *others))[0] if others else value


def bucket_index(offset):
    distance = jnp.abs(offset)
    far_bucket = 8 + sum([(distance >= level).astype(jnp.int32) for level in BOUNDS])
    near_bucket = jnp.where(distance < 8, distance, far_bucket)
    return jnp.where(offset > 0, 16, 0) + near_bucket


def norm_apply(inputs, gain_vec):
    return inputs * lax.rsqrt(jnp.mean(inputs * inputs, axis=-1, keepdims=True) + EPS) * gain_vec


def tile_offsets(query_block, key_block):
    rows = query_block * BLOCK + lax.broadcasted_iota(jnp.int32, (BLOCK, BLOCK), 0)
    cols = key_block * BLOCK + lax.broadcasted_iota(jnp.int32, (BLOCK, BLOCK), 1)
    return rows, cols


def offset_bias(table):
    offsets = jnp.arange(4 * BLOCK, dtype=jnp.int32) - 2 * BLOCK
    hot = (bucket_index(offsets)[None] == jnp.arange(table.shape[1], dtype=jnp.int32)[:, None]).astype(jnp.float32)
    return jnp.dot(table, hot, precision=TOP_PRECISION)


def table_gradient(bands, buckets):
    rows, cols = tile_offsets(0, 0)
    ids = [jnp.full((BLOCK, BLOCK), bucket_far(), jnp.int32)]
    ids += [bucket_index(shift * BLOCK + cols - rows) for shift in (-1, 0, 1)]
    hot = (jnp.stack(ids)[..., None] == jnp.arange(buckets, dtype=jnp.int32)).astype(jnp.float32)
    return jnp.einsum("hdxy,dxyb->hb", bands, hot, precision=TOP_PRECISION)


def bucket_far():
    return 8 + len(BOUNDS)


def on_device(
    tokens,
    qkv_weight,
    out_weight,
    position_bias_table,
    gain_attn,
    gain_moe,
    router,
    w_in,
    w_out,
    routes,
    prefix,
    valid_mask,
    teacher,
    cotangent,
):
    length, width = tokens.shape
    bf16, f32 = jnp.bfloat16, jnp.float32
    expert_count = router.shape[1]
    top_count = routes.shape[1]
    groups = lax.axis_size("expert")
    copies = lax.axis_size("dp")
    inner = w_in.shape[2]
    capacity = 5 * length * top_count // (4 * expert_count)
    total_tokens = length * copies * groups
    sources = 2 * groups
    blocks = length // BLOCK
    here_dp, here_group = lax.axis_index("dp"), lax.axis_index("expert")
    half = (here_dp >> 1) & 1
    core = here_group & 1
    rest = copies // 4

    def swap(value, dp_mask, group_mask):
        pairs = [
            (i, ((i // groups) ^ dp_mask) * groups + ((i % groups) ^ group_mask))
            for i in range(copies * groups)
        ]
        return lax.ppermute(value, AXES, pairs)

    def bits(count):
        return [1 << place for place in range(count.bit_length() - 1)]

    def partial_sums(value):
        sums = []
        for masks in [(0, mask) for mask in bits(groups)] + [(mask, 0) for mask in bits(copies)]:
            value = value + swap(value, *masks)
            sums.append(value)
        return sums

    chips = groups

    def across(value, place):
        return swap(value, PAIR * (place // (groups // 2)), 2 * (place % (groups // 2)))

    def to_chips(pieces):
        return [pieces[0]] + [across(pieces[place], place) for place in range(1, chips)]

    def through(visit, sends):
        direct, relay = to_chips(sends[::2]), to_chips(sends[1::2])
        seen, direct = visit(direct)
        direct = to_chips(direct)
        relay = [after(part, seen) for part in relay]
        passed = visit(swap(jnp.concatenate(relay), 0, 1))
        return direct, [swap(after(part, *direct), 0, 1) for part in passed]

    def weave(direct, relay):
        return [part for pair in zip(direct, to_chips(relay)) for part in pair]

    ring = list(range(0, copies, 2)) + list(range(copies - 1, 0, -2))
    turns = [(1, step) for step in range(1, copies // 2 + 1)] + [(-1, step) for step in range(1, copies // 2)]

    def gather_ring(shard, due):
        got = [shard]
        for turn in (1, -1):
            held = shard
            pairs = [(ring[i], ring[(i + turn) % copies]) for i in range(copies)]
            for step in [step for way, step in turns if way == turn]:
                held = lax.ppermute(after(held, *due[step - 2 : step - 1]) if step > 1 else held, "dp", pairs)
                got.append(held)
        return got

    def ring_places():
        place = jnp.where(here_dp & 1 == 0, here_dp >> 1, copies - 1 - (here_dp >> 1))
        shift = jnp.array([0] + [turn * step for turn, step in turns], jnp.int32)
        place = (place - shift) & (copies - 1)
        return jnp.where(place < copies // 2, 2 * place, 2 * (copies - 1 - place) + 1).astype(jnp.int32)


    flat_routes = routes.reshape(-1)
    pair_count = length * top_count
    slot_count = sources * capacity
    route_hits = (flat_routes[:, None] == jnp.arange(expert_count, dtype=jnp.int32)[None, :]).astype(bf16)
    lower_ones = (
        lax.broadcasted_iota(jnp.int32, (pair_count, pair_count), 0)
        >= lax.broadcasted_iota(jnp.int32, (pair_count, pair_count), 1)
    ).astype(bf16)
    running = jnp.dot(lower_ones, route_hits, preferred_element_type=f32)
    pair_rank = jnp.sum((running - 1.0) * route_hits.astype(f32), axis=1).astype(jnp.int32)
    away = (flat_routes >> 1) ^ here_group
    chip = ((flat_routes & 1) ^ half) * (groups // 2) + (away >> 1)
    slots = ((chip * 2 + (away & 1)) * capacity + pair_rank).reshape(length, top_count)
    slots_t = slots.T

    resid = tokens.astype(f32)
    normed1 = norm_apply(resid, gain_attn).astype(bf16)
    columns = width // 2
    core_index = core.reshape(1).astype(jnp.int32)
    valid_rows = valid_mask.astype(f32)[:, None]
    counts = [jnp.broadcast_to(jnp.sum(valid_rows), (8, 128))]
    count_trades = [(0, mask) for mask in bits(groups)] + [(mask, 0) for mask in bits(copies)]

    def count_beside(before, value):
        if len(counts) > len(count_trades):
            return value
        counts.append(counts[-1] + swap(after(counts[-1], before), *count_trades[len(counts) - 1]))
        return after(value, counts[-1])

    shards = [
        lax.dynamic_slice_in_dim(part, core * columns, columns, 2)
        for part in (qkv_weight[:2], jnp.concatenate([qkv_weight[2:], out_weight[None]]))
    ]
    if copies > 8:
        mine = lax.all_gather(jnp.concatenate(shards), "dp", axis=1, tiled=True)
    else:
        mine = join(ring_places(), [gather_ring(shards[0], ()), gather_ring(shards[1], (slots_t, normed1))])
    other = count_beside(mine, swap(mine, 0, 1))
    qkv_rows = count_beside(other, project(core_index, normed1, mine, other, 3))
    offsets = offset_bias(position_bias_table)
    attended, probs = attention_forward(position_bias_table[:, bucket_far()], prefix, qkv_rows, offsets)
    middle, normed2, gates, *sends = route(
        core_index, count_beside(qkv_rows, attended), tokens, mine, other, gain_moe, router, routes, slots_t, 2 * chips, capacity
    )

    pick = half.reshape(1).astype(jnp.int32)
    hidden, slopes, rows_in = [], [], []

    def expert(pieces):
        one = not isinstance(pieces, list)
        pieces = [pieces] if one else pieces
        hidden_t, slope, rows_t, *results = expert_forward(pick, pieces, chips, w_in, w_out)
        hidden_t = count_beside(pieces[-1], hidden_t)
        for kept, value in zip((hidden, slopes, rows_in), (hidden_t, slope, rows_t)):
            kept.append(value)
        return results if one else (hidden_t, results)

    back = weave(*through(expert, sends))
    while len(counts) <= len(count_trades):
        back[0] = count_beside(back[0], back[0])
    valid_count = counts[-1][0, 0]
    scale = (total_tokens / valid_count).reshape(1, 1)
    output, grad_y, grad_logits, squares, *sends = combine(
        slots, slots_t, scale, back, middle, teacher, cotangent, valid_rows, gates, routes, expert_count
    )

    out_rows = inner // copies
    in_rows = width // copies
    far_bit = here_dp % 2
    slices = jnp.arange(rest, dtype=jnp.int32) * 4

    def picks(bit0):
        return jnp.concatenate([slices + ((half ^ other_half) * 2 + bit0) for other_half in (1, 0)]).astype(jnp.int32)

    sent, kept = picks(1 - far_bit), picks(far_bit)

    def add(left, right):
        return (left.astype(f32) + right.astype(f32)).astype(bf16)

    def fold(unit, bit, axis=0):
        unit = unit.reshape(unit.shape[:axis] + (2, unit.shape[axis] // 2) + unit.shape[axis + 1 :])
        away_part = lax.dynamic_index_in_dim(unit, 1 - bit, axis, keepdims=False)
        return away_part, lax.dynamic_index_in_dim(unit, bit, axis, keepdims=False)

    far_masks = list(reversed(bits(copies)[2:]))

    def near_add(got, keep):
        away_part, stay_part = fold(add(got, keep), (here_dp // far_masks[0]) % 2)
        return away_part, stay_part

    def far_trade(away_part):
        return swap(away_part, far_masks[0], 0)

    def finish(got, stay):
        unit = add(got, stay)
        for mask in far_masks[1:]:
            away_part, stay_part = fold(unit, (here_dp // mask) % 2)
            unit = add(swap(away_part, mask, 0), stay_part)
        return unit[0]

    plan_a, plan_b, plan_c = ((0, 0), (0, 1)), ((0, 2), (1, 0)), ((1, 1), (1, 2))
    plan_d, plan_e, plan_f = plan_a, plan_b, plan_c
    out_plans, in_plans = (plan_a, plan_b, plan_c), (plan_d, plan_e, plan_f)

    grad_rows, grad_pre, parts = [], [], []

    def expert_back(pieces):
        if isinstance(pieces, list):
            grad_pre_rows, grads, *results = expert_backward(pick, pieces, chips, w_in, w_out, slopes[0])
            grad_rows.append(grads)
            grad_pre.append(grad_pre_rows)
            return grad_pre_rows, results
        grad_rows.append(pieces)
        parts.extend(weight_part(sent, hidden, grad_rows, out_rows, out_plans, rest, width))
        parts[0] = swap(parts[0], 1, 0)
        pieces = after(pieces, parts[1])
        grad_pre_rows, _, *results = expert_backward(pick, [pieces], chips, w_in, w_out, slopes[1])
        grad_pre.append(grad_pre_rows)
        return results

    direct, relay = through(expert_back, sends)
    got_a, send_b, send_c = parts
    relay = [after(part, got_a) for part in relay]
    got_b = swap(after(send_b, relay[0]), 1, 0)
    back = weave(direct, relay)
    grad_rows, grad_pre = lax.optimization_barrier((grad_rows, grad_pre, relay))[:2]
    keep_a, keep_b, keep_c = weight_part(kept, hidden, grad_rows, out_rows, out_plans, rest, width)
    away_a, stay_a = near_add(got_a, keep_a)
    far_a = far_trade(away_a)
    send_d, send_e, send_f = weight_part(sent, rows_in, after(grad_pre, away_a), in_rows, in_plans, rest, inner // 2)
    back = [after(part, send_d) for part in back]
    got_c = swap(after(send_c, send_d), 1, 0)
    grad_middle, grad_attn_proj, grad_attended, gain_moe_parts = collect(
        core_index, slots, back, middle, gain_moe, grad_logits, router, grad_y, mine, other
    )
    away_b, stay_b = near_add(after(got_b, grad_attended), keep_b)
    got_d = swap(after(send_d, grad_attended), 1, 0)
    grad_attended, away_b = lax.optimization_barrier((grad_attended, away_b))
    grad_qkv_rows, bands = attention_backward(qkv_rows, grad_attended, probs)
    grad_qkv_rows, got_c, far_a = lax.optimization_barrier((grad_qkv_rows, got_c, far_a))
    done_a = finish(far_a, stay_a)

    away_c, stay_c = near_add(got_c, keep_c)
    far_c = far_trade(jnp.concatenate([away_b, away_c], axis=1))
    stay_c = jnp.concatenate([stay_b, stay_c], axis=1)
    *weights_away, stay_1, stay_2 = outer_halves(
        core_index, normed1, attended, after(grad_qkv_rows, away_c), grad_attn_proj
    )
    weights_away, got_d = lax.optimization_barrier((weights_away, got_d))
    got_e = swap(after(send_e, got_d), 1, 0)
    keep_d, keep_e, keep_f = weight_part(
        kept, rows_in, after(grad_pre, *weights_away), in_rows, in_plans, rest, inner // 2
    )
    group_masks = bits(groups)[1:]
    dp_masks = sorted(bits(copies), key=lambda mask: (mask != PAIR, mask))

    def over_groups(got, stay, *due):
        got = add(after(got, *due), stay).reshape(2, copies, in_rows, columns)
        for mask in group_masks[:-1]:
            away_part, stay_part = fold(got, (here_group // mask) % 2, 2)
            got = add(swap(away_part, 0, mask), stay_part)
        away_part, stay_part = fold(got, (here_group // group_masks[-1]) % 2, 2)
        return swap(away_part, 0, group_masks[-1]), stay_part

    def over_dp(total, mask, passed):
        axis = 1 + sorted([other for other in dp_masks if other not in passed], reverse=True).index(mask)
        bit = (here_dp // mask) % 2
        away_part = lax.dynamic_index_in_dim(total, 1 - bit, axis, keepdims=False)
        stay_part = lax.dynamic_index_in_dim(total, bit, axis, keepdims=False)
        return swap(away_part, mask, 0), stay_part

    weights_got = [swap(part, 0, 1) for part in weights_away]
    first = over_groups(weights_got[0], stay_1, keep_d)
    second = over_groups(weights_got[1], stay_2, first[1])
    away_d, stay_d = near_add(after(got_d, second[1]), keep_d)
    far_d = far_trade(away_d)
    grad_input, gain_attn_parts = enter(
        core_index, after(grad_qkv_rows, away_d), mine, other, tokens, gain_attn, grad_middle
    )
    done_c = finish(after(far_c, gain_attn_parts), stay_c)
    grad_table = table_gradient(after(bands, second[1]), position_bias_table.shape[1])

    chains = [add(after(first[0], away_d, gain_attn_parts), first[1]).reshape((2,) + (2,) * len(dp_masks) + (-1, columns)), None]
    trades = [over_dp(chains[0], dp_masks[0], ()), None]
    away_e, stay_e = near_add(after(got_e, chains[0]), keep_e)
    got_f = swap(after(send_f, away_e), 1, 0)
    chains[1] = add(after(second[0], done_c, grad_table, away_e), second[1]).reshape(chains[0].shape)
    trades[1] = over_dp(chains[1], dp_masks[0], ())
    total = trades[1][1]
    far_e = far_trade(after(away_e, total))
    done_d = finish(after(far_d, chains[0]), stay_d)
    away_f, stay_f = near_add(after(got_f, total), keep_f)
    far_f = far_trade(away_f)
    trades = [(after(trades[0][0], total, done_d), trades[0][1]), (after(trades[1][0], away_f), trades[1][1])]

    normed2, squares, gain_moe_parts = after((normed2, squares, gain_moe_parts), second[1])
    grad_router = jnp.einsum("td,te->de", normed2, grad_logits, preferred_element_type=f32)
    small = [
        jnp.sum(gain_moe_parts, axis=0),
        jnp.sum(gain_attn_parts, axis=0),
        grad_router,
        grad_table,
        jnp.sum(squares),
    ]
    sizes = [value.size for value in small]
    flat = jnp.concatenate([value.reshape(-1) for value in small])
    flat = after(jnp.pad(flat, (0, -sum(sizes) % 1024)).reshape(-1, 128), total)

    flat = flat + swap(flat, 0, 1)
    for place, mask in enumerate(dp_masks):
        flat_got = swap(flat, 0, group_masks[0]) if mask == PAIR else swap(flat, mask, 0)
        if place + 1 == len(dp_masks):
            trades[1] = (after(trades[1][0], out_theirs), trades[1][1])
        if place == 1:
            done_e = finish(after(far_e, chains[1]), stay_e)
            trades[1] = (after(trades[1][0], done_e), trades[1][1])
        chains = [add(*trades[0]), None]
        if place + 1 < len(dp_masks):
            trades_next = [over_dp(chains[0], dp_masks[place + 1], dp_masks[: place + 1]), None]
        chains[1] = add(after(trades[1][0], chains[0]), trades[1][1])
        flat = flat + flat_got
        if place + 1 < len(dp_masks):
            trades_next[1] = over_dp(chains[1], dp_masks[place + 1], dp_masks[: place + 1])
            trades = trades_next
        if mask == PAIR:
            in_first = swap(done_d, PAIR, 0)
            out_theirs = swap(after(jnp.concatenate([done_a, done_c[:1]]), chains[1]), PAIR, 0)
        flat = after(flat, chains[1])
    total = jnp.concatenate(chains)
    in_theirs = jnp.concatenate([in_first, swap(done_e[:1], PAIR, 0)])
    for mask in reversed(group_masks):
        bit = (here_group // mask) % 2
        other_part = swap(total, 0, mask)
        total = jnp.concatenate([jnp.where(bit == 0, total, other_part), jnp.where(bit == 0, other_part, total)], axis=1)
        if mask == group_masks[0]:
            done_f = finish(after(far_f, total), stay_f)
            total = after(total, done_f)
            flat = flat + swap(flat, PAIR, 0)
        else:
            flat = flat + swap(flat, 0, mask)
        total, flat = lax.optimization_barrier((total, flat))
    other_part = swap(total, 0, 1)
    total = jnp.concatenate([jnp.where(core == 0, total, other_part), jnp.where(core == 0, other_part, total)], axis=2)
    weights_done = total.astype(f32)
    grad_qkv, grad_out_weight = weights_done[:3], weights_done[3]
    flat = flat.reshape(-1)
    starts = [sum(sizes[:place]) for place in range(len(sizes))]
    grad_gain_moe, grad_gain_attn, grad_router, grad_table, square_total = [
        flat[start : start + value.size].reshape(value.shape) for start, value in zip(starts, small)
    ]

    out_mine, in_mine = done_c[1:], jnp.concatenate([done_e[1:], done_f])

    def both_experts(mine, theirs):
        mine, theirs = [part.reshape(-1, part.shape[-1]).astype(f32) for part in (mine, theirs)]
        return jnp.stack([jnp.where(half == 0, mine, theirs), jnp.where(half == 0, theirs, mine)])

    grad_w_out = both_experts(out_mine, out_theirs)
    grad_w_in = both_experts(in_mine, in_theirs)

    distill_loss = square_total / (width * valid_count)
    return (
        output.astype(bf16),
        distill_loss,
        grad_input,
        grad_qkv,
        grad_out_weight,
        grad_w_in,
        grad_w_out,
        grad_router,
        grad_table,
        grad_gain_attn,
        grad_gain_moe,
    )


def solution(mesh):
    rows = P(AXES, None)
    return jax.shard_map(
        on_device,
        mesh=mesh,
        in_specs=(
            rows,
            P(None, "dp", None),
            P("dp", None),
            P(),
            P(),
            P(),
            P(),
            P("expert", None, None),
            P("expert", None, None),
            rows,
            P(AXES),
            P(AXES),
            rows,
            rows,
        ),
        out_specs=(
            rows,
            P(),
            rows,
            P(None, "dp", None),
            P("dp", None),
            P("expert", "dp", None),
            P("expert", "dp", None),
            P(),
            P(),
            P(),
            P(),
        ),
        check_vma=False,
    )
```

```python
import math
import jax
import jax.numpy as jnp
from jax import lax
from jax.experimental import pallas as pl
from jax.experimental.pallas import tpu as pltpu
from jax.sharding import PartitionSpec as P

BLOCK = 128
THIRDS = 3
EPS = 1e-06
GELU_A = math.sqrt(2.0 / math.pi)
GELU_B = 0.044715
NT = (((1,), (1,)), ((), ()))
TN = (((0,), (0,)), ((), ()))
VMEM_BYTES = 56 * 1024 * 1024


def cost(micros):
    return pl.CostEstimate(flops=int(micros * 0.37e9), bytes_accessed=0, transcendentals=0)


def dot_f32(left, right, dims=(((1,), (0,)), ((), ()))):
    return lax.dot_general(left, right, dims, preferred_element_type=jnp.float32)


def assemble(rows, pieces):
    start = 0
    for piece in pieces:
        rows[pl.ds(start, piece.shape[0]), :] = piece[...]
        start += piece.shape[0]


def hand_out(total, outs):
    start = 0
    for out in outs:
        out[...] = total[pl.ds(start, out.shape[0]), :].astype(out.dtype)
        start += out.shape[0]


def whole(shape):
    return pl.BlockSpec(shape, lambda *step: (0,) * len(shape))


def expert_forward_kernel(pick, *refs, chunk, count):
    pieces, w_in, w_out = refs[:count], refs[count], refs[count + 1]
    hidden_t, slope, rows_t = refs[count + 2 : count + 5]
    outs, rows, total = refs[count + 5 : -2], refs[-2], refs[-1]
    step = pl.program_id(0)

    @pl.when(step == 0)
    def _():
        assemble(rows, pieces)
        total[...] = jnp.zeros_like(total)
        rows_t[...] = rows[...].T

    for start in range(0, rows.shape[0], chunk):
        part = pl.ds(start, chunk)
        pre = dot_f32(rows[part, :], w_in[0])
        square = pre * pre
        bend = jnp.tanh(pre * (GELU_A + (GELU_A * GELU_B) * square))
        half = 0.5 + 0.5 * bend
        act = (pre * half).astype(jnp.bfloat16)
        lift = pre * (0.5 * GELU_A + (1.5 * GELU_A * GELU_B) * square)
        slope[part, :] = (half + lift * (1.0 - bend * bend)).astype(jnp.bfloat16)
        hidden_t[:, part] = act.T
        total[part, :] += dot_f32(act, w_out[0])

    @pl.when(step == pl.num_programs(0) - 1)
    def _():
        hand_out(total, outs)


def expert_forward(pick, pieces, results, w_in, w_out, tile=768, chunk=320):
    many, width = sum(piece.shape[0] for piece in pieces), pieces[0].shape[1]
    inner = w_in.shape[2]
    bf16 = jnp.bfloat16
    return pl.pallas_call(
        lambda *refs: expert_forward_kernel(*refs, chunk=chunk, count=len(pieces)),
        grid_spec=pltpu.PrefetchScalarGridSpec(
            num_scalar_prefetch=1,
            grid=(inner // tile,),
            in_specs=[whole(piece.shape) for piece in pieces]
            + [
                pl.BlockSpec((1, width, tile), lambda f, pick: (pick[0], 0, f)),
                pl.BlockSpec((1, tile, width), lambda f, pick: (pick[0], f, 0)),
            ],
            out_specs=[
                pl.BlockSpec((tile, many), lambda f, pick: (f, 0)),
                pl.BlockSpec((many, tile), lambda f, pick: (0, f)),
                whole((width, many)),
            ]
            + [whole((many // results, width))] * results,
            scratch_shapes=[pltpu.VMEM((many, width), bf16), pltpu.VMEM((many, width), jnp.float32)],
        ),
        out_shape=[
            jax.ShapeDtypeStruct((inner, many), bf16),
            jax.ShapeDtypeStruct((many, inner), bf16),
            jax.ShapeDtypeStruct((width, many), bf16),
        ]
        + [jax.ShapeDtypeStruct((many // results, width), bf16)] * results,
        compiler_params=pltpu.CompilerParams(vmem_limit_bytes=VMEM_BYTES),
        cost_estimate=cost(13),
        name="expert_forward",
    )(pick, *pieces, w_in, w_out)


def expert_backward_kernel(pick, *refs, chunk, count):
    pieces, w_in, w_out, slope = refs[:count], refs[count], refs[count + 1], refs[count + 2]
    grad_pre, rows = refs[count + 3 : count + 5]
    outs, total = refs[count + 5 : -1], refs[-1]
    step = pl.program_id(0)

    @pl.when(step == 0)
    def _():
        assemble(rows, pieces)
        total[...] = jnp.zeros_like(total)

    for start in range(0, rows.shape[0], chunk):
        part = pl.ds(start, chunk)
        back = dot_f32(rows[part, :], w_out[0], NT) * slope[part, :].astype(jnp.float32)
        back = back.astype(jnp.bfloat16)
        grad_pre[part, :] = back
        total[part, :] += dot_f32(back, w_in[0], NT)

    @pl.when(step == pl.num_programs(0) - 1)
    def _():
        hand_out(total, outs)


def expert_backward(pick, pieces, results, w_in, w_out, slope, tile=768, chunk=640):
    many, width = sum(piece.shape[0] for piece in pieces), pieces[0].shape[1]
    inner = w_in.shape[2]
    bf16 = jnp.bfloat16
    return pl.pallas_call(
        lambda *refs: expert_backward_kernel(*refs, chunk=chunk, count=len(pieces)),
        grid_spec=pltpu.PrefetchScalarGridSpec(
            num_scalar_prefetch=1,
            grid=(inner // tile,),
            in_specs=[whole(piece.shape) for piece in pieces]
            + [
                pl.BlockSpec((1, width, tile), lambda f, pick: (pick[0], 0, f)),
                pl.BlockSpec((1, tile, width), lambda f, pick: (pick[0], f, 0)),
                pl.BlockSpec((many, tile), lambda f, pick: (0, f)),
            ],
            out_specs=[pl.BlockSpec((many, tile), lambda f, pick: (0, f)), whole((many, width))]
            + [whole((many // results, width))] * results,
            scratch_shapes=[pltpu.VMEM((many, width), jnp.float32)],
        ),
        out_shape=[jax.ShapeDtypeStruct((many, inner), bf16), jax.ShapeDtypeStruct((many, width), bf16)]
        + [jax.ShapeDtypeStruct((many // results, width), bf16)] * results,
        compiler_params=pltpu.CompilerParams(vmem_limit_bytes=VMEM_BYTES),
        cost_estimate=cost(11),
        name="expert_backward",
    )(pick, *pieces, w_in, w_out, slope)


def seen_blocks(row_block, blocks):
    return max(row_block + 1, blocks // 2)


def attention_forward_kernel(far, prefix, queries, keys, values, offsets, attended, probs, *, heads, blocks):
    pair = pl.program_id(0)
    lane = lax.broadcasted_iota(jnp.int32, queries.shape, 1)
    row = lax.broadcasted_iota(jnp.int32, (BLOCK, BLOCK), 0)
    col = lax.broadcasted_iota(jnp.int32, (BLOCK, BLOCK), 1)
    outs = []
    for head in range(2):
        line = jnp.broadcast_to(offsets[head : head + 1, :], (BLOCK, 4 * BLOCK))
        turned = pltpu.roll(line, 0, 1, stride=1, stride_axis=0)
        far_bias = far[pair * 2 + head]
        mine = (lane < heads) if head == 0 else (lane >= heads)
        query = jnp.where(mine, queries[...] * 0.125, 0.0).astype(jnp.bfloat16)
        score = dot_f32(query, keys[...], NT)
        strips = []
        for row_block in range(blocks):
            span = seen_blocks(row_block, blocks)
            pieces = []
            for key_block in range(span):
                piece = score[row_block * BLOCK : (row_block + 1) * BLOCK, key_block * BLOCK : (key_block + 1) * BLOCK]
                shift = key_block - row_block
                if shift < -1:
                    piece = piece + far_bias
                elif shift < 2:
                    piece = piece + turned[:, (2 + shift) * BLOCK : (3 + shift) * BLOCK]
                else:
                    raise ValueError(shift)
                if shift >= 0:
                    shown = col + key_block * BLOCK < prefix[0]
                    piece = jnp.where((shown | (col <= row)) if shift == 0 else shown, piece, -1e30)
                pieces.append(piece)
            peak = pieces[0]
            for piece in pieces[1:]:
                peak = jnp.maximum(peak, piece)
            peak = jnp.max(peak, axis=1, keepdims=True)
            pieces = [jnp.exp(piece - peak) for piece in pieces]
            mass = pieces[0]
            for piece in pieces[1:]:
                mass = mass + piece
            scale = 1.0 / jnp.sum(mass, axis=1, keepdims=True)
            pieces = [(piece * scale).astype(jnp.bfloat16) for piece in pieces]
            pieces += [jnp.zeros((BLOCK, BLOCK), jnp.bfloat16)] * (blocks - span)
            strips.append(jnp.concatenate(pieces, axis=1))
        weights = jnp.concatenate(strips, axis=0)
        probs[head] = weights
        outs.append(dot_f32(weights, values[...]))
    attended[...] = jnp.where(lane < heads, outs[0], outs[1]).astype(jnp.bfloat16)


def attention_forward(far, prefix, qkv_rows, offsets):
    length, width = qkv_rows.shape[1:]
    pairs = width // 128
    blocks = length // BLOCK
    return pl.pallas_call(
        lambda *refs: attention_forward_kernel(*refs, heads=64, blocks=blocks),
        grid_spec=pltpu.PrefetchScalarGridSpec(
            num_scalar_prefetch=2,
            grid=(pairs,),
            in_specs=[pl.BlockSpec((None, length, 128), lambda h, far, prefix, c=c: (c, 0, h)) for c in range(3)]
            + [pl.BlockSpec((None, 2, 4 * BLOCK), lambda h, far, prefix: (h, 0, 0))],
            out_specs=[
                pl.BlockSpec((length, 128), lambda h, far, prefix: (0, h)),
                pl.BlockSpec((2, length, length), lambda h, far, prefix: (h, 0, 0)),
            ],
        ),
        out_shape=[
            jax.ShapeDtypeStruct((length, width), jnp.bfloat16),
            jax.ShapeDtypeStruct((2 * pairs, length, length), jnp.bfloat16),
        ],
        compiler_params=pltpu.CompilerParams(vmem_limit_bytes=VMEM_BYTES),
        cost_estimate=cost(13),
        name="attention_forward",
    )(far, prefix, qkv_rows, qkv_rows, qkv_rows, offsets.reshape(pairs, 2, 4 * BLOCK))


def attention_backward_kernel(queries, keys, values, grads, probs, grad_rows, bands, *, heads, blocks):
    lane = lax.broadcasted_iota(jnp.int32, queries.shape, 1)
    query_t = (queries[...] * 0.125).astype(jnp.bfloat16).T
    grad_t = grads[...].T
    dq, dk, dv = [], [], []
    for head in range(2):
        mine = (lane < heads) if head == 0 else (lane >= heads)
        sums = [None] * 4
        grad = jnp.where(mine, grads[...], 0.0).astype(jnp.bfloat16)
        back = dot_f32(grad, values[...], NT)
        strips = []
        for row_block in range(blocks):
            span = seen_blocks(row_block, blocks)
            rows = slice(row_block * BLOCK, (row_block + 1) * BLOCK)
            soft = probs[head, pl.ds(row_block * BLOCK, BLOCK), pl.ds(0, span * BLOCK)].astype(jnp.float32)
            part = back[rows, : span * BLOCK]
            inner = jnp.sum(soft * part, axis=1, keepdims=True)
            score_grad = (soft * (part - inner)).astype(jnp.bfloat16)
            for key_block in range(span):
                band = max(key_block - row_block, -2)
                tile = score_grad[:, key_block * BLOCK : (key_block + 1) * BLOCK].astype(jnp.float32)
                sums[band + 2] = tile if sums[band + 2] is None else sums[band + 2] + tile
            if span < blocks:
                rest = jnp.zeros((BLOCK, (blocks - span) * BLOCK), jnp.bfloat16)
                score_grad = jnp.concatenate([score_grad, rest], axis=1)
            strips.append(score_grad)
        flow = jnp.concatenate(strips, axis=0)
        for band in range(4):
            bands[head, band] = sums[band]
        part = slice(head * heads, (head + 1) * heads)
        dq.append(dot_f32(flow, keys[...]) * 0.125)
        dk.append(dot_f32(query_t[part], flow))
        dv.append(dot_f32(grad_t[part], probs[head]))
    grad_rows[0] = jnp.where(lane < heads, dq[0], dq[1]).astype(jnp.bfloat16)
    grad_rows[1] = jnp.concatenate(dk, axis=0).T.astype(jnp.bfloat16)
    grad_rows[2] = jnp.concatenate(dv, axis=0).T.astype(jnp.bfloat16)


def attention_backward(qkv_rows, grads, probs):
    length, width = grads.shape
    pairs = width // 128
    blocks = length // BLOCK
    block = pl.BlockSpec((length, 128), lambda h: (0, h))
    of_three = [pl.BlockSpec((None, length, 128), lambda h, c=c: (c, 0, h)) for c in range(3)]
    return pl.pallas_call(
        lambda *refs: attention_backward_kernel(*refs, heads=64, blocks=blocks),
        grid=(pairs,),
        in_specs=[*of_three, block, pl.BlockSpec((2, length, length), lambda h: (h, 0, 0))],
        out_specs=[pl.BlockSpec((3, length, 128), lambda h: (0, 0, h)), pl.BlockSpec((2, 4, BLOCK, BLOCK), lambda h: (h, 0, 0, 0))],
        out_shape=[jax.ShapeDtypeStruct((3, length, width), jnp.bfloat16)]
        + [jax.ShapeDtypeStruct((2 * pairs, 4, BLOCK, BLOCK), jnp.float32)],
        compiler_params=pltpu.CompilerParams(vmem_limit_bytes=VMEM_BYTES),
        cost_estimate=cost(4),
        name="attention_backward",
    )(qkv_rows, qkv_rows, qkv_rows, grads, probs)


def pieces_left(lefts, plans, many):
    part = lefts[0][0].shape[0] // THIRDS
    return jnp.concatenate(
        [
            jnp.concatenate([ref[pl.ds(third * part, part), :] for ref in lefts[group * many + k]], axis=1)
            for plan in plans
            for group, third in plan
            for k in range(many)
        ]
    )


def put_pieces(result, outs):
    place = 0
    for out in outs:
        many, pieces, part = out.shape[:3]
        for piece in range(pieces):
            for k in range(many):
                out[k, piece] = result[place : place + part]
                place += part


def weight_part_kernel(picks, *refs, count, plans, many):
    lefts, rights, outs = refs[: 2 * count], refs[2 * count : 2 * count + 2], refs[2 * count + 2 :]
    left = pieces_left(list(zip(lefts[:count], lefts[count:])), plans, many)
    right = jnp.concatenate([ref[...] for ref in rights], axis=0)
    put_pieces(dot_f32(left, right).astype(jnp.bfloat16), outs)


def weight_part_plain(picks, lefts, rights, rows, plans, many):
    left, right = jnp.concatenate(lefts, axis=1), jnp.concatenate(rights, axis=0)
    depth, width = right.shape
    part = rows // THIRDS
    result = jnp.take(left.reshape(-1, rows, depth), picks, axis=0)
    result = jnp.einsum("srd,dw->srw", result, right, preferred_element_type=jnp.float32).astype(jnp.bfloat16)
    result = result.reshape(-1, many, THIRDS, part, width)
    return [jnp.stack([result[group, :, third] for group, third in plan], axis=1) for plan in plans]


def weight_part(picks, lefts, rights, rows, plans, many, tile):
    depth, width = rights[0].shape
    count, part = picks.shape[0], rows // THIRDS
    if part % 16:
        return weight_part_plain(picks, lefts, rights, rows, plans, many)
    return pl.pallas_call(
        lambda *refs: weight_part_kernel(*refs, count=count, plans=plans, many=many),
        grid_spec=pltpu.PrefetchScalarGridSpec(
            num_scalar_prefetch=1,
            grid=(width // tile,),
            in_specs=[pl.BlockSpec((rows, depth), lambda i, picks, k=k: (picks[k], 0)) for k in range(count)] * 2
            + [pl.BlockSpec((depth, tile), lambda i, picks: (0, i))] * 2,
            out_specs=[pl.BlockSpec((many, len(plan), part, tile), lambda i, picks: (0, 0, 0, i)) for plan in plans],
        ),
        out_shape=[jax.ShapeDtypeStruct((many, len(plan), part, width), jnp.bfloat16) for plan in plans],
        compiler_params=pltpu.CompilerParams(vmem_limit_bytes=VMEM_BYTES),
        cost_estimate=cost(4),
        name="weight_part",
    )(picks, *([lefts[0]] * count), *([lefts[1]] * count), *rights)


def hot_columns(slots, first, count):
    rows = first + lax.broadcasted_iota(jnp.int32, (count, slots.shape[1]), 0)
    return (rows == slots).astype(jnp.bfloat16)


def halves(core, mine, other):
    return jnp.where(core == 0, mine, other), jnp.where(core == 0, other, mine)


def join_kernel(places, *refs):
    pieces, out = refs[:-1], refs[-1]
    rows = pieces[0].shape[1]
    count = pieces[0].shape[0]
    for chunk in range(out.shape[0] // count):
        for step in range(len(pieces) * count // out.shape[0]):
            piece = pieces[chunk * (len(pieces) * count // out.shape[0]) + step]
            start = pl.multiple_of(places[step] * rows, rows)
            out[pl.ds(chunk * count, count), pl.ds(start, rows), :] = piece[...]


def join(places, chunks):
    count, rows, columns = chunks[0][0].shape
    steps = len(chunks[0])
    return pl.pallas_call(
        join_kernel,
        in_specs=[pl.BlockSpec(memory_space=pltpu.SMEM)] + [pl.BlockSpec(memory_space=pltpu.VMEM)] * (steps * len(chunks)),
        out_shape=jax.ShapeDtypeStruct((count * len(chunks), steps * rows, columns), jnp.bfloat16),
        compiler_params=pltpu.CompilerParams(vmem_limit_bytes=VMEM_BYTES),
        cost_estimate=cost(3),
        name="join",
    )(places, *[piece for chunk in chunks for piece in chunk])


def project_kernel(core, rows, mine, other, result):
    half = mine.shape[1]
    first, second = halves(core[0], mine[...], other[...])
    result[:, :half] = dot_f32(rows[...], first).astype(jnp.bfloat16)
    result[:, half:] = dot_f32(rows[...], second).astype(jnp.bfloat16)


def project(core, rows, mine, other, used):
    width, half = mine.shape[1:]
    length = rows.shape[0]
    return pl.pallas_call(
        project_kernel,
        grid_spec=pltpu.PrefetchScalarGridSpec(
            num_scalar_prefetch=1,
            grid=(used,),
            in_specs=[
                whole((length, width)),
                pl.BlockSpec((None, width, half), lambda i, core: (i, 0, 0)),
                pl.BlockSpec((None, width, half), lambda i, core: (i, 0, 0)),
            ],
            out_specs=pl.BlockSpec((None, length, 2 * half), lambda i, core: (i, 0, 0)),
        ),
        out_shape=jax.ShapeDtypeStruct((used, length, 2 * half), jnp.bfloat16),
        compiler_params=pltpu.CompilerParams(vmem_limit_bytes=VMEM_BYTES),
        cost_estimate=cost(4),
        name="project",
    )(core, rows, mine, other)


def route_kernel(core, attended, tokens, mine, other, gain, router, routes, slots, middle, normed, gates, *outs):
    f32 = jnp.float32
    first, second = halves(core[0], mine[...], other[...])
    rows = attended[...]
    moved = jnp.concatenate([dot_f32(rows, first), dot_f32(rows, second)], axis=1)
    value = tokens[...].astype(f32) + moved
    middle[...] = value
    low = (value * lax.rsqrt(jnp.mean(value * value, axis=1, keepdims=True) + EPS) * gain[...]).astype(jnp.bfloat16)
    normed[...] = low
    start = 0
    for first_out, second_out in zip(outs[::2], outs[1::2]):
        size = first_out.shape[0]
        hot = hot_columns(slots[0:1, :], start, 2 * size) + hot_columns(slots[1:2, :], start, 2 * size)
        part = dot_f32(hot, low).astype(jnp.bfloat16)
        first_out[...] = part[:size]
        second_out[...] = part[size:]
        start += 2 * size
    logits = dot_f32(low, router[...])
    soft = jnp.exp(logits - jnp.max(logits, axis=1, keepdims=True))
    soft = soft / jnp.sum(soft, axis=1, keepdims=True)
    expert = lax.broadcasted_iota(jnp.int32, soft.shape, 1)
    chosen = [jnp.sum(jnp.where(expert == routes[:, k : k + 1], soft, 0.0), axis=1, keepdims=True) for k in range(2)]
    for k in range(2):
        gates[:, k : k + 1] = chosen[k] / (chosen[0] + chosen[1])


def route(core, attended, tokens, mine, other, gain, router, routes, slots, pieces, count):
    length, width = tokens.shape
    last, half = mine.shape[0] - 1, mine.shape[2]
    f32, bf16 = jnp.float32, jnp.bfloat16
    weight = pl.BlockSpec((None, width, half), lambda i, core: (last, 0, 0))
    shapes = [((length, width), f32), ((length, width), bf16), ((length, 2), f32)] + [((count, width), bf16)] * pieces
    return pl.pallas_call(
        route_kernel,
        grid_spec=pltpu.PrefetchScalarGridSpec(
            num_scalar_prefetch=1,
            grid=(1,),
            in_specs=[whole((length, width)), whole((length, width)), weight, weight, whole((1, width)), whole(router.shape), whole(routes.shape), whole(slots.shape)],
            out_specs=[whole(shape) for shape, _ in shapes],
        ),
        out_shape=[jax.ShapeDtypeStruct(shape, kind) for shape, kind in shapes],
        compiler_params=pltpu.CompilerParams(vmem_limit_bytes=VMEM_BYTES),
        cost_estimate=cost(6),
        name="route",
    )(core, attended, tokens, mine, other, gain.reshape(1, -1), router, routes, slots)


def hot_route(slots, k, count):
    cols = lax.broadcasted_iota(jnp.int32, (slots.shape[0], count), 1)
    return cols == slots[:, k : k + 1]


def combine_kernel(*refs, count):
    slots, slots_t, scale = refs[:3]
    pieces = refs[3 : 3 + count]
    middle, teacher, cotangent, valid, gates, routes = refs[3 + count : 9 + count]
    output, grad_y, grad_logits, square = refs[9 + count : 13 + count]
    sends, rows = refs[13 + count : 13 + 2 * count], refs[13 + 2 * count]
    f32, bf16 = jnp.float32, jnp.bfloat16
    assemble(rows, pieces)
    table = rows[...]
    picked = [dot_f32(hot_route(slots, k, rows.shape[0]).astype(bf16), table) for k in range(2)]
    result = middle[...] + (gates[:, 0:1] * picked[0] + gates[:, 1:2] * picked[1])
    output[...] = result.astype(bf16)
    misfit = valid[...] * (result - teacher[...].astype(f32))
    square[...] = jnp.sum((misfit * misfit).reshape(-1, 8, misfit.shape[1]), axis=0)
    grad = cotangent[...].astype(f32) + misfit * scale[0, 0]
    grad_y[...] = grad
    steep = [jnp.sum(grad * picked[k], axis=1, keepdims=True) for k in range(2)]
    slack = gates[:, 0:1] * steep[0] + gates[:, 1:2] * steep[1]
    expert = lax.broadcasted_iota(jnp.int32, grad_logits.shape, 1)
    turn = [jnp.where(expert == routes[:, k : k + 1], gates[:, k : k + 1] * (steep[k] - slack), 0.0) for k in range(2)]
    grad_logits[...] = (turn[0] + turn[1]).astype(bf16)
    scaled = [(gates[:, k : k + 1] * grad).astype(bf16) for k in range(2)]
    start = 0
    for first, second in zip(sends[::2], sends[1::2]):
        size = first.shape[0]
        part = [dot_f32(hot_columns(slots_t[k : k + 1, :], start, 2 * size), scaled[k]) for k in range(2)]
        part = (part[0] + part[1]).astype(bf16)
        first[...] = part[:size]
        second[...] = part[size:]
        start += 2 * size


def combine(slots, slots_t, scale, pieces, middle, teacher, cotangent, valid, gates, routes, experts):
    length, width = middle.shape
    count = len(pieces)
    f32, bf16 = jnp.float32, jnp.bfloat16
    return pl.pallas_call(
        lambda *refs: combine_kernel(*refs, count=count),
        in_specs=[pl.BlockSpec(memory_space=pltpu.VMEM)] * 2
        + [pl.BlockSpec(memory_space=pltpu.SMEM)]
        + [pl.BlockSpec(memory_space=pltpu.VMEM)] * (6 + count),
        out_shape=[
            jax.ShapeDtypeStruct((length, width), bf16),
            jax.ShapeDtypeStruct((length, width), f32),
            jax.ShapeDtypeStruct((length, experts), bf16),
            jax.ShapeDtypeStruct((8, width), f32),
        ]
        + [jax.ShapeDtypeStruct(piece.shape, bf16) for piece in pieces],
        scratch_shapes=[pltpu.VMEM((sum(piece.shape[0] for piece in pieces), width), bf16)],
        compiler_params=pltpu.CompilerParams(vmem_limit_bytes=VMEM_BYTES),
        cost_estimate=cost(8),
        name="combine",
    )(slots, slots_t, scale, *pieces, middle, teacher, cotangent, valid, gates, routes)


def norm_back(value, gain, grad):
    root = lax.rsqrt(jnp.mean(value * value, axis=1, keepdims=True) + EPS)
    normed = value * root
    scaled = grad * gain
    inner = jnp.mean(scaled * normed, axis=1, keepdims=True)
    return root * (scaled - normed * inner), jnp.sum((grad * normed).reshape(-1, 8, value.shape[1]), axis=0)


def collect_kernel(core, *refs, count):
    slots, pieces = refs[0], refs[1 : 1 + count]
    middle, gain, grad_logits, router, grad_y, mine, other = refs[1 + count : 8 + count]
    grad_middle, rounded, grad_attended, grad_gain, rows = refs[8 + count :]
    assemble(rows, pieces)
    hot = (hot_route(slots, 0, rows.shape[0]) | hot_route(slots, 1, rows.shape[0])).astype(jnp.bfloat16)
    grad = dot_f32(grad_logits[...], router[...], NT) + dot_f32(hot, rows[...])
    turned, grad_gain[...] = norm_back(middle[...], gain[...], grad)
    result = grad_y[...] + turned
    grad_middle[...] = result
    low = result.astype(jnp.bfloat16)
    rounded[...] = low
    first, second = halves(core[0], mine[...], other[...])
    half = first.shape[1]
    grad_attended[...] = (dot_f32(low[:, :half], first, NT) + dot_f32(low[:, half:], second, NT)).astype(jnp.bfloat16)


def collect(core, slots, pieces, middle, gain, grad_logits, router, grad_y, mine, other):
    length, width = middle.shape
    last, half = mine.shape[0] - 1, mine.shape[2]
    f32, bf16 = jnp.float32, jnp.bfloat16
    weight = pl.BlockSpec((None, width, half), lambda i, core: (last, 0, 0))
    plain = [slots, *pieces, middle, gain.reshape(1, -1), grad_logits, router, grad_y]
    shapes = [((length, width), f32), ((length, width), bf16), ((length, width), bf16), ((8, width), f32)]
    return pl.pallas_call(
        lambda *refs: collect_kernel(*refs, count=len(pieces)),
        grid_spec=pltpu.PrefetchScalarGridSpec(
            num_scalar_prefetch=1,
            grid=(1,),
            in_specs=[whole(array.shape) for array in plain] + [weight, weight],
            out_specs=[whole(shape) for shape, _ in shapes],
            scratch_shapes=[pltpu.VMEM((sum(piece.shape[0] for piece in pieces), width), bf16)],
        ),
        out_shape=[jax.ShapeDtypeStruct(shape, kind) for shape, kind in shapes],
        compiler_params=pltpu.CompilerParams(vmem_limit_bytes=VMEM_BYTES),
        cost_estimate=cost(8),
        name="collect",
    )(core, *plain, mine, other)


def outer_halves_kernel(core, normed, attended, rights, last, *refs, count):
    aways, stays, normed_t, attended_t = refs[:2], refs[2:4], refs[4], refs[5]
    step = pl.program_id(0)

    @pl.when(step == 0)
    def _():
        normed_t[...] = normed[...].T
        attended_t[...] = attended[...].T

    for place in range(count + 1):

        @pl.when(step == place)
        def _():
            result = dot_f32(normed_t[...], rights[...]) if place < count else dot_f32(attended_t[...], last[...])
            result = result.astype(jnp.bfloat16)
            half = result.shape[1] // 2
            away, stay = aways[place // 2], stays[place // 2]
            slot = place % 2

            @pl.when(core[0] == 0)
            def _():
                stay[slot] = result[:, :half]
                away[slot] = result[:, half:]

            @pl.when(core[0] != 0)
            def _():
                away[slot] = result[:, :half]
                stay[slot] = result[:, half:]


def outer_halves(core, normed, attended, rights, last):
    length, width = normed.shape
    count, half = rights.shape[0], width // 2
    shape = jax.ShapeDtypeStruct((2, width, half), jnp.bfloat16)
    return pl.pallas_call(
        lambda *refs: outer_halves_kernel(*refs, count=count),
        grid_spec=pltpu.PrefetchScalarGridSpec(
            num_scalar_prefetch=1,
            grid=(count + 1,),
            in_specs=[
                whole((length, width)),
                whole((length, width)),
                pl.BlockSpec((None, length, width), lambda i, core: (jnp.minimum(i, count - 1), 0, 0)),
                whole((length, width)),
            ],
            out_specs=[whole(shape.shape)] * 4,
            scratch_shapes=[pltpu.VMEM((width, length), jnp.bfloat16)] * 2,
        ),
        out_shape=[shape] * 4,
        compiler_params=pltpu.CompilerParams(vmem_limit_bytes=VMEM_BYTES),
        cost_estimate=cost(2),
        name="outer_halves",
    )(core, normed, attended, rights, last)


def enter_kernel(core, grads, mine, other, tokens, gain, grad_middle, grad_input, grad_gain, total):
    step = pl.program_id(0)
    first, second = halves(core[0], mine[...], other[...])
    half = first.shape[1]
    rows = grads[...]
    part = dot_f32(rows[:, :half], first, NT) + dot_f32(rows[:, half:], second, NT)

    @pl.when(step == 0)
    def _():
        total[...] = part

    @pl.when(step > 0)
    def _():
        total[...] += part

    @pl.when(step == pl.num_programs(0) - 1)
    def _():
        turned, grad_gain[...] = norm_back(tokens[...].astype(jnp.float32), gain[...], total[...])
        grad_input[...] = grad_middle[...] + turned


def enter(core, grads, mine, other, tokens, gain, grad_middle):
    length, width = tokens.shape
    count, half = grads.shape[0], mine.shape[2]
    weight = pl.BlockSpec((None, width, half), lambda i, core: (i, 0, 0))
    return pl.pallas_call(
        enter_kernel,
        grid_spec=pltpu.PrefetchScalarGridSpec(
            num_scalar_prefetch=1,
            grid=(count,),
            in_specs=[pl.BlockSpec((None, length, width), lambda i, core: (i, 0, 0)), weight, weight, whole((length, width)), whole((1, width)), whole((length, width))],
            out_specs=[whole((length, width)), whole((8, width))],
            scratch_shapes=[pltpu.VMEM((length, width), jnp.float32)],
        ),
        out_shape=[jax.ShapeDtypeStruct((length, width), jnp.float32), jax.ShapeDtypeStruct((8, width), jnp.float32)],
        compiler_params=pltpu.CompilerParams(vmem_limit_bytes=VMEM_BYTES),
        cost_estimate=cost(6),
        name="enter",
    )(core, grads, mine, other, tokens, gain.reshape(1, -1), grad_middle)


BOUNDS = (12, 16, 23, 32, 46, 64, 91)
TOP_PRECISION = lax.Precision.HIGHEST
AXES = ("dp", "expert")
PAIR = 2


def after(value, *others):
    return lax.optimization_barrier((value, *others))[0] if others else value


def bucket_index(offset):
    distance = jnp.abs(offset)
    far_bucket = 8 + sum([(distance >= level).astype(jnp.int32) for level in BOUNDS])
    near_bucket = jnp.where(distance < 8, distance, far_bucket)
    return jnp.where(offset > 0, 16, 0) + near_bucket


def norm_apply(inputs, gain_vec):
    return inputs * lax.rsqrt(jnp.mean(inputs * inputs, axis=-1, keepdims=True) + EPS) * gain_vec


def tile_offsets(query_block, key_block):
    rows = query_block * BLOCK + lax.broadcasted_iota(jnp.int32, (BLOCK, BLOCK), 0)
    cols = key_block * BLOCK + lax.broadcasted_iota(jnp.int32, (BLOCK, BLOCK), 1)
    return rows, cols


def offset_bias(table):
    offsets = jnp.arange(4 * BLOCK, dtype=jnp.int32) - 2 * BLOCK
    hot = (bucket_index(offsets)[None] == jnp.arange(table.shape[1], dtype=jnp.int32)[:, None]).astype(jnp.float32)
    return jnp.dot(table, hot, precision=TOP_PRECISION)


def table_gradient(bands, buckets):
    rows, cols = tile_offsets(0, 0)
    ids = [jnp.full((BLOCK, BLOCK), bucket_far(), jnp.int32)]
    ids += [bucket_index(shift * BLOCK + cols - rows) for shift in (-1, 0, 1)]
    hot = (jnp.stack(ids)[..., None] == jnp.arange(buckets, dtype=jnp.int32)).astype(jnp.float32)
    return jnp.einsum("hdxy,dxyb->hb", bands, hot, precision=TOP_PRECISION)


def bucket_far():
    return 8 + len(BOUNDS)


def on_device(
    tokens,
    qkv_weight,
    out_weight,
    position_bias_table,
    gain_attn,
    gain_moe,
    router,
    w_in,
    w_out,
    routes,
    prefix,
    valid_mask,
    teacher,
    cotangent,
):
    length, width = tokens.shape
    bf16, f32 = jnp.bfloat16, jnp.float32
    expert_count = router.shape[1]
    top_count = routes.shape[1]
    groups = lax.axis_size("expert")
    copies = lax.axis_size("dp")
    inner = w_in.shape[2]
    capacity = 5 * length * top_count // (4 * expert_count)
    total_tokens = length * copies * groups
    sources = 2 * groups
    blocks = length // BLOCK
    here_dp, here_group = lax.axis_index("dp"), lax.axis_index("expert")
    half = (here_dp >> 1) & 1
    core = here_group & 1
    rest = copies // 4

    def swap(value, dp_mask, group_mask):
        pairs = [
            (i, ((i // groups) ^ dp_mask) * groups + ((i % groups) ^ group_mask))
            for i in range(copies * groups)
        ]
        return lax.ppermute(value, AXES, pairs)

    def bits(count):
        return [1 << place for place in range(count.bit_length() - 1)]

    def partial_sums(value):
        sums = []
        for masks in [(0, mask) for mask in bits(groups)] + [(mask, 0) for mask in bits(copies)]:
            value = value + swap(value, *masks)
            sums.append(value)
        return sums

    chips = groups

    def across(value, place):
        return swap(value, PAIR * (place // (groups // 2)), 2 * (place % (groups // 2)))

    def to_chips(pieces):
        return [pieces[0]] + [across(pieces[place], place) for place in range(1, chips)]

    def through(visit, sends):
        direct, relay = to_chips(sends[::2]), to_chips(sends[1::2])
        seen, direct = visit(direct)
        direct = to_chips(direct)
        relay = [after(part, seen) for part in relay]
        passed = visit(swap(jnp.concatenate(relay), 0, 1))
        return direct, [swap(after(part, *direct), 0, 1) for part in passed]

    def weave(direct, relay):
        return [part for pair in zip(direct, to_chips(relay)) for part in pair]

    ring = list(range(0, copies, 2)) + list(range(copies - 1, 0, -2))
    turns = [(1, step) for step in range(1, copies // 2 + 1)] + [(-1, step) for step in range(1, copies // 2)]

    def gather_ring(shard, due):
        got = [shard]
        for turn in (1, -1):
            held = shard
            pairs = [(ring[i], ring[(i + turn) % copies]) for i in range(copies)]
            for step in [step for way, step in turns if way == turn]:
                held = lax.ppermute(after(held, *due[step - 2 : step - 1]) if step > 1 else held, "dp", pairs)
                got.append(held)
        return got

    def ring_places():
        place = jnp.where(here_dp & 1 == 0, here_dp >> 1, copies - 1 - (here_dp >> 1))
        shift = jnp.array([0] + [turn * step for turn, step in turns], jnp.int32)
        place = (place - shift) & (copies - 1)
        return jnp.where(place < copies // 2, 2 * place, 2 * (copies - 1 - place) + 1).astype(jnp.int32)


    flat_routes = routes.reshape(-1)
    pair_count = length * top_count
    slot_count = sources * capacity
    route_hits = (flat_routes[:, None] == jnp.arange(expert_count, dtype=jnp.int32)[None, :]).astype(bf16)
    lower_ones = (
        lax.broadcasted_iota(jnp.int32, (pair_count, pair_count), 0)
        >= lax.broadcasted_iota(jnp.int32, (pair_count, pair_count), 1)
    ).astype(bf16)
    running = jnp.dot(lower_ones, route_hits, preferred_element_type=f32)
    pair_rank = jnp.sum((running - 1.0) * route_hits.astype(f32), axis=1).astype(jnp.int32)
    away = (flat_routes >> 1) ^ here_group
    chip = ((flat_routes & 1) ^ half) * (groups // 2) + (away >> 1)
    slots = ((chip * 2 + (away & 1)) * capacity + pair_rank).reshape(length, top_count)
    slots_t = slots.T

    resid = tokens.astype(f32)
    normed1 = norm_apply(resid, gain_attn).astype(bf16)
    columns = width // 2
    core_index = core.reshape(1).astype(jnp.int32)
    valid_rows = valid_mask.astype(f32)[:, None]
    counts = [jnp.broadcast_to(jnp.sum(valid_rows), (8, 128))]
    count_trades = [(0, mask) for mask in bits(groups)] + [(mask, 0) for mask in bits(copies)]

    def count_beside(before, value):
        if len(counts) > len(count_trades):
            return value
        counts.append(counts[-1] + swap(after(counts[-1], before), *count_trades[len(counts) - 1]))
        return after(value, counts[-1])

    shards = [
        lax.dynamic_slice_in_dim(part, core * columns, columns, 2)
        for part in (qkv_weight[:2], jnp.concatenate([qkv_weight[2:], out_weight[None]]))
    ]
    if copies > 8:
        mine = lax.all_gather(jnp.concatenate(shards), "dp", axis=1, tiled=True)
    else:
        mine = join(ring_places(), [gather_ring(shards[0], ()), gather_ring(shards[1], (slots_t, normed1))])
    other = count_beside(mine, swap(mine, 0, 1))
    qkv_rows = count_beside(other, project(core_index, normed1, mine, other, 3))
    offsets = offset_bias(position_bias_table)
    attended, probs = attention_forward(position_bias_table[:, bucket_far()], prefix, qkv_rows, offsets)
    middle, normed2, gates, *sends = route(
        core_index, count_beside(qkv_rows, attended), tokens, mine, other, gain_moe, router, routes, slots_t, 2 * chips, capacity
    )

    pick = half.reshape(1).astype(jnp.int32)
    hidden, slopes, rows_in = [], [], []

    def expert(pieces):
        one = not isinstance(pieces, list)
        pieces = [pieces] if one else pieces
        hidden_t, slope, rows_t, *results = expert_forward(pick, pieces, chips, w_in, w_out)
        hidden_t = count_beside(pieces[-1], hidden_t)
        for kept, value in zip((hidden, slopes, rows_in), (hidden_t, slope, rows_t)):
            kept.append(value)
        return results if one else (hidden_t, results)

    back = weave(*through(expert, sends))
    while len(counts) <= len(count_trades):
        back[0] = count_beside(back[0], back[0])
    valid_count = counts[-1][0, 0]
    scale = (total_tokens / valid_count).reshape(1, 1)
    output, grad_y, grad_logits, squares, *sends = combine(
        slots, slots_t, scale, back, middle, teacher, cotangent, valid_rows, gates, routes, expert_count
    )

    out_rows = inner // copies
    in_rows = width // copies
    far_bit = here_dp % 2
    slices = jnp.arange(rest, dtype=jnp.int32) * 4

    def picks(bit0):
        return jnp.concatenate([slices + ((half ^ other_half) * 2 + bit0) for other_half in (1, 0)]).astype(jnp.int32)

    sent, kept = picks(1 - far_bit), picks(far_bit)

    def add(left, right):
        return (left.astype(f32) + right.astype(f32)).astype(bf16)

    def fold(unit, bit, axis=0):
        unit = unit.reshape(unit.shape[:axis] + (2, unit.shape[axis] // 2) + unit.shape[axis + 1 :])
        away_part = lax.dynamic_index_in_dim(unit, 1 - bit, axis, keepdims=False)
        return away_part, lax.dynamic_index_in_dim(unit, bit, axis, keepdims=False)

    far_masks = list(reversed(bits(copies)[2:]))

    def near_add(got, keep):
        away_part, stay_part = fold(add(got, keep), (here_dp // far_masks[0]) % 2)
        return away_part, stay_part

    def far_trade(away_part):
        return swap(away_part, far_masks[0], 0)

    def finish(got, stay):
        unit = add(got, stay)
        for mask in far_masks[1:]:
            away_part, stay_part = fold(unit, (here_dp // mask) % 2)
            unit = add(swap(away_part, mask, 0), stay_part)
        return unit[0]

    plan_a, plan_b, plan_c = ((0, 0), (0, 1)), ((0, 2), (1, 0)), ((1, 1), (1, 2))
    plan_d, plan_e, plan_f = plan_a, plan_b, plan_c
    out_plans, in_plans = (plan_a, plan_b, plan_c), (plan_d, plan_e, plan_f)

    grad_rows, grad_pre, parts = [], [], []

    def expert_back(pieces):
        if isinstance(pieces, list):
            grad_pre_rows, grads, *results = expert_backward(pick, pieces, chips, w_in, w_out, slopes[0])
            grad_rows.append(grads)
            grad_pre.append(grad_pre_rows)
            return grad_pre_rows, results
        grad_rows.append(pieces)
        parts.extend(weight_part(sent, hidden, grad_rows, out_rows, out_plans, rest, width))
        parts[0] = swap(parts[0], 1, 0)
        pieces = after(pieces, parts[1])
        grad_pre_rows, _, *results = expert_backward(pick, [pieces], chips, w_in, w_out, slopes[1])
        grad_pre.append(grad_pre_rows)
        return results

    direct, relay = through(expert_back, sends)
    got_a, send_b, send_c = parts
    relay = [after(part, got_a) for part in relay]
    got_b = swap(after(send_b, relay[0]), 1, 0)
    back = weave(direct, relay)
    grad_rows, grad_pre = lax.optimization_barrier((grad_rows, grad_pre, relay))[:2]
    keep_a, keep_b, keep_c = weight_part(kept, hidden, grad_rows, out_rows, out_plans, rest, width)
    away_a, stay_a = near_add(got_a, keep_a)
    far_a = far_trade(away_a)
    send_d, send_e, send_f = weight_part(sent, rows_in, after(grad_pre, away_a), in_rows, in_plans, rest, inner // 2)
    back = [after(part, send_d) for part in back]
    got_c = swap(after(send_c, send_d), 1, 0)
    grad_middle, grad_attn_proj, grad_attended, gain_moe_parts = collect(
        core_index, slots, back, middle, gain_moe, grad_logits, router, grad_y, mine, other
    )
    away_b, stay_b = near_add(after(got_b, grad_attended), keep_b)
    got_d = swap(after(send_d, grad_attended), 1, 0)
    grad_attended, away_b = lax.optimization_barrier((grad_attended, away_b))
    grad_qkv_rows, bands = attention_backward(qkv_rows, grad_attended, probs)
    grad_qkv_rows, got_c, far_a = lax.optimization_barrier((grad_qkv_rows, got_c, far_a))
    done_a = finish(far_a, stay_a)

    away_c, stay_c = near_add(got_c, keep_c)
    far_c = far_trade(jnp.concatenate([away_b, away_c], axis=1))
    stay_c = jnp.concatenate([stay_b, stay_c], axis=1)
    *weights_away, stay_1, stay_2 = outer_halves(
        core_index, normed1, attended, after(grad_qkv_rows, away_c), grad_attn_proj
    )
    weights_away, got_d = lax.optimization_barrier((weights_away, got_d))
    got_e = swap(after(send_e, got_d), 1, 0)
    keep_d, keep_e, keep_f = weight_part(
        kept, rows_in, after(grad_pre, *weights_away), in_rows, in_plans, rest, inner // 2
    )
    group_masks = bits(groups)[1:]
    dp_masks = sorted(bits(copies), key=lambda mask: (mask != PAIR, mask))

    def over_dp(total, mask, passed):
        axis = 1 + sorted([other for other in dp_masks if other not in passed], reverse=True).index(mask)
        bit = (here_dp // mask) % 2
        away_part = lax.dynamic_index_in_dim(total, 1 - bit, axis, keepdims=False)
        stay_part = lax.dynamic_index_in_dim(total, bit, axis, keepdims=False)
        return swap(away_part, mask, 0), stay_part

    weights_got = [swap(part, 0, 1) for part in weights_away]
    halves_sum = [
        add(after(got, keep_d), stay).reshape(2, copies, in_rows, columns) for got, stay in zip(weights_got, (stay_1, stay_2))
    ]
    for mask in group_masks[:-1]:
        folded = [fold(part, (here_group // mask) % 2, 2) for part in halves_sum]
        halves_sum = [add(swap(away_part, 0, mask), stay_part) for away_part, stay_part in folded]
    folded = [fold(part, (here_group // group_masks[-1]) % 2, 2) for part in halves_sum]
    y_stay = jnp.concatenate([stay_part for _, stay_part in folded])
    y_got = swap(jnp.concatenate([away_part for away_part, _ in folded]), 0, group_masks[-1])
    away_d, stay_d = near_add(after(got_d, y_stay), keep_d)
    far_d = far_trade(away_d)
    grad_input, gain_attn_parts = enter(
        core_index, after(grad_qkv_rows, away_d), mine, other, tokens, gain_attn, grad_middle
    )
    grad_table = table_gradient(after(bands, y_stay), position_bias_table.shape[1])

    away_e, stay_e = near_add(after(got_e, gain_attn_parts), keep_e)
    got_f = swap(after(send_f, away_e), 1, 0)
    normed2, squares, gain_moe_parts = after((normed2, squares, gain_moe_parts), y_stay)
    grad_router = jnp.einsum("td,te->de", normed2, grad_logits, preferred_element_type=f32)
    small = [
        jnp.sum(gain_moe_parts, axis=0),
        jnp.sum(gain_attn_parts, axis=0),
        grad_router,
        grad_table,
        jnp.sum(squares),
    ]
    sizes = [value.size for value in small]
    flat = jnp.concatenate([value.reshape(-1) for value in small])
    flat = jnp.pad(flat, (0, -sum(sizes) % 1024)).reshape(-1, 128)
    flat = flat + swap(flat, 0, 1)
    done_c = finish(after(far_c, away_e), stay_c)
    total = add(after(y_got, away_e, flat, done_c), y_stay)
    total = total.reshape((4,) + (2,) * len(dp_masks) + (-1, columns))


    passed_masks = []
    for mask in dp_masks:
        got, stay = over_dp(total, mask, passed_masks)
        passed_masks.append(mask)
        flat_got = swap(after(flat, stay), 0, group_masks[0]) if mask == PAIR else swap(flat, mask, 0)
        if mask == PAIR:
            far_e = far_trade(after(away_e, stay))
            away_f, stay_f = near_add(after(got_f, stay), keep_f)
            far_f = far_trade(away_f)
            got = after(got, away_f)
        total = add(got, stay)
        flat = flat + flat_got
        if mask == PAIR:
            done_d = finish(after(far_d, total), stay_d)
            in_first = swap(done_d, PAIR, 0)
            out_theirs = swap(after(jnp.concatenate([done_a, done_c[:1]]), total), PAIR, 0)
        elif len(passed_masks) == 2:
            done_e = finish(after(far_e, total), stay_e)
        flat = after(flat, total)
    in_theirs = jnp.concatenate([in_first, swap(done_e[:1], PAIR, 0)])
    for mask in reversed(group_masks):
        bit = (here_group // mask) % 2
        other_part = swap(total, 0, mask)
        total = jnp.concatenate([jnp.where(bit == 0, total, other_part), jnp.where(bit == 0, other_part, total)], axis=1)
        if mask == group_masks[0]:
            done_f = finish(after(far_f, total), stay_f)
            total = after(total, done_f)
            flat = flat + swap(flat, PAIR, 0)
        else:
            flat = flat + swap(flat, 0, mask)
        total, flat = lax.optimization_barrier((total, flat))
    other_part = swap(total, 0, 1)
    total = jnp.concatenate([jnp.where(core == 0, total, other_part), jnp.where(core == 0, other_part, total)], axis=2)
    weights_done = total.astype(f32)
    grad_qkv, grad_out_weight = weights_done[:3], weights_done[3]
    flat = flat.reshape(-1)
    starts = [sum(sizes[:place]) for place in range(len(sizes))]
    grad_gain_moe, grad_gain_attn, grad_router, grad_table, square_total = [
        flat[start : start + value.size].reshape(value.shape) for start, value in zip(starts, small)
    ]

    out_mine, in_mine = done_c[1:], jnp.concatenate([done_e[1:], done_f])

    def both_experts(mine, theirs):
        mine, theirs = [part.reshape(-1, part.shape[-1]).astype(f32) for part in (mine, theirs)]
        return jnp.stack([jnp.where(half == 0, mine, theirs), jnp.where(half == 0, theirs, mine)])

    grad_w_out = both_experts(out_mine, out_theirs)
    grad_w_in = both_experts(in_mine, in_theirs)

    distill_loss = square_total / (width * valid_count)
    return (
        output.astype(bf16),
        distill_loss,
        grad_input,
        grad_qkv,
        grad_out_weight,
        grad_w_in,
        grad_w_out,
        grad_router,
        grad_table,
        grad_gain_attn,
        grad_gain_moe,
    )


def solution(mesh):
    rows = P(AXES, None)
    return jax.shard_map(
        on_device,
        mesh=mesh,
        in_specs=(
            rows,
            P(None, "dp", None),
            P("dp", None),
            P(),
            P(),
            P(),
            P(),
            P("expert", None, None),
            P("expert", None, None),
            rows,
            P(AXES),
            P(AXES),
            rows,
            rows,
        ),
        out_specs=(
            rows,
            P(),
            rows,
            P(None, "dp", None),
            P("dp", None),
            P("expert", "dp", None),
            P("expert", "dp", None),
            P(),
            P(),
            P(),
            P(),
        ),
        check_vma=False,
    )
```

```python
import math
import jax
import jax.numpy as jnp
from jax import lax
from jax.experimental import pallas as pl
from jax.experimental.pallas import tpu as pltpu
from jax.sharding import PartitionSpec as P

BLOCK = 128
THIRDS = 3
EPS = 1e-06
GELU_A = math.sqrt(2.0 / math.pi)
GELU_B = 0.044715
NT = (((1,), (1,)), ((), ()))
TN = (((0,), (0,)), ((), ()))
VMEM_BYTES = 56 * 1024 * 1024


def cost(micros):
    return pl.CostEstimate(flops=int(micros * 0.37e9), bytes_accessed=0, transcendentals=0)


def dot_f32(left, right, dims=(((1,), (0,)), ((), ()))):
    return lax.dot_general(left, right, dims, preferred_element_type=jnp.float32)


def assemble(rows, pieces):
    start = 0
    for piece in pieces:
        rows[pl.ds(start, piece.shape[0]), :] = piece[...]
        start += piece.shape[0]


def hand_out(total, outs):
    start = 0
    for out in outs:
        out[...] = total[pl.ds(start, out.shape[0]), :].astype(out.dtype)
        start += out.shape[0]


def whole(shape):
    return pl.BlockSpec(shape, lambda *step: (0,) * len(shape))


def expert_forward_kernel(pick, *refs, chunk, count):
    pieces, w_in, w_out = refs[:count], refs[count], refs[count + 1]
    hidden_t, slope, rows_t = refs[count + 2 : count + 5]
    outs, rows, total = refs[count + 5 : -2], refs[-2], refs[-1]
    step = pl.program_id(0)

    @pl.when(step == 0)
    def _():
        assemble(rows, pieces)
        total[...] = jnp.zeros_like(total)
        rows_t[...] = rows[...].T

    for start in range(0, rows.shape[0], chunk):
        part = pl.ds(start, chunk)
        pre = dot_f32(rows[part, :], w_in[0])
        square = pre * pre
        bend = jnp.tanh(pre * (GELU_A + (GELU_A * GELU_B) * square))
        half = 0.5 + 0.5 * bend
        act = (pre * half).astype(jnp.bfloat16)
        lift = pre * (0.5 * GELU_A + (1.5 * GELU_A * GELU_B) * square)
        slope[part, :] = (half + lift * (1.0 - bend * bend)).astype(jnp.bfloat16)
        hidden_t[:, part] = act.T
        total[part, :] += dot_f32(act, w_out[0])

    @pl.when(step == pl.num_programs(0) - 1)
    def _():
        hand_out(total, outs)


def expert_forward(pick, pieces, results, w_in, w_out, tile=768, chunk=320):
    many, width = sum(piece.shape[0] for piece in pieces), pieces[0].shape[1]
    inner = w_in.shape[2]
    bf16 = jnp.bfloat16
    return pl.pallas_call(
        lambda *refs: expert_forward_kernel(*refs, chunk=chunk, count=len(pieces)),
        grid_spec=pltpu.PrefetchScalarGridSpec(
            num_scalar_prefetch=1,
            grid=(inner // tile,),
            in_specs=[whole(piece.shape) for piece in pieces]
            + [
                pl.BlockSpec((1, width, tile), lambda f, pick: (pick[0], 0, f)),
                pl.BlockSpec((1, tile, width), lambda f, pick: (pick[0], f, 0)),
            ],
            out_specs=[
                pl.BlockSpec((tile, many), lambda f, pick: (f, 0)),
                pl.BlockSpec((many, tile), lambda f, pick: (0, f)),
                whole((width, many)),
            ]
            + [whole((many // results, width))] * results,
            scratch_shapes=[pltpu.VMEM((many, width), bf16), pltpu.VMEM((many, width), jnp.float32)],
        ),
        out_shape=[
            jax.ShapeDtypeStruct((inner, many), bf16),
            jax.ShapeDtypeStruct((many, inner), bf16),
            jax.ShapeDtypeStruct((width, many), bf16),
        ]
        + [jax.ShapeDtypeStruct((many // results, width), bf16)] * results,
        compiler_params=pltpu.CompilerParams(vmem_limit_bytes=VMEM_BYTES),
        cost_estimate=cost(13),
        name="expert_forward",
    )(pick, *pieces, w_in, w_out)


def expert_backward_kernel(pick, *refs, chunk, count):
    pieces, w_in, w_out, slope = refs[:count], refs[count], refs[count + 1], refs[count + 2]
    grad_pre, rows = refs[count + 3 : count + 5]
    outs, total = refs[count + 5 : -1], refs[-1]
    step = pl.program_id(0)

    @pl.when(step == 0)
    def _():
        assemble(rows, pieces)
        total[...] = jnp.zeros_like(total)

    for start in range(0, rows.shape[0], chunk):
        part = pl.ds(start, chunk)
        back = dot_f32(rows[part, :], w_out[0], NT) * slope[part, :].astype(jnp.float32)
        back = back.astype(jnp.bfloat16)
        grad_pre[part, :] = back
        total[part, :] += dot_f32(back, w_in[0], NT)

    @pl.when(step == pl.num_programs(0) - 1)
    def _():
        hand_out(total, outs)


def expert_backward(pick, pieces, results, w_in, w_out, slope, tile=768, chunk=640):
    many, width = sum(piece.shape[0] for piece in pieces), pieces[0].shape[1]
    inner = w_in.shape[2]
    bf16 = jnp.bfloat16
    return pl.pallas_call(
        lambda *refs: expert_backward_kernel(*refs, chunk=chunk, count=len(pieces)),
        grid_spec=pltpu.PrefetchScalarGridSpec(
            num_scalar_prefetch=1,
            grid=(inner // tile,),
            in_specs=[whole(piece.shape) for piece in pieces]
            + [
                pl.BlockSpec((1, width, tile), lambda f, pick: (pick[0], 0, f)),
                pl.BlockSpec((1, tile, width), lambda f, pick: (pick[0], f, 0)),
                pl.BlockSpec((many, tile), lambda f, pick: (0, f)),
            ],
            out_specs=[pl.BlockSpec((many, tile), lambda f, pick: (0, f)), whole((many, width))]
            + [whole((many // results, width))] * results,
            scratch_shapes=[pltpu.VMEM((many, width), jnp.float32)],
        ),
        out_shape=[jax.ShapeDtypeStruct((many, inner), bf16), jax.ShapeDtypeStruct((many, width), bf16)]
        + [jax.ShapeDtypeStruct((many // results, width), bf16)] * results,
        compiler_params=pltpu.CompilerParams(vmem_limit_bytes=VMEM_BYTES),
        cost_estimate=cost(11),
        name="expert_backward",
    )(pick, *pieces, w_in, w_out, slope)


def seen_blocks(row_block, blocks):
    return max(row_block + 1, blocks // 2)


def attention_forward_kernel(far, prefix, queries, keys, values, offsets, attended, probs, *, heads, blocks):
    pair = pl.program_id(0)
    lane = lax.broadcasted_iota(jnp.int32, queries.shape, 1)
    row = lax.broadcasted_iota(jnp.int32, (BLOCK, BLOCK), 0)
    col = lax.broadcasted_iota(jnp.int32, (BLOCK, BLOCK), 1)
    outs = []
    for head in range(2):
        line = jnp.broadcast_to(offsets[head : head + 1, :], (BLOCK, 4 * BLOCK))
        turned = pltpu.roll(line, 0, 1, stride=1, stride_axis=0)
        far_bias = far[pair * 2 + head]
        mine = (lane < heads) if head == 0 else (lane >= heads)
        query = jnp.where(mine, queries[...] * 0.125, 0.0).astype(jnp.bfloat16)
        score = dot_f32(query, keys[...], NT)
        strips = []
        for row_block in range(blocks):
            span = seen_blocks(row_block, blocks)
            pieces = []
            for key_block in range(span):
                piece = score[row_block * BLOCK : (row_block + 1) * BLOCK, key_block * BLOCK : (key_block + 1) * BLOCK]
                shift = key_block - row_block
                if shift < -1:
                    piece = piece + far_bias
                elif shift < 2:
                    piece = piece + turned[:, (2 + shift) * BLOCK : (3 + shift) * BLOCK]
                else:
                    raise ValueError(shift)
                if shift >= 0:
                    shown = col + key_block * BLOCK < prefix[0]
                    piece = jnp.where((shown | (col <= row)) if shift == 0 else shown, piece, -1e30)
                pieces.append(piece)
            peak = pieces[0]
            for piece in pieces[1:]:
                peak = jnp.maximum(peak, piece)
            peak = jnp.max(peak, axis=1, keepdims=True)
            pieces = [jnp.exp(piece - peak) for piece in pieces]
            mass = pieces[0]
            for piece in pieces[1:]:
                mass = mass + piece
            scale = 1.0 / jnp.sum(mass, axis=1, keepdims=True)
            pieces = [(piece * scale).astype(jnp.bfloat16) for piece in pieces]
            pieces += [jnp.zeros((BLOCK, BLOCK), jnp.bfloat16)] * (blocks - span)
            strips.append(jnp.concatenate(pieces, axis=1))
        weights = jnp.concatenate(strips, axis=0)
        probs[head] = weights
        outs.append(dot_f32(weights, values[...]))
    attended[...] = jnp.where(lane < heads, outs[0], outs[1]).astype(jnp.bfloat16)


def attention_forward(far, prefix, qkv_rows, offsets):
    length, width = qkv_rows.shape[1:]
    pairs = width // 128
    blocks = length // BLOCK
    return pl.pallas_call(
        lambda *refs: attention_forward_kernel(*refs, heads=64, blocks=blocks),
        grid_spec=pltpu.PrefetchScalarGridSpec(
            num_scalar_prefetch=2,
            grid=(pairs,),
            in_specs=[pl.BlockSpec((None, length, 128), lambda h, far, prefix, c=c: (c, 0, h)) for c in range(3)]
            + [pl.BlockSpec((None, 2, 4 * BLOCK), lambda h, far, prefix: (h, 0, 0))],
            out_specs=[
                pl.BlockSpec((length, 128), lambda h, far, prefix: (0, h)),
                pl.BlockSpec((2, length, length), lambda h, far, prefix: (h, 0, 0)),
            ],
        ),
        out_shape=[
            jax.ShapeDtypeStruct((length, width), jnp.bfloat16),
            jax.ShapeDtypeStruct((2 * pairs, length, length), jnp.bfloat16),
        ],
        compiler_params=pltpu.CompilerParams(vmem_limit_bytes=VMEM_BYTES),
        cost_estimate=cost(13),
        name="attention_forward",
    )(far, prefix, qkv_rows, qkv_rows, qkv_rows, offsets.reshape(pairs, 2, 4 * BLOCK))


def attention_backward_kernel(queries, keys, values, grads, probs, grad_rows, bands, *, heads, blocks):
    lane = lax.broadcasted_iota(jnp.int32, queries.shape, 1)
    query_t = (queries[...] * 0.125).astype(jnp.bfloat16).T
    grad_t = grads[...].T
    dq, dk, dv = [], [], []
    for head in range(2):
        mine = (lane < heads) if head == 0 else (lane >= heads)
        sums = [None] * 4
        grad = jnp.where(mine, grads[...], 0.0).astype(jnp.bfloat16)
        back = dot_f32(grad, values[...], NT)
        strips = []
        for row_block in range(blocks):
            span = seen_blocks(row_block, blocks)
            rows = slice(row_block * BLOCK, (row_block + 1) * BLOCK)
            soft = probs[head, pl.ds(row_block * BLOCK, BLOCK), pl.ds(0, span * BLOCK)].astype(jnp.float32)
            part = back[rows, : span * BLOCK]
            inner = jnp.sum(soft * part, axis=1, keepdims=True)
            score_grad = (soft * (part - inner)).astype(jnp.bfloat16)
            for key_block in range(span):
                band = max(key_block - row_block, -2)
                tile = score_grad[:, key_block * BLOCK : (key_block + 1) * BLOCK].astype(jnp.float32)
                sums[band + 2] = tile if sums[band + 2] is None else sums[band + 2] + tile
            if span < blocks:
                rest = jnp.zeros((BLOCK, (blocks - span) * BLOCK), jnp.bfloat16)
                score_grad = jnp.concatenate([score_grad, rest], axis=1)
            strips.append(score_grad)
        flow = jnp.concatenate(strips, axis=0)
        for band in range(4):
            bands[head, band] = sums[band]
        part = slice(head * heads, (head + 1) * heads)
        dq.append(dot_f32(flow, keys[...]) * 0.125)
        dk.append(dot_f32(query_t[part], flow))
        dv.append(dot_f32(grad_t[part], probs[head]))
    grad_rows[0] = jnp.where(lane < heads, dq[0], dq[1]).astype(jnp.bfloat16)
    grad_rows[1] = jnp.concatenate(dk, axis=0).T.astype(jnp.bfloat16)
    grad_rows[2] = jnp.concatenate(dv, axis=0).T.astype(jnp.bfloat16)


def attention_backward(qkv_rows, grads, probs):
    length, width = grads.shape
    pairs = width // 128
    blocks = length // BLOCK
    block = pl.BlockSpec((length, 128), lambda h: (0, h))
    of_three = [pl.BlockSpec((None, length, 128), lambda h, c=c: (c, 0, h)) for c in range(3)]
    return pl.pallas_call(
        lambda *refs: attention_backward_kernel(*refs, heads=64, blocks=blocks),
        grid=(pairs,),
        in_specs=[*of_three, block, pl.BlockSpec((2, length, length), lambda h: (h, 0, 0))],
        out_specs=[pl.BlockSpec((3, length, 128), lambda h: (0, 0, h)), pl.BlockSpec((2, 4, BLOCK, BLOCK), lambda h: (h, 0, 0, 0))],
        out_shape=[jax.ShapeDtypeStruct((3, length, width), jnp.bfloat16)]
        + [jax.ShapeDtypeStruct((2 * pairs, 4, BLOCK, BLOCK), jnp.float32)],
        compiler_params=pltpu.CompilerParams(vmem_limit_bytes=VMEM_BYTES),
        cost_estimate=cost(4),
        name="attention_backward",
    )(qkv_rows, qkv_rows, qkv_rows, grads, probs)


def pieces_left(lefts, plans, many):
    part = lefts[0][0].shape[0] // THIRDS
    return jnp.concatenate(
        [
            jnp.concatenate([ref[pl.ds(third * part, part), :] for ref in lefts[group * many + k]], axis=1)
            for plan in plans
            for group, third in plan
            for k in range(many)
        ]
    )


def put_pieces(result, outs):
    place = 0
    for out in outs:
        many, pieces, part = out.shape[:3]
        for piece in range(pieces):
            for k in range(many):
                out[k, piece] = result[place : place + part]
                place += part


def weight_part_kernel(picks, *refs, count, plans, many):
    lefts, rights, outs = refs[: 2 * count], refs[2 * count : 2 * count + 2], refs[2 * count + 2 :]
    left = pieces_left(list(zip(lefts[:count], lefts[count:])), plans, many)
    right = jnp.concatenate([ref[...] for ref in rights], axis=0)
    put_pieces(dot_f32(left, right).astype(jnp.bfloat16), outs)


def weight_part_plain(picks, lefts, rights, rows, plans, many):
    left, right = jnp.concatenate(lefts, axis=1), jnp.concatenate(rights, axis=0)
    depth, width = right.shape
    part = rows // THIRDS
    result = jnp.take(left.reshape(-1, rows, depth), picks, axis=0)
    result = jnp.einsum("srd,dw->srw", result, right, preferred_element_type=jnp.float32).astype(jnp.bfloat16)
    result = result.reshape(-1, many, THIRDS, part, width)
    return [jnp.stack([result[group, :, third] for group, third in plan], axis=1) for plan in plans]


def weight_part(picks, lefts, rights, rows, plans, many, tile):
    depth, width = rights[0].shape
    count, part = picks.shape[0], rows // THIRDS
    if part % 16:
        return weight_part_plain(picks, lefts, rights, rows, plans, many)
    return pl.pallas_call(
        lambda *refs: weight_part_kernel(*refs, count=count, plans=plans, many=many),
        grid_spec=pltpu.PrefetchScalarGridSpec(
            num_scalar_prefetch=1,
            grid=(width // tile,),
            in_specs=[pl.BlockSpec((rows, depth), lambda i, picks, k=k: (picks[k], 0)) for k in range(count)] * 2
            + [pl.BlockSpec((depth, tile), lambda i, picks: (0, i))] * 2,
            out_specs=[pl.BlockSpec((many, len(plan), part, tile), lambda i, picks: (0, 0, 0, i)) for plan in plans],
        ),
        out_shape=[jax.ShapeDtypeStruct((many, len(plan), part, width), jnp.bfloat16) for plan in plans],
        compiler_params=pltpu.CompilerParams(vmem_limit_bytes=VMEM_BYTES),
        cost_estimate=cost(4),
        name="weight_part",
    )(picks, *([lefts[0]] * count), *([lefts[1]] * count), *rights)


def hot_columns(slots, first, count):
    rows = first + lax.broadcasted_iota(jnp.int32, (count, slots.shape[1]), 0)
    return (rows == slots).astype(jnp.bfloat16)


def halves(core, mine, other):
    return jnp.where(core == 0, mine, other), jnp.where(core == 0, other, mine)


def join_kernel(places, *refs):
    pieces, out = refs[:-1], refs[-1]
    rows = pieces[0].shape[1]
    count = pieces[0].shape[0]
    for chunk in range(out.shape[0] // count):
        for step in range(len(pieces) * count // out.shape[0]):
            piece = pieces[chunk * (len(pieces) * count // out.shape[0]) + step]
            start = pl.multiple_of(places[step] * rows, rows)
            out[pl.ds(chunk * count, count), pl.ds(start, rows), :] = piece[...]


def join(places, chunks):
    count, rows, columns = chunks[0][0].shape
    steps = len(chunks[0])
    return pl.pallas_call(
        join_kernel,
        in_specs=[pl.BlockSpec(memory_space=pltpu.SMEM)] + [pl.BlockSpec(memory_space=pltpu.VMEM)] * (steps * len(chunks)),
        out_shape=jax.ShapeDtypeStruct((count * len(chunks), steps * rows, columns), jnp.bfloat16),
        compiler_params=pltpu.CompilerParams(vmem_limit_bytes=VMEM_BYTES),
        cost_estimate=cost(3),
        name="join",
    )(places, *[piece for chunk in chunks for piece in chunk])


def project_kernel(core, rows, mine, other, result):
    half = mine.shape[1]
    first, second = halves(core[0], mine[...], other[...])
    result[:, :half] = dot_f32(rows[...], first).astype(jnp.bfloat16)
    result[:, half:] = dot_f32(rows[...], second).astype(jnp.bfloat16)


def project(core, rows, mine, other, used):
    width, half = mine.shape[1:]
    length = rows.shape[0]
    return pl.pallas_call(
        project_kernel,
        grid_spec=pltpu.PrefetchScalarGridSpec(
            num_scalar_prefetch=1,
            grid=(used,),
            in_specs=[
                whole((length, width)),
                pl.BlockSpec((None, width, half), lambda i, core: (i, 0, 0)),
                pl.BlockSpec((None, width, half), lambda i, core: (i, 0, 0)),
            ],
            out_specs=pl.BlockSpec((None, length, 2 * half), lambda i, core: (i, 0, 0)),
        ),
        out_shape=jax.ShapeDtypeStruct((used, length, 2 * half), jnp.bfloat16),
        compiler_params=pltpu.CompilerParams(vmem_limit_bytes=VMEM_BYTES),
        cost_estimate=cost(4),
        name="project",
    )(core, rows, mine, other)


def route_kernel(core, attended, tokens, mine, other, gain, router, routes, slots, middle, normed, gates, *outs):
    f32 = jnp.float32
    first, second = halves(core[0], mine[...], other[...])
    rows = attended[...]
    moved = jnp.concatenate([dot_f32(rows, first), dot_f32(rows, second)], axis=1)
    value = tokens[...].astype(f32) + moved
    middle[...] = value
    low = (value * lax.rsqrt(jnp.mean(value * value, axis=1, keepdims=True) + EPS) * gain[...]).astype(jnp.bfloat16)
    normed[...] = low
    start = 0
    for first_out, second_out in zip(outs[::2], outs[1::2]):
        size = first_out.shape[0]
        hot = hot_columns(slots[0:1, :], start, 2 * size) + hot_columns(slots[1:2, :], start, 2 * size)
        part = dot_f32(hot, low).astype(jnp.bfloat16)
        first_out[...] = part[:size]
        second_out[...] = part[size:]
        start += 2 * size
    logits = dot_f32(low, router[...])
    soft = jnp.exp(logits - jnp.max(logits, axis=1, keepdims=True))
    soft = soft / jnp.sum(soft, axis=1, keepdims=True)
    expert = lax.broadcasted_iota(jnp.int32, soft.shape, 1)
    chosen = [jnp.sum(jnp.where(expert == routes[:, k : k + 1], soft, 0.0), axis=1, keepdims=True) for k in range(2)]
    for k in range(2):
        gates[:, k : k + 1] = chosen[k] / (chosen[0] + chosen[1])


def route(core, attended, tokens, mine, other, gain, router, routes, slots, pieces, count):
    length, width = tokens.shape
    last, half = mine.shape[0] - 1, mine.shape[2]
    f32, bf16 = jnp.float32, jnp.bfloat16
    weight = pl.BlockSpec((None, width, half), lambda i, core: (last, 0, 0))
    shapes = [((length, width), f32), ((length, width), bf16), ((length, 2), f32)] + [((count, width), bf16)] * pieces
    return pl.pallas_call(
        route_kernel,
        grid_spec=pltpu.PrefetchScalarGridSpec(
            num_scalar_prefetch=1,
            grid=(1,),
            in_specs=[whole((length, width)), whole((length, width)), weight, weight, whole((1, width)), whole(router.shape), whole(routes.shape), whole(slots.shape)],
            out_specs=[whole(shape) for shape, _ in shapes],
        ),
        out_shape=[jax.ShapeDtypeStruct(shape, kind) for shape, kind in shapes],
        compiler_params=pltpu.CompilerParams(vmem_limit_bytes=VMEM_BYTES),
        cost_estimate=cost(6),
        name="route",
    )(core, attended, tokens, mine, other, gain.reshape(1, -1), router, routes, slots)


def hot_route(slots, k, count):
    cols = lax.broadcasted_iota(jnp.int32, (slots.shape[0], count), 1)
    return cols == slots[:, k : k + 1]


def combine_kernel(*refs, count):
    slots, slots_t, scale = refs[:3]
    pieces = refs[3 : 3 + count]
    middle, teacher, cotangent, valid, gates, routes = refs[3 + count : 9 + count]
    output, grad_y, grad_logits, square = refs[9 + count : 13 + count]
    sends, rows = refs[13 + count : 13 + 2 * count], refs[13 + 2 * count]
    f32, bf16 = jnp.float32, jnp.bfloat16
    assemble(rows, pieces)
    table = rows[...]
    picked = [dot_f32(hot_route(slots, k, rows.shape[0]).astype(bf16), table) for k in range(2)]
    result = middle[...] + (gates[:, 0:1] * picked[0] + gates[:, 1:2] * picked[1])
    output[...] = result.astype(bf16)
    misfit = valid[...] * (result - teacher[...].astype(f32))
    square[...] = jnp.sum((misfit * misfit).reshape(-1, 8, misfit.shape[1]), axis=0)
    grad = cotangent[...].astype(f32) + misfit * scale[0, 0]
    grad_y[...] = grad
    steep = [jnp.sum(grad * picked[k], axis=1, keepdims=True) for k in range(2)]
    slack = gates[:, 0:1] * steep[0] + gates[:, 1:2] * steep[1]
    expert = lax.broadcasted_iota(jnp.int32, grad_logits.shape, 1)
    turn = [jnp.where(expert == routes[:, k : k + 1], gates[:, k : k + 1] * (steep[k] - slack), 0.0) for k in range(2)]
    grad_logits[...] = (turn[0] + turn[1]).astype(bf16)
    scaled = [(gates[:, k : k + 1] * grad).astype(bf16) for k in range(2)]
    start = 0
    for first, second in zip(sends[::2], sends[1::2]):
        size = first.shape[0]
        part = [dot_f32(hot_columns(slots_t[k : k + 1, :], start, 2 * size), scaled[k]) for k in range(2)]
        part = (part[0] + part[1]).astype(bf16)
        first[...] = part[:size]
        second[...] = part[size:]
        start += 2 * size


def combine(slots, slots_t, scale, pieces, middle, teacher, cotangent, valid, gates, routes, experts):
    length, width = middle.shape
    count = len(pieces)
    f32, bf16 = jnp.float32, jnp.bfloat16
    return pl.pallas_call(
        lambda *refs: combine_kernel(*refs, count=count),
        in_specs=[pl.BlockSpec(memory_space=pltpu.VMEM)] * 2
        + [pl.BlockSpec(memory_space=pltpu.SMEM)]
        + [pl.BlockSpec(memory_space=pltpu.VMEM)] * (6 + count),
        out_shape=[
            jax.ShapeDtypeStruct((length, width), bf16),
            jax.ShapeDtypeStruct((length, width), f32),
            jax.ShapeDtypeStruct((length, experts), bf16),
            jax.ShapeDtypeStruct((8, width), f32),
        ]
        + [jax.ShapeDtypeStruct(piece.shape, bf16) for piece in pieces],
        scratch_shapes=[pltpu.VMEM((sum(piece.shape[0] for piece in pieces), width), bf16)],
        compiler_params=pltpu.CompilerParams(vmem_limit_bytes=VMEM_BYTES),
        cost_estimate=cost(8),
        name="combine",
    )(slots, slots_t, scale, *pieces, middle, teacher, cotangent, valid, gates, routes)


def norm_back(value, gain, grad):
    root = lax.rsqrt(jnp.mean(value * value, axis=1, keepdims=True) + EPS)
    normed = value * root
    scaled = grad * gain
    inner = jnp.mean(scaled * normed, axis=1, keepdims=True)
    return root * (scaled - normed * inner), jnp.sum((grad * normed).reshape(-1, 8, value.shape[1]), axis=0)


def collect_kernel(core, *refs, count):
    slots, pieces = refs[0], refs[1 : 1 + count]
    middle, gain, grad_logits, router, grad_y, mine, other = refs[1 + count : 8 + count]
    grad_middle, rounded, grad_attended, grad_gain, rows = refs[8 + count :]
    assemble(rows, pieces)
    hot = (hot_route(slots, 0, rows.shape[0]) | hot_route(slots, 1, rows.shape[0])).astype(jnp.bfloat16)
    grad = dot_f32(grad_logits[...], router[...], NT) + dot_f32(hot, rows[...])
    turned, grad_gain[...] = norm_back(middle[...], gain[...], grad)
    result = grad_y[...] + turned
    grad_middle[...] = result
    low = result.astype(jnp.bfloat16)
    rounded[...] = low
    first, second = halves(core[0], mine[...], other[...])
    half = first.shape[1]
    grad_attended[...] = (dot_f32(low[:, :half], first, NT) + dot_f32(low[:, half:], second, NT)).astype(jnp.bfloat16)


def collect(core, slots, pieces, middle, gain, grad_logits, router, grad_y, mine, other):
    length, width = middle.shape
    last, half = mine.shape[0] - 1, mine.shape[2]
    f32, bf16 = jnp.float32, jnp.bfloat16
    weight = pl.BlockSpec((None, width, half), lambda i, core: (last, 0, 0))
    plain = [slots, *pieces, middle, gain.reshape(1, -1), grad_logits, router, grad_y]
    shapes = [((length, width), f32), ((length, width), bf16), ((length, width), bf16), ((8, width), f32)]
    return pl.pallas_call(
        lambda *refs: collect_kernel(*refs, count=len(pieces)),
        grid_spec=pltpu.PrefetchScalarGridSpec(
            num_scalar_prefetch=1,
            grid=(1,),
            in_specs=[whole(array.shape) for array in plain] + [weight, weight],
            out_specs=[whole(shape) for shape, _ in shapes],
            scratch_shapes=[pltpu.VMEM((sum(piece.shape[0] for piece in pieces), width), bf16)],
        ),
        out_shape=[jax.ShapeDtypeStruct(shape, kind) for shape, kind in shapes],
        compiler_params=pltpu.CompilerParams(vmem_limit_bytes=VMEM_BYTES),
        cost_estimate=cost(8),
        name="collect",
    )(core, *plain, mine, other)


def outer_halves_kernel(core, normed, attended, rights, last, *refs, count):
    aways, stays, normed_t, attended_t = refs[:2], refs[2:4], refs[4], refs[5]
    step = pl.program_id(0)

    @pl.when(step == 0)
    def _():
        normed_t[...] = normed[...].T
        attended_t[...] = attended[...].T

    for place in range(count + 1):

        @pl.when(step == place)
        def _():
            result = dot_f32(normed_t[...], rights[...]) if place < count else dot_f32(attended_t[...], last[...])
            result = result.astype(jnp.bfloat16)
            half = result.shape[1] // 2
            away, stay = aways[place // 2], stays[place // 2]
            slot = place % 2

            @pl.when(core[0] == 0)
            def _():
                stay[slot] = result[:, :half]
                away[slot] = result[:, half:]

            @pl.when(core[0] != 0)
            def _():
                away[slot] = result[:, :half]
                stay[slot] = result[:, half:]


def outer_halves(core, normed, attended, rights, last):
    length, width = normed.shape
    count, half = rights.shape[0], width // 2
    shape = jax.ShapeDtypeStruct((2, width, half), jnp.bfloat16)
    return pl.pallas_call(
        lambda *refs: outer_halves_kernel(*refs, count=count),
        grid_spec=pltpu.PrefetchScalarGridSpec(
            num_scalar_prefetch=1,
            grid=(count + 1,),
            in_specs=[
                whole((length, width)),
                whole((length, width)),
                pl.BlockSpec((None, length, width), lambda i, core: (jnp.minimum(i, count - 1), 0, 0)),
                whole((length, width)),
            ],
            out_specs=[whole(shape.shape)] * 4,
            scratch_shapes=[pltpu.VMEM((width, length), jnp.bfloat16)] * 2,
        ),
        out_shape=[shape] * 4,
        compiler_params=pltpu.CompilerParams(vmem_limit_bytes=VMEM_BYTES),
        cost_estimate=cost(2),
        name="outer_halves",
    )(core, normed, attended, rights, last)


def enter_kernel(core, grads, mine, other, tokens, gain, grad_middle, grad_input, grad_gain, total):
    step = pl.program_id(0)
    first, second = halves(core[0], mine[...], other[...])
    half = first.shape[1]
    rows = grads[...]
    part = dot_f32(rows[:, :half], first, NT) + dot_f32(rows[:, half:], second, NT)

    @pl.when(step == 0)
    def _():
        total[...] = part

    @pl.when(step > 0)
    def _():
        total[...] += part

    @pl.when(step == pl.num_programs(0) - 1)
    def _():
        turned, grad_gain[...] = norm_back(tokens[...].astype(jnp.float32), gain[...], total[...])
        grad_input[...] = grad_middle[...] + turned


def enter(core, grads, mine, other, tokens, gain, grad_middle):
    length, width = tokens.shape
    count, half = grads.shape[0], mine.shape[2]
    weight = pl.BlockSpec((None, width, half), lambda i, core: (i, 0, 0))
    return pl.pallas_call(
        enter_kernel,
        grid_spec=pltpu.PrefetchScalarGridSpec(
            num_scalar_prefetch=1,
            grid=(count,),
            in_specs=[pl.BlockSpec((None, length, width), lambda i, core: (i, 0, 0)), weight, weight, whole((length, width)), whole((1, width)), whole((length, width))],
            out_specs=[whole((length, width)), whole((8, width))],
            scratch_shapes=[pltpu.VMEM((length, width), jnp.float32)],
        ),
        out_shape=[jax.ShapeDtypeStruct((length, width), jnp.float32), jax.ShapeDtypeStruct((8, width), jnp.float32)],
        compiler_params=pltpu.CompilerParams(vmem_limit_bytes=VMEM_BYTES),
        cost_estimate=cost(6),
        name="enter",
    )(core, grads, mine, other, tokens, gain.reshape(1, -1), grad_middle)


BOUNDS = (12, 16, 23, 32, 46, 64, 91)
TOP_PRECISION = lax.Precision.HIGHEST
AXES = ("dp", "expert")
PAIR = 2


def after(value, *others):
    return lax.optimization_barrier((value, *others))[0] if others else value


def bucket_index(offset):
    distance = jnp.abs(offset)
    far_bucket = 8 + sum([(distance >= level).astype(jnp.int32) for level in BOUNDS])
    near_bucket = jnp.where(distance < 8, distance, far_bucket)
    return jnp.where(offset > 0, 16, 0) + near_bucket


def norm_apply(inputs, gain_vec):
    return inputs * lax.rsqrt(jnp.mean(inputs * inputs, axis=-1, keepdims=True) + EPS) * gain_vec


def tile_offsets(query_block, key_block):
    rows = query_block * BLOCK + lax.broadcasted_iota(jnp.int32, (BLOCK, BLOCK), 0)
    cols = key_block * BLOCK + lax.broadcasted_iota(jnp.int32, (BLOCK, BLOCK), 1)
    return rows, cols


def offset_bias(table):
    offsets = jnp.arange(4 * BLOCK, dtype=jnp.int32) - 2 * BLOCK
    hot = (bucket_index(offsets)[None] == jnp.arange(table.shape[1], dtype=jnp.int32)[:, None]).astype(jnp.float32)
    return jnp.dot(table, hot, precision=TOP_PRECISION)


def table_gradient(bands, buckets):
    rows, cols = tile_offsets(0, 0)
    ids = [jnp.full((BLOCK, BLOCK), bucket_far(), jnp.int32)]
    ids += [bucket_index(shift * BLOCK + cols - rows) for shift in (-1, 0, 1)]
    hot = (jnp.stack(ids)[..., None] == jnp.arange(buckets, dtype=jnp.int32)).astype(jnp.float32)
    return jnp.einsum("hdxy,dxyb->hb", bands, hot, precision=TOP_PRECISION)


def bucket_far():
    return 8 + len(BOUNDS)


def on_device(
    tokens,
    qkv_weight,
    out_weight,
    position_bias_table,
    gain_attn,
    gain_moe,
    router,
    w_in,
    w_out,
    routes,
    prefix,
    valid_mask,
    teacher,
    cotangent,
):
    length, width = tokens.shape
    bf16, f32 = jnp.bfloat16, jnp.float32
    expert_count = router.shape[1]
    top_count = routes.shape[1]
    groups = lax.axis_size("expert")
    copies = lax.axis_size("dp")
    inner = w_in.shape[2]
    capacity = 5 * length * top_count // (4 * expert_count)
    total_tokens = length * copies * groups
    sources = 2 * groups
    blocks = length // BLOCK
    here_dp, here_group = lax.axis_index("dp"), lax.axis_index("expert")
    half = (here_dp >> 1) & 1
    core = here_group & 1
    rest = copies // 4

    def swap(value, dp_mask, group_mask):
        pairs = [
            (i, ((i // groups) ^ dp_mask) * groups + ((i % groups) ^ group_mask))
            for i in range(copies * groups)
        ]
        return lax.ppermute(value, AXES, pairs)

    def bits(count):
        return [1 << place for place in range(count.bit_length() - 1)]

    def partial_sums(value):
        sums = []
        for masks in [(0, mask) for mask in bits(groups)] + [(mask, 0) for mask in bits(copies)]:
            value = value + swap(value, *masks)
            sums.append(value)
        return sums

    chips = groups

    def across(value, place):
        return swap(value, PAIR * (place // (groups // 2)), 2 * (place % (groups // 2)))

    def to_chips(pieces):
        return [pieces[0]] + [across(pieces[place], place) for place in range(1, chips)]

    def through(visit, sends):
        direct, relay = to_chips(sends[::2]), to_chips(sends[1::2])
        seen, direct = visit(direct)
        direct = to_chips(direct)
        relay = [after(part, seen) for part in relay]
        passed = visit(swap(jnp.concatenate(relay), 0, 1))
        return direct, [swap(after(part, *direct), 0, 1) for part in passed]

    def weave(direct, relay):
        return [part for pair in zip(direct, to_chips(relay)) for part in pair]

    ring = list(range(0, copies, 2)) + list(range(copies - 1, 0, -2))
    turns = [(1, step) for step in range(1, copies // 2 + 1)] + [(-1, step) for step in range(1, copies // 2)]

    def gather_ring(shard, due):
        got = [shard]
        for turn in (1, -1):
            held = shard
            pairs = [(ring[i], ring[(i + turn) % copies]) for i in range(copies)]
            for step in [step for way, step in turns if way == turn]:
                held = lax.ppermute(after(held, *due[step - 2 : step - 1]) if step > 1 else held, "dp", pairs)
                got.append(held)
        return got

    def ring_places():
        place = jnp.where(here_dp & 1 == 0, here_dp >> 1, copies - 1 - (here_dp >> 1))
        shift = jnp.array([0] + [turn * step for turn, step in turns], jnp.int32)
        place = (place - shift) & (copies - 1)
        return jnp.where(place < copies // 2, 2 * place, 2 * (copies - 1 - place) + 1).astype(jnp.int32)


    flat_routes = routes.reshape(-1)
    pair_count = length * top_count
    slot_count = sources * capacity
    route_hits = (flat_routes[:, None] == jnp.arange(expert_count, dtype=jnp.int32)[None, :]).astype(bf16)
    lower_ones = (
        lax.broadcasted_iota(jnp.int32, (pair_count, pair_count), 0)
        >= lax.broadcasted_iota(jnp.int32, (pair_count, pair_count), 1)
    ).astype(bf16)
    running = jnp.dot(lower_ones, route_hits, preferred_element_type=f32)
    pair_rank = jnp.sum((running - 1.0) * route_hits.astype(f32), axis=1).astype(jnp.int32)
    away = (flat_routes >> 1) ^ here_group
    chip = ((flat_routes & 1) ^ half) * (groups // 2) + (away >> 1)
    slots = ((chip * 2 + (away & 1)) * capacity + pair_rank).reshape(length, top_count)
    slots_t = slots.T

    resid = tokens.astype(f32)
    normed1 = norm_apply(resid, gain_attn).astype(bf16)
    columns = width // 2
    core_index = core.reshape(1).astype(jnp.int32)
    valid_rows = valid_mask.astype(f32)[:, None]
    counts = [jnp.broadcast_to(jnp.sum(valid_rows), (8, 128))]
    count_trades = [(0, mask) for mask in bits(groups)] + [(mask, 0) for mask in bits(copies)]

    def count_beside(before, value):
        if len(counts) > len(count_trades):
            return value
        counts.append(counts[-1] + swap(after(counts[-1], before), *count_trades[len(counts) - 1]))
        return after(value, counts[-1])

    shards = [
        lax.dynamic_slice_in_dim(part, core * columns, columns, 2)
        for part in (qkv_weight[:2], jnp.concatenate([qkv_weight[2:], out_weight[None]]))
    ]
    if copies > 8:
        mine = lax.all_gather(jnp.concatenate(shards), "dp", axis=1, tiled=True)
    else:
        mine = join(ring_places(), [gather_ring(shards[0], ()), gather_ring(shards[1], (slots_t, normed1))])
    other = count_beside(mine, swap(mine, 0, 1))
    qkv_rows = count_beside(other, project(core_index, normed1, mine, other, 3))
    offsets = offset_bias(position_bias_table)
    attended, probs = attention_forward(position_bias_table[:, bucket_far()], prefix, qkv_rows, offsets)
    middle, normed2, gates, *sends = route(
        core_index, count_beside(qkv_rows, attended), tokens, mine, other, gain_moe, router, routes, slots_t, 2 * chips, capacity
    )

    pick = half.reshape(1).astype(jnp.int32)
    hidden, slopes, rows_in = [], [], []

    def expert(pieces):
        one = not isinstance(pieces, list)
        pieces = [pieces] if one else pieces
        hidden_t, slope, rows_t, *results = expert_forward(pick, pieces, chips, w_in, w_out)
        hidden_t = count_beside(pieces[-1], hidden_t)
        for kept, value in zip((hidden, slopes, rows_in), (hidden_t, slope, rows_t)):
            kept.append(value)
        return results if one else (hidden_t, results)

    back = weave(*through(expert, sends))
    while len(counts) <= len(count_trades):
        back[0] = count_beside(back[0], back[0])
    valid_count = counts[-1][0, 0]
    scale = (total_tokens / valid_count).reshape(1, 1)
    output, grad_y, grad_logits, squares, *sends = combine(
        slots, slots_t, scale, back, middle, teacher, cotangent, valid_rows, gates, routes, expert_count
    )

    out_rows = inner // copies
    in_rows = width // copies
    far_bit = here_dp % 2
    slices = jnp.arange(rest, dtype=jnp.int32) * 4

    def picks(bit0):
        return jnp.concatenate([slices + ((half ^ other_half) * 2 + bit0) for other_half in (1, 0)]).astype(jnp.int32)

    sent, kept = picks(1 - far_bit), picks(far_bit)

    def add(left, right):
        return (left.astype(f32) + right.astype(f32)).astype(bf16)

    def fold(unit, bit, axis=0):
        unit = unit.reshape(unit.shape[:axis] + (2, unit.shape[axis] // 2) + unit.shape[axis + 1 :])
        away_part = lax.dynamic_index_in_dim(unit, 1 - bit, axis, keepdims=False)
        return away_part, lax.dynamic_index_in_dim(unit, bit, axis, keepdims=False)

    far_masks = list(reversed(bits(copies)[2:]))

    def near_add(got, keep):
        away_part, stay_part = fold(add(got, keep), (here_dp // far_masks[0]) % 2)
        return away_part, stay_part

    def far_trade(away_part):
        return swap(away_part, far_masks[0], 0)

    def finish(got, stay):
        unit = add(got, stay)
        for mask in far_masks[1:]:
            away_part, stay_part = fold(unit, (here_dp // mask) % 2)
            unit = add(swap(away_part, mask, 0), stay_part)
        return unit[0]

    plan_a, plan_b, plan_c = ((0, 0), (0, 1)), ((0, 2), (1, 0)), ((1, 1), (1, 2))
    plan_d, plan_e, plan_f = plan_a, plan_b, plan_c
    out_plans, in_plans = (plan_a, plan_b, plan_c), (plan_d, plan_e, plan_f)

    grad_rows, grad_pre, parts = [], [], []

    def expert_back(pieces):
        if isinstance(pieces, list):
            grad_pre_rows, grads, *results = expert_backward(pick, pieces, chips, w_in, w_out, slopes[0])
            grad_rows.append(grads)
            grad_pre.append(grad_pre_rows)
            return grad_pre_rows, results
        grad_rows.append(pieces)
        parts.extend(weight_part(sent, hidden, grad_rows, out_rows, out_plans, rest, width))
        parts[0] = swap(parts[0], 1, 0)
        pieces = after(pieces, parts[1])
        grad_pre_rows, _, *results = expert_backward(pick, [pieces], chips, w_in, w_out, slopes[1])
        grad_pre.append(grad_pre_rows)
        return results

    direct, relay = through(expert_back, sends)
    got_a, send_b, send_c = parts
    relay = [after(part, got_a) for part in relay]
    got_b = swap(after(send_b, relay[0]), 1, 0)
    back = weave(direct, relay)
    grad_rows, grad_pre = lax.optimization_barrier((grad_rows, grad_pre, relay))[:2]
    keep_a, keep_b, keep_c = weight_part(kept, hidden, grad_rows, out_rows, out_plans, rest, width)
    away_a, stay_a = near_add(got_a, keep_a)
    far_a = far_trade(away_a)
    send_d, send_e, send_f = weight_part(sent, rows_in, after(grad_pre, away_a), in_rows, in_plans, rest, inner // 2)
    back = [after(part, send_d) for part in back]
    got_c = swap(after(send_c, send_d), 1, 0)
    grad_middle, grad_attn_proj, grad_attended, gain_moe_parts = collect(
        core_index, slots, back, middle, gain_moe, grad_logits, router, grad_y, mine, other
    )
    away_b, stay_b = near_add(after(got_b, grad_attended), keep_b)
    got_d = swap(after(send_d, grad_attended), 1, 0)
    grad_attended, away_b = lax.optimization_barrier((grad_attended, away_b))
    grad_qkv_rows, bands = attention_backward(qkv_rows, grad_attended, probs)
    grad_qkv_rows, got_c, far_a = lax.optimization_barrier((grad_qkv_rows, got_c, far_a))
    done_a = finish(far_a, stay_a)

    away_c, stay_c = near_add(got_c, keep_c)
    far_c = far_trade(jnp.concatenate([away_b, away_c], axis=1))
    stay_c = jnp.concatenate([stay_b, stay_c], axis=1)
    *weights_away, stay_1, stay_2 = outer_halves(
        core_index, normed1, attended, after(grad_qkv_rows, away_c), grad_attn_proj
    )
    weights_away, got_d = lax.optimization_barrier((weights_away, got_d))
    got_e = swap(after(send_e, got_d), 1, 0)
    keep_d, keep_e, keep_f = weight_part(
        kept, rows_in, after(grad_pre, *weights_away), in_rows, in_plans, rest, inner // 2
    )
    group_masks = bits(groups)[1:]
    dp_masks = sorted(bits(copies), key=lambda mask: (mask != PAIR, mask))

    def over_dp(total, mask, passed):
        axis = 1 + sorted([other for other in dp_masks if other not in passed], reverse=True).index(mask)
        bit = (here_dp // mask) % 2
        away_part = lax.dynamic_index_in_dim(total, 1 - bit, axis, keepdims=False)
        stay_part = lax.dynamic_index_in_dim(total, bit, axis, keepdims=False)
        return swap(away_part, mask, 0), stay_part

    weights_got = [swap(part, 0, 1) for part in weights_away]
    halves_sum = [
        add(after(got, keep_d), stay).reshape(2, copies, in_rows, columns) for got, stay in zip(weights_got, (stay_1, stay_2))
    ]
    for mask in group_masks[:-1]:
        folded = [fold(part, (here_group // mask) % 2, 2) for part in halves_sum]
        halves_sum = [add(swap(away_part, 0, mask), stay_part) for away_part, stay_part in folded]
    folded = [fold(part, (here_group // group_masks[-1]) % 2, 2) for part in halves_sum]
    y_stay = jnp.concatenate([stay_part for _, stay_part in folded])
    y_got = swap(jnp.concatenate([away_part for away_part, _ in folded]), 0, group_masks[-1])
    away_d, stay_d = near_add(after(got_d, y_stay), keep_d)
    far_d = far_trade(away_d)
    grad_input, gain_attn_parts = enter(
        core_index, after(grad_qkv_rows, away_d), mine, other, tokens, gain_attn, grad_middle
    )

    away_e, stay_e = near_add(after(got_e, gain_attn_parts), keep_e)
    got_f = swap(after(send_f, away_e), 1, 0)
    away_f, stay_f = near_add(after(got_f, away_e), keep_f)
    grad_table = table_gradient(after(bands, away_e), position_bias_table.shape[1])
    normed2, squares, gain_moe_parts = after((normed2, squares, gain_moe_parts), y_stay)
    grad_router = jnp.einsum("td,te->de", normed2, grad_logits, preferred_element_type=f32)
    small = [
        jnp.sum(gain_moe_parts, axis=0),
        jnp.sum(gain_attn_parts, axis=0),
        grad_router,
        grad_table,
        jnp.sum(squares),
    ]
    sizes = [value.size for value in small]
    flat = jnp.concatenate([value.reshape(-1) for value in small])
    flat = jnp.pad(flat, (0, -sum(sizes) % 1024)).reshape(-1, 128)
    done_c = finish(after(far_c, away_e), stay_c)
    total = add(after(y_got, away_f, far_c, grad_table), y_stay)
    total = total.reshape((4,) + (2,) * len(dp_masks) + (-1, columns))


    small_trades = [(0, 1), (0, group_masks[0])] + [(mask, 0) for mask in dp_masks if mask != PAIR] + [(PAIR, 0)]
    small_trades += [(0, mask) for mask in group_masks[1:]]
    passed_masks = []
    for mask in dp_masks:
        got, stay = over_dp(total, mask, passed_masks)
        passed_masks.append(mask)
        flat_got = swap(after(flat, stay), *small_trades.pop(0))
        if mask == PAIR:
            far_e, far_f = far_trade(after(away_e, stay)), far_trade(after(away_f, stay))
            got = after(got, far_e)
            done_e = finish(far_e, stay_e)
        elif len(passed_masks) == len(dp_masks):
            got = after(got, far_f)
            done_f = finish(far_f, stay_f)
        total = add(got, stay)
        flat = flat + flat_got
        if mask == PAIR:
            done_d = finish(after(far_d, total), stay_d)
            in_first = swap(done_d, PAIR, 0)
            out_theirs = swap(after(jnp.concatenate([done_a, done_c[:1]]), total), PAIR, 0)
        flat = after(flat, total)
    in_theirs = jnp.concatenate([in_first, swap(done_e[:1], PAIR, 0)])
    for mask in reversed(group_masks):
        bit = (here_group // mask) % 2
        other_part = swap(total, 0, mask)
        total = jnp.concatenate([jnp.where(bit == 0, total, other_part), jnp.where(bit == 0, other_part, total)], axis=1)
        flat = flat + swap(flat, *small_trades.pop(0))
        total, flat = lax.optimization_barrier((total, flat))
    other_part = swap(total, 0, 1)
    for trade in small_trades:
        flat = flat + swap(flat, *trade)
    total = jnp.concatenate([jnp.where(core == 0, total, other_part), jnp.where(core == 0, other_part, total)], axis=2)
    weights_done = total.astype(f32)
    grad_qkv, grad_out_weight = weights_done[:3], weights_done[3]
    flat = flat.reshape(-1)
    starts = [sum(sizes[:place]) for place in range(len(sizes))]
    grad_gain_moe, grad_gain_attn, grad_router, grad_table, square_total = [
        flat[start : start + value.size].reshape(value.shape) for start, value in zip(starts, small)
    ]

    out_mine, in_mine = done_c[1:], jnp.concatenate([done_e[1:], done_f])

    def both_experts(mine, theirs):
        mine, theirs = [part.reshape(-1, part.shape[-1]).astype(f32) for part in (mine, theirs)]
        return jnp.stack([jnp.where(half == 0, mine, theirs), jnp.where(half == 0, theirs, mine)])

    grad_w_out = both_experts(out_mine, out_theirs)
    grad_w_in = both_experts(in_mine, in_theirs)

    distill_loss = square_total / (width * valid_count)
    return (
        output.astype(bf16),
        distill_loss,
        grad_input,
        grad_qkv,
        grad_out_weight,
        grad_w_in,
        grad_w_out,
        grad_router,
        grad_table,
        grad_gain_attn,
        grad_gain_moe,
    )


def solution(mesh):
    rows = P(AXES, None)
    return jax.shard_map(
        on_device,
        mesh=mesh,
        in_specs=(
            rows,
            P(None, "dp", None),
            P("dp", None),
            P(),
            P(),
            P(),
            P(),
            P("expert", None, None),
            P("expert", None, None),
            rows,
            P(AXES),
            P(AXES),
            rows,
            rows,
        ),
        out_specs=(
            rows,
            P(),
            rows,
            P(None, "dp", None),
            P("dp", None),
            P("expert", "dp", None),
            P("expert", "dp", None),
            P(),
            P(),
            P(),
            P(),
        ),
        check_vma=False,
    )
```

```python
import math
import jax
import jax.numpy as jnp
from jax import lax
from jax.experimental import pallas as pl
from jax.experimental.pallas import tpu as pltpu
from jax.sharding import PartitionSpec as P

BLOCK = 128
THIRDS = 3
SMALL = 8
EPS = 1e-06
GELU_A = math.sqrt(2.0 / math.pi)
GELU_B = 0.044715
NT = (((1,), (1,)), ((), ()))
TN = (((0,), (0,)), ((), ()))
VMEM_BYTES = 56 * 1024 * 1024


def cost(micros):
    return pl.CostEstimate(flops=int(micros * 0.37e9), bytes_accessed=0, transcendentals=0)


def dot_f32(left, right, dims=(((1,), (0,)), ((), ()))):
    return lax.dot_general(left, right, dims, preferred_element_type=jnp.float32)


def assemble(rows, pieces):
    start = 0
    for piece in pieces:
        rows[pl.ds(start, piece.shape[0]), :] = piece[...]
        start += piece.shape[0]


def hand_out(total, outs):
    start = 0
    for out in outs:
        out[...] = total[pl.ds(start, out.shape[0]), :].astype(out.dtype)
        start += out.shape[0]


def whole(shape):
    return pl.BlockSpec(shape, lambda *step: (0,) * len(shape))


def expert_forward_kernel(pick, *refs, chunk, count):
    pieces, w_in, w_out = refs[:count], refs[count], refs[count + 1]
    hidden_t, slope, rows_t = refs[count + 2 : count + 5]
    outs, rows, total = refs[count + 5 : -2], refs[-2], refs[-1]
    step = pl.program_id(0)

    @pl.when(step == 0)
    def _():
        assemble(rows, pieces)
        total[...] = jnp.zeros_like(total)
        rows_t[...] = rows[...].T

    for start in range(0, rows.shape[0], chunk):
        part = pl.ds(start, chunk)
        pre = dot_f32(rows[part, :], w_in[0])
        square = pre * pre
        bend = jnp.tanh(pre * (GELU_A + (GELU_A * GELU_B) * square))
        half = 0.5 + 0.5 * bend
        act = (pre * half).astype(jnp.bfloat16)
        lift = pre * (0.5 * GELU_A + (1.5 * GELU_A * GELU_B) * square)
        slope[part, :] = (half + lift * (1.0 - bend * bend)).astype(jnp.bfloat16)
        hidden_t[:, part] = act.T
        total[part, :] += dot_f32(act, w_out[0])

    @pl.when(step == pl.num_programs(0) - 1)
    def _():
        hand_out(total, outs)


def expert_forward(pick, pieces, results, w_in, w_out, tile=768, chunk=320):
    many, width = sum(piece.shape[0] for piece in pieces), pieces[0].shape[1]
    inner = w_in.shape[2]
    bf16 = jnp.bfloat16
    return pl.pallas_call(
        lambda *refs: expert_forward_kernel(*refs, chunk=chunk, count=len(pieces)),
        grid_spec=pltpu.PrefetchScalarGridSpec(
            num_scalar_prefetch=1,
            grid=(inner // tile,),
            in_specs=[whole(piece.shape) for piece in pieces]
            + [
                pl.BlockSpec((1, width, tile), lambda f, pick: (pick[0], 0, f)),
                pl.BlockSpec((1, tile, width), lambda f, pick: (pick[0], f, 0)),
            ],
            out_specs=[
                pl.BlockSpec((tile, many), lambda f, pick: (f, 0)),
                pl.BlockSpec((many, tile), lambda f, pick: (0, f)),
                whole((width, many)),
            ]
            + [whole((many // results, width))] * results,
            scratch_shapes=[pltpu.VMEM((many, width), bf16), pltpu.VMEM((many, width), jnp.float32)],
        ),
        out_shape=[
            jax.ShapeDtypeStruct((inner, many), bf16),
            jax.ShapeDtypeStruct((many, inner), bf16),
            jax.ShapeDtypeStruct((width, many), bf16),
        ]
        + [jax.ShapeDtypeStruct((many // results, width), bf16)] * results,
        compiler_params=pltpu.CompilerParams(vmem_limit_bytes=VMEM_BYTES),
        cost_estimate=cost(13),
        name="expert_forward",
    )(pick, *pieces, w_in, w_out)


def expert_backward_kernel(pick, *refs, chunk, count):
    pieces, w_in, w_out, slope = refs[:count], refs[count], refs[count + 1], refs[count + 2]
    grad_pre, rows = refs[count + 3 : count + 5]
    outs, total = refs[count + 5 : -1], refs[-1]
    step = pl.program_id(0)

    @pl.when(step == 0)
    def _():
        assemble(rows, pieces)
        total[...] = jnp.zeros_like(total)

    for start in range(0, rows.shape[0], chunk):
        part = pl.ds(start, chunk)
        back = dot_f32(rows[part, :], w_out[0], NT) * slope[part, :].astype(jnp.float32)
        back = back.astype(jnp.bfloat16)
        grad_pre[part, :] = back
        total[part, :] += dot_f32(back, w_in[0], NT)

    @pl.when(step == pl.num_programs(0) - 1)
    def _():
        hand_out(total, outs)


def expert_backward(pick, pieces, results, w_in, w_out, slope, tile=768, chunk=640):
    many, width = sum(piece.shape[0] for piece in pieces), pieces[0].shape[1]
    inner = w_in.shape[2]
    bf16 = jnp.bfloat16
    return pl.pallas_call(
        lambda *refs: expert_backward_kernel(*refs, chunk=chunk, count=len(pieces)),
        grid_spec=pltpu.PrefetchScalarGridSpec(
            num_scalar_prefetch=1,
            grid=(inner // tile,),
            in_specs=[whole(piece.shape) for piece in pieces]
            + [
                pl.BlockSpec((1, width, tile), lambda f, pick: (pick[0], 0, f)),
                pl.BlockSpec((1, tile, width), lambda f, pick: (pick[0], f, 0)),
                pl.BlockSpec((many, tile), lambda f, pick: (0, f)),
            ],
            out_specs=[pl.BlockSpec((many, tile), lambda f, pick: (0, f)), whole((many, width))]
            + [whole((many // results, width))] * results,
            scratch_shapes=[pltpu.VMEM((many, width), jnp.float32)],
        ),
        out_shape=[jax.ShapeDtypeStruct((many, inner), bf16), jax.ShapeDtypeStruct((many, width), bf16)]
        + [jax.ShapeDtypeStruct((many // results, width), bf16)] * results,
        compiler_params=pltpu.CompilerParams(vmem_limit_bytes=VMEM_BYTES),
        cost_estimate=cost(11),
        name="expert_backward",
    )(pick, *pieces, w_in, w_out, slope)


def seen_blocks(row_block, blocks):
    return max(row_block + 1, blocks // 2)


def attention_forward_kernel(far, prefix, queries, keys, values, offsets, attended, probs, *, heads, blocks):
    pair = pl.program_id(0)
    lane = lax.broadcasted_iota(jnp.int32, queries.shape, 1)
    row = lax.broadcasted_iota(jnp.int32, (BLOCK, BLOCK), 0)
    col = lax.broadcasted_iota(jnp.int32, (BLOCK, BLOCK), 1)
    outs = []
    for head in range(2):
        line = jnp.broadcast_to(offsets[head : head + 1, :], (BLOCK, 4 * BLOCK))
        turned = pltpu.roll(line, 0, 1, stride=1, stride_axis=0)
        far_bias = far[pair * 2 + head]
        mine = (lane < heads) if head == 0 else (lane >= heads)
        query = jnp.where(mine, queries[...] * 0.125, 0.0).astype(jnp.bfloat16)
        score = dot_f32(query, keys[...], NT)
        strips = []
        for row_block in range(blocks):
            span = seen_blocks(row_block, blocks)
            pieces = []
            for key_block in range(span):
                piece = score[row_block * BLOCK : (row_block + 1) * BLOCK, key_block * BLOCK : (key_block + 1) * BLOCK]
                shift = key_block - row_block
                if shift < -1:
                    piece = piece + far_bias
                elif shift < 2:
                    piece = piece + turned[:, (2 + shift) * BLOCK : (3 + shift) * BLOCK]
                else:
                    raise ValueError(shift)
                if shift >= 0:
                    shown = col + key_block * BLOCK < prefix[0]
                    piece = jnp.where((shown | (col <= row)) if shift == 0 else shown, piece, -1e30)
                pieces.append(piece)
            peak = pieces[0]
            for piece in pieces[1:]:
                peak = jnp.maximum(peak, piece)
            peak = jnp.max(peak, axis=1, keepdims=True)
            pieces = [jnp.exp(piece - peak) for piece in pieces]
            mass = pieces[0]
            for piece in pieces[1:]:
                mass = mass + piece
            scale = 1.0 / jnp.sum(mass, axis=1, keepdims=True)
            pieces = [(piece * scale).astype(jnp.bfloat16) for piece in pieces]
            pieces += [jnp.zeros((BLOCK, BLOCK), jnp.bfloat16)] * (blocks - span)
            strips.append(jnp.concatenate(pieces, axis=1))
        weights = jnp.concatenate(strips, axis=0)
        probs[head] = weights
        outs.append(dot_f32(weights, values[...]))
    attended[...] = jnp.where(lane < heads, outs[0], outs[1]).astype(jnp.bfloat16)


def attention_forward(far, prefix, qkv_rows, offsets):
    length, width = qkv_rows.shape[1:]
    pairs = width // 128
    blocks = length // BLOCK
    return pl.pallas_call(
        lambda *refs: attention_forward_kernel(*refs, heads=64, blocks=blocks),
        grid_spec=pltpu.PrefetchScalarGridSpec(
            num_scalar_prefetch=2,
            grid=(pairs,),
            in_specs=[pl.BlockSpec((None, length, 128), lambda h, far, prefix, c=c: (c, 0, h)) for c in range(3)]
            + [pl.BlockSpec((None, 2, 4 * BLOCK), lambda h, far, prefix: (h, 0, 0))],
            out_specs=[
                pl.BlockSpec((length, 128), lambda h, far, prefix: (0, h)),
                pl.BlockSpec((2, length, length), lambda h, far, prefix: (h, 0, 0)),
            ],
        ),
        out_shape=[
            jax.ShapeDtypeStruct((length, width), jnp.bfloat16),
            jax.ShapeDtypeStruct((2 * pairs, length, length), jnp.bfloat16),
        ],
        compiler_params=pltpu.CompilerParams(vmem_limit_bytes=VMEM_BYTES),
        cost_estimate=cost(13),
        name="attention_forward",
    )(far, prefix, qkv_rows, qkv_rows, qkv_rows, offsets.reshape(pairs, 2, 4 * BLOCK))


def attention_backward_kernel(queries, keys, values, grads, probs, grad_rows, bands, *, heads, blocks):
    lane = lax.broadcasted_iota(jnp.int32, queries.shape, 1)
    query_t = (queries[...] * 0.125).astype(jnp.bfloat16).T
    grad_t = grads[...].T
    dq, dk, dv = [], [], []
    for head in range(2):
        mine = (lane < heads) if head == 0 else (lane >= heads)
        sums = [None] * 4
        grad = jnp.where(mine, grads[...], 0.0).astype(jnp.bfloat16)
        back = dot_f32(grad, values[...], NT)
        strips = []
        for row_block in range(blocks):
            span = seen_blocks(row_block, blocks)
            rows = slice(row_block * BLOCK, (row_block + 1) * BLOCK)
            soft = probs[head, pl.ds(row_block * BLOCK, BLOCK), pl.ds(0, span * BLOCK)].astype(jnp.float32)
            part = back[rows, : span * BLOCK]
            inner = jnp.sum(soft * part, axis=1, keepdims=True)
            score_grad = (soft * (part - inner)).astype(jnp.bfloat16)
            for key_block in range(span):
                band = max(key_block - row_block, -2)
                tile = score_grad[:, key_block * BLOCK : (key_block + 1) * BLOCK].astype(jnp.float32)
                sums[band + 2] = tile if sums[band + 2] is None else sums[band + 2] + tile
            if span < blocks:
                rest = jnp.zeros((BLOCK, (blocks - span) * BLOCK), jnp.bfloat16)
                score_grad = jnp.concatenate([score_grad, rest], axis=1)
            strips.append(score_grad)
        flow = jnp.concatenate(strips, axis=0)
        for band in range(4):
            bands[head, band] = sums[band]
        part = slice(head * heads, (head + 1) * heads)
        dq.append(dot_f32(flow, keys[...]) * 0.125)
        dk.append(dot_f32(query_t[part], flow))
        dv.append(dot_f32(grad_t[part], probs[head]))
    grad_rows[0] = jnp.where(lane < heads, dq[0], dq[1]).astype(jnp.bfloat16)
    grad_rows[1] = jnp.concatenate(dk, axis=0).T.astype(jnp.bfloat16)
    grad_rows[2] = jnp.concatenate(dv, axis=0).T.astype(jnp.bfloat16)


def attention_backward(qkv_rows, grads, probs):
    length, width = grads.shape
    pairs = width // 128
    blocks = length // BLOCK
    block = pl.BlockSpec((length, 128), lambda h: (0, h))
    of_three = [pl.BlockSpec((None, length, 128), lambda h, c=c: (c, 0, h)) for c in range(3)]
    return pl.pallas_call(
        lambda *refs: attention_backward_kernel(*refs, heads=64, blocks=blocks),
        grid=(pairs,),
        in_specs=[*of_three, block, pl.BlockSpec((2, length, length), lambda h: (h, 0, 0))],
        out_specs=[pl.BlockSpec((3, length, 128), lambda h: (0, 0, h)), pl.BlockSpec((2, 4, BLOCK, BLOCK), lambda h: (h, 0, 0, 0))],
        out_shape=[jax.ShapeDtypeStruct((3, length, width), jnp.bfloat16)]
        + [jax.ShapeDtypeStruct((2 * pairs, 4, BLOCK, BLOCK), jnp.float32)],
        compiler_params=pltpu.CompilerParams(vmem_limit_bytes=VMEM_BYTES),
        cost_estimate=cost(4),
        name="attention_backward",
    )(qkv_rows, qkv_rows, qkv_rows, grads, probs)


def pieces_left(lefts, plans, many):
    part = lefts[0][0].shape[0] // THIRDS
    return jnp.concatenate(
        [
            jnp.concatenate([ref[pl.ds(third * part, part), :] for ref in lefts[group * many + k]], axis=1)
            for plan in plans
            for group, third in plan
            for k in range(many)
        ]
    )


def put_pieces(result, outs):
    place = 0
    for out in outs:
        many, pieces, part = out.shape[:3]
        for piece in range(pieces):
            for k in range(many):
                out[k, piece] = result[place : place + part]
                place += part


def weight_part_kernel(picks, *refs, count, plans, many):
    lefts, rights, outs = refs[: 2 * count], refs[2 * count : 2 * count + 2], refs[2 * count + 2 :]
    left = pieces_left(list(zip(lefts[:count], lefts[count:])), plans, many)
    right = jnp.concatenate([ref[...] for ref in rights], axis=0)
    put_pieces(dot_f32(left, right).astype(jnp.bfloat16), outs)


def weight_part_plain(picks, lefts, rights, rows, plans, many):
    left, right = jnp.concatenate(lefts, axis=1), jnp.concatenate(rights, axis=0)
    depth, width = right.shape
    part = rows // THIRDS
    result = jnp.take(left.reshape(-1, rows, depth), picks, axis=0)
    result = jnp.einsum("srd,dw->srw", result, right, preferred_element_type=jnp.float32).astype(jnp.bfloat16)
    result = result.reshape(-1, many, THIRDS, part, width)
    return [jnp.stack([result[group, :, third] for group, third in plan], axis=1) for plan in plans]


def weight_part(picks, lefts, rights, rows, plans, many, tile, micros=4):
    depth, width = rights[0].shape
    count, part = picks.shape[0], rows // THIRDS
    if part % 16:
        return weight_part_plain(picks, lefts, rights, rows, plans, many)
    return pl.pallas_call(
        lambda *refs: weight_part_kernel(*refs, count=count, plans=plans, many=many),
        grid_spec=pltpu.PrefetchScalarGridSpec(
            num_scalar_prefetch=1,
            grid=(width // tile,),
            in_specs=[pl.BlockSpec((rows, depth), lambda i, picks, k=k: (picks[k], 0)) for k in range(count)] * 2
            + [pl.BlockSpec((depth, tile), lambda i, picks: (0, i))] * 2,
            out_specs=[pl.BlockSpec((many, len(plan), part, tile), lambda i, picks: (0, 0, 0, i)) for plan in plans],
        ),
        out_shape=[jax.ShapeDtypeStruct((many, len(plan), part, width), jnp.bfloat16) for plan in plans],
        compiler_params=pltpu.CompilerParams(vmem_limit_bytes=VMEM_BYTES),
        cost_estimate=cost(micros),
        name="weight_part",
    )(picks, *([lefts[0]] * count), *([lefts[1]] * count), *rights)


def hot_columns(slots, first, count):
    rows = first + lax.broadcasted_iota(jnp.int32, (count, slots.shape[1]), 0)
    return (rows == slots).astype(jnp.bfloat16)


def halves(core, mine, other):
    return jnp.where(core == 0, mine, other), jnp.where(core == 0, other, mine)


def join_kernel(places, *refs):
    pieces, out = refs[:-1], refs[-1]
    rows = pieces[0].shape[1]
    count = pieces[0].shape[0]
    for chunk in range(out.shape[0] // count):
        for step in range(len(pieces) * count // out.shape[0]):
            piece = pieces[chunk * (len(pieces) * count // out.shape[0]) + step]
            start = pl.multiple_of(places[step] * rows, rows)
            out[pl.ds(chunk * count, count), pl.ds(start, rows), :] = piece[...]


def join(places, chunks):
    count, rows, columns = chunks[0][0].shape
    steps = len(chunks[0])
    return pl.pallas_call(
        join_kernel,
        in_specs=[pl.BlockSpec(memory_space=pltpu.SMEM)] + [pl.BlockSpec(memory_space=pltpu.VMEM)] * (steps * len(chunks)),
        out_shape=jax.ShapeDtypeStruct((count * len(chunks), steps * rows, columns), jnp.bfloat16),
        compiler_params=pltpu.CompilerParams(vmem_limit_bytes=VMEM_BYTES),
        cost_estimate=cost(3),
        name="join",
    )(places, *[piece for chunk in chunks for piece in chunk])


def project_kernel(core, rows, mine, other, result):
    half = mine.shape[1]
    first, second = halves(core[0], mine[...], other[...])
    result[:, :half] = dot_f32(rows[...], first).astype(jnp.bfloat16)
    result[:, half:] = dot_f32(rows[...], second).astype(jnp.bfloat16)


def project(core, rows, mine, other, used):
    width, half = mine.shape[1:]
    length = rows.shape[0]
    return pl.pallas_call(
        project_kernel,
        grid_spec=pltpu.PrefetchScalarGridSpec(
            num_scalar_prefetch=1,
            grid=(used,),
            in_specs=[
                whole((length, width)),
                pl.BlockSpec((None, width, half), lambda i, core: (i, 0, 0)),
                pl.BlockSpec((None, width, half), lambda i, core: (i, 0, 0)),
            ],
            out_specs=pl.BlockSpec((None, length, 2 * half), lambda i, core: (i, 0, 0)),
        ),
        out_shape=jax.ShapeDtypeStruct((used, length, 2 * half), jnp.bfloat16),
        compiler_params=pltpu.CompilerParams(vmem_limit_bytes=VMEM_BYTES),
        cost_estimate=cost(4),
        name="project",
    )(core, rows, mine, other)


def route_kernel(core, attended, tokens, mine, other, gain, router, routes, slots, middle, normed, gates, *outs):
    f32 = jnp.float32
    first, second = halves(core[0], mine[...], other[...])
    rows = attended[...]
    moved = jnp.concatenate([dot_f32(rows, first), dot_f32(rows, second)], axis=1)
    value = tokens[...].astype(f32) + moved
    middle[...] = value
    low = (value * lax.rsqrt(jnp.mean(value * value, axis=1, keepdims=True) + EPS) * gain[...]).astype(jnp.bfloat16)
    normed[...] = low
    start = 0
    for first_out, second_out in zip(outs[::2], outs[1::2]):
        size = first_out.shape[0]
        hot = hot_columns(slots[0:1, :], start, 2 * size) + hot_columns(slots[1:2, :], start, 2 * size)
        part = dot_f32(hot, low).astype(jnp.bfloat16)
        first_out[...] = part[:size]
        second_out[...] = part[size:]
        start += 2 * size
    logits = dot_f32(low, router[...])
    soft = jnp.exp(logits - jnp.max(logits, axis=1, keepdims=True))
    soft = soft / jnp.sum(soft, axis=1, keepdims=True)
    expert = lax.broadcasted_iota(jnp.int32, soft.shape, 1)
    chosen = [jnp.sum(jnp.where(expert == routes[:, k : k + 1], soft, 0.0), axis=1, keepdims=True) for k in range(2)]
    for k in range(2):
        gates[:, k : k + 1] = chosen[k] / (chosen[0] + chosen[1])


def route(core, attended, tokens, mine, other, gain, router, routes, slots, pieces, count):
    length, width = tokens.shape
    last, half = mine.shape[0] - 1, mine.shape[2]
    f32, bf16 = jnp.float32, jnp.bfloat16
    weight = pl.BlockSpec((None, width, half), lambda i, core: (last, 0, 0))
    shapes = [((length, width), f32), ((length, width), bf16), ((length, 2), f32)] + [((count, width), bf16)] * pieces
    return pl.pallas_call(
        route_kernel,
        grid_spec=pltpu.PrefetchScalarGridSpec(
            num_scalar_prefetch=1,
            grid=(1,),
            in_specs=[whole((length, width)), whole((length, width)), weight, weight, whole((1, width)), whole(router.shape), whole(routes.shape), whole(slots.shape)],
            out_specs=[whole(shape) for shape, _ in shapes],
        ),
        out_shape=[jax.ShapeDtypeStruct(shape, kind) for shape, kind in shapes],
        compiler_params=pltpu.CompilerParams(vmem_limit_bytes=VMEM_BYTES),
        cost_estimate=cost(6),
        name="route",
    )(core, attended, tokens, mine, other, gain.reshape(1, -1), router, routes, slots)


def hot_route(slots, k, count):
    cols = lax.broadcasted_iota(jnp.int32, (slots.shape[0], count), 1)
    return cols == slots[:, k : k + 1]


def combine_kernel(*refs, count):
    slots, slots_t, scale = refs[:3]
    pieces = refs[3 : 3 + count]
    middle, teacher, cotangent, valid, gates, routes = refs[3 + count : 9 + count]
    output, grad_y, grad_logits, square = refs[9 + count : 13 + count]
    sends, rows = refs[13 + count : 13 + 2 * count], refs[13 + 2 * count]
    f32, bf16 = jnp.float32, jnp.bfloat16
    assemble(rows, pieces)
    table = rows[...]
    picked = [dot_f32(hot_route(slots, k, rows.shape[0]).astype(bf16), table) for k in range(2)]
    result = middle[...] + (gates[:, 0:1] * picked[0] + gates[:, 1:2] * picked[1])
    output[...] = result.astype(bf16)
    misfit = valid[...] * (result - teacher[...].astype(f32))
    square[...] = jnp.sum((misfit * misfit).reshape(-1, 8, misfit.shape[1]), axis=0)
    grad = cotangent[...].astype(f32) + misfit * scale[0, 0]
    grad_y[...] = grad
    steep = [jnp.sum(grad * picked[k], axis=1, keepdims=True) for k in range(2)]
    slack = gates[:, 0:1] * steep[0] + gates[:, 1:2] * steep[1]
    expert = lax.broadcasted_iota(jnp.int32, grad_logits.shape, 1)
    turn = [jnp.where(expert == routes[:, k : k + 1], gates[:, k : k + 1] * (steep[k] - slack), 0.0) for k in range(2)]
    grad_logits[...] = (turn[0] + turn[1]).astype(bf16)
    scaled = [(gates[:, k : k + 1] * grad).astype(bf16) for k in range(2)]
    start = 0
    for first, second in zip(sends[::2], sends[1::2]):
        size = first.shape[0]
        part = [dot_f32(hot_columns(slots_t[k : k + 1, :], start, 2 * size), scaled[k]) for k in range(2)]
        part = (part[0] + part[1]).astype(bf16)
        first[...] = part[:size]
        second[...] = part[size:]
        start += 2 * size


def combine(slots, slots_t, scale, pieces, middle, teacher, cotangent, valid, gates, routes, experts):
    length, width = middle.shape
    count = len(pieces)
    f32, bf16 = jnp.float32, jnp.bfloat16
    return pl.pallas_call(
        lambda *refs: combine_kernel(*refs, count=count),
        in_specs=[pl.BlockSpec(memory_space=pltpu.VMEM)] * 2
        + [pl.BlockSpec(memory_space=pltpu.SMEM)]
        + [pl.BlockSpec(memory_space=pltpu.VMEM)] * (6 + count),
        out_shape=[
            jax.ShapeDtypeStruct((length, width), bf16),
            jax.ShapeDtypeStruct((length, width), f32),
            jax.ShapeDtypeStruct((length, experts), bf16),
            jax.ShapeDtypeStruct((8, width), f32),
        ]
        + [jax.ShapeDtypeStruct(piece.shape, bf16) for piece in pieces],
        scratch_shapes=[pltpu.VMEM((sum(piece.shape[0] for piece in pieces), width), bf16)],
        compiler_params=pltpu.CompilerParams(vmem_limit_bytes=VMEM_BYTES),
        cost_estimate=cost(8),
        name="combine",
    )(slots, slots_t, scale, *pieces, middle, teacher, cotangent, valid, gates, routes)


def norm_back(value, gain, grad):
    root = lax.rsqrt(jnp.mean(value * value, axis=1, keepdims=True) + EPS)
    normed = value * root
    scaled = grad * gain
    inner = jnp.mean(scaled * normed, axis=1, keepdims=True)
    return root * (scaled - normed * inner), jnp.sum((grad * normed).reshape(-1, 8, value.shape[1]), axis=0)


def collect_kernel(core, *refs, count):
    slots, pieces = refs[0], refs[1 : 1 + count]
    middle, gain, grad_logits, router, grad_y, mine, other = refs[1 + count : 8 + count]
    grad_middle, rounded, grad_attended, grad_gain, rows = refs[8 + count :]
    assemble(rows, pieces)
    hot = (hot_route(slots, 0, rows.shape[0]) | hot_route(slots, 1, rows.shape[0])).astype(jnp.bfloat16)
    grad = dot_f32(grad_logits[...], router[...], NT) + dot_f32(hot, rows[...])
    turned, grad_gain[...] = norm_back(middle[...], gain[...], grad)
    result = grad_y[...] + turned
    grad_middle[...] = result
    low = result.astype(jnp.bfloat16)
    rounded[...] = low
    first, second = halves(core[0], mine[...], other[...])
    half = first.shape[1]
    grad_attended[...] = (dot_f32(low[:, :half], first, NT) + dot_f32(low[:, half:], second, NT)).astype(jnp.bfloat16)


def collect(core, slots, pieces, middle, gain, grad_logits, router, grad_y, mine, other):
    length, width = middle.shape
    last, half = mine.shape[0] - 1, mine.shape[2]
    f32, bf16 = jnp.float32, jnp.bfloat16
    weight = pl.BlockSpec((None, width, half), lambda i, core: (last, 0, 0))
    plain = [slots, *pieces, middle, gain.reshape(1, -1), grad_logits, router, grad_y]
    shapes = [((length, width), f32), ((length, width), bf16), ((length, width), bf16), ((8, width), f32)]
    return pl.pallas_call(
        lambda *refs: collect_kernel(*refs, count=len(pieces)),
        grid_spec=pltpu.PrefetchScalarGridSpec(
            num_scalar_prefetch=1,
            grid=(1,),
            in_specs=[whole(array.shape) for array in plain] + [weight, weight],
            out_specs=[whole(shape) for shape, _ in shapes],
            scratch_shapes=[pltpu.VMEM((sum(piece.shape[0] for piece in pieces), width), bf16)],
        ),
        out_shape=[jax.ShapeDtypeStruct(shape, kind) for shape, kind in shapes],
        compiler_params=pltpu.CompilerParams(vmem_limit_bytes=VMEM_BYTES),
        cost_estimate=cost(8),
        name="collect",
    )(core, *plain, mine, other)


def outer_halves_kernel(core, normed, attended, rights, last, *refs, count):
    aways, stays, normed_t, attended_t = refs[:2], refs[2:4], refs[4], refs[5]
    step = pl.program_id(0)

    @pl.when(step == 0)
    def _():
        normed_t[...] = normed[...].T
        attended_t[...] = attended[...].T

    for place in range(count + 1):

        @pl.when(step == place)
        def _():
            result = dot_f32(normed_t[...], rights[...]) if place < count else dot_f32(attended_t[...], last[...])
            result = result.astype(jnp.bfloat16)
            half = result.shape[1] // 2
            away, stay = aways[place // 2], stays[place // 2]
            slot = place % 2

            @pl.when(core[0] == 0)
            def _():
                stay[slot] = result[:, :half]
                away[slot] = result[:, half:]

            @pl.when(core[0] != 0)
            def _():
                away[slot] = result[:, :half]
                stay[slot] = result[:, half:]


def outer_halves(core, normed, attended, rights, last):
    length, width = normed.shape
    count, half = rights.shape[0], width // 2
    shape = jax.ShapeDtypeStruct((2, width, half), jnp.bfloat16)
    return pl.pallas_call(
        lambda *refs: outer_halves_kernel(*refs, count=count),
        grid_spec=pltpu.PrefetchScalarGridSpec(
            num_scalar_prefetch=1,
            grid=(count + 1,),
            in_specs=[
                whole((length, width)),
                whole((length, width)),
                pl.BlockSpec((None, length, width), lambda i, core: (jnp.minimum(i, count - 1), 0, 0)),
                whole((length, width)),
            ],
            out_specs=[whole(shape.shape)] * 4,
            scratch_shapes=[pltpu.VMEM((width, length), jnp.bfloat16)] * 2,
        ),
        out_shape=[shape] * 4,
        compiler_params=pltpu.CompilerParams(vmem_limit_bytes=VMEM_BYTES),
        cost_estimate=cost(2),
        name="outer_halves",
    )(core, normed, attended, rights, last)


def enter_kernel(
    core, grads, mine, other, tokens, gain, grad_middle, moe_parts, squares, normed, grad_logits, grad_input, small, total
):
    step = pl.program_id(0)
    first, second = halves(core[0], mine[...], other[...])
    half = first.shape[1]
    rows = grads[...]
    part = dot_f32(rows[:, :half], first, NT) + dot_f32(rows[:, half:], second, NT)

    @pl.when(step == 0)
    def _():
        total[...] = part

    @pl.when(step > 0)
    def _():
        total[...] += part

    @pl.when(step == pl.num_programs(0) - 1)
    def _():
        turned, gain_parts = norm_back(tokens[...].astype(jnp.float32), gain[...], total[...])
        grad_input[...] = grad_middle[...] + turned
        sums = [jnp.sum(part, axis=0, keepdims=True) for part in (moe_parts[...], gain_parts, squares[...])]
        sums.append(jnp.zeros((SMALL - len(sums), gain.shape[1]), jnp.float32))
        small[pl.ds(0, SMALL), :] = jnp.concatenate(sums)
        small[pl.ds(SMALL, grad_logits.shape[1]), :] = dot_f32(grad_logits[...], normed[...], TN)


def enter(core, grads, mine, other, tokens, gain, grad_middle, moe_parts, squares, normed, grad_logits):
    length, width = tokens.shape
    count, half, experts = grads.shape[0], mine.shape[2], grad_logits.shape[1]
    weight = pl.BlockSpec((None, width, half), lambda i, core: (i, 0, 0))
    plain = [tokens, gain.reshape(1, -1), grad_middle, moe_parts, squares, normed, grad_logits]
    shapes = [(length, width), (SMALL + experts, width)]
    return pl.pallas_call(
        enter_kernel,
        grid_spec=pltpu.PrefetchScalarGridSpec(
            num_scalar_prefetch=1,
            grid=(count,),
            in_specs=[pl.BlockSpec((None, length, width), lambda i, core: (i, 0, 0)), weight, weight]
            + [whole(array.shape) for array in plain],
            out_specs=[whole(shape) for shape in shapes],
            scratch_shapes=[pltpu.VMEM((length, width), jnp.float32)],
        ),
        out_shape=[jax.ShapeDtypeStruct(shape, jnp.float32) for shape in shapes],
        compiler_params=pltpu.CompilerParams(vmem_limit_bytes=VMEM_BYTES),
        cost_estimate=cost(6),
        name="enter",
    )(core, grads, mine, other, *plain)


BOUNDS = (12, 16, 23, 32, 46, 64, 91)
TOP_PRECISION = lax.Precision.HIGHEST
AXES = ("dp", "expert")
PAIR = 2


def after(value, *others):
    return lax.optimization_barrier((value, *others))[0] if others else value


def bucket_index(offset):
    distance = jnp.abs(offset)
    far_bucket = 8 + sum([(distance >= level).astype(jnp.int32) for level in BOUNDS])
    near_bucket = jnp.where(distance < 8, distance, far_bucket)
    return jnp.where(offset > 0, 16, 0) + near_bucket


def norm_apply(inputs, gain_vec):
    return inputs * lax.rsqrt(jnp.mean(inputs * inputs, axis=-1, keepdims=True) + EPS) * gain_vec


def tile_offsets(query_block, key_block):
    rows = query_block * BLOCK + lax.broadcasted_iota(jnp.int32, (BLOCK, BLOCK), 0)
    cols = key_block * BLOCK + lax.broadcasted_iota(jnp.int32, (BLOCK, BLOCK), 1)
    return rows, cols


def offset_bias(table):
    offsets = jnp.arange(4 * BLOCK, dtype=jnp.int32) - 2 * BLOCK
    hot = (bucket_index(offsets)[None] == jnp.arange(table.shape[1], dtype=jnp.int32)[:, None]).astype(jnp.float32)
    return jnp.dot(table, hot, precision=TOP_PRECISION)


def table_gradient(bands, buckets):
    rows, cols = tile_offsets(0, 0)
    ids = [jnp.full((BLOCK, BLOCK), bucket_far(), jnp.int32)]
    ids += [bucket_index(shift * BLOCK + cols - rows) for shift in (-1, 0, 1)]
    hot = (jnp.stack(ids)[..., None] == jnp.arange(buckets, dtype=jnp.int32)).astype(jnp.float32)
    return jnp.einsum("hdxy,dxyb->hb", bands, hot, precision=TOP_PRECISION)


def bucket_far():
    return 8 + len(BOUNDS)


def on_device(
    tokens,
    qkv_weight,
    out_weight,
    position_bias_table,
    gain_attn,
    gain_moe,
    router,
    w_in,
    w_out,
    routes,
    prefix,
    valid_mask,
    teacher,
    cotangent,
):
    length, width = tokens.shape
    bf16, f32 = jnp.bfloat16, jnp.float32
    expert_count = router.shape[1]
    top_count = routes.shape[1]
    groups = lax.axis_size("expert")
    copies = lax.axis_size("dp")
    inner = w_in.shape[2]
    capacity = 5 * length * top_count // (4 * expert_count)
    total_tokens = length * copies * groups
    sources = 2 * groups
    blocks = length // BLOCK
    here_dp, here_group = lax.axis_index("dp"), lax.axis_index("expert")
    half = (here_dp >> 1) & 1
    core = here_group & 1
    rest = copies // 4

    def swap(value, dp_mask, group_mask):
        pairs = [
            (i, ((i // groups) ^ dp_mask) * groups + ((i % groups) ^ group_mask))
            for i in range(copies * groups)
        ]
        return lax.ppermute(value, AXES, pairs)

    def bits(count):
        return [1 << place for place in range(count.bit_length() - 1)]

    def partial_sums(value):
        sums = []
        for masks in [(0, mask) for mask in bits(groups)] + [(mask, 0) for mask in bits(copies)]:
            value = value + swap(value, *masks)
            sums.append(value)
        return sums

    chips = groups

    def across(value, place):
        return swap(value, PAIR * (place // (groups // 2)), 2 * (place % (groups // 2)))

    def to_chips(pieces):
        return [pieces[0]] + [across(pieces[place], place) for place in range(1, chips)]

    def through(visit, sends):
        direct, relay = to_chips(sends[::2]), to_chips(sends[1::2])
        seen, direct = visit(direct)
        direct = to_chips(direct)
        relay = [after(part, seen) for part in relay]
        passed = visit(swap(jnp.concatenate(relay), 0, 1))
        return direct, [swap(after(part, *direct), 0, 1) for part in passed]

    def weave(direct, relay):
        return [part for pair in zip(direct, to_chips(relay)) for part in pair]

    ring = list(range(0, copies, 2)) + list(range(copies - 1, 0, -2))
    turns = [(1, step) for step in range(1, copies // 2 + 1)] + [(-1, step) for step in range(1, copies // 2)]

    def gather_ring(shard, due):
        got = [shard]
        for turn in (1, -1):
            held = shard
            pairs = [(ring[i], ring[(i + turn) % copies]) for i in range(copies)]
            for step in [step for way, step in turns if way == turn]:
                held = lax.ppermute(after(held, *due[step - 2 : step - 1]) if step > 1 else held, "dp", pairs)
                got.append(held)
        return got

    def ring_places():
        place = jnp.where(here_dp & 1 == 0, here_dp >> 1, copies - 1 - (here_dp >> 1))
        shift = jnp.array([0] + [turn * step for turn, step in turns], jnp.int32)
        place = (place - shift) & (copies - 1)
        return jnp.where(place < copies // 2, 2 * place, 2 * (copies - 1 - place) + 1).astype(jnp.int32)


    flat_routes = routes.reshape(-1)
    pair_count = length * top_count
    slot_count = sources * capacity
    route_hits = (flat_routes[:, None] == jnp.arange(expert_count, dtype=jnp.int32)[None, :]).astype(bf16)
    lower_ones = (
        lax.broadcasted_iota(jnp.int32, (pair_count, pair_count), 0)
        >= lax.broadcasted_iota(jnp.int32, (pair_count, pair_count), 1)
    ).astype(bf16)
    running = jnp.dot(lower_ones, route_hits, preferred_element_type=f32)
    pair_rank = jnp.sum((running - 1.0) * route_hits.astype(f32), axis=1).astype(jnp.int32)
    away = (flat_routes >> 1) ^ here_group
    chip = ((flat_routes & 1) ^ half) * (groups // 2) + (away >> 1)
    slots = ((chip * 2 + (away & 1)) * capacity + pair_rank).reshape(length, top_count)
    slots_t = slots.T

    resid = tokens.astype(f32)
    normed1 = norm_apply(resid, gain_attn).astype(bf16)
    columns = width // 2
    core_index = core.reshape(1).astype(jnp.int32)
    valid_rows = valid_mask.astype(f32)[:, None]
    counts = [jnp.broadcast_to(jnp.sum(valid_rows), (8, 128))]
    count_trades = [(0, mask) for mask in bits(groups)] + [(mask, 0) for mask in bits(copies)]

    def count_beside(before, value):
        if len(counts) > len(count_trades):
            return value
        counts.append(counts[-1] + swap(after(counts[-1], before), *count_trades[len(counts) - 1]))
        return after(value, counts[-1])

    shards = [
        lax.dynamic_slice_in_dim(part, core * columns, columns, 2)
        for part in (qkv_weight[:2], jnp.concatenate([qkv_weight[2:], out_weight[None]]))
    ]
    if copies > 8:
        mine = lax.all_gather(jnp.concatenate(shards), "dp", axis=1, tiled=True)
    else:
        mine = join(ring_places(), [gather_ring(shards[0], ()), gather_ring(shards[1], (slots_t, normed1))])
    other = count_beside(mine, swap(mine, 0, 1))
    qkv_rows = count_beside(other, project(core_index, normed1, mine, other, 3))
    offsets = offset_bias(position_bias_table)
    attended, probs = attention_forward(position_bias_table[:, bucket_far()], prefix, qkv_rows, offsets)
    middle, normed2, gates, *sends = route(
        core_index, count_beside(qkv_rows, attended), tokens, mine, other, gain_moe, router, routes, slots_t, 2 * chips, capacity
    )

    pick = half.reshape(1).astype(jnp.int32)
    hidden, slopes, rows_in = [], [], []

    def expert(pieces):
        one = not isinstance(pieces, list)
        pieces = [pieces] if one else pieces
        hidden_t, slope, rows_t, *results = expert_forward(pick, pieces, chips, w_in, w_out)
        hidden_t = count_beside(pieces[-1], hidden_t)
        for kept, value in zip((hidden, slopes, rows_in), (hidden_t, slope, rows_t)):
            kept.append(value)
        return results if one else (hidden_t, results)

    back = weave(*through(expert, sends))
    while len(counts) <= len(count_trades):
        back[0] = count_beside(back[0], back[0])
    valid_count = counts[-1][0, 0]
    scale = (total_tokens / valid_count).reshape(1, 1)
    output, grad_y, grad_logits, squares, *sends = combine(
        slots, slots_t, scale, back, middle, teacher, cotangent, valid_rows, gates, routes, expert_count
    )

    out_rows = inner // copies
    in_rows = width // copies
    far_bit = here_dp % 2
    slices = jnp.arange(rest, dtype=jnp.int32) * 4

    def picks(bit0):
        return jnp.concatenate([slices + ((half ^ other_half) * 2 + bit0) for other_half in (1, 0)]).astype(jnp.int32)

    sent, kept = picks(1 - far_bit), picks(far_bit)

    def add(left, right):
        return (left.astype(f32) + right.astype(f32)).astype(bf16)

    def fold(unit, bit, axis=0):
        unit = unit.reshape(unit.shape[:axis] + (2, unit.shape[axis] // 2) + unit.shape[axis + 1 :])
        away_part = lax.dynamic_index_in_dim(unit, 1 - bit, axis, keepdims=False)
        return away_part, lax.dynamic_index_in_dim(unit, bit, axis, keepdims=False)

    far_masks = list(reversed(bits(copies)[2:]))

    def near_add(got, keep):
        away_part, stay_part = fold(add(got, keep), (here_dp // far_masks[0]) % 2)
        return away_part, stay_part

    def far_trade(away_part):
        return swap(away_part, far_masks[0], 0)

    def finish(got, stay):
        unit = add(got, stay)
        for mask in far_masks[1:]:
            away_part, stay_part = fold(unit, (here_dp // mask) % 2)
            unit = add(swap(away_part, mask, 0), stay_part)
        return unit[0]

    plan_a, plan_b, plan_c = ((0, 0), (0, 1)), ((0, 2), (1, 0)), ((1, 1), (1, 2))
    plan_d, plan_e, plan_f = plan_a, plan_b, plan_c
    out_plans, in_plans = (plan_a, plan_b, plan_c), (plan_d, plan_e, plan_f)

    grad_rows, grad_pre, parts = [], [], []

    def expert_back(pieces):
        if isinstance(pieces, list):
            grad_pre_rows, grads, *results = expert_backward(pick, pieces, chips, w_in, w_out, slopes[0])
            grad_rows.append(grads)
            grad_pre.append(grad_pre_rows)
            return grad_pre_rows, results
        grad_rows.append(pieces)
        parts.extend(weight_part(sent, hidden, grad_rows, out_rows, out_plans, rest, width))
        parts[0] = swap(parts[0], 1, 0)
        pieces = after(pieces, parts[1])
        grad_pre_rows, _, *results = expert_backward(pick, [pieces], chips, w_in, w_out, slopes[1])
        grad_pre.append(grad_pre_rows)
        return results

    direct, relay = through(expert_back, sends)
    got_a, send_b, send_c = parts
    relay = [after(part, got_a) for part in relay]
    got_b = swap(after(send_b, relay[0]), 1, 0)
    back = weave(direct, relay)
    grad_rows, grad_pre = lax.optimization_barrier((grad_rows, grad_pre, relay))[:2]
    keep_a, keep_b, keep_c = weight_part(kept, hidden, grad_rows, out_rows, out_plans, rest, width)
    away_a, stay_a = near_add(got_a, keep_a)
    far_a = far_trade(away_a)
    send_d, send_e, send_f = weight_part(sent, rows_in, after(grad_pre, away_a), in_rows, in_plans, rest, inner // 2)
    back = [after(part, send_d) for part in back]
    got_c = swap(after(send_c, send_d), 1, 0)
    grad_middle, grad_attn_proj, grad_attended, gain_moe_parts = collect(
        core_index, slots, back, middle, gain_moe, grad_logits, router, grad_y, mine, other
    )
    away_b, stay_b = near_add(after(got_b, grad_attended), keep_b)
    got_d = swap(after(send_d, grad_attended), 1, 0)
    grad_attended, away_b = lax.optimization_barrier((grad_attended, away_b))
    grad_qkv_rows, bands = attention_backward(qkv_rows, grad_attended, probs)
    grad_qkv_rows, got_c, far_a = lax.optimization_barrier((grad_qkv_rows, got_c, far_a))
    done_a = finish(far_a, stay_a)

    away_c, stay_c = near_add(got_c, keep_c)
    far_c = far_trade(jnp.concatenate([away_b, away_c], axis=1))
    stay_c = jnp.concatenate([stay_b, stay_c], axis=1)
    *weights_away, stay_1, stay_2 = outer_halves(
        core_index, normed1, attended, after(grad_qkv_rows, away_c), grad_attn_proj
    )
    weights_away, got_d = lax.optimization_barrier((weights_away, got_d))
    got_e = swap(after(send_e, got_d), 1, 0)
    group_masks = bits(groups)[1:]
    dp_masks = bits(copies)

    def over_dp(total, mask, passed):
        axis = 1 + sorted([other for other in dp_masks if other not in passed], reverse=True).index(mask)
        bit = (here_dp // mask) % 2
        away_part = lax.dynamic_index_in_dim(total, 1 - bit, axis, keepdims=False)
        stay_part = lax.dynamic_index_in_dim(total, bit, axis, keepdims=False)
        return away_part, swap(away_part, mask, 0), stay_part

    weights_got = [swap(part, 0, 1) for part in weights_away]
    halves_sum = [
        add(got, stay).reshape(2, copies, in_rows, columns) for got, stay in zip(weights_got, (stay_1, stay_2))
    ]
    for mask in group_masks[:-1]:
        folded = [fold(part, (here_group // mask) % 2, 2) for part in halves_sum]
        halves_sum = [add(swap(away_part, 0, mask), stay_part) for away_part, stay_part in folded]
    folded = [fold(part, (here_group // group_masks[-1]) % 2, 2) for part in halves_sum]
    y_stay = jnp.concatenate([stay_part for _, stay_part in folded])
    y_away = jnp.concatenate([away_part for away_part, _ in folded])
    y_got = swap(y_away, 0, group_masks[-1])
    keep_d, keep_e, keep_f = weight_part(
        kept, rows_in, after(grad_pre, y_away), in_rows, in_plans, rest, inner // 2, 40
    )
    away_d, stay_d = near_add(got_d, keep_d)
    far_d = far_trade(away_d)
    away_e, stay_e = near_add(after(got_e, away_d), keep_e)
    done_c = finish(after(far_c, away_e), stay_c)
    total = add(after(y_got, away_e, far_c), y_stay)
    total = total.reshape((4,) + (2,) * len(dp_masks) + (-1, columns))


    small_trades = [(0, 1), (0, group_masks[0])] + [(mask, 0) for mask in dp_masks if mask != PAIR] + [(PAIR, 0)]
    small_trades += [(0, mask) for mask in group_masks[1:]]
    passed_masks = []
    for mask in dp_masks:
        gone, got, stay = over_dp(total, mask, passed_masks)
        passed_masks.append(mask)
        if len(passed_masks) == 1:
            grad_input, small = enter(
                core_index,
                after(grad_qkv_rows, gone),
                mine,
                other,
                tokens,
                gain_attn,
                grad_middle,
                gain_moe_parts,
                squares,
                normed2,
                grad_logits,
            )
            grad_table = table_gradient(after(bands, gone), position_bias_table.shape[1])
            flat = lax.dynamic_update_slice(small, grad_table.reshape(1, -1), (3, 0))
        for _ in range((0, 2, 1)[min(len(passed_masks), 3) - 1]):
            flat = flat + swap(after(flat, gone), *small_trades.pop(0))
        if len(passed_masks) == 1:
            far_e = far_trade(after(away_e, gone))
            got = after(got, far_d)
            got_f = swap(after(send_f, gone), 1, 0)
            done_e = finish(far_e, stay_e)
        elif mask == PAIR:
            got = after(got, far_e)
        elif len(passed_masks) == len(dp_masks):
            away_f, stay_f = near_add(after(got_f, stay), keep_f)
            far_f = far_trade(away_f)
            got = after(got, away_f)
            done_f = finish(far_f, stay_f)
        total = add(got, stay)
        if mask == PAIR:
            done_d = finish(after(far_d, total), stay_d)
            in_first = swap(done_d, PAIR, 0)
            out_theirs = swap(after(jnp.concatenate([done_a, done_c[:1]]), total), PAIR, 0)
        flat = after(flat, total)
    in_theirs = jnp.concatenate([in_first, swap(done_e[:1], PAIR, 0)])
    for mask in reversed(group_masks):
        bit = (here_group // mask) % 2
        other_part = swap(total, 0, mask)
        if mask == group_masks[-1]:
            other_part = after(other_part, out_theirs, in_first)
        total = jnp.concatenate([jnp.where(bit == 0, total, other_part), jnp.where(bit == 0, other_part, total)], axis=1)
        flat = flat + swap(flat, *small_trades.pop(0))
        total, flat = lax.optimization_barrier((total, flat))
    other_part = swap(total, 0, 1)
    for trade in small_trades:
        flat = flat + swap(flat, *trade)
    total = jnp.concatenate([jnp.where(core == 0, total, other_part), jnp.where(core == 0, other_part, total)], axis=2)
    weights_done = total.astype(f32)
    grad_qkv, grad_out_weight = weights_done[:3], weights_done[3]
    grad_gain_moe, grad_gain_attn, square_total = flat[0], flat[1], jnp.sum(flat[2])
    grad_table = flat[3, : grad_table.size].reshape(grad_table.shape)
    grad_router = flat[SMALL:].T

    out_mine, in_mine = done_c[1:], jnp.concatenate([done_e[1:], done_f])

    def both_experts(mine, theirs):
        mine, theirs = [part.reshape(-1, part.shape[-1]).astype(f32) for part in (mine, theirs)]
        return jnp.stack([jnp.where(half == 0, mine, theirs), jnp.where(half == 0, theirs, mine)])

    grad_w_out = both_experts(out_mine, out_theirs)
    grad_w_in = both_experts(in_mine, in_theirs)

    distill_loss = square_total / (width * valid_count)
    return (
        output.astype(bf16),
        distill_loss,
        grad_input,
        grad_qkv,
        grad_out_weight,
        grad_w_in,
        grad_w_out,
        grad_router,
        grad_table,
        grad_gain_attn,
        grad_gain_moe,
    )


def solution(mesh):
    rows = P(AXES, None)
    return jax.shard_map(
        on_device,
        mesh=mesh,
        in_specs=(
            rows,
            P(None, "dp", None),
            P("dp", None),
            P(),
            P(),
            P(),
            P(),
            P("expert", None, None),
            P("expert", None, None),
            rows,
            P(AXES),
            P(AXES),
            rows,
            rows,
        ),
        out_specs=(
            rows,
            P(),
            rows,
            P(None, "dp", None),
            P("dp", None),
            P("expert", "dp", None),
            P("expert", "dp", None),
            P(),
            P(),
            P(),
            P(),
        ),
        check_vma=False,
    )
```

```python
import math
import jax
import jax.numpy as jnp
from jax import lax
from jax.experimental import pallas as pl
from jax.experimental.pallas import tpu as pltpu
from jax.sharding import PartitionSpec as P

BLOCK = 128
THIRDS = 3
SMALL = 8
EPS = 1e-06
GELU_A = math.sqrt(2.0 / math.pi)
GELU_B = 0.044715
NT = (((1,), (1,)), ((), ()))
TN = (((0,), (0,)), ((), ()))
VMEM_BYTES = 56 * 1024 * 1024


def cost(micros):
    return pl.CostEstimate(flops=int(micros * 0.37e9), bytes_accessed=0, transcendentals=0)


def dot_f32(left, right, dims=(((1,), (0,)), ((), ()))):
    return lax.dot_general(left, right, dims, preferred_element_type=jnp.float32)


def assemble(rows, pieces):
    start = 0
    for piece in pieces:
        rows[pl.ds(start, piece.shape[0]), :] = piece[...]
        start += piece.shape[0]


def hand_out(total, outs):
    start = 0
    for out in outs:
        out[...] = total[pl.ds(start, out.shape[0]), :].astype(out.dtype)
        start += out.shape[0]


def whole(shape):
    return pl.BlockSpec(shape, lambda *step: (0,) * len(shape))


def expert_forward_kernel(pick, *refs, chunk, count):
    pieces, w_in, w_out = refs[:count], refs[count], refs[count + 1]
    hidden_t, slope, rows_t = refs[count + 2 : count + 5]
    outs, rows, total = refs[count + 5 : -2], refs[-2], refs[-1]
    step = pl.program_id(0)

    @pl.when(step == 0)
    def _():
        assemble(rows, pieces)
        total[...] = jnp.zeros_like(total)
        rows_t[...] = rows[...].T

    for start in range(0, rows.shape[0], chunk):
        part = pl.ds(start, chunk)
        pre = dot_f32(rows[part, :], w_in[0])
        square = pre * pre
        bend = jnp.tanh(pre * (GELU_A + (GELU_A * GELU_B) * square))
        half = 0.5 + 0.5 * bend
        act = (pre * half).astype(jnp.bfloat16)
        lift = pre * (0.5 * GELU_A + (1.5 * GELU_A * GELU_B) * square)
        slope[part, :] = (half + lift * (1.0 - bend * bend)).astype(jnp.bfloat16)
        hidden_t[:, part] = act.T
        total[part, :] += dot_f32(act, w_out[0])

    @pl.when(step == pl.num_programs(0) - 1)
    def _():
        hand_out(total, outs)


def expert_forward(pick, pieces, results, w_in, w_out, tile=768, chunk=320):
    many, width = sum(piece.shape[0] for piece in pieces), pieces[0].shape[1]
    inner = w_in.shape[2]
    bf16 = jnp.bfloat16
    return pl.pallas_call(
        lambda *refs: expert_forward_kernel(*refs, chunk=chunk, count=len(pieces)),
        grid_spec=pltpu.PrefetchScalarGridSpec(
            num_scalar_prefetch=1,
            grid=(inner // tile,),
            in_specs=[whole(piece.shape) for piece in pieces]
            + [
                pl.BlockSpec((1, width, tile), lambda f, pick: (pick[0], 0, f)),
                pl.BlockSpec((1, tile, width), lambda f, pick: (pick[0], f, 0)),
            ],
            out_specs=[
                pl.BlockSpec((tile, many), lambda f, pick: (f, 0)),
                pl.BlockSpec((many, tile), lambda f, pick: (0, f)),
                whole((width, many)),
            ]
            + [whole((many // results, width))] * results,
            scratch_shapes=[pltpu.VMEM((many, width), bf16), pltpu.VMEM((many, width), jnp.float32)],
        ),
        out_shape=[
            jax.ShapeDtypeStruct((inner, many), bf16),
            jax.ShapeDtypeStruct((many, inner), bf16),
            jax.ShapeDtypeStruct((width, many), bf16),
        ]
        + [jax.ShapeDtypeStruct((many // results, width), bf16)] * results,
        compiler_params=pltpu.CompilerParams(vmem_limit_bytes=VMEM_BYTES),
        cost_estimate=cost(13),
        name="expert_forward",
    )(pick, *pieces, w_in, w_out)


def expert_backward_kernel(pick, *refs, chunk, count):
    pieces, w_in, w_out, slope = refs[:count], refs[count], refs[count + 1], refs[count + 2]
    grad_pre, rows = refs[count + 3 : count + 5]
    outs, total = refs[count + 5 : -1], refs[-1]
    step = pl.program_id(0)

    @pl.when(step == 0)
    def _():
        assemble(rows, pieces)
        total[...] = jnp.zeros_like(total)

    for start in range(0, rows.shape[0], chunk):
        part = pl.ds(start, chunk)
        back = dot_f32(rows[part, :], w_out[0], NT) * slope[part, :].astype(jnp.float32)
        back = back.astype(jnp.bfloat16)
        grad_pre[part, :] = back
        total[part, :] += dot_f32(back, w_in[0], NT)

    @pl.when(step == pl.num_programs(0) - 1)
    def _():
        hand_out(total, outs)


def expert_backward(pick, pieces, results, w_in, w_out, slope, tile=768, chunk=640):
    many, width = sum(piece.shape[0] for piece in pieces), pieces[0].shape[1]
    inner = w_in.shape[2]
    bf16 = jnp.bfloat16
    return pl.pallas_call(
        lambda *refs: expert_backward_kernel(*refs, chunk=chunk, count=len(pieces)),
        grid_spec=pltpu.PrefetchScalarGridSpec(
            num_scalar_prefetch=1,
            grid=(inner // tile,),
            in_specs=[whole(piece.shape) for piece in pieces]
            + [
                pl.BlockSpec((1, width, tile), lambda f, pick: (pick[0], 0, f)),
                pl.BlockSpec((1, tile, width), lambda f, pick: (pick[0], f, 0)),
                pl.BlockSpec((many, tile), lambda f, pick: (0, f)),
            ],
            out_specs=[pl.BlockSpec((many, tile), lambda f, pick: (0, f)), whole((many, width))]
            + [whole((many // results, width))] * results,
            scratch_shapes=[pltpu.VMEM((many, width), jnp.float32)],
        ),
        out_shape=[jax.ShapeDtypeStruct((many, inner), bf16), jax.ShapeDtypeStruct((many, width), bf16)]
        + [jax.ShapeDtypeStruct((many // results, width), bf16)] * results,
        compiler_params=pltpu.CompilerParams(vmem_limit_bytes=VMEM_BYTES),
        cost_estimate=cost(11),
        name="expert_backward",
    )(pick, *pieces, w_in, w_out, slope)


def seen_blocks(row_block, blocks):
    return max(row_block + 1, blocks // 2)


def attention_forward_kernel(far, prefix, queries, keys, values, offsets, attended, probs, *, heads, blocks):
    pair = pl.program_id(0)
    lane = lax.broadcasted_iota(jnp.int32, queries.shape, 1)
    row = lax.broadcasted_iota(jnp.int32, (BLOCK, BLOCK), 0)
    col = lax.broadcasted_iota(jnp.int32, (BLOCK, BLOCK), 1)
    outs = []
    for head in range(2):
        line = jnp.broadcast_to(offsets[head : head + 1, :], (BLOCK, 4 * BLOCK))
        turned = pltpu.roll(line, 0, 1, stride=1, stride_axis=0)
        far_bias = far[pair * 2 + head]
        mine = (lane < heads) if head == 0 else (lane >= heads)
        query = jnp.where(mine, queries[...] * 0.125, 0.0).astype(jnp.bfloat16)
        score = dot_f32(query, keys[...], NT)
        strips = []
        for row_block in range(blocks):
            span = seen_blocks(row_block, blocks)
            pieces = []
            for key_block in range(span):
                piece = score[row_block * BLOCK : (row_block + 1) * BLOCK, key_block * BLOCK : (key_block + 1) * BLOCK]
                shift = key_block - row_block
                if shift < -1:
                    piece = piece + far_bias
                elif shift < 2:
                    piece = piece + turned[:, (2 + shift) * BLOCK : (3 + shift) * BLOCK]
                else:
                    raise ValueError(shift)
                if shift >= 0:
                    shown = col + key_block * BLOCK < prefix[0]
                    piece = jnp.where((shown | (col <= row)) if shift == 0 else shown, piece, -1e30)
                pieces.append(piece)
            peak = pieces[0]
            for piece in pieces[1:]:
                peak = jnp.maximum(peak, piece)
            peak = jnp.max(peak, axis=1, keepdims=True)
            pieces = [jnp.exp(piece - peak) for piece in pieces]
            mass = pieces[0]
            for piece in pieces[1:]:
                mass = mass + piece
            scale = 1.0 / jnp.sum(mass, axis=1, keepdims=True)
            pieces = [(piece * scale).astype(jnp.bfloat16) for piece in pieces]
            pieces += [jnp.zeros((BLOCK, BLOCK), jnp.bfloat16)] * (blocks - span)
            strips.append(jnp.concatenate(pieces, axis=1))
        weights = jnp.concatenate(strips, axis=0)
        probs[head] = weights
        outs.append(dot_f32(weights, values[...]))
    attended[...] = jnp.where(lane < heads, outs[0], outs[1]).astype(jnp.bfloat16)


def attention_forward(far, prefix, qkv_rows, offsets):
    length, width = qkv_rows.shape[1:]
    pairs = width // 128
    blocks = length // BLOCK
    return pl.pallas_call(
        lambda *refs: attention_forward_kernel(*refs, heads=64, blocks=blocks),
        grid_spec=pltpu.PrefetchScalarGridSpec(
            num_scalar_prefetch=2,
            grid=(pairs,),
            in_specs=[pl.BlockSpec((None, length, 128), lambda h, far, prefix, c=c: (c, 0, h)) for c in range(3)]
            + [pl.BlockSpec((None, 2, 4 * BLOCK), lambda h, far, prefix: (h, 0, 0))],
            out_specs=[
                pl.BlockSpec((length, 128), lambda h, far, prefix: (0, h)),
                pl.BlockSpec((2, length, length), lambda h, far, prefix: (h, 0, 0)),
            ],
        ),
        out_shape=[
            jax.ShapeDtypeStruct((length, width), jnp.bfloat16),
            jax.ShapeDtypeStruct((2 * pairs, length, length), jnp.bfloat16),
        ],
        compiler_params=pltpu.CompilerParams(vmem_limit_bytes=VMEM_BYTES),
        cost_estimate=cost(13),
        name="attention_forward",
    )(far, prefix, qkv_rows, qkv_rows, qkv_rows, offsets.reshape(pairs, 2, 4 * BLOCK))


def attention_backward_kernel(queries, keys, values, grads, probs, grad_rows, bands, *, heads, blocks):
    lane = lax.broadcasted_iota(jnp.int32, queries.shape, 1)
    query_t = (queries[...] * 0.125).astype(jnp.bfloat16).T
    grad_t = grads[...].T
    dq, dk, dv = [], [], []
    for head in range(2):
        mine = (lane < heads) if head == 0 else (lane >= heads)
        sums = [None] * 4
        grad = jnp.where(mine, grads[...], 0.0).astype(jnp.bfloat16)
        back = dot_f32(grad, values[...], NT)
        strips = []
        for row_block in range(blocks):
            span = seen_blocks(row_block, blocks)
            rows = slice(row_block * BLOCK, (row_block + 1) * BLOCK)
            soft = probs[head, pl.ds(row_block * BLOCK, BLOCK), pl.ds(0, span * BLOCK)].astype(jnp.float32)
            part = back[rows, : span * BLOCK]
            inner = jnp.sum(soft * part, axis=1, keepdims=True)
            score_grad = (soft * (part - inner)).astype(jnp.bfloat16)
            for key_block in range(span):
                band = max(key_block - row_block, -2)
                tile = score_grad[:, key_block * BLOCK : (key_block + 1) * BLOCK].astype(jnp.float32)
                sums[band + 2] = tile if sums[band + 2] is None else sums[band + 2] + tile
            if span < blocks:
                rest = jnp.zeros((BLOCK, (blocks - span) * BLOCK), jnp.bfloat16)
                score_grad = jnp.concatenate([score_grad, rest], axis=1)
            strips.append(score_grad)
        flow = jnp.concatenate(strips, axis=0)
        for band in range(4):
            bands[head, band] = sums[band]
        part = slice(head * heads, (head + 1) * heads)
        dq.append(dot_f32(flow, keys[...]) * 0.125)
        dk.append(dot_f32(query_t[part], flow))
        dv.append(dot_f32(grad_t[part], probs[head]))
    grad_rows[0] = jnp.where(lane < heads, dq[0], dq[1]).astype(jnp.bfloat16)
    grad_rows[1] = jnp.concatenate(dk, axis=0).T.astype(jnp.bfloat16)
    grad_rows[2] = jnp.concatenate(dv, axis=0).T.astype(jnp.bfloat16)


def attention_backward(qkv_rows, grads, probs):
    length, width = grads.shape
    pairs = width // 128
    blocks = length // BLOCK
    block = pl.BlockSpec((length, 128), lambda h: (0, h))
    of_three = [pl.BlockSpec((None, length, 128), lambda h, c=c: (c, 0, h)) for c in range(3)]
    return pl.pallas_call(
        lambda *refs: attention_backward_kernel(*refs, heads=64, blocks=blocks),
        grid=(pairs,),
        in_specs=[*of_three, block, pl.BlockSpec((2, length, length), lambda h: (h, 0, 0))],
        out_specs=[pl.BlockSpec((3, length, 128), lambda h: (0, 0, h)), pl.BlockSpec((2, 4, BLOCK, BLOCK), lambda h: (h, 0, 0, 0))],
        out_shape=[jax.ShapeDtypeStruct((3, length, width), jnp.bfloat16)]
        + [jax.ShapeDtypeStruct((2 * pairs, 4, BLOCK, BLOCK), jnp.float32)],
        compiler_params=pltpu.CompilerParams(vmem_limit_bytes=VMEM_BYTES),
        cost_estimate=cost(4),
        name="attention_backward",
    )(qkv_rows, qkv_rows, qkv_rows, grads, probs)


def pieces_left(lefts, plans, many):
    part = lefts[0][0].shape[0] // THIRDS
    return jnp.concatenate(
        [
            jnp.concatenate([ref[pl.ds(third * part, part), :] for ref in lefts[group * many + k]], axis=1)
            for plan in plans
            for group, third in plan
            for k in range(many)
        ]
    )


def put_pieces(result, outs):
    place = 0
    for out in outs:
        many, pieces, part = out.shape[:3]
        for piece in range(pieces):
            for k in range(many):
                out[k, piece] = result[place : place + part]
                place += part


def weight_part_kernel(picks, *refs, count, plans, many):
    lefts, rights, outs = refs[: 2 * count], refs[2 * count : 2 * count + 2], refs[2 * count + 2 :]
    left = pieces_left(list(zip(lefts[:count], lefts[count:])), plans, many)
    right = jnp.concatenate([ref[...] for ref in rights], axis=0)
    put_pieces(dot_f32(left, right).astype(jnp.bfloat16), outs)


def weight_part_plain(picks, lefts, rights, rows, plans, many):
    left, right = jnp.concatenate(lefts, axis=1), jnp.concatenate(rights, axis=0)
    depth, width = right.shape
    part = rows // THIRDS
    result = jnp.take(left.reshape(-1, rows, depth), picks, axis=0)
    result = jnp.einsum("srd,dw->srw", result, right, preferred_element_type=jnp.float32).astype(jnp.bfloat16)
    result = result.reshape(-1, many, THIRDS, part, width)
    return [jnp.stack([result[group, :, third] for group, third in plan], axis=1) for plan in plans]


def weight_part(picks, lefts, rights, rows, plans, many, tile, micros=4):
    depth, width = rights[0].shape
    count, part = picks.shape[0], rows // THIRDS
    if part % 16:
        return weight_part_plain(picks, lefts, rights, rows, plans, many)
    return pl.pallas_call(
        lambda *refs: weight_part_kernel(*refs, count=count, plans=plans, many=many),
        grid_spec=pltpu.PrefetchScalarGridSpec(
            num_scalar_prefetch=1,
            grid=(width // tile,),
            in_specs=[pl.BlockSpec((rows, depth), lambda i, picks, k=k: (picks[k], 0)) for k in range(count)] * 2
            + [pl.BlockSpec((depth, tile), lambda i, picks: (0, i))] * 2,
            out_specs=[pl.BlockSpec((many, len(plan), part, tile), lambda i, picks: (0, 0, 0, i)) for plan in plans],
        ),
        out_shape=[jax.ShapeDtypeStruct((many, len(plan), part, width), jnp.bfloat16) for plan in plans],
        compiler_params=pltpu.CompilerParams(vmem_limit_bytes=VMEM_BYTES),
        cost_estimate=cost(micros),
        name="weight_part",
    )(picks, *([lefts[0]] * count), *([lefts[1]] * count), *rights)


def hot_columns(slots, first, count):
    rows = first + lax.broadcasted_iota(jnp.int32, (count, slots.shape[1]), 0)
    return (rows == slots).astype(jnp.bfloat16)


def halves(core, mine, other):
    return jnp.where(core == 0, mine, other), jnp.where(core == 0, other, mine)


def join_kernel(places, *refs):
    pieces, out = refs[:-1], refs[-1]
    rows = pieces[0].shape[1]
    count = pieces[0].shape[0]
    for chunk in range(out.shape[0] // count):
        for step in range(len(pieces) * count // out.shape[0]):
            piece = pieces[chunk * (len(pieces) * count // out.shape[0]) + step]
            start = pl.multiple_of(places[step] * rows, rows)
            out[pl.ds(chunk * count, count), pl.ds(start, rows), :] = piece[...]


def join(places, chunks):
    count, rows, columns = chunks[0][0].shape
    steps = len(chunks[0])
    return pl.pallas_call(
        join_kernel,
        in_specs=[pl.BlockSpec(memory_space=pltpu.SMEM)] + [pl.BlockSpec(memory_space=pltpu.VMEM)] * (steps * len(chunks)),
        out_shape=jax.ShapeDtypeStruct((count * len(chunks), steps * rows, columns), jnp.bfloat16),
        compiler_params=pltpu.CompilerParams(vmem_limit_bytes=VMEM_BYTES),
        cost_estimate=cost(3),
        name="join",
    )(places, *[piece for chunk in chunks for piece in chunk])


def project_kernel(core, rows, mine, other, result):
    half = mine.shape[1]
    first, second = halves(core[0], mine[...], other[...])
    result[:, :half] = dot_f32(rows[...], first).astype(jnp.bfloat16)
    result[:, half:] = dot_f32(rows[...], second).astype(jnp.bfloat16)


def project(core, rows, mine, other, used):
    width, half = mine.shape[1:]
    length = rows.shape[0]
    return pl.pallas_call(
        project_kernel,
        grid_spec=pltpu.PrefetchScalarGridSpec(
            num_scalar_prefetch=1,
            grid=(used,),
            in_specs=[
                whole((length, width)),
                pl.BlockSpec((None, width, half), lambda i, core: (i, 0, 0)),
                pl.BlockSpec((None, width, half), lambda i, core: (i, 0, 0)),
            ],
            out_specs=pl.BlockSpec((None, length, 2 * half), lambda i, core: (i, 0, 0)),
        ),
        out_shape=jax.ShapeDtypeStruct((used, length, 2 * half), jnp.bfloat16),
        compiler_params=pltpu.CompilerParams(vmem_limit_bytes=VMEM_BYTES),
        cost_estimate=cost(4),
        name="project",
    )(core, rows, mine, other)


def route_kernel(core, attended, tokens, mine, other, gain, router, routes, slots, middle, normed, gates, *outs):
    f32 = jnp.float32
    first, second = halves(core[0], mine[...], other[...])
    rows = attended[...]
    moved = jnp.concatenate([dot_f32(rows, first), dot_f32(rows, second)], axis=1)
    value = tokens[...].astype(f32) + moved
    middle[...] = value
    low = (value * lax.rsqrt(jnp.mean(value * value, axis=1, keepdims=True) + EPS) * gain[...]).astype(jnp.bfloat16)
    normed[...] = low
    start = 0
    for first_out, second_out in zip(outs[::2], outs[1::2]):
        size = first_out.shape[0]
        hot = hot_columns(slots[0:1, :], start, 2 * size) + hot_columns(slots[1:2, :], start, 2 * size)
        part = dot_f32(hot, low).astype(jnp.bfloat16)
        first_out[...] = part[:size]
        second_out[...] = part[size:]
        start += 2 * size
    logits = dot_f32(low, router[...])
    soft = jnp.exp(logits - jnp.max(logits, axis=1, keepdims=True))
    soft = soft / jnp.sum(soft, axis=1, keepdims=True)
    expert = lax.broadcasted_iota(jnp.int32, soft.shape, 1)
    chosen = [jnp.sum(jnp.where(expert == routes[:, k : k + 1], soft, 0.0), axis=1, keepdims=True) for k in range(2)]
    for k in range(2):
        gates[:, k : k + 1] = chosen[k] / (chosen[0] + chosen[1])


def route(core, attended, tokens, mine, other, gain, router, routes, slots, pieces, count):
    length, width = tokens.shape
    last, half = mine.shape[0] - 1, mine.shape[2]
    f32, bf16 = jnp.float32, jnp.bfloat16
    weight = pl.BlockSpec((None, width, half), lambda i, core: (last, 0, 0))
    shapes = [((length, width), f32), ((length, width), bf16), ((length, 2), f32)] + [((count, width), bf16)] * pieces
    return pl.pallas_call(
        route_kernel,
        grid_spec=pltpu.PrefetchScalarGridSpec(
            num_scalar_prefetch=1,
            grid=(1,),
            in_specs=[whole((length, width)), whole((length, width)), weight, weight, whole((1, width)), whole(router.shape), whole(routes.shape), whole(slots.shape)],
            out_specs=[whole(shape) for shape, _ in shapes],
        ),
        out_shape=[jax.ShapeDtypeStruct(shape, kind) for shape, kind in shapes],
        compiler_params=pltpu.CompilerParams(vmem_limit_bytes=VMEM_BYTES),
        cost_estimate=cost(6),
        name="route",
    )(core, attended, tokens, mine, other, gain.reshape(1, -1), router, routes, slots)


def hot_route(slots, k, count):
    cols = lax.broadcasted_iota(jnp.int32, (slots.shape[0], count), 1)
    return cols == slots[:, k : k + 1]


def combine_kernel(*refs, count):
    slots, slots_t, scale = refs[:3]
    pieces = refs[3 : 3 + count]
    middle, teacher, cotangent, valid, gates, routes = refs[3 + count : 9 + count]
    output, grad_y, grad_logits, square = refs[9 + count : 13 + count]
    sends, rows = refs[13 + count : 13 + 2 * count], refs[13 + 2 * count]
    f32, bf16 = jnp.float32, jnp.bfloat16
    assemble(rows, pieces)
    table = rows[...]
    picked = [dot_f32(hot_route(slots, k, rows.shape[0]).astype(bf16), table) for k in range(2)]
    result = middle[...] + (gates[:, 0:1] * picked[0] + gates[:, 1:2] * picked[1])
    output[...] = result.astype(bf16)
    misfit = valid[...] * (result - teacher[...].astype(f32))
    square[...] = jnp.sum((misfit * misfit).reshape(-1, 8, misfit.shape[1]), axis=0)
    grad = cotangent[...].astype(f32) + misfit * scale[0, 0]
    grad_y[...] = grad
    steep = [jnp.sum(grad * picked[k], axis=1, keepdims=True) for k in range(2)]
    slack = gates[:, 0:1] * steep[0] + gates[:, 1:2] * steep[1]
    expert = lax.broadcasted_iota(jnp.int32, grad_logits.shape, 1)
    turn = [jnp.where(expert == routes[:, k : k + 1], gates[:, k : k + 1] * (steep[k] - slack), 0.0) for k in range(2)]
    grad_logits[...] = (turn[0] + turn[1]).astype(bf16)
    scaled = [(gates[:, k : k + 1] * grad).astype(bf16) for k in range(2)]
    start = 0
    for first, second in zip(sends[::2], sends[1::2]):
        size = first.shape[0]
        part = [dot_f32(hot_columns(slots_t[k : k + 1, :], start, 2 * size), scaled[k]) for k in range(2)]
        part = (part[0] + part[1]).astype(bf16)
        first[...] = part[:size]
        second[...] = part[size:]
        start += 2 * size


def combine(slots, slots_t, scale, pieces, middle, teacher, cotangent, valid, gates, routes, experts):
    length, width = middle.shape
    count = len(pieces)
    f32, bf16 = jnp.float32, jnp.bfloat16
    return pl.pallas_call(
        lambda *refs: combine_kernel(*refs, count=count),
        in_specs=[pl.BlockSpec(memory_space=pltpu.VMEM)] * 2
        + [pl.BlockSpec(memory_space=pltpu.SMEM)]
        + [pl.BlockSpec(memory_space=pltpu.VMEM)] * (6 + count),
        out_shape=[
            jax.ShapeDtypeStruct((length, width), bf16),
            jax.ShapeDtypeStruct((length, width), f32),
            jax.ShapeDtypeStruct((length, experts), bf16),
            jax.ShapeDtypeStruct((8, width), f32),
        ]
        + [jax.ShapeDtypeStruct(piece.shape, bf16) for piece in pieces],
        scratch_shapes=[pltpu.VMEM((sum(piece.shape[0] for piece in pieces), width), bf16)],
        compiler_params=pltpu.CompilerParams(vmem_limit_bytes=VMEM_BYTES),
        cost_estimate=cost(8),
        name="combine",
    )(slots, slots_t, scale, *pieces, middle, teacher, cotangent, valid, gates, routes)


def norm_back(value, gain, grad):
    root = lax.rsqrt(jnp.mean(value * value, axis=1, keepdims=True) + EPS)
    normed = value * root
    scaled = grad * gain
    inner = jnp.mean(scaled * normed, axis=1, keepdims=True)
    return root * (scaled - normed * inner), jnp.sum((grad * normed).reshape(-1, 8, value.shape[1]), axis=0)


def collect_kernel(core, *refs, count):
    slots, pieces = refs[0], refs[1 : 1 + count]
    middle, gain, grad_logits, router, grad_y, mine, other = refs[1 + count : 8 + count]
    grad_middle, rounded, grad_attended, grad_gain, rows = refs[8 + count :]
    assemble(rows, pieces)
    hot = (hot_route(slots, 0, rows.shape[0]) | hot_route(slots, 1, rows.shape[0])).astype(jnp.bfloat16)
    grad = dot_f32(grad_logits[...], router[...], NT) + dot_f32(hot, rows[...])
    turned, grad_gain[...] = norm_back(middle[...], gain[...], grad)
    result = grad_y[...] + turned
    grad_middle[...] = result
    low = result.astype(jnp.bfloat16)
    rounded[...] = low
    first, second = halves(core[0], mine[...], other[...])
    half = first.shape[1]
    grad_attended[...] = (dot_f32(low[:, :half], first, NT) + dot_f32(low[:, half:], second, NT)).astype(jnp.bfloat16)


def collect(core, slots, pieces, middle, gain, grad_logits, router, grad_y, mine, other):
    length, width = middle.shape
    last, half = mine.shape[0] - 1, mine.shape[2]
    f32, bf16 = jnp.float32, jnp.bfloat16
    weight = pl.BlockSpec((None, width, half), lambda i, core: (last, 0, 0))
    plain = [slots, *pieces, middle, gain.reshape(1, -1), grad_logits, router, grad_y]
    shapes = [((length, width), f32), ((length, width), bf16), ((length, width), bf16), ((8, width), f32)]
    return pl.pallas_call(
        lambda *refs: collect_kernel(*refs, count=len(pieces)),
        grid_spec=pltpu.PrefetchScalarGridSpec(
            num_scalar_prefetch=1,
            grid=(1,),
            in_specs=[whole(array.shape) for array in plain] + [weight, weight],
            out_specs=[whole(shape) for shape, _ in shapes],
            scratch_shapes=[pltpu.VMEM((sum(piece.shape[0] for piece in pieces), width), bf16)],
        ),
        out_shape=[jax.ShapeDtypeStruct(shape, kind) for shape, kind in shapes],
        compiler_params=pltpu.CompilerParams(vmem_limit_bytes=VMEM_BYTES),
        cost_estimate=cost(8),
        name="collect",
    )(core, *plain, mine, other)


def outer_halves_kernel(core, normed, attended, rights, last, *refs, count):
    aways, stays, normed_t, attended_t = refs[:2], refs[2:4], refs[4], refs[5]
    step = pl.program_id(0)

    @pl.when(step == 0)
    def _():
        normed_t[...] = normed[...].T
        attended_t[...] = attended[...].T

    for place in range(count + 1):

        @pl.when(step == place)
        def _():
            result = dot_f32(normed_t[...], rights[...]) if place < count else dot_f32(attended_t[...], last[...])
            result = result.astype(jnp.bfloat16)
            half = result.shape[1] // 2
            away, stay = aways[place // 2], stays[place // 2]
            slot = place % 2

            @pl.when(core[0] == 0)
            def _():
                stay[slot] = result[:, :half]
                away[slot] = result[:, half:]

            @pl.when(core[0] != 0)
            def _():
                away[slot] = result[:, :half]
                stay[slot] = result[:, half:]


def outer_halves(core, normed, attended, rights, last):
    length, width = normed.shape
    count, half = rights.shape[0], width // 2
    shape = jax.ShapeDtypeStruct((2, width, half), jnp.bfloat16)
    return pl.pallas_call(
        lambda *refs: outer_halves_kernel(*refs, count=count),
        grid_spec=pltpu.PrefetchScalarGridSpec(
            num_scalar_prefetch=1,
            grid=(count + 1,),
            in_specs=[
                whole((length, width)),
                whole((length, width)),
                pl.BlockSpec((None, length, width), lambda i, core: (jnp.minimum(i, count - 1), 0, 0)),
                whole((length, width)),
            ],
            out_specs=[whole(shape.shape)] * 4,
            scratch_shapes=[pltpu.VMEM((width, length), jnp.bfloat16)] * 2,
        ),
        out_shape=[shape] * 4,
        compiler_params=pltpu.CompilerParams(vmem_limit_bytes=VMEM_BYTES),
        cost_estimate=cost(2),
        name="outer_halves",
    )(core, normed, attended, rights, last)


def enter_kernel(
    core, grads, mine, other, tokens, gain, grad_middle, moe_parts, squares, normed, grad_logits, grad_input, small, total
):
    step = pl.program_id(0)
    first, second = halves(core[0], mine[...], other[...])
    half = first.shape[1]
    rows = grads[...]
    part = dot_f32(rows[:, :half], first, NT) + dot_f32(rows[:, half:], second, NT)

    @pl.when(step == 0)
    def _():
        total[...] = part

    @pl.when(step > 0)
    def _():
        total[...] += part

    @pl.when(step == pl.num_programs(0) - 1)
    def _():
        turned, gain_parts = norm_back(tokens[...].astype(jnp.float32), gain[...], total[...])
        grad_input[...] = grad_middle[...] + turned
        sums = [jnp.sum(part, axis=0, keepdims=True) for part in (moe_parts[...], gain_parts, squares[...])]
        sums.append(jnp.zeros((SMALL - len(sums), gain.shape[1]), jnp.float32))
        small[pl.ds(0, SMALL), :] = jnp.concatenate(sums)
        small[pl.ds(SMALL, grad_logits.shape[1]), :] = dot_f32(grad_logits[...], normed[...], TN)


def enter(core, grads, mine, other, tokens, gain, grad_middle, moe_parts, squares, normed, grad_logits):
    length, width = tokens.shape
    count, half, experts = grads.shape[0], mine.shape[2], grad_logits.shape[1]
    weight = pl.BlockSpec((None, width, half), lambda i, core: (i, 0, 0))
    plain = [tokens, gain.reshape(1, -1), grad_middle, moe_parts, squares, normed, grad_logits]
    shapes = [(length, width), (SMALL + experts, width)]
    return pl.pallas_call(
        enter_kernel,
        grid_spec=pltpu.PrefetchScalarGridSpec(
            num_scalar_prefetch=1,
            grid=(count,),
            in_specs=[pl.BlockSpec((None, length, width), lambda i, core: (i, 0, 0)), weight, weight]
            + [whole(array.shape) for array in plain],
            out_specs=[whole(shape) for shape in shapes],
            scratch_shapes=[pltpu.VMEM((length, width), jnp.float32)],
        ),
        out_shape=[jax.ShapeDtypeStruct(shape, jnp.float32) for shape in shapes],
        compiler_params=pltpu.CompilerParams(vmem_limit_bytes=VMEM_BYTES),
        cost_estimate=cost(6),
        name="enter",
    )(core, grads, mine, other, *plain)


BOUNDS = (12, 16, 23, 32, 46, 64, 91)
TOP_PRECISION = lax.Precision.HIGHEST
AXES = ("dp", "expert")
PAIR = 2


def after(value, *others):
    return lax.optimization_barrier((value, *others))[0] if others else value


def bucket_index(offset):
    distance = jnp.abs(offset)
    far_bucket = 8 + sum([(distance >= level).astype(jnp.int32) for level in BOUNDS])
    near_bucket = jnp.where(distance < 8, distance, far_bucket)
    return jnp.where(offset > 0, 16, 0) + near_bucket


def norm_apply(inputs, gain_vec):
    return inputs * lax.rsqrt(jnp.mean(inputs * inputs, axis=-1, keepdims=True) + EPS) * gain_vec


def tile_offsets(query_block, key_block):
    rows = query_block * BLOCK + lax.broadcasted_iota(jnp.int32, (BLOCK, BLOCK), 0)
    cols = key_block * BLOCK + lax.broadcasted_iota(jnp.int32, (BLOCK, BLOCK), 1)
    return rows, cols


def offset_bias(table):
    offsets = jnp.arange(4 * BLOCK, dtype=jnp.int32) - 2 * BLOCK
    hot = (bucket_index(offsets)[None] == jnp.arange(table.shape[1], dtype=jnp.int32)[:, None]).astype(jnp.float32)
    return jnp.dot(table, hot, precision=TOP_PRECISION)


def table_gradient(bands, buckets):
    rows, cols = tile_offsets(0, 0)
    ids = [jnp.full((BLOCK, BLOCK), bucket_far(), jnp.int32)]
    ids += [bucket_index(shift * BLOCK + cols - rows) for shift in (-1, 0, 1)]
    hot = (jnp.stack(ids)[..., None] == jnp.arange(buckets, dtype=jnp.int32)).astype(jnp.float32)
    return jnp.einsum("hdxy,dxyb->hb", bands, hot, precision=TOP_PRECISION)


def bucket_far():
    return 8 + len(BOUNDS)


def on_device(
    tokens,
    qkv_weight,
    out_weight,
    position_bias_table,
    gain_attn,
    gain_moe,
    router,
    w_in,
    w_out,
    routes,
    prefix,
    valid_mask,
    teacher,
    cotangent,
):
    length, width = tokens.shape
    bf16, f32 = jnp.bfloat16, jnp.float32
    expert_count = router.shape[1]
    top_count = routes.shape[1]
    groups = lax.axis_size("expert")
    copies = lax.axis_size("dp")
    inner = w_in.shape[2]
    capacity = 5 * length * top_count // (4 * expert_count)
    total_tokens = length * copies * groups
    sources = 2 * groups
    blocks = length // BLOCK
    here_dp, here_group = lax.axis_index("dp"), lax.axis_index("expert")
    half = (here_dp >> 1) & 1
    core = here_group & 1
    rest = copies // 4

    def swap(value, dp_mask, group_mask):
        pairs = [
            (i, ((i // groups) ^ dp_mask) * groups + ((i % groups) ^ group_mask))
            for i in range(copies * groups)
        ]
        return lax.ppermute(value, AXES, pairs)

    def bits(count):
        return [1 << place for place in range(count.bit_length() - 1)]

    def partial_sums(value):
        sums = []
        for masks in [(0, mask) for mask in bits(groups)] + [(mask, 0) for mask in bits(copies)]:
            value = value + swap(value, *masks)
            sums.append(value)
        return sums

    chips = groups

    def across(value, place):
        return swap(value, PAIR * (place // (groups // 2)), 2 * (place % (groups // 2)))

    def to_chips(pieces):
        return [pieces[0]] + [across(pieces[place], place) for place in range(1, chips)]

    def through(visit, sends):
        direct, relay = to_chips(sends[::2]), to_chips(sends[1::2])
        seen, direct = visit(direct)
        direct = to_chips(direct)
        relay = [after(part, seen) for part in relay]
        passed = visit(swap(jnp.concatenate(relay), 0, 1))
        return direct, [swap(after(part, *direct), 0, 1) for part in passed]

    def weave(direct, relay):
        return [part for pair in zip(direct, to_chips(relay)) for part in pair]

    ring = list(range(0, copies, 2)) + list(range(copies - 1, 0, -2))
    turns = [(1, step) for step in range(1, copies // 2 + 1)] + [(-1, step) for step in range(1, copies // 2)]

    def gather_ring(shard, due):
        got = [shard]
        for turn in (1, -1):
            held = shard
            pairs = [(ring[i], ring[(i + turn) % copies]) for i in range(copies)]
            for step in [step for way, step in turns if way == turn]:
                held = lax.ppermute(after(held, *due[step - 2 : step - 1]) if step > 1 else held, "dp", pairs)
                got.append(held)
        return got

    def ring_places():
        place = jnp.where(here_dp & 1 == 0, here_dp >> 1, copies - 1 - (here_dp >> 1))
        shift = jnp.array([0] + [turn * step for turn, step in turns], jnp.int32)
        place = (place - shift) & (copies - 1)
        return jnp.where(place < copies // 2, 2 * place, 2 * (copies - 1 - place) + 1).astype(jnp.int32)


    flat_routes = routes.reshape(-1)
    pair_count = length * top_count
    slot_count = sources * capacity
    route_hits = (flat_routes[:, None] == jnp.arange(expert_count, dtype=jnp.int32)[None, :]).astype(bf16)
    lower_ones = (
        lax.broadcasted_iota(jnp.int32, (pair_count, pair_count), 0)
        >= lax.broadcasted_iota(jnp.int32, (pair_count, pair_count), 1)
    ).astype(bf16)
    running = jnp.dot(lower_ones, route_hits, preferred_element_type=f32)
    pair_rank = jnp.sum((running - 1.0) * route_hits.astype(f32), axis=1).astype(jnp.int32)
    away = (flat_routes >> 1) ^ here_group
    chip = ((flat_routes & 1) ^ half) * (groups // 2) + (away >> 1)
    slots = ((chip * 2 + (away & 1)) * capacity + pair_rank).reshape(length, top_count)
    slots_t = slots.T

    resid = tokens.astype(f32)
    normed1 = norm_apply(resid, gain_attn).astype(bf16)
    columns = width // 2
    core_index = core.reshape(1).astype(jnp.int32)
    valid_rows = valid_mask.astype(f32)[:, None]
    counts = [jnp.broadcast_to(jnp.sum(valid_rows), (8, 128))]
    count_trades = [(0, mask) for mask in bits(groups)] + [(mask, 0) for mask in bits(copies)]

    def count_beside(before, value):
        if len(counts) > len(count_trades):
            return value
        counts.append(counts[-1] + swap(after(counts[-1], before), *count_trades[len(counts) - 1]))
        return after(value, counts[-1])

    shards = [
        lax.dynamic_slice_in_dim(part, core * columns, columns, 2)
        for part in (qkv_weight[:2], jnp.concatenate([qkv_weight[2:], out_weight[None]]))
    ]
    if copies > 8:
        mine = lax.all_gather(jnp.concatenate(shards), "dp", axis=1, tiled=True)
    else:
        mine = join(ring_places(), [gather_ring(shards[0], ()), gather_ring(shards[1], (slots_t, normed1))])
    other = count_beside(mine, swap(mine, 0, 1))
    qkv_rows = count_beside(other, project(core_index, normed1, mine, other, 3))
    offsets = offset_bias(position_bias_table)
    attended, probs = attention_forward(position_bias_table[:, bucket_far()], prefix, qkv_rows, offsets)
    middle, normed2, gates, *sends = route(
        core_index, count_beside(qkv_rows, attended), tokens, mine, other, gain_moe, router, routes, slots_t, 2 * chips, capacity
    )

    pick = half.reshape(1).astype(jnp.int32)
    hidden, slopes, rows_in = [], [], []

    def expert(pieces):
        one = not isinstance(pieces, list)
        pieces = [pieces] if one else pieces
        hidden_t, slope, rows_t, *results = expert_forward(pick, pieces, chips, w_in, w_out)
        hidden_t = count_beside(pieces[-1], hidden_t)
        for kept, value in zip((hidden, slopes, rows_in), (hidden_t, slope, rows_t)):
            kept.append(value)
        return results if one else (hidden_t, results)

    back = weave(*through(expert, sends))
    while len(counts) <= len(count_trades):
        back[0] = count_beside(back[0], back[0])
    valid_count = counts[-1][0, 0]
    scale = (total_tokens / valid_count).reshape(1, 1)
    output, grad_y, grad_logits, squares, *sends = combine(
        slots, slots_t, scale, back, middle, teacher, cotangent, valid_rows, gates, routes, expert_count
    )

    out_rows = inner // copies
    in_rows = width // copies
    far_bit = here_dp % 2
    slices = jnp.arange(rest, dtype=jnp.int32) * 4

    def picks(bit0):
        return jnp.concatenate([slices + ((half ^ other_half) * 2 + bit0) for other_half in (1, 0)]).astype(jnp.int32)

    sent, kept = picks(1 - far_bit), picks(far_bit)

    def add(left, right):
        return (left.astype(f32) + right.astype(f32)).astype(bf16)

    def fold(unit, bit, axis=0):
        unit = unit.reshape(unit.shape[:axis] + (2, unit.shape[axis] // 2) + unit.shape[axis + 1 :])
        away_part = lax.dynamic_index_in_dim(unit, 1 - bit, axis, keepdims=False)
        return away_part, lax.dynamic_index_in_dim(unit, bit, axis, keepdims=False)

    far_masks = list(reversed(bits(copies)[2:]))

    def near_add(got, keep):
        away_part, stay_part = fold(add(got, keep), (here_dp // far_masks[0]) % 2)
        return away_part, stay_part

    def far_trade(away_part):
        return swap(away_part, far_masks[0], 0)

    def finish(got, stay):
        unit = add(got, stay)
        for mask in far_masks[1:]:
            away_part, stay_part = fold(unit, (here_dp // mask) % 2)
            unit = add(swap(away_part, mask, 0), stay_part)
        return unit[0]

    plan_a, plan_b, plan_c = ((0, 0), (0, 1)), ((0, 2), (1, 0)), ((1, 1), (1, 2))
    plan_d, plan_e, plan_f = plan_a, plan_b, plan_c
    out_plans, in_plans = (plan_a, plan_b, plan_c), (plan_d, plan_e, plan_f)

    grad_rows, grad_pre, parts = [], [], []

    def expert_back(pieces):
        if isinstance(pieces, list):
            grad_pre_rows, grads, *results = expert_backward(pick, pieces, chips, w_in, w_out, slopes[0])
            grad_rows.append(grads)
            grad_pre.append(grad_pre_rows)
            return grad_pre_rows, results
        grad_rows.append(pieces)
        parts.extend(weight_part(sent, hidden, grad_rows, out_rows, out_plans, rest, width))
        parts[0] = swap(parts[0], 1, 0)
        pieces = after(pieces, parts[1])
        grad_pre_rows, _, *results = expert_backward(pick, [pieces], chips, w_in, w_out, slopes[1])
        grad_pre.append(grad_pre_rows)
        return results

    direct, relay = through(expert_back, sends)
    got_a, send_b, send_c = parts
    relay = [after(part, got_a) for part in relay]
    got_b = swap(after(send_b, relay[0]), 1, 0)
    back = weave(direct, relay)
    grad_rows, grad_pre = lax.optimization_barrier((grad_rows, grad_pre, relay))[:2]
    keep_a, keep_b, keep_c = weight_part(kept, hidden, grad_rows, out_rows, out_plans, rest, width)
    away_a, stay_a = near_add(got_a, keep_a)
    far_a = far_trade(away_a)
    send_d, send_e, send_f = weight_part(sent, rows_in, after(grad_pre, away_a), in_rows, in_plans, rest, inner // 2)
    back = [after(part, send_d) for part in back]
    got_c = swap(after(send_c, send_d), 1, 0)
    grad_middle, grad_attn_proj, grad_attended, gain_moe_parts = collect(
        core_index, slots, back, middle, gain_moe, grad_logits, router, grad_y, mine, other
    )
    away_b, stay_b = near_add(after(got_b, grad_attended), keep_b)
    got_d = swap(after(send_d, grad_attended), 1, 0)
    grad_attended, away_b = lax.optimization_barrier((grad_attended, away_b))
    grad_qkv_rows, bands = attention_backward(qkv_rows, grad_attended, probs)
    grad_qkv_rows, got_c, far_a = lax.optimization_barrier((grad_qkv_rows, got_c, far_a))
    done_a = finish(far_a, stay_a)

    away_c, stay_c = near_add(got_c, keep_c)
    far_c = far_trade(jnp.concatenate([away_b, away_c], axis=1))
    stay_c = jnp.concatenate([stay_b, stay_c], axis=1)
    *weights_away, stay_1, stay_2 = outer_halves(
        core_index, normed1, attended, after(grad_qkv_rows, away_c), grad_attn_proj
    )
    weights_away, got_d = lax.optimization_barrier((weights_away, got_d))
    got_e = swap(after(send_e, got_d), 1, 0)
    group_masks = bits(groups)[1:]
    dp_masks = bits(copies)

    def over_dp(total, mask, passed):
        axis = 1 + sorted([other for other in dp_masks if other not in passed], reverse=True).index(mask)
        bit = (here_dp // mask) % 2
        away_part = lax.dynamic_index_in_dim(total, 1 - bit, axis, keepdims=False)
        stay_part = lax.dynamic_index_in_dim(total, bit, axis, keepdims=False)
        return away_part, swap(away_part, mask, 0), stay_part

    weights_got = [swap(part, 0, 1) for part in weights_away]
    halves_sum = [
        add(got, stay).reshape(2, copies, in_rows, columns) for got, stay in zip(weights_got, (stay_1, stay_2))
    ]
    for mask in group_masks[:-1]:
        folded = [fold(part, (here_group // mask) % 2, 2) for part in halves_sum]
        halves_sum = [add(swap(away_part, 0, mask), stay_part) for away_part, stay_part in folded]
    folded = [fold(part, (here_group // group_masks[-1]) % 2, 2) for part in halves_sum]
    y_stay = jnp.concatenate([stay_part for _, stay_part in folded])
    y_away = jnp.concatenate([away_part for away_part, _ in folded])
    y_got = swap(y_away, 0, group_masks[-1])
    keep_d, keep_e, keep_f = weight_part(
        kept, rows_in, after(grad_pre, y_away), in_rows, in_plans, rest, inner // 2, 40
    )
    away_d, stay_d = near_add(got_d, keep_d)
    far_d = far_trade(after(away_d, far_c))
    away_e, stay_e = near_add(after(got_e, away_d), keep_e)
    done_c = finish(after(far_c, away_e), stay_c)
    total = add(after(y_got, away_e), y_stay)
    total = total.reshape((4,) + (2,) * len(dp_masks) + (-1, columns))


    small_trades = [(0, 1), (0, group_masks[0])] + [(mask, 0) for mask in reversed(dp_masks) if mask != PAIR] + [(PAIR, 0)]
    small_trades += [(0, mask) for mask in group_masks[1:]]
    passed_masks = []
    for mask in dp_masks:
        gone, got, stay = over_dp(total, mask, passed_masks)
        passed_masks.append(mask)
        if len(passed_masks) == 1:
            grad_input, small = enter(
                core_index,
                after(grad_qkv_rows, gone),
                mine,
                other,
                tokens,
                gain_attn,
                grad_middle,
                gain_moe_parts,
                squares,
                normed2,
                grad_logits,
            )
            grad_table = table_gradient(after(bands, gone), position_bias_table.shape[1])
            flat = lax.dynamic_update_slice(small, grad_table.reshape(1, -1), (3, 0))
        for _ in range((0, 2, 1)[min(len(passed_masks), 3) - 1]):
            flat = flat + swap(after(flat, gone), *small_trades.pop(0))
        if len(passed_masks) == 1:
            far_e = far_trade(after(away_e, small))
            got_f = swap(after(send_f, gone), 1, 0)
        elif mask == PAIR:
            got = after(got, far_d)
        elif len(passed_masks) == len(dp_masks):
            away_f, stay_f = near_add(after(got_f, stay), keep_f)
            far_f = far_trade(away_f)
            far_e = after(far_e, gone)
            done_e = finish(far_e, stay_e)
            got = after(got, away_f, in_first, far_e)
            done_f = finish(far_f, stay_f)
        total = add(got, stay)
        if mask == PAIR:
            done_d = finish(after(far_d, total), stay_d)
            in_first = swap(done_d, PAIR, 0)
            out_theirs = swap(after(jnp.concatenate([done_a, done_c[:1]]), total), PAIR, 0)
        flat = after(flat, total)
    in_theirs = jnp.concatenate([in_first, swap(done_e[:1], PAIR, 0)])
    for mask in reversed(group_masks):
        bit = (here_group // mask) % 2
        other_part = swap(total, 0, mask)
        if mask == group_masks[-1]:
            other_part = after(other_part, out_theirs, in_first)
        total = jnp.concatenate([jnp.where(bit == 0, total, other_part), jnp.where(bit == 0, other_part, total)], axis=1)
        flat = flat + swap(flat, *small_trades.pop(0))
        total, flat = lax.optimization_barrier((total, flat))
    other_part = swap(total, 0, 1)
    for trade in small_trades:
        flat = flat + swap(flat, *trade)
    total = jnp.concatenate([jnp.where(core == 0, total, other_part), jnp.where(core == 0, other_part, total)], axis=2)
    weights_done = total.astype(f32)
    grad_qkv, grad_out_weight = weights_done[:3], weights_done[3]
    grad_gain_moe, grad_gain_attn, square_total = flat[0], flat[1], jnp.sum(flat[2])
    grad_table = flat[3, : grad_table.size].reshape(grad_table.shape)
    grad_router = flat[SMALL:].T

    out_mine, in_mine = done_c[1:], jnp.concatenate([done_e[1:], done_f])

    def both_experts(mine, theirs):
        mine, theirs = [part.reshape(-1, part.shape[-1]).astype(f32) for part in (mine, theirs)]
        return jnp.stack([jnp.where(half == 0, mine, theirs), jnp.where(half == 0, theirs, mine)])

    grad_w_out = both_experts(out_mine, out_theirs)
    grad_w_in = both_experts(in_mine, in_theirs)

    distill_loss = square_total / (width * valid_count)
    return (
        output.astype(bf16),
        distill_loss,
        grad_input,
        grad_qkv,
        grad_out_weight,
        grad_w_in,
        grad_w_out,
        grad_router,
        grad_table,
        grad_gain_attn,
        grad_gain_moe,
    )


def solution(mesh):
    rows = P(AXES, None)
    return jax.shard_map(
        on_device,
        mesh=mesh,
        in_specs=(
            rows,
            P(None, "dp", None),
            P("dp", None),
            P(),
            P(),
            P(),
            P(),
            P("expert", None, None),
            P("expert", None, None),
            rows,
            P(AXES),
            P(AXES),
            rows,
            rows,
        ),
        out_specs=(
            rows,
            P(),
            rows,
            P(None, "dp", None),
            P("dp", None),
            P("expert", "dp", None),
            P("expert", "dp", None),
            P(),
            P(),
            P(),
            P(),
        ),
        check_vma=False,
    )
```

```python
import math
import jax
import jax.numpy as jnp
from jax import lax
from jax.experimental import pallas as pl
from jax.experimental.pallas import tpu as pltpu
from jax.sharding import PartitionSpec as P

BLOCK = 128
THIRDS = 3
SMALL = 8
EPS = 1e-06
GELU_A = math.sqrt(2.0 / math.pi)
GELU_B = 0.044715
NT = (((1,), (1,)), ((), ()))
TN = (((0,), (0,)), ((), ()))
VMEM_BYTES = 56 * 1024 * 1024


def cost(micros):
    return pl.CostEstimate(flops=int(micros * 0.37e9), bytes_accessed=0, transcendentals=0)


def dot_f32(left, right, dims=(((1,), (0,)), ((), ()))):
    return lax.dot_general(left, right, dims, preferred_element_type=jnp.float32)


def assemble(rows, pieces):
    start = 0
    for piece in pieces:
        rows[pl.ds(start, piece.shape[0]), :] = piece[...]
        start += piece.shape[0]


def hand_out(total, outs):
    start = 0
    for out in outs:
        out[...] = total[pl.ds(start, out.shape[0]), :].astype(out.dtype)
        start += out.shape[0]


def whole(shape):
    return pl.BlockSpec(shape, lambda *step: (0,) * len(shape))


def expert_forward_kernel(pick, *refs, chunk, count):
    pieces, w_in, w_out = refs[:count], refs[count], refs[count + 1]
    hidden_t, slope, rows_t = refs[count + 2 : count + 5]
    outs, rows, total = refs[count + 5 : -2], refs[-2], refs[-1]
    step = pl.program_id(0)

    @pl.when(step == 0)
    def _():
        assemble(rows, pieces)
        total[...] = jnp.zeros_like(total)
        rows_t[...] = rows[...].T

    for start in range(0, rows.shape[0], chunk):
        part = pl.ds(start, chunk)
        pre = dot_f32(rows[part, :], w_in[0])
        square = pre * pre
        bend = jnp.tanh(pre * (GELU_A + (GELU_A * GELU_B) * square))
        half = 0.5 + 0.5 * bend
        act = (pre * half).astype(jnp.bfloat16)
        lift = pre * (0.5 * GELU_A + (1.5 * GELU_A * GELU_B) * square)
        slope[part, :] = (half + lift * (1.0 - bend * bend)).astype(jnp.bfloat16)
        hidden_t[:, part] = act.T
        total[part, :] += dot_f32(act, w_out[0])

    @pl.when(step == pl.num_programs(0) - 1)
    def _():
        hand_out(total, outs)


def expert_forward(pick, pieces, results, w_in, w_out, tile=768, chunk=320):
    many, width = sum(piece.shape[0] for piece in pieces), pieces[0].shape[1]
    inner = w_in.shape[2]
    bf16 = jnp.bfloat16
    return pl.pallas_call(
        lambda *refs: expert_forward_kernel(*refs, chunk=chunk, count=len(pieces)),
        grid_spec=pltpu.PrefetchScalarGridSpec(
            num_scalar_prefetch=1,
            grid=(inner // tile,),
            in_specs=[whole(piece.shape) for piece in pieces]
            + [
                pl.BlockSpec((1, width, tile), lambda f, pick: (pick[0], 0, f)),
                pl.BlockSpec((1, tile, width), lambda f, pick: (pick[0], f, 0)),
            ],
            out_specs=[
                pl.BlockSpec((tile, many), lambda f, pick: (f, 0)),
                pl.BlockSpec((many, tile), lambda f, pick: (0, f)),
                whole((width, many)),
            ]
            + [whole((many // results, width))] * results,
            scratch_shapes=[pltpu.VMEM((many, width), bf16), pltpu.VMEM((many, width), jnp.float32)],
        ),
        out_shape=[
            jax.ShapeDtypeStruct((inner, many), bf16),
            jax.ShapeDtypeStruct((many, inner), bf16),
            jax.ShapeDtypeStruct((width, many), bf16),
        ]
        + [jax.ShapeDtypeStruct((many // results, width), bf16)] * results,
        compiler_params=pltpu.CompilerParams(vmem_limit_bytes=VMEM_BYTES),
        cost_estimate=cost(13),
        name="expert_forward",
    )(pick, *pieces, w_in, w_out)


def expert_backward_kernel(pick, *refs, chunk, count):
    pieces, w_in, w_out, slope = refs[:count], refs[count], refs[count + 1], refs[count + 2]
    grad_pre, rows = refs[count + 3 : count + 5]
    outs, total = refs[count + 5 : -1], refs[-1]
    step = pl.program_id(0)

    @pl.when(step == 0)
    def _():
        assemble(rows, pieces)
        total[...] = jnp.zeros_like(total)

    for start in range(0, rows.shape[0], chunk):
        part = pl.ds(start, chunk)
        back = dot_f32(rows[part, :], w_out[0], NT) * slope[part, :].astype(jnp.float32)
        back = back.astype(jnp.bfloat16)
        grad_pre[part, :] = back
        total[part, :] += dot_f32(back, w_in[0], NT)

    @pl.when(step == pl.num_programs(0) - 1)
    def _():
        hand_out(total, outs)


def expert_backward(pick, pieces, results, w_in, w_out, slope, tile=768, chunk=640):
    many, width = sum(piece.shape[0] for piece in pieces), pieces[0].shape[1]
    inner = w_in.shape[2]
    bf16 = jnp.bfloat16
    return pl.pallas_call(
        lambda *refs: expert_backward_kernel(*refs, chunk=chunk, count=len(pieces)),
        grid_spec=pltpu.PrefetchScalarGridSpec(
            num_scalar_prefetch=1,
            grid=(inner // tile,),
            in_specs=[whole(piece.shape) for piece in pieces]
            + [
                pl.BlockSpec((1, width, tile), lambda f, pick: (pick[0], 0, f)),
                pl.BlockSpec((1, tile, width), lambda f, pick: (pick[0], f, 0)),
                pl.BlockSpec((many, tile), lambda f, pick: (0, f)),
            ],
            out_specs=[pl.BlockSpec((many, tile), lambda f, pick: (0, f)), whole((many, width))]
            + [whole((many // results, width))] * results,
            scratch_shapes=[pltpu.VMEM((many, width), jnp.float32)],
        ),
        out_shape=[jax.ShapeDtypeStruct((many, inner), bf16), jax.ShapeDtypeStruct((many, width), bf16)]
        + [jax.ShapeDtypeStruct((many // results, width), bf16)] * results,
        compiler_params=pltpu.CompilerParams(vmem_limit_bytes=VMEM_BYTES),
        cost_estimate=cost(11),
        name="expert_backward",
    )(pick, *pieces, w_in, w_out, slope)


def seen_blocks(row_block, blocks):
    return max(row_block + 1, blocks // 2)


def attention_forward_kernel(far, prefix, queries, keys, values, offsets, attended, probs, *, heads, blocks):
    pair = pl.program_id(0)
    lane = lax.broadcasted_iota(jnp.int32, queries.shape, 1)
    row = lax.broadcasted_iota(jnp.int32, (BLOCK, BLOCK), 0)
    col = lax.broadcasted_iota(jnp.int32, (BLOCK, BLOCK), 1)
    outs = []
    for head in range(2):
        line = jnp.broadcast_to(offsets[head : head + 1, :], (BLOCK, 4 * BLOCK))
        turned = pltpu.roll(line, 0, 1, stride=1, stride_axis=0)
        far_bias = far[pair * 2 + head]
        mine = (lane < heads) if head == 0 else (lane >= heads)
        query = jnp.where(mine, queries[...] * 0.125, 0.0).astype(jnp.bfloat16)
        score = dot_f32(query, keys[...], NT)
        strips = []
        for row_block in range(blocks):
            span = seen_blocks(row_block, blocks)
            pieces = []
            for key_block in range(span):
                piece = score[row_block * BLOCK : (row_block + 1) * BLOCK, key_block * BLOCK : (key_block + 1) * BLOCK]
                shift = key_block - row_block
                if shift < -1:
                    piece = piece + far_bias
                elif shift < 2:
                    piece = piece + turned[:, (2 + shift) * BLOCK : (3 + shift) * BLOCK]
                else:
                    raise ValueError(shift)
                if shift >= 0:
                    shown = col + key_block * BLOCK < prefix[0]
                    piece = jnp.where((shown | (col <= row)) if shift == 0 else shown, piece, -1e30)
                pieces.append(piece)
            peak = pieces[0]
            for piece in pieces[1:]:
                peak = jnp.maximum(peak, piece)
            peak = jnp.max(peak, axis=1, keepdims=True)
            pieces = [jnp.exp(piece - peak) for piece in pieces]
            mass = pieces[0]
            for piece in pieces[1:]:
                mass = mass + piece
            scale = 1.0 / jnp.sum(mass, axis=1, keepdims=True)
            pieces = [(piece * scale).astype(jnp.bfloat16) for piece in pieces]
            pieces += [jnp.zeros((BLOCK, BLOCK), jnp.bfloat16)] * (blocks - span)
            strips.append(jnp.concatenate(pieces, axis=1))
        weights = jnp.concatenate(strips, axis=0)
        probs[head] = weights
        outs.append(dot_f32(weights, values[...]))
    attended[...] = jnp.where(lane < heads, outs[0], outs[1]).astype(jnp.bfloat16)


def attention_forward(far, prefix, qkv_rows, offsets):
    length, width = qkv_rows.shape[1:]
    pairs = width // 128
    blocks = length // BLOCK
    return pl.pallas_call(
        lambda *refs: attention_forward_kernel(*refs, heads=64, blocks=blocks),
        grid_spec=pltpu.PrefetchScalarGridSpec(
            num_scalar_prefetch=2,
            grid=(pairs,),
            in_specs=[pl.BlockSpec((None, length, 128), lambda h, far, prefix, c=c: (c, 0, h)) for c in range(3)]
            + [pl.BlockSpec((None, 2, 4 * BLOCK), lambda h, far, prefix: (h, 0, 0))],
            out_specs=[
                pl.BlockSpec((length, 128), lambda h, far, prefix: (0, h)),
                pl.BlockSpec((2, length, length), lambda h, far, prefix: (h, 0, 0)),
            ],
        ),
        out_shape=[
            jax.ShapeDtypeStruct((length, width), jnp.bfloat16),
            jax.ShapeDtypeStruct((2 * pairs, length, length), jnp.bfloat16),
        ],
        compiler_params=pltpu.CompilerParams(vmem_limit_bytes=VMEM_BYTES),
        cost_estimate=cost(13),
        name="attention_forward",
    )(far, prefix, qkv_rows, qkv_rows, qkv_rows, offsets.reshape(pairs, 2, 4 * BLOCK))


def attention_backward_kernel(queries, keys, values, grads, probs, grad_rows, bands, *, heads, blocks):
    lane = lax.broadcasted_iota(jnp.int32, queries.shape, 1)
    query_t = (queries[...] * 0.125).astype(jnp.bfloat16).T
    grad_t = grads[...].T
    dq, dk, dv = [], [], []
    for head in range(2):
        mine = (lane < heads) if head == 0 else (lane >= heads)
        sums = [None] * 4
        grad = jnp.where(mine, grads[...], 0.0).astype(jnp.bfloat16)
        back = dot_f32(grad, values[...], NT)
        strips = []
        for row_block in range(blocks):
            span = seen_blocks(row_block, blocks)
            rows = slice(row_block * BLOCK, (row_block + 1) * BLOCK)
            soft = probs[head, pl.ds(row_block * BLOCK, BLOCK), pl.ds(0, span * BLOCK)].astype(jnp.float32)
            part = back[rows, : span * BLOCK]
            inner = jnp.sum(soft * part, axis=1, keepdims=True)
            score_grad = (soft * (part - inner)).astype(jnp.bfloat16)
            for key_block in range(span):
                band = max(key_block - row_block, -2)
                tile = score_grad[:, key_block * BLOCK : (key_block + 1) * BLOCK].astype(jnp.float32)
                sums[band + 2] = tile if sums[band + 2] is None else sums[band + 2] + tile
            if span < blocks:
                rest = jnp.zeros((BLOCK, (blocks - span) * BLOCK), jnp.bfloat16)
                score_grad = jnp.concatenate([score_grad, rest], axis=1)
            strips.append(score_grad)
        flow = jnp.concatenate(strips, axis=0)
        for band in range(4):
            bands[head, band] = sums[band]
        part = slice(head * heads, (head + 1) * heads)
        dq.append(dot_f32(flow, keys[...]) * 0.125)
        dk.append(dot_f32(query_t[part], flow))
        dv.append(dot_f32(grad_t[part], probs[head]))
    grad_rows[0] = jnp.where(lane < heads, dq[0], dq[1]).astype(jnp.bfloat16)
    grad_rows[1] = jnp.concatenate(dk, axis=0).T.astype(jnp.bfloat16)
    grad_rows[2] = jnp.concatenate(dv, axis=0).T.astype(jnp.bfloat16)


def attention_backward(qkv_rows, grads, probs):
    length, width = grads.shape
    pairs = width // 128
    blocks = length // BLOCK
    block = pl.BlockSpec((length, 128), lambda h: (0, h))
    of_three = [pl.BlockSpec((None, length, 128), lambda h, c=c: (c, 0, h)) for c in range(3)]
    return pl.pallas_call(
        lambda *refs: attention_backward_kernel(*refs, heads=64, blocks=blocks),
        grid=(pairs,),
        in_specs=[*of_three, block, pl.BlockSpec((2, length, length), lambda h: (h, 0, 0))],
        out_specs=[pl.BlockSpec((3, length, 128), lambda h: (0, 0, h)), pl.BlockSpec((2, 4, BLOCK, BLOCK), lambda h: (h, 0, 0, 0))],
        out_shape=[jax.ShapeDtypeStruct((3, length, width), jnp.bfloat16)]
        + [jax.ShapeDtypeStruct((2 * pairs, 4, BLOCK, BLOCK), jnp.float32)],
        compiler_params=pltpu.CompilerParams(vmem_limit_bytes=VMEM_BYTES),
        cost_estimate=cost(4),
        name="attention_backward",
    )(qkv_rows, qkv_rows, qkv_rows, grads, probs)


def pieces_left(lefts, plans, many):
    part = lefts[0][0].shape[0] // THIRDS
    return jnp.concatenate(
        [
            jnp.concatenate([ref[pl.ds(third * part, part), :] for ref in lefts[group * many + k]], axis=1)
            for plan in plans
            for group, third in plan
            for k in range(many)
        ]
    )


def put_pieces(result, outs):
    place = 0
    for out in outs:
        many, pieces, part = out.shape[:3]
        for piece in range(pieces):
            for k in range(many):
                out[k, piece] = result[place : place + part]
                place += part


def weight_part_kernel(picks, *refs, count, plans, many):
    lefts, rights, outs = refs[: 2 * count], refs[2 * count : 2 * count + 2], refs[2 * count + 2 :]
    left = pieces_left(list(zip(lefts[:count], lefts[count:])), plans, many)
    right = jnp.concatenate([ref[...] for ref in rights], axis=0)
    put_pieces(dot_f32(left, right).astype(jnp.bfloat16), outs)


def weight_part_plain(picks, lefts, rights, rows, plans, many):
    left, right = jnp.concatenate(lefts, axis=1), jnp.concatenate(rights, axis=0)
    depth, width = right.shape
    part = rows // THIRDS
    result = jnp.take(left.reshape(-1, rows, depth), picks, axis=0)
    result = jnp.einsum("srd,dw->srw", result, right, preferred_element_type=jnp.float32).astype(jnp.bfloat16)
    result = result.reshape(-1, many, THIRDS, part, width)
    return [jnp.stack([result[group, :, third] for group, third in plan], axis=1) for plan in plans]


def weight_part(picks, lefts, rights, rows, plans, many, tile, micros=4):
    depth, width = rights[0].shape
    count, part = picks.shape[0], rows // THIRDS
    if part % 16:
        return weight_part_plain(picks, lefts, rights, rows, plans, many)
    return pl.pallas_call(
        lambda *refs: weight_part_kernel(*refs, count=count, plans=plans, many=many),
        grid_spec=pltpu.PrefetchScalarGridSpec(
            num_scalar_prefetch=1,
            grid=(width // tile,),
            in_specs=[pl.BlockSpec((rows, depth), lambda i, picks, k=k: (picks[k], 0)) for k in range(count)] * 2
            + [pl.BlockSpec((depth, tile), lambda i, picks: (0, i))] * 2,
            out_specs=[pl.BlockSpec((many, len(plan), part, tile), lambda i, picks: (0, 0, 0, i)) for plan in plans],
        ),
        out_shape=[jax.ShapeDtypeStruct((many, len(plan), part, width), jnp.bfloat16) for plan in plans],
        compiler_params=pltpu.CompilerParams(vmem_limit_bytes=VMEM_BYTES),
        cost_estimate=cost(micros),
        name="weight_part",
    )(picks, *([lefts[0]] * count), *([lefts[1]] * count), *rights)


def hot_columns(slots, first, count):
    rows = first + lax.broadcasted_iota(jnp.int32, (count, slots.shape[1]), 0)
    return (rows == slots).astype(jnp.bfloat16)


def halves(core, mine, other):
    return jnp.where(core == 0, mine, other), jnp.where(core == 0, other, mine)


def join_kernel(places, *refs):
    pieces, out = refs[:-1], refs[-1]
    rows = pieces[0].shape[1]
    count = pieces[0].shape[0]
    for chunk in range(out.shape[0] // count):
        for step in range(len(pieces) * count // out.shape[0]):
            piece = pieces[chunk * (len(pieces) * count // out.shape[0]) + step]
            start = pl.multiple_of(places[step] * rows, rows)
            out[pl.ds(chunk * count, count), pl.ds(start, rows), :] = piece[...]


def join(places, chunks):
    count, rows, columns = chunks[0][0].shape
    steps = len(chunks[0])
    return pl.pallas_call(
        join_kernel,
        in_specs=[pl.BlockSpec(memory_space=pltpu.SMEM)] + [pl.BlockSpec(memory_space=pltpu.VMEM)] * (steps * len(chunks)),
        out_shape=jax.ShapeDtypeStruct((count * len(chunks), steps * rows, columns), jnp.bfloat16),
        compiler_params=pltpu.CompilerParams(vmem_limit_bytes=VMEM_BYTES),
        cost_estimate=cost(3),
        name="join",
    )(places, *[piece for chunk in chunks for piece in chunk])


def project_kernel(core, rows, mine, other, result):
    half = mine.shape[1]
    first, second = halves(core[0], mine[...], other[...])
    result[:, :half] = dot_f32(rows[...], first).astype(jnp.bfloat16)
    result[:, half:] = dot_f32(rows[...], second).astype(jnp.bfloat16)


def project(core, rows, mine, other, used):
    width, half = mine.shape[1:]
    length = rows.shape[0]
    return pl.pallas_call(
        project_kernel,
        grid_spec=pltpu.PrefetchScalarGridSpec(
            num_scalar_prefetch=1,
            grid=(used,),
            in_specs=[
                whole((length, width)),
                pl.BlockSpec((None, width, half), lambda i, core: (i, 0, 0)),
                pl.BlockSpec((None, width, half), lambda i, core: (i, 0, 0)),
            ],
            out_specs=pl.BlockSpec((None, length, 2 * half), lambda i, core: (i, 0, 0)),
        ),
        out_shape=jax.ShapeDtypeStruct((used, length, 2 * half), jnp.bfloat16),
        compiler_params=pltpu.CompilerParams(vmem_limit_bytes=VMEM_BYTES),
        cost_estimate=cost(4),
        name="project",
    )(core, rows, mine, other)


def route_kernel(core, attended, tokens, mine, other, gain, router, routes, slots, middle, normed, gates, *outs):
    f32 = jnp.float32
    first, second = halves(core[0], mine[...], other[...])
    rows = attended[...]
    moved = jnp.concatenate([dot_f32(rows, first), dot_f32(rows, second)], axis=1)
    value = tokens[...].astype(f32) + moved
    middle[...] = value
    low = (value * lax.rsqrt(jnp.mean(value * value, axis=1, keepdims=True) + EPS) * gain[...]).astype(jnp.bfloat16)
    normed[...] = low
    start = 0
    for first_out, second_out in zip(outs[::2], outs[1::2]):
        size = first_out.shape[0]
        hot = hot_columns(slots[0:1, :], start, 2 * size) + hot_columns(slots[1:2, :], start, 2 * size)
        part = dot_f32(hot, low).astype(jnp.bfloat16)
        first_out[...] = part[:size]
        second_out[...] = part[size:]
        start += 2 * size
    logits = dot_f32(low, router[...])
    soft = jnp.exp(logits - jnp.max(logits, axis=1, keepdims=True))
    soft = soft / jnp.sum(soft, axis=1, keepdims=True)
    expert = lax.broadcasted_iota(jnp.int32, soft.shape, 1)
    chosen = [jnp.sum(jnp.where(expert == routes[:, k : k + 1], soft, 0.0), axis=1, keepdims=True) for k in range(2)]
    for k in range(2):
        gates[:, k : k + 1] = chosen[k] / (chosen[0] + chosen[1])


def route(core, attended, tokens, mine, other, gain, router, routes, slots, pieces, count):
    length, width = tokens.shape
    last, half = mine.shape[0] - 1, mine.shape[2]
    f32, bf16 = jnp.float32, jnp.bfloat16
    weight = pl.BlockSpec((None, width, half), lambda i, core: (last, 0, 0))
    shapes = [((length, width), f32), ((length, width), bf16), ((length, 2), f32)] + [((count, width), bf16)] * pieces
    return pl.pallas_call(
        route_kernel,
        grid_spec=pltpu.PrefetchScalarGridSpec(
            num_scalar_prefetch=1,
            grid=(1,),
            in_specs=[whole((length, width)), whole((length, width)), weight, weight, whole((1, width)), whole(router.shape), whole(routes.shape), whole(slots.shape)],
            out_specs=[whole(shape) for shape, _ in shapes],
        ),
        out_shape=[jax.ShapeDtypeStruct(shape, kind) for shape, kind in shapes],
        compiler_params=pltpu.CompilerParams(vmem_limit_bytes=VMEM_BYTES),
        cost_estimate=cost(6),
        name="route",
    )(core, attended, tokens, mine, other, gain.reshape(1, -1), router, routes, slots)


def hot_route(slots, k, count):
    cols = lax.broadcasted_iota(jnp.int32, (slots.shape[0], count), 1)
    return cols == slots[:, k : k + 1]


def combine_kernel(*refs, count):
    slots, slots_t, scale = refs[:3]
    pieces = refs[3 : 3 + count]
    middle, teacher, cotangent, valid, gates, routes = refs[3 + count : 9 + count]
    output, grad_y, grad_logits, square = refs[9 + count : 13 + count]
    sends, rows = refs[13 + count : 13 + 2 * count], refs[13 + 2 * count]
    f32, bf16 = jnp.float32, jnp.bfloat16
    assemble(rows, pieces)
    table = rows[...]
    picked = [dot_f32(hot_route(slots, k, rows.shape[0]).astype(bf16), table) for k in range(2)]
    result = middle[...] + (gates[:, 0:1] * picked[0] + gates[:, 1:2] * picked[1])
    output[...] = result.astype(bf16)
    misfit = valid[...] * (result - teacher[...].astype(f32))
    square[...] = jnp.sum((misfit * misfit).reshape(-1, 8, misfit.shape[1]), axis=0)
    grad = cotangent[...].astype(f32) + misfit * scale[0, 0]
    grad_y[...] = grad
    steep = [jnp.sum(grad * picked[k], axis=1, keepdims=True) for k in range(2)]
    slack = gates[:, 0:1] * steep[0] + gates[:, 1:2] * steep[1]
    expert = lax.broadcasted_iota(jnp.int32, grad_logits.shape, 1)
    turn = [jnp.where(expert == routes[:, k : k + 1], gates[:, k : k + 1] * (steep[k] - slack), 0.0) for k in range(2)]
    grad_logits[...] = (turn[0] + turn[1]).astype(bf16)
    scaled = [(gates[:, k : k + 1] * grad).astype(bf16) for k in range(2)]
    start = 0
    for first, second in zip(sends[::2], sends[1::2]):
        size = first.shape[0]
        part = [dot_f32(hot_columns(slots_t[k : k + 1, :], start, 2 * size), scaled[k]) for k in range(2)]
        part = (part[0] + part[1]).astype(bf16)
        first[...] = part[:size]
        second[...] = part[size:]
        start += 2 * size


def combine(slots, slots_t, scale, pieces, middle, teacher, cotangent, valid, gates, routes, experts):
    length, width = middle.shape
    count = len(pieces)
    f32, bf16 = jnp.float32, jnp.bfloat16
    return pl.pallas_call(
        lambda *refs: combine_kernel(*refs, count=count),
        in_specs=[pl.BlockSpec(memory_space=pltpu.VMEM)] * 2
        + [pl.BlockSpec(memory_space=pltpu.SMEM)]
        + [pl.BlockSpec(memory_space=pltpu.VMEM)] * (6 + count),
        out_shape=[
            jax.ShapeDtypeStruct((length, width), bf16),
            jax.ShapeDtypeStruct((length, width), f32),
            jax.ShapeDtypeStruct((length, experts), bf16),
            jax.ShapeDtypeStruct((8, width), f32),
        ]
        + [jax.ShapeDtypeStruct(piece.shape, bf16) for piece in pieces],
        scratch_shapes=[pltpu.VMEM((sum(piece.shape[0] for piece in pieces), width), bf16)],
        compiler_params=pltpu.CompilerParams(vmem_limit_bytes=VMEM_BYTES),
        cost_estimate=cost(8),
        name="combine",
    )(slots, slots_t, scale, *pieces, middle, teacher, cotangent, valid, gates, routes)


def norm_back(value, gain, grad):
    root = lax.rsqrt(jnp.mean(value * value, axis=1, keepdims=True) + EPS)
    normed = value * root
    scaled = grad * gain
    inner = jnp.mean(scaled * normed, axis=1, keepdims=True)
    return root * (scaled - normed * inner), jnp.sum((grad * normed).reshape(-1, 8, value.shape[1]), axis=0)


def collect_kernel(core, *refs, count):
    slots, pieces = refs[0], refs[1 : 1 + count]
    middle, gain, grad_logits, router, grad_y, mine, other = refs[1 + count : 8 + count]
    grad_middle, rounded, grad_attended, grad_gain, rows = refs[8 + count :]
    assemble(rows, pieces)
    hot = (hot_route(slots, 0, rows.shape[0]) | hot_route(slots, 1, rows.shape[0])).astype(jnp.bfloat16)
    grad = dot_f32(grad_logits[...], router[...], NT) + dot_f32(hot, rows[...])
    turned, grad_gain[...] = norm_back(middle[...], gain[...], grad)
    result = grad_y[...] + turned
    grad_middle[...] = result
    low = result.astype(jnp.bfloat16)
    rounded[...] = low
    first, second = halves(core[0], mine[...], other[...])
    half = first.shape[1]
    grad_attended[...] = (dot_f32(low[:, :half], first, NT) + dot_f32(low[:, half:], second, NT)).astype(jnp.bfloat16)


def collect(core, slots, pieces, middle, gain, grad_logits, router, grad_y, mine, other):
    length, width = middle.shape
    last, half = mine.shape[0] - 1, mine.shape[2]
    f32, bf16 = jnp.float32, jnp.bfloat16
    weight = pl.BlockSpec((None, width, half), lambda i, core: (last, 0, 0))
    plain = [slots, *pieces, middle, gain.reshape(1, -1), grad_logits, router, grad_y]
    shapes = [((length, width), f32), ((length, width), bf16), ((length, width), bf16), ((8, width), f32)]
    return pl.pallas_call(
        lambda *refs: collect_kernel(*refs, count=len(pieces)),
        grid_spec=pltpu.PrefetchScalarGridSpec(
            num_scalar_prefetch=1,
            grid=(1,),
            in_specs=[whole(array.shape) for array in plain] + [weight, weight],
            out_specs=[whole(shape) for shape, _ in shapes],
            scratch_shapes=[pltpu.VMEM((sum(piece.shape[0] for piece in pieces), width), bf16)],
        ),
        out_shape=[jax.ShapeDtypeStruct(shape, kind) for shape, kind in shapes],
        compiler_params=pltpu.CompilerParams(vmem_limit_bytes=VMEM_BYTES),
        cost_estimate=cost(8),
        name="collect",
    )(core, *plain, mine, other)


def outer_halves_kernel(core, normed, attended, rights, last, *refs, count):
    aways, stays, normed_t, attended_t = refs[:2], refs[2:4], refs[4], refs[5]
    step = pl.program_id(0)

    @pl.when(step == 0)
    def _():
        normed_t[...] = normed[...].T
        attended_t[...] = attended[...].T

    for place in range(count + 1):

        @pl.when(step == place)
        def _():
            result = dot_f32(normed_t[...], rights[...]) if place < count else dot_f32(attended_t[...], last[...])
            result = result.astype(jnp.bfloat16)
            half = result.shape[1] // 2
            away, stay = aways[place // 2], stays[place // 2]
            slot = place % 2

            @pl.when(core[0] == 0)
            def _():
                stay[slot] = result[:, :half]
                away[slot] = result[:, half:]

            @pl.when(core[0] != 0)
            def _():
                away[slot] = result[:, :half]
                stay[slot] = result[:, half:]


def outer_halves(core, normed, attended, rights, last):
    length, width = normed.shape
    count, half = rights.shape[0], width // 2
    shape = jax.ShapeDtypeStruct((2, width, half), jnp.bfloat16)
    return pl.pallas_call(
        lambda *refs: outer_halves_kernel(*refs, count=count),
        grid_spec=pltpu.PrefetchScalarGridSpec(
            num_scalar_prefetch=1,
            grid=(count + 1,),
            in_specs=[
                whole((length, width)),
                whole((length, width)),
                pl.BlockSpec((None, length, width), lambda i, core: (jnp.minimum(i, count - 1), 0, 0)),
                whole((length, width)),
            ],
            out_specs=[whole(shape.shape)] * 4,
            scratch_shapes=[pltpu.VMEM((width, length), jnp.bfloat16)] * 2,
        ),
        out_shape=[shape] * 4,
        compiler_params=pltpu.CompilerParams(vmem_limit_bytes=VMEM_BYTES),
        cost_estimate=cost(2),
        name="outer_halves",
    )(core, normed, attended, rights, last)


def enter_kernel(
    core, grads, mine, other, tokens, gain, grad_middle, moe_parts, squares, normed, grad_logits, grad_input, small, total
):
    step = pl.program_id(0)
    first, second = halves(core[0], mine[...], other[...])
    half = first.shape[1]
    rows = grads[...]
    part = dot_f32(rows[:, :half], first, NT) + dot_f32(rows[:, half:], second, NT)

    @pl.when(step == 0)
    def _():
        total[...] = part

    @pl.when(step > 0)
    def _():
        total[...] += part

    @pl.when(step == pl.num_programs(0) - 1)
    def _():
        turned, gain_parts = norm_back(tokens[...].astype(jnp.float32), gain[...], total[...])
        grad_input[...] = grad_middle[...] + turned
        sums = [jnp.sum(part, axis=0, keepdims=True) for part in (moe_parts[...], gain_parts, squares[...])]
        sums.append(jnp.zeros((SMALL - len(sums), gain.shape[1]), jnp.float32))
        small[pl.ds(0, SMALL), :] = jnp.concatenate(sums)
        small[pl.ds(SMALL, grad_logits.shape[1]), :] = dot_f32(grad_logits[...], normed[...], TN)


def enter(core, grads, mine, other, tokens, gain, grad_middle, moe_parts, squares, normed, grad_logits):
    length, width = tokens.shape
    count, half, experts = grads.shape[0], mine.shape[2], grad_logits.shape[1]
    weight = pl.BlockSpec((None, width, half), lambda i, core: (i, 0, 0))
    plain = [tokens, gain.reshape(1, -1), grad_middle, moe_parts, squares, normed, grad_logits]
    shapes = [(length, width), (SMALL + experts, width)]
    return pl.pallas_call(
        enter_kernel,
        grid_spec=pltpu.PrefetchScalarGridSpec(
            num_scalar_prefetch=1,
            grid=(count,),
            in_specs=[pl.BlockSpec((None, length, width), lambda i, core: (i, 0, 0)), weight, weight]
            + [whole(array.shape) for array in plain],
            out_specs=[whole(shape) for shape in shapes],
            scratch_shapes=[pltpu.VMEM((length, width), jnp.float32)],
        ),
        out_shape=[jax.ShapeDtypeStruct(shape, jnp.float32) for shape in shapes],
        compiler_params=pltpu.CompilerParams(vmem_limit_bytes=VMEM_BYTES),
        cost_estimate=cost(6),
        name="enter",
    )(core, grads, mine, other, *plain)


BOUNDS = (12, 16, 23, 32, 46, 64, 91)
TOP_PRECISION = lax.Precision.HIGHEST
AXES = ("dp", "expert")
PAIR = 2


def after(value, *others):
    return lax.optimization_barrier((value, *others))[0] if others else value


def bucket_index(offset):
    distance = jnp.abs(offset)
    far_bucket = 8 + sum([(distance >= level).astype(jnp.int32) for level in BOUNDS])
    near_bucket = jnp.where(distance < 8, distance, far_bucket)
    return jnp.where(offset > 0, 16, 0) + near_bucket


def norm_apply(inputs, gain_vec):
    return inputs * lax.rsqrt(jnp.mean(inputs * inputs, axis=-1, keepdims=True) + EPS) * gain_vec


def tile_offsets(query_block, key_block):
    rows = query_block * BLOCK + lax.broadcasted_iota(jnp.int32, (BLOCK, BLOCK), 0)
    cols = key_block * BLOCK + lax.broadcasted_iota(jnp.int32, (BLOCK, BLOCK), 1)
    return rows, cols


def offset_bias(table):
    offsets = jnp.arange(4 * BLOCK, dtype=jnp.int32) - 2 * BLOCK
    hot = (bucket_index(offsets)[None] == jnp.arange(table.shape[1], dtype=jnp.int32)[:, None]).astype(jnp.float32)
    return jnp.dot(table, hot, precision=TOP_PRECISION)


def table_gradient(bands, buckets):
    rows, cols = tile_offsets(0, 0)
    ids = [jnp.full((BLOCK, BLOCK), bucket_far(), jnp.int32)]
    ids += [bucket_index(shift * BLOCK + cols - rows) for shift in (-1, 0, 1)]
    hot = (jnp.stack(ids)[..., None] == jnp.arange(buckets, dtype=jnp.int32)).astype(jnp.float32)
    return jnp.einsum("hdxy,dxyb->hb", bands, hot, precision=TOP_PRECISION)


def bucket_far():
    return 8 + len(BOUNDS)


def on_device(
    tokens,
    qkv_weight,
    out_weight,
    position_bias_table,
    gain_attn,
    gain_moe,
    router,
    w_in,
    w_out,
    routes,
    prefix,
    valid_mask,
    teacher,
    cotangent,
):
    length, width = tokens.shape
    bf16, f32 = jnp.bfloat16, jnp.float32
    expert_count = router.shape[1]
    top_count = routes.shape[1]
    groups = lax.axis_size("expert")
    copies = lax.axis_size("dp")
    inner = w_in.shape[2]
    capacity = 5 * length * top_count // (4 * expert_count)
    total_tokens = length * copies * groups
    sources = 2 * groups
    blocks = length // BLOCK
    here_dp, here_group = lax.axis_index("dp"), lax.axis_index("expert")
    half = (here_dp >> 1) & 1
    core = here_group & 1
    rest = copies // 4

    def swap(value, dp_mask, group_mask):
        pairs = [
            (i, ((i // groups) ^ dp_mask) * groups + ((i % groups) ^ group_mask))
            for i in range(copies * groups)
        ]
        return lax.ppermute(value, AXES, pairs)

    def bits(count):
        return [1 << place for place in range(count.bit_length() - 1)]

    def partial_sums(value):
        sums = []
        for masks in [(0, mask) for mask in bits(groups)] + [(mask, 0) for mask in bits(copies)]:
            value = value + swap(value, *masks)
            sums.append(value)
        return sums

    chips = groups

    def across(value, place):
        return swap(value, PAIR * (place // (groups // 2)), 2 * (place % (groups // 2)))

    def to_chips(pieces):
        return [pieces[0]] + [across(pieces[place], place) for place in range(1, chips)]

    def through(visit, sends):
        direct, relay = to_chips(sends[::2]), to_chips(sends[1::2])
        seen, direct = visit(direct)
        direct = to_chips(direct)
        relay = [after(part, seen) for part in relay]
        passed = visit(swap(jnp.concatenate(relay), 0, 1))
        return direct, [swap(after(part, *direct), 0, 1) for part in passed]

    def weave(direct, relay):
        return [part for pair in zip(direct, to_chips(relay)) for part in pair]

    ring = list(range(0, copies, 2)) + list(range(copies - 1, 0, -2))
    turns = [(1, step) for step in range(1, copies // 2 + 1)] + [(-1, step) for step in range(1, copies // 2)]

    def gather_ring(shard, due):
        got = [shard]
        for turn in (1, -1):
            held = shard
            pairs = [(ring[i], ring[(i + turn) % copies]) for i in range(copies)]
            for step in [step for way, step in turns if way == turn]:
                held = lax.ppermute(after(held, *due[step - 2 : step - 1]) if step > 1 else held, "dp", pairs)
                got.append(held)
        return got

    def ring_places():
        place = jnp.where(here_dp & 1 == 0, here_dp >> 1, copies - 1 - (here_dp >> 1))
        shift = jnp.array([0] + [turn * step for turn, step in turns], jnp.int32)
        place = (place - shift) & (copies - 1)
        return jnp.where(place < copies // 2, 2 * place, 2 * (copies - 1 - place) + 1).astype(jnp.int32)


    flat_routes = routes.reshape(-1)
    pair_count = length * top_count
    slot_count = sources * capacity
    route_hits = (flat_routes[:, None] == jnp.arange(expert_count, dtype=jnp.int32)[None, :]).astype(bf16)
    lower_ones = (
        lax.broadcasted_iota(jnp.int32, (pair_count, pair_count), 0)
        >= lax.broadcasted_iota(jnp.int32, (pair_count, pair_count), 1)
    ).astype(bf16)
    running = jnp.dot(lower_ones, route_hits, preferred_element_type=f32)
    pair_rank = jnp.sum((running - 1.0) * route_hits.astype(f32), axis=1).astype(jnp.int32)
    away = (flat_routes >> 1) ^ here_group
    chip = ((flat_routes & 1) ^ half) * (groups // 2) + (away >> 1)
    slots = ((chip * 2 + (away & 1)) * capacity + pair_rank).reshape(length, top_count)
    slots_t = slots.T

    resid = tokens.astype(f32)
    normed1 = norm_apply(resid, gain_attn).astype(bf16)
    columns = width // 2
    core_index = core.reshape(1).astype(jnp.int32)
    valid_rows = valid_mask.astype(f32)[:, None]
    counts = [jnp.broadcast_to(jnp.sum(valid_rows), (8, 128))]
    count_trades = [(0, mask) for mask in bits(groups)] + [(mask, 0) for mask in bits(copies)]

    def count_beside(before, value):
        if len(counts) > len(count_trades):
            return value
        counts.append(counts[-1] + swap(after(counts[-1], before), *count_trades[len(counts) - 1]))
        return after(value, counts[-1])

    shards = [
        lax.dynamic_slice_in_dim(part, core * columns, columns, 2)
        for part in (qkv_weight[:2], jnp.concatenate([qkv_weight[2:], out_weight[None]]))
    ]
    if copies > 8:
        mine = lax.all_gather(jnp.concatenate(shards), "dp", axis=1, tiled=True)
    else:
        mine = join(ring_places(), [gather_ring(shards[0], ()), gather_ring(shards[1], (slots_t, normed1))])
    other = count_beside(mine, swap(mine, 0, 1))
    qkv_rows = count_beside(other, project(core_index, normed1, mine, other, 3))
    offsets = offset_bias(position_bias_table)
    attended, probs = attention_forward(position_bias_table[:, bucket_far()], prefix, qkv_rows, offsets)
    middle, normed2, gates, *sends = route(
        core_index, count_beside(qkv_rows, attended), tokens, mine, other, gain_moe, router, routes, slots_t, 2 * chips, capacity
    )

    pick = half.reshape(1).astype(jnp.int32)
    hidden, slopes, rows_in = [], [], []

    def expert(pieces):
        one = not isinstance(pieces, list)
        pieces = [pieces] if one else pieces
        hidden_t, slope, rows_t, *results = expert_forward(pick, pieces, chips, w_in, w_out)
        hidden_t = count_beside(pieces[-1], hidden_t)
        for kept, value in zip((hidden, slopes, rows_in), (hidden_t, slope, rows_t)):
            kept.append(value)
        return results if one else (hidden_t, results)

    back = weave(*through(expert, sends))
    while len(counts) <= len(count_trades):
        back[0] = count_beside(back[0], back[0])
    valid_count = counts[-1][0, 0]
    scale = (total_tokens / valid_count).reshape(1, 1)
    output, grad_y, grad_logits, squares, *sends = combine(
        slots, slots_t, scale, back, middle, teacher, cotangent, valid_rows, gates, routes, expert_count
    )

    out_rows = inner // copies
    in_rows = width // copies
    far_bit = here_dp % 2
    slices = jnp.arange(rest, dtype=jnp.int32) * 4

    def picks(bit0):
        return jnp.concatenate([slices + ((half ^ other_half) * 2 + bit0) for other_half in (1, 0)]).astype(jnp.int32)

    sent, kept = picks(1 - far_bit), picks(far_bit)

    def add(left, right):
        return (left.astype(f32) + right.astype(f32)).astype(bf16)

    def fold(unit, bit, axis=0):
        unit = unit.reshape(unit.shape[:axis] + (2, unit.shape[axis] // 2) + unit.shape[axis + 1 :])
        away_part = lax.dynamic_index_in_dim(unit, 1 - bit, axis, keepdims=False)
        return away_part, lax.dynamic_index_in_dim(unit, bit, axis, keepdims=False)

    far_masks = list(reversed(bits(copies)[2:]))

    def near_add(got, keep):
        away_part, stay_part = fold(add(got, keep), (here_dp // far_masks[0]) % 2)
        return away_part, stay_part

    def far_trade(away_part):
        return swap(away_part, far_masks[0], 0)

    def finish(got, stay):
        unit = add(got, stay)
        for mask in far_masks[1:]:
            away_part, stay_part = fold(unit, (here_dp // mask) % 2)
            unit = add(swap(away_part, mask, 0), stay_part)
        return unit[0]

    plan_a, plan_b, plan_c = ((0, 0), (0, 1)), ((0, 2), (1, 0)), ((1, 1), (1, 2))
    plan_d, plan_e, plan_f = plan_a, plan_b, plan_c
    out_plans, in_plans = (plan_a, plan_b, plan_c), (plan_d, plan_e, plan_f)

    grad_rows, grad_pre, parts = [], [], []

    def expert_back(pieces):
        if isinstance(pieces, list):
            grad_pre_rows, grads, *results = expert_backward(pick, pieces, chips, w_in, w_out, slopes[0])
            grad_rows.append(grads)
            grad_pre.append(grad_pre_rows)
            return grad_pre_rows, results
        grad_rows.append(pieces)
        parts.extend(weight_part(sent, hidden, grad_rows, out_rows, out_plans, rest, width))
        parts[0] = swap(parts[0], 1, 0)
        pieces = after(pieces, parts[1])
        grad_pre_rows, _, *results = expert_backward(pick, [pieces], chips, w_in, w_out, slopes[1])
        grad_pre.append(grad_pre_rows)
        return results

    direct, relay = through(expert_back, sends)
    got_a, send_b, send_c = parts
    relay = [after(part, got_a) for part in relay]
    got_b = swap(after(send_b, relay[0]), 1, 0)
    back = weave(direct, relay)
    grad_rows, grad_pre = lax.optimization_barrier((grad_rows, grad_pre, relay))[:2]
    keep_a, keep_b, keep_c = weight_part(kept, hidden, grad_rows, out_rows, out_plans, rest, width)
    away_a, stay_a = near_add(got_a, keep_a)
    far_a = far_trade(away_a)
    send_d, send_e, send_f = weight_part(sent, rows_in, after(grad_pre, away_a), in_rows, in_plans, rest, inner // 2)
    back = [after(part, send_d) for part in back]
    got_c = swap(after(send_c, send_d), 1, 0)
    grad_middle, grad_attn_proj, grad_attended, gain_moe_parts = collect(
        core_index, slots, back, middle, gain_moe, grad_logits, router, grad_y, mine, other
    )
    away_b, stay_b = near_add(after(got_b, grad_attended), keep_b)
    got_d = swap(after(send_d, grad_attended), 1, 0)
    grad_attended, away_b = lax.optimization_barrier((grad_attended, away_b))
    grad_qkv_rows, bands = attention_backward(qkv_rows, grad_attended, probs)
    grad_qkv_rows, got_c, far_a = lax.optimization_barrier((grad_qkv_rows, got_c, far_a))
    done_a = finish(far_a, stay_a)

    away_c, stay_c = near_add(got_c, keep_c)
    far_c = far_trade(jnp.concatenate([away_b, away_c], axis=1))
    stay_c = jnp.concatenate([stay_b, stay_c], axis=1)
    *weights_away, stay_1, stay_2 = outer_halves(
        core_index, normed1, attended, after(grad_qkv_rows, away_c), grad_attn_proj
    )
    weights_away, got_d = lax.optimization_barrier((weights_away, got_d))
    got_e = swap(after(send_e, got_d), 1, 0)
    group_masks = bits(groups)[1:]
    dp_masks = bits(copies)

    def over_dp(total, mask, passed):
        axis = 1 + sorted([other for other in dp_masks if other not in passed], reverse=True).index(mask)
        bit = (here_dp // mask) % 2
        away_part = lax.dynamic_index_in_dim(total, 1 - bit, axis, keepdims=False)
        stay_part = lax.dynamic_index_in_dim(total, bit, axis, keepdims=False)
        return away_part, swap(away_part, mask, 0), stay_part

    weights_got = [swap(part, 0, 1) for part in weights_away]
    halves_sum = [
        add(got, stay).reshape(2, copies, in_rows, columns) for got, stay in zip(weights_got, (stay_1, stay_2))
    ]
    for mask in group_masks[:-1]:
        folded = [fold(part, (here_group // mask) % 2, 2) for part in halves_sum]
        halves_sum = [add(swap(away_part, 0, mask), stay_part) for away_part, stay_part in folded]
    folded = [fold(part, (here_group // group_masks[-1]) % 2, 2) for part in halves_sum]
    y_stay = jnp.concatenate([stay_part for _, stay_part in folded])
    y_away = jnp.concatenate([away_part for away_part, _ in folded])
    y_got = swap(y_away, 0, group_masks[-1])
    keep_d, keep_e, keep_f = weight_part(
        kept, rows_in, after(grad_pre, y_away), in_rows, in_plans, rest, inner // 2, 40
    )
    away_d, stay_d = near_add(got_d, keep_d)
    far_d = far_trade(after(away_d, far_c))
    away_e, stay_e = near_add(after(got_e, away_d), keep_e)
    done_c = finish(after(far_c, away_e), stay_c)
    total = add(after(y_got, away_e), y_stay)
    total = total.reshape((4,) + (2,) * len(dp_masks) + (-1, columns))


    small_trades = [(0, 1), (0, group_masks[0])] + [(mask, 0) for mask in reversed(dp_masks) if mask != PAIR] + [(PAIR, 0)]
    small_trades += [(0, mask) for mask in group_masks[1:]]
    passed_masks = []
    for mask in dp_masks:
        gone, got, stay = over_dp(total, mask, passed_masks)
        passed_masks.append(mask)
        if len(passed_masks) == 1:
            grad_input, small = enter(
                core_index,
                after(grad_qkv_rows, gone),
                mine,
                other,
                tokens,
                gain_attn,
                grad_middle,
                gain_moe_parts,
                squares,
                normed2,
                grad_logits,
            )
            grad_table = table_gradient(after(bands, gone), position_bias_table.shape[1])
            flat = lax.dynamic_update_slice(small, grad_table.reshape(1, -1), (3, 0))
        for _ in range((0, 2, 1)[min(len(passed_masks), 3) - 1]):
            flat = flat + swap(after(flat, gone), *small_trades.pop(0))
        if len(passed_masks) == 1:
            far_e = far_trade(after(away_e, gone))
            got_f = swap(after(send_f, gone), 1, 0)
        elif mask == PAIR:
            got = after(got, far_d, far_e)
            done_e = finish(far_e, stay_e)
        elif len(passed_masks) == len(dp_masks):
            away_f, stay_f = near_add(after(got_f, stay), keep_f)
            far_f = far_trade(after(away_f, got))
            got = after(got, away_f, in_first)
            done_f = finish(far_f, stay_f)
        total = add(got, stay)
        if mask == PAIR:
            done_d = finish(after(far_d, total), stay_d)
            in_first = swap(done_d, PAIR, 0)
            out_theirs = swap(after(jnp.concatenate([done_a, done_c[:1]]), total), PAIR, 0)
        flat = after(flat, total)
    in_theirs = jnp.concatenate([in_first, swap(done_e[:1], PAIR, 0)])
    for mask in reversed(group_masks):
        bit = (here_group // mask) % 2
        other_part = swap(total, 0, mask)
        total = jnp.concatenate([jnp.where(bit == 0, total, other_part), jnp.where(bit == 0, other_part, total)], axis=1)
        flat = flat + swap(flat, *small_trades.pop(0))
        total, flat = lax.optimization_barrier((total, flat))
    other_part = after(swap(total, 0, 1), out_theirs)
    for trade in small_trades:
        flat = flat + swap(flat, *trade)
    total = jnp.concatenate([jnp.where(core == 0, total, other_part), jnp.where(core == 0, other_part, total)], axis=2)
    weights_done = total.astype(f32)
    grad_qkv, grad_out_weight = weights_done[:3], weights_done[3]
    grad_gain_moe, grad_gain_attn, square_total = flat[0], flat[1], jnp.sum(flat[2])
    grad_table = flat[3, : grad_table.size].reshape(grad_table.shape)
    grad_router = flat[SMALL:].T

    out_mine, in_mine = done_c[1:], jnp.concatenate([done_e[1:], done_f])

    def both_experts(mine, theirs):
        mine, theirs = [part.reshape(-1, part.shape[-1]).astype(f32) for part in (mine, theirs)]
        return jnp.stack([jnp.where(half == 0, mine, theirs), jnp.where(half == 0, theirs, mine)])

    grad_w_out = both_experts(out_mine, out_theirs)
    grad_w_in = both_experts(in_mine, in_theirs)

    distill_loss = square_total / (width * valid_count)
    return (
        output.astype(bf16),
        distill_loss,
        grad_input,
        grad_qkv,
        grad_out_weight,
        grad_w_in,
        grad_w_out,
        grad_router,
        grad_table,
        grad_gain_attn,
        grad_gain_moe,
    )


def solution(mesh):
    rows = P(AXES, None)
    return jax.shard_map(
        on_device,
        mesh=mesh,
        in_specs=(
            rows,
            P(None, "dp", None),
            P("dp", None),
            P(),
            P(),
            P(),
            P(),
            P("expert", None, None),
            P("expert", None, None),
            rows,
            P(AXES),
            P(AXES),
            rows,
            rows,
        ),
        out_specs=(
            rows,
            P(),
            rows,
            P(None, "dp", None),
            P("dp", None),
            P("expert", "dp", None),
            P("expert", "dp", None),
            P(),
            P(),
            P(),
            P(),
        ),
        check_vma=False,
    )
```

```python
import math
import jax
import jax.numpy as jnp
from jax import lax
from jax.experimental import pallas as pl
from jax.experimental.pallas import tpu as pltpu
from jax.sharding import PartitionSpec as P

BLOCK = 128
THIRDS = 3
SMALL = 8
EPS = 1e-06
GELU_A = math.sqrt(2.0 / math.pi)
GELU_B = 0.044715
NT = (((1,), (1,)), ((), ()))
TN = (((0,), (0,)), ((), ()))
VMEM_BYTES = 56 * 1024 * 1024


def cost(micros):
    return pl.CostEstimate(flops=int(micros * 0.37e9), bytes_accessed=0, transcendentals=0)


def dot_f32(left, right, dims=(((1,), (0,)), ((), ()))):
    return lax.dot_general(left, right, dims, preferred_element_type=jnp.float32)


def assemble(rows, pieces):
    start = 0
    for piece in pieces:
        rows[pl.ds(start, piece.shape[0]), :] = piece[...]
        start += piece.shape[0]


def hand_out(total, outs):
    start = 0
    for out in outs:
        out[...] = total[pl.ds(start, out.shape[0]), :].astype(out.dtype)
        start += out.shape[0]


def whole(shape):
    return pl.BlockSpec(shape, lambda *step: (0,) * len(shape))


def expert_forward_kernel(pick, *refs, chunk, count):
    pieces, w_in, w_out = refs[:count], refs[count], refs[count + 1]
    hidden_t, slope, rows_t = refs[count + 2 : count + 5]
    outs, rows, total = refs[count + 5 : -2], refs[-2], refs[-1]
    step = pl.program_id(0)

    @pl.when(step == 0)
    def _():
        assemble(rows, pieces)
        total[...] = jnp.zeros_like(total)
        rows_t[...] = rows[...].T

    for start in range(0, rows.shape[0], chunk):
        part = pl.ds(start, chunk)
        pre = dot_f32(rows[part, :], w_in[0])
        square = pre * pre
        bend = jnp.tanh(pre * (GELU_A + (GELU_A * GELU_B) * square))
        half = 0.5 + 0.5 * bend
        act = (pre * half).astype(jnp.bfloat16)
        lift = pre * (0.5 * GELU_A + (1.5 * GELU_A * GELU_B) * square)
        slope[part, :] = (half + lift * (1.0 - bend * bend)).astype(jnp.bfloat16)
        hidden_t[:, part] = act.T
        total[part, :] += dot_f32(act, w_out[0])

    @pl.when(step == pl.num_programs(0) - 1)
    def _():
        hand_out(total, outs)


def expert_forward(pick, pieces, results, w_in, w_out, tile=768, chunk=320):
    many, width = sum(piece.shape[0] for piece in pieces), pieces[0].shape[1]
    inner = w_in.shape[2]
    bf16 = jnp.bfloat16
    return pl.pallas_call(
        lambda *refs: expert_forward_kernel(*refs, chunk=chunk, count=len(pieces)),
        grid_spec=pltpu.PrefetchScalarGridSpec(
            num_scalar_prefetch=1,
            grid=(inner // tile,),
            in_specs=[whole(piece.shape) for piece in pieces]
            + [
                pl.BlockSpec((1, width, tile), lambda f, pick: (pick[0], 0, f)),
                pl.BlockSpec((1, tile, width), lambda f, pick: (pick[0], f, 0)),
            ],
            out_specs=[
                pl.BlockSpec((tile, many), lambda f, pick: (f, 0)),
                pl.BlockSpec((many, tile), lambda f, pick: (0, f)),
                whole((width, many)),
            ]
            + [whole((many // results, width))] * results,
            scratch_shapes=[pltpu.VMEM((many, width), bf16), pltpu.VMEM((many, width), jnp.float32)],
        ),
        out_shape=[
            jax.ShapeDtypeStruct((inner, many), bf16),
            jax.ShapeDtypeStruct((many, inner), bf16),
            jax.ShapeDtypeStruct((width, many), bf16),
        ]
        + [jax.ShapeDtypeStruct((many // results, width), bf16)] * results,
        compiler_params=pltpu.CompilerParams(vmem_limit_bytes=VMEM_BYTES),
        cost_estimate=cost(13),
        name="expert_forward",
    )(pick, *pieces, w_in, w_out)


def expert_backward_kernel(pick, *refs, chunk, count):
    pieces, w_in, w_out, slope = refs[:count], refs[count], refs[count + 1], refs[count + 2]
    grad_pre, rows = refs[count + 3 : count + 5]
    outs, total = refs[count + 5 : -1], refs[-1]
    step = pl.program_id(0)

    @pl.when(step == 0)
    def _():
        assemble(rows, pieces)
        total[...] = jnp.zeros_like(total)

    for start in range(0, rows.shape[0], chunk):
        part = pl.ds(start, chunk)
        back = dot_f32(rows[part, :], w_out[0], NT) * slope[part, :].astype(jnp.float32)
        back = back.astype(jnp.bfloat16)
        grad_pre[part, :] = back
        total[part, :] += dot_f32(back, w_in[0], NT)

    @pl.when(step == pl.num_programs(0) - 1)
    def _():
        hand_out(total, outs)


def expert_backward(pick, pieces, results, w_in, w_out, slope, tile=768, chunk=640):
    many, width = sum(piece.shape[0] for piece in pieces), pieces[0].shape[1]
    inner = w_in.shape[2]
    bf16 = jnp.bfloat16
    return pl.pallas_call(
        lambda *refs: expert_backward_kernel(*refs, chunk=chunk, count=len(pieces)),
        grid_spec=pltpu.PrefetchScalarGridSpec(
            num_scalar_prefetch=1,
            grid=(inner // tile,),
            in_specs=[whole(piece.shape) for piece in pieces]
            + [
                pl.BlockSpec((1, width, tile), lambda f, pick: (pick[0], 0, f)),
                pl.BlockSpec((1, tile, width), lambda f, pick: (pick[0], f, 0)),
                pl.BlockSpec((many, tile), lambda f, pick: (0, f)),
            ],
            out_specs=[pl.BlockSpec((many, tile), lambda f, pick: (0, f)), whole((many, width))]
            + [whole((many // results, width))] * results,
            scratch_shapes=[pltpu.VMEM((many, width), jnp.float32)],
        ),
        out_shape=[jax.ShapeDtypeStruct((many, inner), bf16), jax.ShapeDtypeStruct((many, width), bf16)]
        + [jax.ShapeDtypeStruct((many // results, width), bf16)] * results,
        compiler_params=pltpu.CompilerParams(vmem_limit_bytes=VMEM_BYTES),
        cost_estimate=cost(11),
        name="expert_backward",
    )(pick, *pieces, w_in, w_out, slope)


def seen_blocks(row_block, blocks):
    return max(row_block + 1, blocks // 2)


def attention_forward_kernel(far, prefix, queries, keys, values, offsets, attended, probs, *, heads, blocks):
    pair = pl.program_id(0)
    lane = lax.broadcasted_iota(jnp.int32, queries.shape, 1)
    row = lax.broadcasted_iota(jnp.int32, (BLOCK, BLOCK), 0)
    col = lax.broadcasted_iota(jnp.int32, (BLOCK, BLOCK), 1)
    outs = []
    for head in range(2):
        line = jnp.broadcast_to(offsets[head : head + 1, :], (BLOCK, 4 * BLOCK))
        turned = pltpu.roll(line, 0, 1, stride=1, stride_axis=0)
        far_bias = far[pair * 2 + head]
        mine = (lane < heads) if head == 0 else (lane >= heads)
        query = jnp.where(mine, queries[...] * 0.125, 0.0).astype(jnp.bfloat16)
        score = dot_f32(query, keys[...], NT)
        strips = []
        for row_block in range(blocks):
            span = seen_blocks(row_block, blocks)
            pieces = []
            for key_block in range(span):
                piece = score[row_block * BLOCK : (row_block + 1) * BLOCK, key_block * BLOCK : (key_block + 1) * BLOCK]
                shift = key_block - row_block
                if shift < -1:
                    piece = piece + far_bias
                elif shift < 2:
                    piece = piece + turned[:, (2 + shift) * BLOCK : (3 + shift) * BLOCK]
                else:
                    raise ValueError(shift)
                if shift >= 0:
                    shown = col + key_block * BLOCK < prefix[0]
                    piece = jnp.where((shown | (col <= row)) if shift == 0 else shown, piece, -1e30)
                pieces.append(piece)
            peak = pieces[0]
            for piece in pieces[1:]:
                peak = jnp.maximum(peak, piece)
            peak = jnp.max(peak, axis=1, keepdims=True)
            pieces = [jnp.exp(piece - peak) for piece in pieces]
            mass = pieces[0]
            for piece in pieces[1:]:
                mass = mass + piece
            scale = 1.0 / jnp.sum(mass, axis=1, keepdims=True)
            pieces = [(piece * scale).astype(jnp.bfloat16) for piece in pieces]
            pieces += [jnp.zeros((BLOCK, BLOCK), jnp.bfloat16)] * (blocks - span)
            strips.append(jnp.concatenate(pieces, axis=1))
        weights = jnp.concatenate(strips, axis=0)
        probs[head] = weights
        outs.append(dot_f32(weights, values[...]))
    attended[...] = jnp.where(lane < heads, outs[0], outs[1]).astype(jnp.bfloat16)


def attention_forward(far, prefix, qkv_rows, offsets):
    length, width = qkv_rows.shape[1:]
    pairs = width // 128
    blocks = length // BLOCK
    return pl.pallas_call(
        lambda *refs: attention_forward_kernel(*refs, heads=64, blocks=blocks),
        grid_spec=pltpu.PrefetchScalarGridSpec(
            num_scalar_prefetch=2,
            grid=(pairs,),
            in_specs=[pl.BlockSpec((None, length, 128), lambda h, far, prefix, c=c: (c, 0, h)) for c in range(3)]
            + [pl.BlockSpec((None, 2, 4 * BLOCK), lambda h, far, prefix: (h, 0, 0))],
            out_specs=[
                pl.BlockSpec((length, 128), lambda h, far, prefix: (0, h)),
                pl.BlockSpec((2, length, length), lambda h, far, prefix: (h, 0, 0)),
            ],
        ),
        out_shape=[
            jax.ShapeDtypeStruct((length, width), jnp.bfloat16),
            jax.ShapeDtypeStruct((2 * pairs, length, length), jnp.bfloat16),
        ],
        compiler_params=pltpu.CompilerParams(vmem_limit_bytes=VMEM_BYTES),
        cost_estimate=cost(13),
        name="attention_forward",
    )(far, prefix, qkv_rows, qkv_rows, qkv_rows, offsets.reshape(pairs, 2, 4 * BLOCK))


def attention_backward_kernel(queries, keys, values, grads, probs, grad_rows, bands, *, heads, blocks):
    lane = lax.broadcasted_iota(jnp.int32, queries.shape, 1)
    query_t = (queries[...] * 0.125).astype(jnp.bfloat16).T
    grad_t = grads[...].T
    dq, dk, dv = [], [], []
    for head in range(2):
        mine = (lane < heads) if head == 0 else (lane >= heads)
        sums = [None] * 4
        grad = jnp.where(mine, grads[...], 0.0).astype(jnp.bfloat16)
        back = dot_f32(grad, values[...], NT)
        strips = []
        for row_block in range(blocks):
            span = seen_blocks(row_block, blocks)
            rows = slice(row_block * BLOCK, (row_block + 1) * BLOCK)
            soft = probs[head, pl.ds(row_block * BLOCK, BLOCK), pl.ds(0, span * BLOCK)].astype(jnp.float32)
            part = back[rows, : span * BLOCK]
            inner = jnp.sum(soft * part, axis=1, keepdims=True)
            score_grad = (soft * (part - inner)).astype(jnp.bfloat16)
            for key_block in range(span):
                band = max(key_block - row_block, -2)
                tile = score_grad[:, key_block * BLOCK : (key_block + 1) * BLOCK].astype(jnp.float32)
                sums[band + 2] = tile if sums[band + 2] is None else sums[band + 2] + tile
            if span < blocks:
                rest = jnp.zeros((BLOCK, (blocks - span) * BLOCK), jnp.bfloat16)
                score_grad = jnp.concatenate([score_grad, rest], axis=1)
            strips.append(score_grad)
        flow = jnp.concatenate(strips, axis=0)
        for band in range(4):
            bands[head, band] = sums[band]
        part = slice(head * heads, (head + 1) * heads)
        dq.append(dot_f32(flow, keys[...]) * 0.125)
        dk.append(dot_f32(query_t[part], flow))
        dv.append(dot_f32(grad_t[part], probs[head]))
    grad_rows[0] = jnp.where(lane < heads, dq[0], dq[1]).astype(jnp.bfloat16)
    grad_rows[1] = jnp.concatenate(dk, axis=0).T.astype(jnp.bfloat16)
    grad_rows[2] = jnp.concatenate(dv, axis=0).T.astype(jnp.bfloat16)


def attention_backward(qkv_rows, grads, probs):
    length, width = grads.shape
    pairs = width // 128
    blocks = length // BLOCK
    block = pl.BlockSpec((length, 128), lambda h: (0, h))
    of_three = [pl.BlockSpec((None, length, 128), lambda h, c=c: (c, 0, h)) for c in range(3)]
    return pl.pallas_call(
        lambda *refs: attention_backward_kernel(*refs, heads=64, blocks=blocks),
        grid=(pairs,),
        in_specs=[*of_three, block, pl.BlockSpec((2, length, length), lambda h: (h, 0, 0))],
        out_specs=[pl.BlockSpec((3, length, 128), lambda h: (0, 0, h)), pl.BlockSpec((2, 4, BLOCK, BLOCK), lambda h: (h, 0, 0, 0))],
        out_shape=[jax.ShapeDtypeStruct((3, length, width), jnp.bfloat16)]
        + [jax.ShapeDtypeStruct((2 * pairs, 4, BLOCK, BLOCK), jnp.float32)],
        compiler_params=pltpu.CompilerParams(vmem_limit_bytes=VMEM_BYTES),
        cost_estimate=cost(4),
        name="attention_backward",
    )(qkv_rows, qkv_rows, qkv_rows, grads, probs)


def pieces_left(lefts, plans, many):
    part = lefts[0][0].shape[0] // THIRDS
    return jnp.concatenate(
        [
            jnp.concatenate([ref[pl.ds(third * part, part), :] for ref in lefts[group * many + k]], axis=1)
            for plan in plans
            for group, third in plan
            for k in range(many)
        ]
    )


def put_pieces(result, outs):
    place = 0
    for out in outs:
        many, pieces, part = out.shape[:3]
        for piece in range(pieces):
            for k in range(many):
                out[k, piece] = result[place : place + part]
                place += part


def weight_part_kernel(picks, *refs, count, plans, many):
    lefts, rights, outs = refs[: 2 * count], refs[2 * count : 2 * count + 2], refs[2 * count + 2 :]
    left = pieces_left(list(zip(lefts[:count], lefts[count:])), plans, many)
    right = jnp.concatenate([ref[...] for ref in rights], axis=0)
    put_pieces(dot_f32(left, right).astype(jnp.bfloat16), outs)


def weight_part_plain(picks, lefts, rights, rows, plans, many):
    left, right = jnp.concatenate(lefts, axis=1), jnp.concatenate(rights, axis=0)
    depth, width = right.shape
    part = rows // THIRDS
    result = jnp.take(left.reshape(-1, rows, depth), picks, axis=0)
    result = jnp.einsum("srd,dw->srw", result, right, preferred_element_type=jnp.float32).astype(jnp.bfloat16)
    result = result.reshape(-1, many, THIRDS, part, width)
    return [jnp.stack([result[group, :, third] for group, third in plan], axis=1) for plan in plans]


def weight_part(picks, lefts, rights, rows, plans, many, tile, micros=4):
    depth, width = rights[0].shape
    count, part = picks.shape[0], rows // THIRDS
    if part % 16:
        return weight_part_plain(picks, lefts, rights, rows, plans, many)
    return pl.pallas_call(
        lambda *refs: weight_part_kernel(*refs, count=count, plans=plans, many=many),
        grid_spec=pltpu.PrefetchScalarGridSpec(
            num_scalar_prefetch=1,
            grid=(width // tile,),
            in_specs=[pl.BlockSpec((rows, depth), lambda i, picks, k=k: (picks[k], 0)) for k in range(count)] * 2
            + [pl.BlockSpec((depth, tile), lambda i, picks: (0, i))] * 2,
            out_specs=[pl.BlockSpec((many, len(plan), part, tile), lambda i, picks: (0, 0, 0, i)) for plan in plans],
        ),
        out_shape=[jax.ShapeDtypeStruct((many, len(plan), part, width), jnp.bfloat16) for plan in plans],
        compiler_params=pltpu.CompilerParams(vmem_limit_bytes=VMEM_BYTES),
        cost_estimate=cost(micros),
        name="weight_part",
    )(picks, *([lefts[0]] * count), *([lefts[1]] * count), *rights)


def hot_columns(slots, first, count):
    rows = first + lax.broadcasted_iota(jnp.int32, (count, slots.shape[1]), 0)
    return (rows == slots).astype(jnp.bfloat16)


def halves(core, mine, other):
    return jnp.where(core == 0, mine, other), jnp.where(core == 0, other, mine)


def join_kernel(places, *refs):
    pieces, out = refs[:-1], refs[-1]
    rows = pieces[0].shape[1]
    count = pieces[0].shape[0]
    for chunk in range(out.shape[0] // count):
        for step in range(len(pieces) * count // out.shape[0]):
            piece = pieces[chunk * (len(pieces) * count // out.shape[0]) + step]
            start = pl.multiple_of(places[step] * rows, rows)
            out[pl.ds(chunk * count, count), pl.ds(start, rows), :] = piece[...]


def join(places, chunks):
    count, rows, columns = chunks[0][0].shape
    steps = len(chunks[0])
    return pl.pallas_call(
        join_kernel,
        in_specs=[pl.BlockSpec(memory_space=pltpu.SMEM)] + [pl.BlockSpec(memory_space=pltpu.VMEM)] * (steps * len(chunks)),
        out_shape=jax.ShapeDtypeStruct((count * len(chunks), steps * rows, columns), jnp.bfloat16),
        compiler_params=pltpu.CompilerParams(vmem_limit_bytes=VMEM_BYTES),
        cost_estimate=cost(3),
        name="join",
    )(places, *[piece for chunk in chunks for piece in chunk])


def project_kernel(core, rows, mine, other, result):
    half = mine.shape[1]
    first, second = halves(core[0], mine[...], other[...])
    result[:, :half] = dot_f32(rows[...], first).astype(jnp.bfloat16)
    result[:, half:] = dot_f32(rows[...], second).astype(jnp.bfloat16)


def project(core, rows, mine, other, used):
    width, half = mine.shape[1:]
    length = rows.shape[0]
    return pl.pallas_call(
        project_kernel,
        grid_spec=pltpu.PrefetchScalarGridSpec(
            num_scalar_prefetch=1,
            grid=(used,),
            in_specs=[
                whole((length, width)),
                pl.BlockSpec((None, width, half), lambda i, core: (i, 0, 0)),
                pl.BlockSpec((None, width, half), lambda i, core: (i, 0, 0)),
            ],
            out_specs=pl.BlockSpec((None, length, 2 * half), lambda i, core: (i, 0, 0)),
        ),
        out_shape=jax.ShapeDtypeStruct((used, length, 2 * half), jnp.bfloat16),
        compiler_params=pltpu.CompilerParams(vmem_limit_bytes=VMEM_BYTES),
        cost_estimate=cost(4),
        name="project",
    )(core, rows, mine, other)


def route_kernel(core, attended, tokens, mine, other, gain, router, routes, slots, middle, normed, gates, *outs):
    f32 = jnp.float32
    first, second = halves(core[0], mine[...], other[...])
    rows = attended[...]
    moved = jnp.concatenate([dot_f32(rows, first), dot_f32(rows, second)], axis=1)
    value = tokens[...].astype(f32) + moved
    middle[...] = value
    low = (value * lax.rsqrt(jnp.mean(value * value, axis=1, keepdims=True) + EPS) * gain[...]).astype(jnp.bfloat16)
    normed[...] = low
    start = 0
    for first_out, second_out in zip(outs[::2], outs[1::2]):
        size = first_out.shape[0]
        hot = hot_columns(slots[0:1, :], start, 2 * size) + hot_columns(slots[1:2, :], start, 2 * size)
        part = dot_f32(hot, low).astype(jnp.bfloat16)
        first_out[...] = part[:size]
        second_out[...] = part[size:]
        start += 2 * size
    logits = dot_f32(low, router[...])
    soft = jnp.exp(logits - jnp.max(logits, axis=1, keepdims=True))
    soft = soft / jnp.sum(soft, axis=1, keepdims=True)
    expert = lax.broadcasted_iota(jnp.int32, soft.shape, 1)
    chosen = [jnp.sum(jnp.where(expert == routes[:, k : k + 1], soft, 0.0), axis=1, keepdims=True) for k in range(2)]
    for k in range(2):
        gates[:, k : k + 1] = chosen[k] / (chosen[0] + chosen[1])


def route(core, attended, tokens, mine, other, gain, router, routes, slots, pieces, count):
    length, width = tokens.shape
    last, half = mine.shape[0] - 1, mine.shape[2]
    f32, bf16 = jnp.float32, jnp.bfloat16
    weight = pl.BlockSpec((None, width, half), lambda i, core: (last, 0, 0))
    shapes = [((length, width), f32), ((length, width), bf16), ((length, 2), f32)] + [((count, width), bf16)] * pieces
    return pl.pallas_call(
        route_kernel,
        grid_spec=pltpu.PrefetchScalarGridSpec(
            num_scalar_prefetch=1,
            grid=(1,),
            in_specs=[whole((length, width)), whole((length, width)), weight, weight, whole((1, width)), whole(router.shape), whole(routes.shape), whole(slots.shape)],
            out_specs=[whole(shape) for shape, _ in shapes],
        ),
        out_shape=[jax.ShapeDtypeStruct(shape, kind) for shape, kind in shapes],
        compiler_params=pltpu.CompilerParams(vmem_limit_bytes=VMEM_BYTES),
        cost_estimate=cost(6),
        name="route",
    )(core, attended, tokens, mine, other, gain.reshape(1, -1), router, routes, slots)


def hot_route(slots, k, count):
    cols = lax.broadcasted_iota(jnp.int32, (slots.shape[0], count), 1)
    return cols == slots[:, k : k + 1]


def combine_kernel(*refs, count):
    slots, slots_t, scale = refs[:3]
    pieces = refs[3 : 3 + count]
    middle, teacher, cotangent, valid, gates, routes = refs[3 + count : 9 + count]
    output, grad_y, grad_logits, square = refs[9 + count : 13 + count]
    sends, rows = refs[13 + count : 13 + 2 * count], refs[13 + 2 * count]
    f32, bf16 = jnp.float32, jnp.bfloat16
    assemble(rows, pieces)
    table = rows[...]
    picked = [dot_f32(hot_route(slots, k, rows.shape[0]).astype(bf16), table) for k in range(2)]
    result = middle[...] + (gates[:, 0:1] * picked[0] + gates[:, 1:2] * picked[1])
    output[...] = result.astype(bf16)
    misfit = valid[...] * (result - teacher[...].astype(f32))
    square[...] = jnp.sum((misfit * misfit).reshape(-1, 8, misfit.shape[1]), axis=0)
    grad = cotangent[...].astype(f32) + misfit * scale[0, 0]
    grad_y[...] = grad
    steep = [jnp.sum(grad * picked[k], axis=1, keepdims=True) for k in range(2)]
    slack = gates[:, 0:1] * steep[0] + gates[:, 1:2] * steep[1]
    expert = lax.broadcasted_iota(jnp.int32, grad_logits.shape, 1)
    turn = [jnp.where(expert == routes[:, k : k + 1], gates[:, k : k + 1] * (steep[k] - slack), 0.0) for k in range(2)]
    grad_logits[...] = (turn[0] + turn[1]).astype(bf16)
    scaled = [(gates[:, k : k + 1] * grad).astype(bf16) for k in range(2)]
    start = 0
    for first, second in zip(sends[::2], sends[1::2]):
        size = first.shape[0]
        part = [dot_f32(hot_columns(slots_t[k : k + 1, :], start, 2 * size), scaled[k]) for k in range(2)]
        part = (part[0] + part[1]).astype(bf16)
        first[...] = part[:size]
        second[...] = part[size:]
        start += 2 * size


def combine(slots, slots_t, scale, pieces, middle, teacher, cotangent, valid, gates, routes, experts):
    length, width = middle.shape
    count = len(pieces)
    f32, bf16 = jnp.float32, jnp.bfloat16
    return pl.pallas_call(
        lambda *refs: combine_kernel(*refs, count=count),
        in_specs=[pl.BlockSpec(memory_space=pltpu.VMEM)] * 2
        + [pl.BlockSpec(memory_space=pltpu.SMEM)]
        + [pl.BlockSpec(memory_space=pltpu.VMEM)] * (6 + count),
        out_shape=[
            jax.ShapeDtypeStruct((length, width), bf16),
            jax.ShapeDtypeStruct((length, width), f32),
            jax.ShapeDtypeStruct((length, experts), bf16),
            jax.ShapeDtypeStruct((8, width), f32),
        ]
        + [jax.ShapeDtypeStruct(piece.shape, bf16) for piece in pieces],
        scratch_shapes=[pltpu.VMEM((sum(piece.shape[0] for piece in pieces), width), bf16)],
        compiler_params=pltpu.CompilerParams(vmem_limit_bytes=VMEM_BYTES),
        cost_estimate=cost(8),
        name="combine",
    )(slots, slots_t, scale, *pieces, middle, teacher, cotangent, valid, gates, routes)


def norm_back(value, gain, grad):
    root = lax.rsqrt(jnp.mean(value * value, axis=1, keepdims=True) + EPS)
    normed = value * root
    scaled = grad * gain
    inner = jnp.mean(scaled * normed, axis=1, keepdims=True)
    return root * (scaled - normed * inner), jnp.sum((grad * normed).reshape(-1, 8, value.shape[1]), axis=0)


def collect_kernel(core, *refs, count):
    slots, pieces = refs[0], refs[1 : 1 + count]
    middle, gain, grad_logits, router, grad_y, mine, other = refs[1 + count : 8 + count]
    grad_middle, rounded, grad_attended, grad_gain, rows = refs[8 + count :]
    assemble(rows, pieces)
    hot = (hot_route(slots, 0, rows.shape[0]) | hot_route(slots, 1, rows.shape[0])).astype(jnp.bfloat16)
    grad = dot_f32(grad_logits[...], router[...], NT) + dot_f32(hot, rows[...])
    turned, grad_gain[...] = norm_back(middle[...], gain[...], grad)
    result = grad_y[...] + turned
    grad_middle[...] = result
    low = result.astype(jnp.bfloat16)
    rounded[...] = low
    first, second = halves(core[0], mine[...], other[...])
    half = first.shape[1]
    grad_attended[...] = (dot_f32(low[:, :half], first, NT) + dot_f32(low[:, half:], second, NT)).astype(jnp.bfloat16)


def collect(core, slots, pieces, middle, gain, grad_logits, router, grad_y, mine, other):
    length, width = middle.shape
    last, half = mine.shape[0] - 1, mine.shape[2]
    f32, bf16 = jnp.float32, jnp.bfloat16
    weight = pl.BlockSpec((None, width, half), lambda i, core: (last, 0, 0))
    plain = [slots, *pieces, middle, gain.reshape(1, -1), grad_logits, router, grad_y]
    shapes = [((length, width), f32), ((length, width), bf16), ((length, width), bf16), ((8, width), f32)]
    return pl.pallas_call(
        lambda *refs: collect_kernel(*refs, count=len(pieces)),
        grid_spec=pltpu.PrefetchScalarGridSpec(
            num_scalar_prefetch=1,
            grid=(1,),
            in_specs=[whole(array.shape) for array in plain] + [weight, weight],
            out_specs=[whole(shape) for shape, _ in shapes],
            scratch_shapes=[pltpu.VMEM((sum(piece.shape[0] for piece in pieces), width), bf16)],
        ),
        out_shape=[jax.ShapeDtypeStruct(shape, kind) for shape, kind in shapes],
        compiler_params=pltpu.CompilerParams(vmem_limit_bytes=VMEM_BYTES),
        cost_estimate=cost(8),
        name="collect",
    )(core, *plain, mine, other)


def outer_halves_kernel(core, normed, attended, rights, last, *refs, count):
    aways, stays, normed_t, attended_t = refs[:2], refs[2:4], refs[4], refs[5]
    step = pl.program_id(0)

    @pl.when(step == 0)
    def _():
        normed_t[...] = normed[...].T
        attended_t[...] = attended[...].T

    for place in range(count + 1):

        @pl.when(step == place)
        def _():
            result = dot_f32(normed_t[...], rights[...]) if place < count else dot_f32(attended_t[...], last[...])
            result = result.astype(jnp.bfloat16)
            half = result.shape[1] // 2
            away, stay = aways[place // 2], stays[place // 2]
            slot = place % 2

            @pl.when(core[0] == 0)
            def _():
                stay[slot] = result[:, :half]
                away[slot] = result[:, half:]

            @pl.when(core[0] != 0)
            def _():
                away[slot] = result[:, :half]
                stay[slot] = result[:, half:]


def outer_halves(core, normed, attended, rights, last):
    length, width = normed.shape
    count, half = rights.shape[0], width // 2
    shape = jax.ShapeDtypeStruct((2, width, half), jnp.bfloat16)
    return pl.pallas_call(
        lambda *refs: outer_halves_kernel(*refs, count=count),
        grid_spec=pltpu.PrefetchScalarGridSpec(
            num_scalar_prefetch=1,
            grid=(count + 1,),
            in_specs=[
                whole((length, width)),
                whole((length, width)),
                pl.BlockSpec((None, length, width), lambda i, core: (jnp.minimum(i, count - 1), 0, 0)),
                whole((length, width)),
            ],
            out_specs=[whole(shape.shape)] * 4,
            scratch_shapes=[pltpu.VMEM((width, length), jnp.bfloat16)] * 2,
        ),
        out_shape=[shape] * 4,
        compiler_params=pltpu.CompilerParams(vmem_limit_bytes=VMEM_BYTES),
        cost_estimate=cost(2),
        name="outer_halves",
    )(core, normed, attended, rights, last)


def enter_kernel(
    core, grads, mine, other, tokens, gain, grad_middle, moe_parts, squares, normed, grad_logits, grad_input, small, total
):
    step = pl.program_id(0)
    first, second = halves(core[0], mine[...], other[...])
    half = first.shape[1]
    rows = grads[...]
    part = dot_f32(rows[:, :half], first, NT) + dot_f32(rows[:, half:], second, NT)

    @pl.when(step == 0)
    def _():
        total[...] = part

    @pl.when(step > 0)
    def _():
        total[...] += part

    @pl.when(step == pl.num_programs(0) - 1)
    def _():
        turned, gain_parts = norm_back(tokens[...].astype(jnp.float32), gain[...], total[...])
        grad_input[...] = grad_middle[...] + turned
        sums = [jnp.sum(part, axis=0, keepdims=True) for part in (moe_parts[...], gain_parts, squares[...])]
        sums.append(jnp.zeros((SMALL - len(sums), gain.shape[1]), jnp.float32))
        small[pl.ds(0, SMALL), :] = jnp.concatenate(sums)
        small[pl.ds(SMALL, grad_logits.shape[1]), :] = dot_f32(grad_logits[...], normed[...], TN)


def enter(core, grads, mine, other, tokens, gain, grad_middle, moe_parts, squares, normed, grad_logits):
    length, width = tokens.shape
    count, half, experts = grads.shape[0], mine.shape[2], grad_logits.shape[1]
    weight = pl.BlockSpec((None, width, half), lambda i, core: (i, 0, 0))
    plain = [tokens, gain.reshape(1, -1), grad_middle, moe_parts, squares, normed, grad_logits]
    shapes = [(length, width), (SMALL + experts, width)]
    return pl.pallas_call(
        enter_kernel,
        grid_spec=pltpu.PrefetchScalarGridSpec(
            num_scalar_prefetch=1,
            grid=(count,),
            in_specs=[pl.BlockSpec((None, length, width), lambda i, core: (i, 0, 0)), weight, weight]
            + [whole(array.shape) for array in plain],
            out_specs=[whole(shape) for shape in shapes],
            scratch_shapes=[pltpu.VMEM((length, width), jnp.float32)],
        ),
        out_shape=[jax.ShapeDtypeStruct(shape, jnp.float32) for shape in shapes],
        compiler_params=pltpu.CompilerParams(vmem_limit_bytes=VMEM_BYTES),
        cost_estimate=cost(6),
        name="enter",
    )(core, grads, mine, other, *plain)


BOUNDS = (12, 16, 23, 32, 46, 64, 91)
TOP_PRECISION = lax.Precision.HIGHEST
AXES = ("dp", "expert")
PAIR = 2


def after(value, *others):
    return lax.optimization_barrier((value, *others))[0] if others else value


def bucket_index(offset):
    distance = jnp.abs(offset)
    far_bucket = 8 + sum([(distance >= level).astype(jnp.int32) for level in BOUNDS])
    near_bucket = jnp.where(distance < 8, distance, far_bucket)
    return jnp.where(offset > 0, 16, 0) + near_bucket


def norm_apply(inputs, gain_vec):
    return inputs * lax.rsqrt(jnp.mean(inputs * inputs, axis=-1, keepdims=True) + EPS) * gain_vec


def tile_offsets(query_block, key_block):
    rows = query_block * BLOCK + lax.broadcasted_iota(jnp.int32, (BLOCK, BLOCK), 0)
    cols = key_block * BLOCK + lax.broadcasted_iota(jnp.int32, (BLOCK, BLOCK), 1)
    return rows, cols


def offset_bias(table):
    offsets = jnp.arange(4 * BLOCK, dtype=jnp.int32) - 2 * BLOCK
    hot = (bucket_index(offsets)[None] == jnp.arange(table.shape[1], dtype=jnp.int32)[:, None]).astype(jnp.float32)
    return jnp.dot(table, hot, precision=TOP_PRECISION)


def table_gradient(bands, buckets):
    rows, cols = tile_offsets(0, 0)
    ids = [jnp.full((BLOCK, BLOCK), bucket_far(), jnp.int32)]
    ids += [bucket_index(shift * BLOCK + cols - rows) for shift in (-1, 0, 1)]
    hot = (jnp.stack(ids)[..., None] == jnp.arange(buckets, dtype=jnp.int32)).astype(jnp.float32)
    return jnp.einsum("hdxy,dxyb->hb", bands, hot, precision=TOP_PRECISION)


def bucket_far():
    return 8 + len(BOUNDS)


def on_device(
    tokens,
    qkv_weight,
    out_weight,
    position_bias_table,
    gain_attn,
    gain_moe,
    router,
    w_in,
    w_out,
    routes,
    prefix,
    valid_mask,
    teacher,
    cotangent,
):
    length, width = tokens.shape
    bf16, f32 = jnp.bfloat16, jnp.float32
    expert_count = router.shape[1]
    top_count = routes.shape[1]
    groups = lax.axis_size("expert")
    copies = lax.axis_size("dp")
    inner = w_in.shape[2]
    capacity = 5 * length * top_count // (4 * expert_count)
    total_tokens = length * copies * groups
    sources = 2 * groups
    blocks = length // BLOCK
    here_dp, here_group = lax.axis_index("dp"), lax.axis_index("expert")
    half = (here_dp >> 1) & 1
    core = here_group & 1
    rest = copies // 4

    def swap(value, dp_mask, group_mask):
        pairs = [
            (i, ((i // groups) ^ dp_mask) * groups + ((i % groups) ^ group_mask))
            for i in range(copies * groups)
        ]
        return lax.ppermute(value, AXES, pairs)

    def bits(count):
        return [1 << place for place in range(count.bit_length() - 1)]

    def partial_sums(value):
        sums = []
        for masks in [(0, mask) for mask in bits(groups)] + [(mask, 0) for mask in bits(copies)]:
            value = value + swap(value, *masks)
            sums.append(value)
        return sums

    chips = groups

    def across(value, place):
        return swap(value, PAIR * (place // (groups // 2)), 2 * (place % (groups // 2)))

    def to_chips(pieces):
        return [pieces[0]] + [across(pieces[place], place) for place in range(1, chips)]

    def through(visit, sends):
        direct, relay = to_chips(sends[::2]), to_chips(sends[1::2])
        seen, direct = visit(direct)
        direct = to_chips(direct)
        relay = [after(part, seen) for part in relay]
        passed = visit(swap(jnp.concatenate(relay), 0, 1))
        return direct, [swap(after(part, *direct), 0, 1) for part in passed]

    def weave(direct, relay):
        return [part for pair in zip(direct, to_chips(relay)) for part in pair]

    ring = list(range(0, copies, 2)) + list(range(copies - 1, 0, -2))
    turns = [(1, step) for step in range(1, copies // 2 + 1)] + [(-1, step) for step in range(1, copies // 2)]

    def gather_ring(shard, due):
        got = [shard]
        for turn in (1, -1):
            held = shard
            pairs = [(ring[i], ring[(i + turn) % copies]) for i in range(copies)]
            for step in [step for way, step in turns if way == turn]:
                held = lax.ppermute(after(held, *due[step - 2 : step - 1]) if step > 1 else held, "dp", pairs)
                got.append(held)
        return got

    def ring_places():
        place = jnp.where(here_dp & 1 == 0, here_dp >> 1, copies - 1 - (here_dp >> 1))
        shift = jnp.array([0] + [turn * step for turn, step in turns], jnp.int32)
        place = (place - shift) & (copies - 1)
        return jnp.where(place < copies // 2, 2 * place, 2 * (copies - 1 - place) + 1).astype(jnp.int32)


    flat_routes = routes.reshape(-1)
    pair_count = length * top_count
    slot_count = sources * capacity
    route_hits = (flat_routes[:, None] == jnp.arange(expert_count, dtype=jnp.int32)[None, :]).astype(bf16)
    lower_ones = (
        lax.broadcasted_iota(jnp.int32, (pair_count, pair_count), 0)
        >= lax.broadcasted_iota(jnp.int32, (pair_count, pair_count), 1)
    ).astype(bf16)
    running = jnp.dot(lower_ones, route_hits, preferred_element_type=f32)
    pair_rank = jnp.sum((running - 1.0) * route_hits.astype(f32), axis=1).astype(jnp.int32)
    away = (flat_routes >> 1) ^ here_group
    chip = ((flat_routes & 1) ^ half) * (groups // 2) + (away >> 1)
    slots = ((chip * 2 + (away & 1)) * capacity + pair_rank).reshape(length, top_count)
    slots_t = slots.T

    resid = tokens.astype(f32)
    normed1 = norm_apply(resid, gain_attn).astype(bf16)
    columns = width // 2
    core_index = core.reshape(1).astype(jnp.int32)
    valid_rows = valid_mask.astype(f32)[:, None]
    counts = [jnp.broadcast_to(jnp.sum(valid_rows), (8, 128))]
    count_trades = [(0, mask) for mask in bits(groups)] + [(mask, 0) for mask in bits(copies)]

    def count_beside(before, value):
        if len(counts) > len(count_trades):
            return value
        counts.append(counts[-1] + swap(after(counts[-1], before), *count_trades[len(counts) - 1]))
        return after(value, counts[-1])

    shards = [
        lax.dynamic_slice_in_dim(part, core * columns, columns, 2)
        for part in (qkv_weight[:2], jnp.concatenate([qkv_weight[2:], out_weight[None]]))
    ]
    if copies > 8:
        mine = lax.all_gather(jnp.concatenate(shards), "dp", axis=1, tiled=True)
    else:
        mine = join(ring_places(), [gather_ring(shards[0], ()), gather_ring(shards[1], (slots_t, normed1))])
    other = count_beside(mine, swap(mine, 0, 1))
    qkv_rows = count_beside(other, project(core_index, normed1, mine, other, 3))
    offsets = offset_bias(position_bias_table)
    attended, probs = attention_forward(position_bias_table[:, bucket_far()], prefix, qkv_rows, offsets)
    middle, normed2, gates, *sends = route(
        core_index, count_beside(qkv_rows, attended), tokens, mine, other, gain_moe, router, routes, slots_t, 2 * chips, capacity
    )

    pick = half.reshape(1).astype(jnp.int32)
    hidden, slopes, rows_in = [], [], []

    def expert(pieces):
        one = not isinstance(pieces, list)
        pieces = [pieces] if one else pieces
        hidden_t, slope, rows_t, *results = expert_forward(pick, pieces, chips, w_in, w_out)
        hidden_t = count_beside(pieces[-1], hidden_t)
        for kept, value in zip((hidden, slopes, rows_in), (hidden_t, slope, rows_t)):
            kept.append(value)
        return results if one else (hidden_t, results)

    back = weave(*through(expert, sends))
    while len(counts) <= len(count_trades):
        back[0] = count_beside(back[0], back[0])
    valid_count = counts[-1][0, 0]
    scale = (total_tokens / valid_count).reshape(1, 1)
    output, grad_y, grad_logits, squares, *sends = combine(
        slots, slots_t, scale, back, middle, teacher, cotangent, valid_rows, gates, routes, expert_count
    )

    out_rows = inner // copies
    in_rows = width // copies
    far_bit = here_dp % 2
    slices = jnp.arange(rest, dtype=jnp.int32) * 4

    def picks(bit0):
        return jnp.concatenate([slices + ((half ^ other_half) * 2 + bit0) for other_half in (1, 0)]).astype(jnp.int32)

    sent, kept = picks(1 - far_bit), picks(far_bit)

    def add(left, right):
        return (left.astype(f32) + right.astype(f32)).astype(bf16)

    def fold(unit, bit, axis=0):
        unit = unit.reshape(unit.shape[:axis] + (2, unit.shape[axis] // 2) + unit.shape[axis + 1 :])
        away_part = lax.dynamic_index_in_dim(unit, 1 - bit, axis, keepdims=False)
        return away_part, lax.dynamic_index_in_dim(unit, bit, axis, keepdims=False)

    far_masks = list(reversed(bits(copies)[2:]))

    def near_add(got, keep):
        away_part, stay_part = fold(add(got, keep), (here_dp // far_masks[0]) % 2)
        return away_part, stay_part

    def far_trade(away_part):
        return swap(away_part, far_masks[0], 0)

    def finish(got, stay):
        unit = add(got, stay)
        for mask in far_masks[1:]:
            away_part, stay_part = fold(unit, (here_dp // mask) % 2)
            unit = add(swap(away_part, mask, 0), stay_part)
        return unit[0]

    plan_a, plan_b, plan_c = ((0, 0), (0, 1)), ((0, 2), (1, 0)), ((1, 1), (1, 2))
    plan_d, plan_e, plan_f = plan_a, plan_b, plan_c
    out_plans, in_plans = (plan_a, plan_b, plan_c), (plan_d, plan_e, plan_f)

    grad_rows, grad_pre, parts = [], [], []

    def expert_back(pieces):
        if isinstance(pieces, list):
            grad_pre_rows, grads, *results = expert_backward(pick, pieces, chips, w_in, w_out, slopes[0])
            grad_rows.append(grads)
            grad_pre.append(grad_pre_rows)
            return grad_pre_rows, results
        grad_rows.append(pieces)
        parts.extend(weight_part(sent, hidden, grad_rows, out_rows, out_plans, rest, width))
        parts[0] = swap(parts[0], 1, 0)
        pieces = after(pieces, parts[1])
        grad_pre_rows, _, *results = expert_backward(pick, [pieces], chips, w_in, w_out, slopes[1])
        grad_pre.append(grad_pre_rows)
        return results

    direct, relay = through(expert_back, sends)
    got_a, send_b, send_c = parts
    relay = [after(part, got_a) for part in relay]
    got_b = swap(after(send_b, relay[0]), 1, 0)
    back = weave(direct, relay)
    grad_rows, grad_pre = lax.optimization_barrier((grad_rows, grad_pre, relay))[:2]
    keep_a, keep_b, keep_c = weight_part(kept, hidden, grad_rows, out_rows, out_plans, rest, width)
    away_a, stay_a = near_add(got_a, keep_a)
    far_a = far_trade(away_a)
    send_d, send_e, send_f = weight_part(sent, rows_in, after(grad_pre, away_a), in_rows, in_plans, rest, inner // 2)
    back = [after(part, send_d) for part in back]
    got_c = swap(after(send_c, send_d), 1, 0)
    grad_middle, grad_attn_proj, grad_attended, gain_moe_parts = collect(
        core_index, slots, back, middle, gain_moe, grad_logits, router, grad_y, mine, other
    )
    away_b, stay_b = near_add(after(got_b, grad_attended), keep_b)
    got_d = swap(after(send_d, grad_attended), 1, 0)
    grad_attended, away_b = lax.optimization_barrier((grad_attended, away_b))
    grad_qkv_rows, bands = attention_backward(qkv_rows, grad_attended, probs)
    grad_qkv_rows, got_c, far_a = lax.optimization_barrier((grad_qkv_rows, got_c, far_a))
    done_a = finish(far_a, stay_a)

    away_c, stay_c = near_add(got_c, keep_c)
    far_c = far_trade(jnp.concatenate([away_b, away_c], axis=1))
    stay_c = jnp.concatenate([stay_b, stay_c], axis=1)
    *weights_away, stay_1, stay_2 = outer_halves(
        core_index, normed1, attended, after(grad_qkv_rows, away_c), grad_attn_proj
    )
    weights_away, got_d = lax.optimization_barrier((weights_away, got_d))
    got_e = swap(after(send_e, got_d), 1, 0)
    group_masks = bits(groups)[1:]
    dp_masks = bits(copies)

    def over_dp(total, mask, passed):
        axis = 1 + sorted([other for other in dp_masks if other not in passed], reverse=True).index(mask)
        bit = (here_dp // mask) % 2
        away_part = lax.dynamic_index_in_dim(total, 1 - bit, axis, keepdims=False)
        stay_part = lax.dynamic_index_in_dim(total, bit, axis, keepdims=False)
        return away_part, swap(away_part, mask, 0), stay_part

    weights_got = [swap(part, 0, 1) for part in weights_away]
    halves_sum = [
        add(got, stay).reshape(2, copies, in_rows, columns) for got, stay in zip(weights_got, (stay_1, stay_2))
    ]
    for mask in group_masks[:-1]:
        folded = [fold(part, (here_group // mask) % 2, 2) for part in halves_sum]
        halves_sum = [add(swap(away_part, 0, mask), stay_part) for away_part, stay_part in folded]
    folded = [fold(part, (here_group // group_masks[-1]) % 2, 2) for part in halves_sum]
    y_stay = jnp.concatenate([stay_part for _, stay_part in folded])
    y_away = jnp.concatenate([away_part for away_part, _ in folded])
    y_got = swap(y_away, 0, group_masks[-1])
    keep_d, keep_e, keep_f = weight_part(
        kept, rows_in, after(grad_pre, y_away), in_rows, in_plans, rest, inner // 2, 40
    )
    away_d, stay_d = near_add(got_d, keep_d)
    far_d = far_trade(after(away_d, far_c))
    away_e, stay_e = near_add(after(got_e, away_d), keep_e)
    done_c = finish(after(far_c, away_e), stay_c)
    total = add(after(y_got, away_e), y_stay)
    total = total.reshape((4,) + (2,) * len(dp_masks) + (-1, columns))


    small_trades = [(0, 1), (0, group_masks[0])] + [(mask, 0) for mask in reversed(dp_masks)]
    small_trades += [(0, mask) for mask in group_masks[1:]]
    passed_masks = []
    for mask in dp_masks:
        gone, got, stay = over_dp(total, mask, passed_masks)
        passed_masks.append(mask)
        if len(passed_masks) == 1:
            grad_input, small = enter(
                core_index,
                after(grad_qkv_rows, gone),
                mine,
                other,
                tokens,
                gain_attn,
                grad_middle,
                gain_moe_parts,
                squares,
                normed2,
                grad_logits,
            )
            grad_table = table_gradient(after(bands, gone), position_bias_table.shape[1])
            flat = lax.dynamic_update_slice(small, grad_table.reshape(1, -1), (3, 0))
        for _ in range((0, 2, 1)[min(len(passed_masks), 3) - 1]):
            flat = flat + swap(after(flat, gone), *small_trades.pop(0))
        if len(passed_masks) == 1:
            far_e = far_trade(after(away_e, gone))
            got_f = swap(after(send_f, got), 1, 0)
            out_theirs = swap(after(jnp.concatenate([done_a, done_c[:1]]), gone), PAIR, 0)
            got = after(got, out_theirs)
        elif mask == PAIR:
            got = after(got, far_d, far_e)
            done_e = finish(far_e, stay_e)
        elif len(passed_masks) == len(dp_masks):
            away_f, stay_f = near_add(after(got_f, stay), keep_f)
            far_f = far_trade(after(away_f, got))
            got = after(got, away_f, in_first)
            done_f = finish(far_f, stay_f)
        total = add(got, stay)
        if mask == PAIR:
            done_d = finish(after(far_d, total), stay_d)
            in_first = swap(done_d, PAIR, 0)
        flat = after(flat, total)
    in_theirs = jnp.concatenate([in_first, swap(done_e[:1], PAIR, 0)])
    for mask in reversed(group_masks):
        bit = (here_group // mask) % 2
        other_part = swap(total, 0, mask)
        total = jnp.concatenate([jnp.where(bit == 0, total, other_part), jnp.where(bit == 0, other_part, total)], axis=1)
        flat = flat + swap(flat, *small_trades.pop(0))
        total, flat = lax.optimization_barrier((total, flat))
    other_part = swap(total, 0, 1)
    for trade in small_trades:
        flat = flat + swap(flat, *trade)
    total = jnp.concatenate([jnp.where(core == 0, total, other_part), jnp.where(core == 0, other_part, total)], axis=2)
    weights_done = total.astype(f32)
    grad_qkv, grad_out_weight = weights_done[:3], weights_done[3]
    grad_gain_moe, grad_gain_attn, square_total = flat[0], flat[1], jnp.sum(flat[2])
    grad_table = flat[3, : grad_table.size].reshape(grad_table.shape)
    grad_router = flat[SMALL:].T

    out_mine, in_mine = done_c[1:], jnp.concatenate([done_e[1:], done_f])

    def both_experts(mine, theirs):
        mine, theirs = [part.reshape(-1, part.shape[-1]).astype(f32) for part in (mine, theirs)]
        return jnp.stack([jnp.where(half == 0, mine, theirs), jnp.where(half == 0, theirs, mine)])

    grad_w_out = both_experts(out_mine, out_theirs)
    grad_w_in = both_experts(in_mine, in_theirs)

    distill_loss = square_total / (width * valid_count)
    return (
        output.astype(bf16),
        distill_loss,
        grad_input,
        grad_qkv,
        grad_out_weight,
        grad_w_in,
        grad_w_out,
        grad_router,
        grad_table,
        grad_gain_attn,
        grad_gain_moe,
    )


def solution(mesh):
    rows = P(AXES, None)
    return jax.shard_map(
        on_device,
        mesh=mesh,
        in_specs=(
            rows,
            P(None, "dp", None),
            P("dp", None),
            P(),
            P(),
            P(),
            P(),
            P("expert", None, None),
            P("expert", None, None),
            rows,
            P(AXES),
            P(AXES),
            rows,
            rows,
        ),
        out_specs=(
            rows,
            P(),
            rows,
            P(None, "dp", None),
            P("dp", None),
            P("expert", "dp", None),
            P("expert", "dp", None),
            P(),
            P(),
            P(),
            P(),
        ),
        check_vma=False,
    )
```
